32 devices in a mesh: dp: 4 (over y, x), row: 2 (over core), col: 4 (over z).
Axes of the slice: x: 2, y: 2, z: 4, core: 2. Of those that a mesh axis runs over, the one named last changes fastest.
Arguments:
- tokens: bfloat16 [16384, 1024], P(('dp', 'row'), 'col'), may hold values from -16 to 16
- encoder: bfloat16 [4096, 1024], P(('dp', 'row'), 'col'), may hold values from -6 to 6
- cotangent: bfloat16 [16384, 1024], P(('dp', 'row'), 'col'), may hold values from -6 to 6
- dec_lengths: int32 [4, 4], P('dp'), may hold values from 1 to 3070, as said below
- src_lengths: int32 [4, 4], P('dp'), may hold values from 113 to 351, as said below
- self_norm_gain: float32 [1024], P('col'), may hold values from 0.25 to 1.75
- self_norm_bias: float32 [1024], P('col'), may hold values from -1.8 to 1.8
- self_query: bfloat16 [1024, 1024], P('col', 'row'), may hold values from -0.1875 to 0.1875
- self_key: bfloat16 [1024, 1024], P('col', 'row'), may hold values from -0.1875 to 0.1875
- self_value: bfloat16 [1024, 1024], P('col', 'row'), may hold values from -0.1875 to 0.1875
- self_query_bias: float32 [1024], P(('row', 'col')), may hold values from -1.8 to 1.8
- self_value_bias: float32 [1024], P(('row', 'col')), may hold values from -1.8 to 1.8
- self_out: bfloat16 [1024, 1024], P('row', 'col'), may hold values from -3 to 3
- self_out_bias: float32 [1024], P('col'), may hold values from -1.8 to 1.8
- cross_norm_gain: float32 [1024], P('col'), may hold values from 0.25 to 1.75
- cross_norm_bias: float32 [1024], P('col'), may hold values from -1.8 to 1.8
- cross_query: bfloat16 [1024, 1024], P('col', 'row'), may hold values from -0.1875 to 0.1875
- cross_key: bfloat16 [1024, 1024], P('col', 'row'), may hold values from -0.1875 to 0.1875
- cross_value: bfloat16 [1024, 1024], P('col', 'row'), may hold values from -0.1875 to 0.1875
- cross_query_bias: float32 [1024], P(('row', 'col')), may hold values from -1.8 to 1.8
- cross_value_bias: float32 [1024], P(('row', 'col')), may hold values from -1.8 to 1.8
- cross_out: bfloat16 [1024, 1024], P('row', 'col'), may hold values from -3 to 3
- cross_out_bias: float32 [1024], P('col'), may hold values from -1.8 to 1.8
- hidden_norm_gain: float32 [1024], P('col'), may hold values from 0.25 to 1.75
- hidden_norm_bias: float32 [1024], P('col'), may hold values from -1.8 to 1.8
- hidden_in: bfloat16 [1024, 8192], P('col', 'row'), may hold values from -0.1875 to 0.1875
- hidden_in_bias: float32 [8192], P(('row', 'col')), may hold values from -1.8 to 1.8
- hidden_out: bfloat16 [8192, 1024], P('row', 'col'), may hold values from -0.0625 to 0.0625
- hidden_out_bias: float32 [1024], P('col'), may hold values from -1.8 to 1.8
Outputs:
- layer_out: bfloat16 [16384, 1024], P(('dp', 'row'), 'col')
- tokens_grad: float32 [16384, 1024], P(('dp', 'row'), 'col')
- encoder_grad: float32 [4096, 1024], P(('dp', 'row'), 'col')
- self_norm_gain_grad: float32 [1024], P('col')
- self_norm_bias_grad: float32 [1024], P('col')
- self_query_grad: float32 [1024, 1024], P('col', 'row')
- self_key_grad: float32 [1024, 1024], P('col', 'row')
- self_value_grad: float32 [1024, 1024], P('col', 'row')
- self_query_bias_grad: float32 [1024], P(('row', 'col'))
- self_value_bias_grad: float32 [1024], P(('row', 'col'))
- self_out_grad: float32 [1024, 1024], P('row', 'col')
- self_out_bias_grad: float32 [1024], P('col')
- cross_norm_gain_grad: float32 [1024], P('col')
- cross_norm_bias_grad: float32 [1024], P('col')
- cross_query_grad: float32 [1024, 1024], P('col', 'row')
- cross_key_grad: float32 [1024, 1024], P('col', 'row')
- cross_value_grad: float32 [1024, 1024], P('col', 'row')
- cross_query_bias_grad: float32 [1024], P(('row', 'col'))
- cross_value_bias_grad: float32 [1024], P(('row', 'col'))
- cross_out_grad: float32 [1024, 1024], P('row', 'col')
- cross_out_bias_grad: float32 [1024], P('col')
- hidden_norm_gain_grad: float32 [1024], P('col')
- hidden_norm_bias_grad: float32 [1024], P('col')
- hidden_in_grad: float32 [1024, 8192], P('col', 'row')
- hidden_in_bias_grad: float32 [8192], P(('row', 'col'))
- hidden_out_grad: float32 [8192, 1024], P('row', 'col')
- hidden_out_bias_grad: float32 [1024], P('col')
The draws below stay inside these ranges and needn't reach their ends.
Inputs may be any that keep to these rules, and one draw needn't show every extreme that they name: `dec_lengths`: row s holds the lengths of the 4 documents of sequence s laid end to end from its first position; the remaining 4096 minus their sum positions, 1 to 512 of them, are padding. `src_lengths`: row s holds the lengths of the 4 source documents of sequence s laid end to end from its first encoder position; the remaining 1024 minus their sum positions, 1 to 128 of them, are padding. Decoder document k reads source document k, decoder padding reads source padding.
All inputs are finite; a program needn't handle non-finite values.
Results may differ from the reference program's by a relative error of at most 0.025.
Values may be sent and summed in bfloat16 or wider, within the bound.
A program may use at most 384 MiB of HBM per device.

```python
import math
import jax
import jax.numpy as jnp
from jax import lax

D = 1024
HEAD_DIM = 64
FF = 8192
SEQ_LEN = 4096
ENC = 1024
WIN = 1024
TOKENS = 16384
ENC_TOKENS = 4096
SEQS_ALL = 4


def draw_tokens(key, part):
    key = jax.random.fold_in(key, 3)
    subkeys = jax.random.split(key, 3)
    places = jnp.arange(D, dtype=jnp.float32) / D - 0.5
    row_scale = jnp.exp(jax.random.uniform(subkeys[1], (TOKENS, 1), jnp.float32, math.log(0.3), math.log(3.0)))
    jitter = jax.random.uniform(subkeys[2], (D,), jnp.float32, -0.6, 0.6)
    column_scale = jnp.exp(math.log(3.0) * places + jitter)
    values = jax.random.normal(subkeys[0], (TOKENS, D), jnp.float32)
    return jnp.clip(values * row_scale * column_scale, -16.0, 16.0).astype(jnp.bfloat16)


def draw_dec_lengths(key, part):
    key = jax.random.fold_in(key, 5)
    subkeys = jax.random.split(key, 5)
    numbers = jnp.arange(SEQS_ALL, dtype=jnp.int32)
    padding = jax.random.randint(subkeys[0], (SEQS_ALL,), 1, SEQ_LEN // 8 + 1, dtype=jnp.int32)
    chosen = jax.random.randint(subkeys[1], (), 0, SEQS_ALL, dtype=jnp.int32)
    widest = (chosen + 1) % SEQS_ALL
    padding = jnp.where(numbers == chosen, SEQ_LEN // 8, padding)
    padding = jnp.where(numbers == widest, 1, padding)
    filled = SEQ_LEN - padding
    middle = SEQ_LEN // 2
    opening = jax.random.randint(subkeys[2], (SEQS_ALL,), SEQ_LEN // 4, middle, dtype=jnp.int32)
    opening = jnp.where(numbers == widest, SEQ_LEN // 4, opening)
    closing = jax.random.randint(subkeys[3], (SEQS_ALL,), middle + 1, filled, dtype=jnp.int32)
    closing = jnp.where(numbers == widest, filled - 1, closing)
    first_cut = jax.random.randint(subkeys[4], (SEQS_ALL,), 1, opening, dtype=jnp.int32)
    first_cut = jnp.where(numbers == widest, 1, first_cut)
    return jnp.stack([first_cut, opening - first_cut, closing - opening, filled - closing], axis=1)


def draw_src_lengths(key, part):
    key = jax.random.fold_in(key, 7)
    subkeys = jax.random.split(key, 5)
    numbers = jnp.arange(SEQS_ALL, dtype=jnp.int32)
    padding = jax.random.randint(subkeys[0], (SEQS_ALL,), 1, ENC // 8 + 1, dtype=jnp.int32)
    chosen = jax.random.randint(subkeys[1], (), 0, SEQS_ALL, dtype=jnp.int32)
    widest = (chosen + 1) % SEQS_ALL
    padding = jnp.where(numbers == chosen, ENC // 8, padding)
    padding = jnp.where(numbers == widest, 1, padding)
    filled = ENC - padding
    quarter = (ENC - ENC // 8) // 4
    jiggle = max(quarter // 2, 2)
    first_shift = jax.random.randint(subkeys[2], (SEQS_ALL,), 0, jiggle, dtype=jnp.int32)
    first_shift = jnp.where((numbers == chosen) | (numbers == widest), jiggle - 1, first_shift)
    second_shift = jax.random.randint(subkeys[3], (SEQS_ALL,), 0, jiggle, dtype=jnp.int32)
    second_shift = jnp.where(numbers == chosen, 0, second_shift)
    third_shift = jax.random.randint(subkeys[4], (SEQS_ALL,), 0, jiggle, dtype=jnp.int32)
    third_shift = jnp.where(numbers == widest, 0, third_shift)
    third_shift = jnp.where(numbers == chosen, jiggle - 1, third_shift)
    first_cut = quarter + first_shift
    second_cut = 2 * quarter + second_shift
    third_cut = 3 * quarter + third_shift
    return jnp.stack([first_cut, second_cut - first_cut, third_cut - second_cut, filled - third_cut], axis=1)


def level_of(own_key, shape, shards, low, largest):
    loudness, own = 1.0, jax.random.fold_in(own_key, 6)
    for axis_at, parts in shards:
        steps = jnp.exp(jax.random.uniform(jax.random.fold_in(own, axis_at), (parts,), jnp.float32, low / len(shards), largest / len(shards)))
        loudness = loudness * jnp.repeat(steps, shape[axis_at] // parts).reshape([-1 if axis == axis_at else 1 for axis in range(len(shape))])
    return loudness


def bell_draw(rng, dims, deviation, bound, cuts=(), kind=jnp.bfloat16):
    entries = jax.random.normal(rng, dims, jnp.float32) * deviation
    if len(cuts) > 0:
        entries = level_of(rng, dims, cuts, -0.22, 0.18) * entries
    return jnp.clip(entries, min=-bound, max=bound).astype(kind)


def setup_inputs(seed: int = 0) -> dict:
    key_list = jax.random.split(jax.random.key(seed), 30)
    return {
        "tokens": draw_tokens(jax.random.fold_in(key_list[29], 71), 0),
        "encoder": bell_draw(key_list[1], (ENC_TOKENS, D), 1.0, 6.0, ((0, 8), (1, 4))),
        "cotangent": bell_draw(key_list[2], (TOKENS, D), 1.0, 6.0, ((0, 8), (1, 4))),
        "dec_lengths": draw_dec_lengths(jax.random.fold_in(key_list[29], 71), 0),
        "src_lengths": draw_src_lengths(jax.random.fold_in(key_list[29], 71), 0),
        "self_norm_gain": jnp.clip(1.0 + 0.15 * jax.random.normal(key_list[5], (D,), jnp.float32), 0.25, 1.75),
        "self_norm_bias": bell_draw(key_list[6], (D,), 0.3, 1.8, ((0, 4),), jnp.float32),
        "self_query": bell_draw(key_list[7], (D, D), D ** -0.5, 0.1875, ((0, 4), (1, 2))),
        "self_key": bell_draw(key_list[8], (D, D), D ** -0.5, 0.1875, ((0, 4), (1, 2))),
        "self_value": bell_draw(key_list[9], (D, D), D ** -0.5, 0.1875, ((0, 4), (1, 2))),
        "self_query_bias": bell_draw(key_list[10], (D,), 0.3, 1.8, ((0, 8),), jnp.float32),
        "self_value_bias": bell_draw(key_list[11], (D,), 0.3, 1.8, ((0, 8),), jnp.float32),
        "self_out": bell_draw(key_list[12], (D, D), (max(1, D // 256)) ** -0.5, 3.0, ((0, 2), (1, 4))),
        "self_out_bias": bell_draw(key_list[13], (D,), 0.3, 1.8, ((0, 4),), jnp.float32),
        "cross_norm_gain": jnp.clip(1.0 + 0.15 * jax.random.normal(key_list[14], (D,), jnp.float32), 0.25, 1.75),
        "cross_norm_bias": bell_draw(key_list[15], (D,), 0.3, 1.8, ((0, 4),), jnp.float32),
        "cross_query": bell_draw(key_list[16], (D, D), D ** -0.5, 0.1875, ((0, 4), (1, 2))),
        "cross_key": bell_draw(key_list[17], (D, D), D ** -0.5, 0.1875, ((0, 4), (1, 2))),
        "cross_value": bell_draw(key_list[18], (D, D), D ** -0.5, 0.1875, ((0, 4), (1, 2))),
        "cross_query_bias": bell_draw(key_list[19], (D,), 0.3, 1.8, ((0, 8),), jnp.float32),
        "cross_value_bias": bell_draw(key_list[20], (D,), 0.3, 1.8, ((0, 8),), jnp.float32),
        "cross_out": bell_draw(key_list[21], (D, D), (max(1, D // 256)) ** -0.5, 3.0, ((0, 2), (1, 4))),
        "cross_out_bias": bell_draw(key_list[22], (D,), 0.3, 1.8, ((0, 4),), jnp.float32),
        "hidden_norm_gain": jnp.clip(1.0 + 0.15 * jax.random.normal(key_list[23], (D,), jnp.float32), 0.25, 1.75),
        "hidden_norm_bias": bell_draw(key_list[24], (D,), 0.3, 1.8, ((0, 4),), jnp.float32),
        "hidden_in": bell_draw(key_list[25], (D, FF), D ** -0.5, 0.1875, ((0, 4), (1, 2))),
        "hidden_in_bias": bell_draw(key_list[26], (FF,), 0.3, 1.8, ((0, 8),), jnp.float32),
        "hidden_out": bell_draw(key_list[27], (FF, D), FF ** -0.5, 0.0625, ((0, 2), (1, 4))),
        "hidden_out_bias": bell_draw(key_list[28], (D,), 0.3, 1.8, ((0, 4),), jnp.float32),
    }


norm_epsilon = 1e-05
masked_fill = -1e+30

@jax.custom_vjp
def low(v):
    return lax.optimization_barrier(v.astype(jnp.bfloat16)).astype(jnp.float32)

@jax.custom_vjp
def low_back(v):
    return v

def low_keep(v):
    return (low(v), None)

def low_pass(kept, grad):
    return (grad,)

def back_keep(v):
    return (v, None)

def back_low(kept, grad):
    return (low(grad),)
low.defvjp(low_keep, low_pass)
low_back.defvjp(back_keep, back_low)

def product(left_side, right_side):
    return jnp.dot(left_side, right_side, precision=lax.Precision.HIGHEST, preferred_element_type=jnp.float32)

def layer_norm(stream, norm_gain, norm_bias):
    center = lax.optimization_barrier(jnp.mean(stream, axis=1, keepdims=True))
    spread = lax.optimization_barrier(jnp.mean(stream * stream, axis=1, keepdims=True)) - center * center
    return (stream - center) * lax.rsqrt(spread + norm_epsilon) * norm_gain + norm_bias

def doc_numbers(lengths, positions):
    bounds = jnp.cumsum(lengths, axis=1, dtype=jnp.int32)
    places = jnp.arange(positions, dtype=jnp.int32)
    return lax.optimization_barrier(jnp.sum((places[None, :, None] >= bounds[:, None, :]).astype(jnp.int32), axis=2, dtype=jnp.int32))

def attention(queries, keys_all, values_all, query_ids, key_ids, windowed):
    sequences = query_ids.shape[0]
    length = query_ids.shape[1]
    key_len = key_ids.shape[1]
    query_rows = min(512, length)
    blocks_per = length // query_rows
    heads_all = queries.shape[1] // HEAD_DIM
    query_heads = queries.reshape(sequences, length, heads_all, HEAD_DIM)
    key_heads = keys_all.reshape(sequences, key_len, heads_all, HEAD_DIM)
    value_heads = values_all.reshape(sequences, key_len, heads_all, HEAD_DIM)
    scaling = HEAD_DIM ** (-0.5)

    def one_block(number):
        zero_index = jnp.zeros((), jnp.int32)
        sequence = (number // blocks_per).astype(jnp.int32)
        begin_row = (number % blocks_per * query_rows).astype(jnp.int32)
        query_block = lax.dynamic_slice(query_heads, (sequence, begin_row, zero_index, zero_index), (1, query_rows, heads_all, HEAD_DIM))[0]
        key_block = lax.dynamic_index_in_dim(key_heads, sequence, 0, keepdims=False)
        value_block = lax.dynamic_index_in_dim(value_heads, sequence, 0, keepdims=False)
        query_doc = lax.dynamic_slice(query_ids, (sequence, begin_row), (1, query_rows))[0]
        key_doc = lax.dynamic_index_in_dim(key_ids, sequence, 0, keepdims=False)
        allowed = query_doc[:, None] == key_doc[None, :]
        if windowed:
            distance = begin_row + jnp.arange(query_rows, dtype=jnp.int32)[:, None] - jnp.arange(key_len, dtype=jnp.int32)[None, :]
            allowed = allowed & (distance >= 0) & (distance < WIN)
        scores = low_back(jnp.einsum('qhd,khd->hqk', query_block, key_block, precision=lax.Precision.HIGHEST) * scaling)
        masked = jnp.where(allowed[None], scores, masked_fill)
        highest = lax.optimization_barrier(jnp.max(masked, axis=2, keepdims=True))
        log_total = jnp.log(lax.optimization_barrier(jnp.sum(jnp.exp(masked - highest), axis=2, keepdims=True))) + highest
        shares = low(jnp.exp(masked - log_total))
        return jnp.einsum('hqk,khd->qhd', shares, value_block, precision=lax.Precision.HIGHEST)
    blocks = lax.map(jax.checkpoint(one_block), jnp.arange(sequences * blocks_per, dtype=jnp.int32))
    return blocks.reshape(sequences * length, heads_all * HEAD_DIM)

def reference(tokens, encoder, cotangent, dec_lengths, src_lengths, self_norm_gain, self_norm_bias, self_query, self_key, self_value, self_query_bias, self_value_bias, self_out, self_out_bias, cross_norm_gain, cross_norm_bias, cross_query, cross_key, cross_value, cross_query_bias, cross_value_bias, cross_out, cross_out_bias, hidden_norm_gain, hidden_norm_bias, hidden_in, hidden_in_bias, hidden_out, hidden_out_bias):
    query_ids = doc_numbers(dec_lengths, SEQ_LEN)
    source_ids = doc_numbers(src_lengths, ENC)

    def forward(stream, states, self_norm_gain, self_norm_bias, self_query, self_key, self_value, self_query_bias, self_value_bias, self_out, self_out_bias, cross_norm_gain, cross_norm_bias, cross_query, cross_key, cross_value, cross_query_bias, cross_value_bias, cross_out, cross_out_bias, hidden_norm_gain, hidden_norm_bias, hidden_in, hidden_in_bias, hidden_out, hidden_out_bias):
        normed = low(layer_norm(stream, self_norm_gain, self_norm_bias))
        queries = low(low_back(product(normed, self_query) + self_query_bias))
        keys_all = low(low_back(product(normed, self_key)))
        values_all = low(low_back(product(normed, self_value) + self_value_bias))
        mixed_out = low(low_back(attention(queries, keys_all, values_all, query_ids, query_ids, True)))
        after_self = stream + low_back(product(mixed_out, self_out) + self_out_bias)
        normed = low(layer_norm(after_self, cross_norm_gain, cross_norm_bias))
        queries = low(low_back(product(normed, cross_query) + cross_query_bias))
        keys_all = low(low_back(product(states, cross_key)))
        values_all = low(low_back(product(states, cross_value) + cross_value_bias))
        mixed_out = low(low_back(attention(queries, keys_all, values_all, query_ids, source_ids, False)))
        after_cross = after_self + low_back(product(mixed_out, cross_out) + cross_out_bias)
        normed = low(layer_norm(after_cross, hidden_norm_gain, hidden_norm_bias))
        hidden_pre = low_back(product(normed, hidden_in) + hidden_in_bias)
        activated = low(jax.nn.gelu(hidden_pre))
        return after_cross + low_back(product(activated, hidden_out) + hidden_out_bias)
    inputs = tuple((argument.astype(jnp.float32) for argument in (tokens, encoder, self_norm_gain, self_norm_bias, self_query, self_key, self_value, self_query_bias, self_value_bias, self_out, self_out_bias, cross_norm_gain, cross_norm_bias, cross_query, cross_key, cross_value, cross_query_bias, cross_value_bias, cross_out, cross_out_bias, hidden_norm_gain, hidden_norm_bias, hidden_in, hidden_in_bias, hidden_out, hidden_out_bias)))
    result, pullback = jax.vjp(forward, *inputs)
    gradients = pullback(cotangent.astype(jnp.float32))
    return (result.astype(jnp.bfloat16), gradients[0], gradients[1], gradients[2], gradients[3], gradients[4], gradients[5], gradients[6], gradients[7], gradients[8], gradients[9], gradients[10], gradients[11], gradients[12], gradients[13], gradients[14], gradients[15], gradients[16], gradients[17], gradients[18], gradients[19], gradients[20], gradients[21], gradients[22], gradients[23], gradients[24], gradients[25])
```

```python
import functools

import jax
import jax.numpy as jnp
from jax import lax
from jax.experimental import pallas as pl
from jax.experimental.pallas import tpu as pltpu
from jax.sharding import PartitionSpec as P

D = 1024
HEAD_DIM = 64
SEQ_LEN = 4096
ENC = 1024
WIN = 1024

norm_epsilon = 1e-05
masked_fill = -1e30
low = jnp.bfloat16
f32 = jnp.float32
PARTS = 4
PAIR = 2 * HEAD_DIM
QUERY_ROWS = 256
VMEM = 56 * 1024 * 1024


def doc_numbers(lengths, positions):
    bounds = jnp.cumsum(lengths, axis=1, dtype=jnp.int32)
    places = jnp.arange(positions, dtype=jnp.int32)
    return jnp.sum(
        (places[None, :, None] >= bounds[:, None, :]).astype(jnp.int32), axis=2, dtype=jnp.int32
    )


def mm(a, b):
    return lax.dot_general(a, b, (((1,), (0,)), ((), ())), preferred_element_type=f32)


def mm_nt(a, b):
    return lax.dot_general(a, b, (((1,), (1,)), ((), ())), preferred_element_type=f32)


def mm_tn(a, b):
    return lax.dot_general(a, b, (((0,), (0,)), ((), ())), preferred_element_type=f32)


def head_masks():
    lane = lax.broadcasted_iota(jnp.int32, (1, PAIR), 1)
    first = jnp.where(lane < HEAD_DIM, 1.0, 0.0)
    return first.astype(low), (1.0 - first).astype(low), lane < HEAD_DIM


def attend_kernel(q_ref, k_ref, v_ref, qid_ref, kid_ref, o_ref, lse_ref, bias, *, span, windowed):
    rows = q_ref.shape[0]
    pairs = q_ref.shape[1] // PAIR
    start = pl.program_id(0) * rows if windowed else 0
    if windowed:
        start = pl.multiple_of(start, rows)
    allowed = qid_ref[...] == kid_ref[0:1, pl.ds(start, span)]
    if windowed:
        at_row = lax.broadcasted_iota(jnp.int32, (rows, span), 0)
        at_key = lax.broadcasted_iota(jnp.int32, (rows, span), 1)
        allowed = allowed & (at_key > at_row) & (at_key <= at_row + WIN)
    bias[...] = jnp.where(allowed, 0.0, masked_fill)
    first, second, is_first = head_masks()

    def one_pair(p, carry):
        lanes = pl.ds(pl.multiple_of(p * PAIR, PAIR), PAIR)
        q2 = q_ref[:, lanes]
        k2 = k_ref[pl.ds(start, span), lanes]
        v2 = v_ref[pl.ds(start, span), lanes]
        outs, logs = [], []
        for mask in (first, second):
            s = mm_nt(q2 * mask, k2) + bias[...]
            top = jnp.max(s, axis=1, keepdims=True)
            e = jnp.exp(s - top)
            total = jnp.sum(e, axis=1, keepdims=True)
            outs.append(mm(e.astype(low), v2) / total)
            logs.append(top + jnp.log(total))
        o_ref[:, lanes] = jnp.where(is_first, outs[0], outs[1]).astype(low)
        stats = jnp.where(is_first, logs[0], logs[1])
        turned = jnp.transpose(stats)
        lse_ref[p, 0:1, :] = turned[0:1]
        lse_ref[p, 1:2, :] = turned[HEAD_DIM : HEAD_DIM + 1]
        return carry

    lax.fori_loop(0, pairs, one_pair, 0)


def attend(q, k, v, qid, kid, windowed):
    tokens, width = q.shape
    keys = k.shape[0]
    pairs = width // PAIR
    rows = QUERY_ROWS
    span = WIN + rows if windowed else keys
    return pl.pallas_call(
        functools.partial(attend_kernel, span=span, windowed=windowed),
        grid=(tokens // rows,),
        in_specs=[
            pl.BlockSpec((rows, width), lambda i: (i, 0)),
            pl.BlockSpec((keys, width), lambda i: (0, 0)),
            pl.BlockSpec((keys, width), lambda i: (0, 0)),
            pl.BlockSpec((rows, 1), lambda i: (i, 0)),
            pl.BlockSpec((1, keys), lambda i: (0, 0)),
        ],
        out_specs=[
            pl.BlockSpec((rows, width), lambda i: (i, 0)),
            pl.BlockSpec((pairs, 8, rows), lambda i: (0, 0, i)),
        ],
        out_shape=[
            jax.ShapeDtypeStruct((tokens, width), low),
            jax.ShapeDtypeStruct((pairs, 8, tokens), f32),
        ],
        scratch_shapes=[pltpu.VMEM((rows, span), f32)],
        compiler_params=pltpu.CompilerParams(vmem_limit_bytes=VMEM),
        cost_estimate=pl.CostEstimate(
            flops=16 * tokens * span * width, bytes_accessed=4 * keys * width, transcendentals=0
        ),
        name="attend",
    )(q, k, v, qid[:, None], kid[None, :])


def attend_back_kernel(
    q_ref, k_ref, v_ref, do_ref, o_ref, lse_ref, qid_ref, kid_ref, dq_ref, dk_ref, dv_ref,
    bias, dk_sum, dv_sum, *, span, windowed,
):
    rows = q_ref.shape[0]
    pairs = q_ref.shape[1] // PAIR
    step = pl.program_id(0)
    start = pl.multiple_of(step * rows, rows) if windowed else 0
    keys = pl.ds(start, span)

    @pl.when(step == 0)
    def _():
        dk_sum[...] = jnp.zeros_like(dk_sum)
        dv_sum[...] = jnp.zeros_like(dv_sum)

    allowed = kid_ref[keys, :] == qid_ref[...]
    if windowed:
        at_key = lax.broadcasted_iota(jnp.int32, (span, rows), 0)
        at_row = lax.broadcasted_iota(jnp.int32, (span, rows), 1)
        allowed = allowed & (at_key > at_row) & (at_key <= at_row + WIN)
    bias[...] = jnp.where(allowed, 0.0, masked_fill)
    first, second, is_first = head_masks()

    def one_pair(p, carry):
        lanes = pl.ds(pl.multiple_of(p * PAIR, PAIR), PAIR)
        q2 = q_ref[:, lanes]
        k2 = k_ref[keys, lanes]
        v2 = v_ref[keys, lanes]
        do2 = do_ref[:, lanes]
        turned = jnp.transpose(do2.astype(f32) * o_ref[:, lanes].astype(f32))
        dk, dv, dqs = 0.0, 0.0, []
        for h, mask in enumerate((first, second)):
            qm, dom = q2 * mask, do2 * mask
            inner = jnp.sum(turned[h * HEAD_DIM : (h + 1) * HEAD_DIM], axis=0, keepdims=True)
            s = mm_nt(k2, qm) + bias[...]
            share = jnp.exp(s - lse_ref[p, h : h + 1, :])
            ds = (share * (mm_nt(v2, dom) - inner)).astype(low)
            dv = dv + mm(share.astype(low), dom)
            dk = dk + mm(ds, qm)
            dqs.append(mm_tn(ds, k2))
        dk_sum[keys, lanes] += dk
        dv_sum[keys, lanes] += dv
        dq_ref[:, lanes] = (jnp.where(is_first, dqs[0], dqs[1]) * HEAD_DIM**-0.5).astype(low)
        return carry

    lax.fori_loop(0, pairs, one_pair, 0)

    @pl.when(step == pl.num_programs(0) - 1)
    def _():
        dk_ref[...] = dk_sum[...].astype(low)
        dv_ref[...] = dv_sum[...].astype(low)


def attend_back(q, k, v, do, o, lse, qid, kid, windowed):
    tokens, width = q.shape
    keys = k.shape[0]
    pairs = width // PAIR
    rows = QUERY_ROWS
    span = WIN + rows if windowed else keys
    by_row = pl.BlockSpec((rows, width), lambda i: (i, 0))
    whole = pl.BlockSpec((keys, width), lambda i: (0, 0))
    return pl.pallas_call(
        functools.partial(attend_back_kernel, span=span, windowed=windowed),
        grid=(tokens // rows,),
        in_specs=[
            by_row,
            whole,
            whole,
            by_row,
            by_row,
            pl.BlockSpec((pairs, 8, rows), lambda i: (0, 0, i)),
            pl.BlockSpec((1, rows), lambda i: (0, i)),
            pl.BlockSpec((keys, 1), lambda i: (0, 0)),
        ],
        out_specs=[by_row, whole, whole],
        out_shape=[
            jax.ShapeDtypeStruct((tokens, width), low),
            jax.ShapeDtypeStruct((keys, width), low),
            jax.ShapeDtypeStruct((keys, width), low),
        ],
        scratch_shapes=[
            pltpu.VMEM((span, rows), f32),
            pltpu.VMEM((keys, width), f32),
            pltpu.VMEM((keys, width), f32),
        ],
        compiler_params=pltpu.CompilerParams(vmem_limit_bytes=VMEM),
        cost_estimate=pl.CostEstimate(
            flops=40 * tokens * span * width, bytes_accessed=8 * keys * width, transcendentals=0
        ),
        name="attend_back",
    )(q, k, v, do, o, lse, qid[None, :], kid[:, None])


ROOT = 0.7978845608028654
CUBE = 0.044715


def hidden_kernel(f_ref, w1_ref, b1_ref, w2_ref, act_ref, slope_ref, out_ref, total):
    step = pl.program_id(0) * pl.num_programs(1) + pl.program_id(1)
    last = pl.num_programs(0) * pl.num_programs(1) - 1

    @pl.when(step == 0)
    def _():
        total[...] = jnp.zeros_like(total)

    def one_part(t, carry):
        rows = pl.ds(pl.multiple_of(t * 256, 256), 256)
        h = mm(f_ref[rows, :], w1_ref[0]) + b1_ref[0]
        square = h * h
        bend = jnp.tanh(h * (ROOT + (ROOT * CUBE) * square))
        half = 0.5 + 0.5 * bend
        act = (h * half).astype(low)
        act_ref[0, rows, :] = act
        slope = half + (0.5 * h) * (1.0 - bend * bend) * (ROOT + (3.0 * ROOT * CUBE) * square)
        slope_ref[0, rows, :] = slope.astype(low)
        total[rows, :] += mm_nt(act, w2_ref[0])
        return carry

    lax.fori_loop(0, f_ref.shape[0] // 256, one_part, 0)

    @pl.when(step == last)
    def _():
        out_ref[...] = total[...].astype(low)


def hidden_forward(f, w1, b1, w2):
    parts, width, inner = w1.shape
    tokens = f.shape[0]
    block = min(512, inner)
    grid = (parts, inner // block)
    weight = pl.BlockSpec((1, width, block), lambda j, n: (j, 0, n))
    active = pl.BlockSpec((1, tokens, block), lambda j, n: (j, 0, n))
    return pl.pallas_call(
        hidden_kernel,
        grid=grid,
        in_specs=[
            pl.BlockSpec((tokens, width), lambda j, n: (0, 0)),
            weight,
            pl.BlockSpec((1, 1, block), lambda j, n: (j, 0, n)),
            weight,
        ],
        out_specs=[active, active, pl.BlockSpec((tokens, width), lambda j, n: (0, 0))],
        out_shape=[
            jax.ShapeDtypeStruct((parts, tokens, inner), low),
            jax.ShapeDtypeStruct((parts, tokens, inner), low),
            jax.ShapeDtypeStruct((tokens, width), low),
        ],
        scratch_shapes=[pltpu.VMEM((tokens, width), f32)],
        compiler_params=pltpu.CompilerParams(vmem_limit_bytes=VMEM),
        cost_estimate=pl.CostEstimate(
            flops=4 * tokens * width * parts * inner,
            bytes_accessed=8 * width * parts * inner,
            transcendentals=0,
        ),
        name="hidden_forward",
    )(f, w1, b1, w2)


def hidden_back_kernel(
    dz_ref, dzt_ref, ft_ref, w1_ref, w2_ref, act_ref, slope_ref,
    g1_ref, g2_ref, gb_ref, df_ref, dh_low, total,
):
    step = pl.program_id(0) * pl.num_programs(1) + pl.program_id(1)
    last = pl.num_programs(0) * pl.num_programs(1) - 1

    @pl.when(step == 0)
    def _():
        total[...] = jnp.zeros_like(total)

    gb_ref[...] = jnp.zeros_like(gb_ref)

    def one_part(t, carry):
        rows = pl.ds(pl.multiple_of(t * 256, 256), 256)
        dh = (mm(dz_ref[rows, :], w2_ref[0]) * slope_ref[0, rows, :].astype(f32)).astype(low)
        dh_low[rows, :] = dh
        gb_ref[0] += jnp.sum(dh.astype(f32), axis=0, keepdims=True)
        total[rows, :] += mm_nt(dh, w1_ref[0])
        return carry

    lax.fori_loop(0, dz_ref.shape[0] // 256, one_part, 0)

    def one_grad(t, carry):
        rows = pl.ds(pl.multiple_of(t * 256, 256), 256)
        g2_ref[0, rows, :] = mm(dzt_ref[rows, :], act_ref[0]).astype(low)
        g1_ref[0, rows, :] = mm(ft_ref[rows, :], dh_low[...]).astype(low)
        return carry

    lax.fori_loop(0, ft_ref.shape[0] // 256, one_grad, 0)

    @pl.when(step == last)
    def _():
        df_ref[...] = total[...].astype(low)


def hidden_backward(dz, f, w1, w2, act, slope):
    parts, width, inner = w1.shape
    tokens = f.shape[0]
    block = min(512, inner)
    grid = (parts, inner // block)
    weight = pl.BlockSpec((1, width, block), lambda j, n: (j, 0, n))
    active = pl.BlockSpec((1, tokens, block), lambda j, n: (j, 0, n))
    whole = pl.BlockSpec((tokens, width), lambda j, n: (0, 0))
    turned = pl.BlockSpec((width, tokens), lambda j, n: (0, 0))
    return pl.pallas_call(
        hidden_back_kernel,
        grid=grid,
        in_specs=[whole, turned, turned, weight, weight, active, active],
        out_specs=[weight, weight, pl.BlockSpec((1, 1, block), lambda j, n: (j, 0, n)), whole],
        out_shape=[
            jax.ShapeDtypeStruct(w1.shape, low),
            jax.ShapeDtypeStruct(w1.shape, low),
            jax.ShapeDtypeStruct((parts, 1, inner), f32),
            jax.ShapeDtypeStruct((tokens, width), low),
        ],
        scratch_shapes=[pltpu.VMEM((tokens, block), low), pltpu.VMEM((tokens, width), f32)],
        compiler_params=pltpu.CompilerParams(vmem_limit_bytes=VMEM),
        cost_estimate=pl.CostEstimate(
            flops=8 * tokens * width * parts * inner,
            bytes_accessed=16 * width * parts * inner,
            transcendentals=0,
        ),
        name="hidden_backward",
    )(dz, dz.T, f.T, w1, w2, act, slope)


def norm_forward(stream, gain, bias):
    center = jnp.mean(stream, axis=1, keepdims=True)
    spread = jnp.mean(stream * stream, axis=1, keepdims=True) - center * center
    scaling = lax.rsqrt(spread + norm_epsilon)
    normed = (stream - center) * scaling
    return (normed * gain + bias).astype(low), normed, scaling


def norm_backward(incoming, normed, scaling, gain):
    gain_grad = jnp.sum(incoming * normed, axis=0)
    bias_grad = jnp.sum(incoming, axis=0)
    upstream = incoming * gain
    mean_up = jnp.mean(upstream, axis=1, keepdims=True)
    mean_both = jnp.mean(upstream * normed, axis=1, keepdims=True)
    return scaling * (upstream - mean_up - normed * mean_both), gain_grad, bias_grad


def build_local(mesh):
    n_dp, n_col = mesh.shape["dp"], mesh.shape["col"]

    def swap(x):
        return lax.ppermute(x, "row", [(0, 1), (1, 0)])

    def from_col(x, k):
        return lax.ppermute(x, "col", [(i, (i - k) % n_col) for i in range(n_col)])

    def to_col(x, k):
        return lax.ppermute(x, "col", [(i, (i + k) % n_col) for i in range(n_col)])

    def across(x, bit):
        return lax.ppermute(x, "dp", [(i, i ^ bit) for i in range(n_dp)])

    def plane_gather(x):
        half = x.shape[0] // 2
        by_x, by_y = across(x, 1), across(x, 2)
        far = jnp.concatenate([across(by_x[:half], 2), across(by_y[half:], 1)], axis=0)
        return [x, by_x, by_y, far]

    def plane_scatter(parts):
        half = parts[0].shape[0] // 2
        a, b = [p[:half] for p in parts], [p[half:] for p in parts]
        got = across(jnp.stack([a[1], a[3]]), 1)
        a0, a2 = a[0] + got[0], a[2] + got[1]
        got = across(jnp.stack([b[2], b[3]]), 2)
        b0, b1 = b[0] + got[0], b[1] + got[1]
        a0 = a0 + across(a2, 2)
        b0 = b0 + across(b1, 1)
        return jnp.concatenate([a0, b0], axis=0)

    def local(
        tokens, encoder, cotangent, dec_lengths, src_lengths,
        self_norm_gain, self_norm_bias, self_query, self_key, self_value,
        self_query_bias, self_value_bias, self_out, self_out_bias,
        cross_norm_gain, cross_norm_bias, cross_query, cross_key, cross_value,
        cross_query_bias, cross_value_bias, cross_out, cross_out_bias,
        hidden_norm_gain, hidden_norm_bias, hidden_in, hidden_in_bias,
        hidden_out, hidden_out_bias,
    ):
        row, col = lax.axis_index("row"), lax.axis_index("col")
        place = lax.axis_index("dp") % PARTS
        wide = tokens.shape[1]
        chunk = tokens.shape[0] // n_col
        span = 2 * chunk

        def by_row(own, other):
            return jnp.where(
                row == 0,
                jnp.concatenate([own, other], axis=0),
                jnp.concatenate([other, own], axis=0),
            )

        def row_gather(own):
            return by_row(own, swap(own))

        def row_scatter(partial):
            half = partial.shape[0] // 2
            away = lax.dynamic_slice_in_dim(partial, (1 - row) * half, half, 0)
            mine = lax.dynamic_slice_in_dim(partial, row * half, half, 0)
            return mine.astype(f32) + swap(away.astype(low)).astype(f32)

        def spread_rows(x):
            cut = x.reshape(2, 2, chunk, wide)
            own = lax.dynamic_index_in_dim(cut, row, 1, keepdims=False)
            other = swap(lax.dynamic_index_in_dim(cut, 1 - row, 1, keepdims=False))
            every = by_row(own, other)
            pieces = []
            for k in range(n_col):
                piece = lax.dynamic_index_in_dim(every, (col - k) % n_col, 0, keepdims=False)
                pieces.append(from_col(piece, k) if k else piece)
            return jnp.concatenate(pieces, axis=1)

        def collect_rows(x):
            every = jnp.zeros((n_col, chunk, wide), x.dtype)
            for k in range(n_col):
                piece = x[:, k * wide : (k + 1) * wide]
                piece = to_col(piece, k) if k else piece
                every = lax.dynamic_update_index_in_dim(every, piece, (col - k) % n_col, 0)
            own = lax.dynamic_slice_in_dim(every, 2 * row, 2, 0)
            other = swap(lax.dynamic_slice_in_dim(every, 2 * (1 - row), 2, 0))
            both = jnp.where(
                row == 0, jnp.stack([own, other], axis=1), jnp.stack([other, own], axis=1)
            )
            return both.reshape(n_col * chunk, wide)

        def in_order(parts):
            stacked = jnp.stack(parts)
            return [
                lax.dynamic_index_in_dim(stacked, i ^ place, 0, keepdims=False)
                for i in range(PARTS)
            ]

        def weights_of(arrays):
            def own(j):
                cuts = []
                for w in arrays:
                    size = w.shape[1] // PARTS
                    cuts.append(lax.dynamic_slice_in_dim(w, (place ^ j) * size, size, 1))
                return jnp.concatenate(cuts, axis=1)

            mine = own(0)
            rest = jnp.concatenate([from_col(mine, k) for k in range(1, n_col)], axis=0)
            return [
                jnp.concatenate([own(j), part], axis=0)
                for j, part in enumerate(plane_gather(rest))
            ]

        def grads_of(parts):
            mine = plane_scatter(parts)
            total = mine[:wide].astype(f32)
            for k in range(1, n_col):
                total = total + to_col(mine[k * wide : (k + 1) * wide], k).astype(f32)
            bit = PARTS
            while bit < n_dp:
                total = total + across(total.astype(low), bit).astype(f32)
                bit *= 2
            return in_order(plane_gather(total.astype(low)))

        feature_vectors = jnp.stack([
            self_norm_gain, self_norm_bias, self_out_bias, cross_norm_gain, cross_norm_bias,
            cross_out_bias, hidden_norm_gain, hidden_norm_bias, hidden_out_bias,
        ])
        column_vectors = jnp.concatenate(
            [self_query_bias, self_value_bias, cross_query_bias, cross_value_bias, hidden_in_bias]
        )
        gathered = lax.all_gather(feature_vectors, "col", axis=0)
        rolled = lax.dynamic_slice_in_dim(jnp.concatenate([gathered, gathered]), col, n_col, 0)
        vectors = jnp.moveaxis(rolled, 0, 1).reshape(feature_vectors.shape[0], n_col * wide)
        (gain1, shift1, out_bias1, gain2, shift2, out_bias2, gain3, shift3, out_bias3) = vectors
        columns = lax.all_gather(column_vectors, "col", axis=0)

        def column_vector(start, size):
            flat = columns[:, start : start + size].reshape(-1)
            parts = flat.reshape(PARTS, -1)
            return jnp.concatenate(
                [
                    lax.dynamic_index_in_dim(parts, place ^ j, 0, keepdims=False)
                    for j in range(PARTS)
                ]
            )

        size = self_query_bias.shape[0]
        q_bias1 = column_vector(0, size)
        v_bias1 = column_vector(size, size)
        q_bias2 = column_vector(2 * size, size)
        v_bias2 = column_vector(3 * size, size)
        hidden_bias = column_vector(4 * size, hidden_in_bias.shape[0])

        self_parts = weights_of([self_query, self_key, self_value, self_out.T])
        cross_parts = weights_of([cross_query, cross_key, cross_value, cross_out.T])
        w1 = jnp.stack(weights_of([hidden_in]))
        w2 = jnp.stack(weights_of([hidden_out.T]))
        step = self_query.shape[1] // PARTS

        def columns_of(parts, index):
            return jnp.concatenate(
                [p[:, index * step : (index + 1) * step] for p in parts], axis=1
            )

        wq1, wk1, wv1, wo1 = [columns_of(self_parts, i) for i in range(4)]
        wq2, wk2, wv2, wo2 = [columns_of(cross_parts, i) for i in range(4)]

        dec_ids = doc_numbers(dec_lengths, SEQ_LEN)[0]
        src_ids = doc_numbers(src_lengths, ENC)[0]
        padded = jnp.pad(dec_ids, (WIN, 0), constant_values=-1)
        key_ids = lax.dynamic_slice_in_dim(padded, col * span, WIN + span, 0)
        query_ids = key_ids[WIN:]

        scale = low(HEAD_DIM**-0.5)
        stream = spread_rows(tokens).astype(f32)
        a_own, normed1, scaling1 = norm_forward(stream, gain1, shift1)
        a = row_gather(a_own)
        before = lax.ppermute(a_own, "col", [(i, i + 1) for i in range(n_col - 1)])
        before = jnp.concatenate([before[:, wide:], before[:, :wide]], axis=1)
        a_ext = jnp.concatenate([row_gather(before), a], axis=0)
        q1 = (mm(a, wq1) + q_bias1).astype(low) * scale
        k1 = mm(a_ext, wk1).astype(low)
        v1 = (mm(a_ext, wv1) + v_bias1).astype(low)
        o1, lse1 = attend(q1, k1, v1, query_ids, key_ids, True)
        x1 = stream + (row_scatter(mm_nt(o1, wo1)) + out_bias1)

        c_own, normed2, scaling2 = norm_forward(x1, gain2, shift2)
        c = row_gather(c_own)
        enc = row_gather(
            jnp.concatenate(
                [encoder] + [from_col(encoder, k) for k in range(1, n_col)], axis=1
            )
        )
        q2 = (mm(c, wq2) + q_bias2).astype(low) * scale
        k2 = mm(enc, wk2).astype(low)
        v2 = (mm(enc, wv2) + v_bias2).astype(low)
        o2, lse2 = attend(q2, k2, v2, query_ids, src_ids, False)
        x2 = x1 + (row_scatter(mm_nt(o2, wo2)) + out_bias2)

        f_own, normed3, scaling3 = norm_forward(x2, gain3, shift3)
        f = row_gather(f_own)
        act, slope, branch = hidden_forward(f, w1, hidden_bias.reshape(PARTS, 1, -1), w2)
        layer_out = collect_rows((x2 + (row_scatter(branch) + out_bias3)).astype(low))

        dz_own = spread_rows(cotangent)
        dz = row_gather(dz_own)
        g1, g2, hidden_bias_grad, df = hidden_backward(dz, f, w1, w2, act, slope)
        g1_parts = grads_of([g1[j] for j in range(PARTS)])
        g2_parts = grads_of([g2[j] for j in range(PARTS)])
        back3, gain_grad3, shift_grad3 = norm_backward(row_scatter(df), normed3, scaling3, gain3)
        dx2 = dz_own.astype(f32) + back3

        dyc_own = dx2.astype(low)
        dyc = row_gather(dyc_own)
        doc = mm(dyc, wo2).astype(low)
        dq2, dk2, dv2 = attend_back(q2, k2, v2, doc, o2, lse2, query_ids, src_ids, False)
        grads = [
            mm_tn(c, dq2).astype(low),
            mm_tn(enc, dk2).astype(low),
            mm_tn(enc, dv2).astype(low),
            mm_tn(dyc, o2).astype(low),
        ]

        def by_part(arrays):
            return [
                jnp.concatenate([g[:, j * step : (j + 1) * step] for g in arrays], axis=1)
                for j in range(PARTS)
            ]

        cross_grads = grads_of(by_part(grads))
        enc_back = row_scatter(mm_nt(dk2, wk2) + mm_nt(dv2, wv2))
        encoder_grad = enc_back[:, :wide]
        for k in range(1, n_col):
            encoder_grad = encoder_grad + to_col(
                enc_back[:, k * wide : (k + 1) * wide].astype(low), k
            ).astype(f32)
        back2, gain_grad2, shift_grad2 = norm_backward(
            row_scatter(mm_nt(dq2, wq2)), normed2, scaling2, gain2
        )
        dx1 = dx2 + back2

        dy_own = dx1.astype(low)
        dy = row_gather(dy_own)
        do = mm(dy, wo1).astype(low)
        dq1, dk1, dv1 = attend_back(q1, k1, v1, do, o1, lse1, query_ids, key_ids, True)
        da_ext = mm_nt(dk1, wk1) + mm_nt(dv1, wv1)
        da_before = row_scatter(da_ext[:WIN]).astype(low)
        da_after = lax.ppermute(da_before, "col", [(i + 1, i) for i in range(n_col - 1)])
        da_after = jnp.concatenate([da_after[:, -wide:], da_after[:, :-wide]], axis=1)
        da = row_scatter(da_ext[WIN:] + mm_nt(dq1, wq1)) + da_after.astype(f32)
        grads = [
            mm_tn(a, dq1).astype(low),
            mm_tn(a_ext, dk1).astype(low),
            mm_tn(a_ext, dv1).astype(low),
            mm_tn(dy, o1).astype(low),
        ]
        self_grads = grads_of(by_part(grads))
        back1, gain_grad1, shift_grad1 = norm_backward(da, normed1, scaling1, gain1)
        tokens_grad = collect_rows((dx1 + back1).astype(low)).astype(f32)

        def total(x):
            return jnp.sum(x, axis=0, dtype=f32)

        feature_grads = jnp.stack([
            gain_grad1, shift_grad1, total(dy_own), gain_grad2, shift_grad2, total(dyc_own),
            gain_grad3, shift_grad3, total(dz_own),
        ])
        count = feature_grads.shape[0]
        chunks = jnp.moveaxis(feature_grads.reshape(count, n_col, wide), 1, 0)
        chunks = lax.dynamic_slice_in_dim(
            jnp.concatenate([chunks, chunks]), (n_col - col) % n_col, n_col, 0
        )
        chunks = lax.psum(chunks, ("dp", "row", "col"))
        feature_grads = lax.dynamic_index_in_dim(chunks, col, 0, keepdims=False)
        column_grads = []
        for vector in (total(dq1), total(dv1), total(dq2), total(dv2), hidden_bias_grad):
            parts = vector.reshape(PARTS, -1)
            column_grads.append(
                jnp.concatenate(in_order([parts[j] for j in range(PARTS)])).reshape(n_col, -1)
            )
        column_grads = lax.psum(jnp.concatenate(column_grads, axis=1), ("dp", "col"))
        column_grads = lax.dynamic_index_in_dim(column_grads, col, 0, keepdims=False)

        def whole(parts, index=None):
            if index is not None:
                parts = [p[:, index * step : (index + 1) * step] for p in parts]
            return jnp.concatenate(parts, axis=1).astype(f32)

        return (
            layer_out,
            tokens_grad,
            encoder_grad,
            feature_grads[0],
            feature_grads[1],
            whole(self_grads, 0),
            whole(self_grads, 1),
            whole(self_grads, 2),
            column_grads[:size],
            column_grads[size : 2 * size],
            whole(self_grads, 3).T,
            feature_grads[2],
            feature_grads[3],
            feature_grads[4],
            whole(cross_grads, 0),
            whole(cross_grads, 1),
            whole(cross_grads, 2),
            column_grads[2 * size : 3 * size],
            column_grads[3 * size : 4 * size],
            whole(cross_grads, 3).T,
            feature_grads[5],
            feature_grads[6],
            feature_grads[7],
            whole(g1_parts),
            column_grads[4 * size :],
            whole(g2_parts).T,
            feature_grads[8],
        )

    return local


def solution(mesh):
    rows = P(("dp", "row"), "col")
    features = P("col")
    columns = P(("row", "col"))
    into, out_of = P("col", "row"), P("row", "col")
    attention = (into, into, into, columns, columns, out_of, features)
    norm = (features, features)
    weights = (
        norm
        + attention
        + norm
        + attention
        + norm
        + (into, columns, out_of, features)
    )
    return jax.shard_map(
        build_local(mesh),
        mesh=mesh,
        in_specs=(rows, rows, rows, P("dp", None), P("dp", None)) + weights,
        out_specs=(rows, rows, rows) + weights,
        check_vma=False,
    )
```

```python
import functools

import jax
import jax.numpy as jnp
from jax import lax
from jax.experimental import pallas as pl
from jax.experimental.pallas import tpu as pltpu
from jax.sharding import PartitionSpec as P

D = 1024
HEAD_DIM = 64
SEQ_LEN = 4096
ENC = 1024
WIN = 1024

norm_epsilon = 1e-05
masked_fill = -1e30
low = jnp.bfloat16
f32 = jnp.float32
PARTS = 4
PAIR = 2 * HEAD_DIM
QUERY_ROWS = 256
VMEM = 56 * 1024 * 1024


def doc_numbers(lengths, positions):
    bounds = jnp.cumsum(lengths, axis=1, dtype=jnp.int32)
    places = jnp.arange(positions, dtype=jnp.int32)
    return jnp.sum(
        (places[None, :, None] >= bounds[:, None, :]).astype(jnp.int32), axis=2, dtype=jnp.int32
    )


def mm(a, b):
    return lax.dot_general(a, b, (((1,), (0,)), ((), ())), preferred_element_type=f32)


def mm_nt(a, b):
    return lax.dot_general(a, b, (((1,), (1,)), ((), ())), preferred_element_type=f32)


def mm_tn(a, b):
    return lax.dot_general(a, b, (((0,), (0,)), ((), ())), preferred_element_type=f32)


def head_masks():
    lane = lax.broadcasted_iota(jnp.int32, (1, PAIR), 1)
    first = jnp.where(lane < HEAD_DIM, 1.0, 0.0)
    return first.astype(low), (1.0 - first).astype(low), lane < HEAD_DIM


def attend_kernel(q_ref, k_ref, v_ref, qid_ref, kid_ref, o_ref, lse_ref, bias, *, span, windowed):
    rows = q_ref.shape[0]
    pairs = q_ref.shape[1] // PAIR
    start = pl.program_id(0) * rows if windowed else 0
    if windowed:
        start = pl.multiple_of(start, rows)
    allowed = qid_ref[...] == kid_ref[0:1, pl.ds(start, span)]
    if windowed:
        at_row = lax.broadcasted_iota(jnp.int32, (rows, span), 0)
        at_key = lax.broadcasted_iota(jnp.int32, (rows, span), 1)
        allowed = allowed & (at_key > at_row) & (at_key <= at_row + WIN)
    bias[...] = jnp.where(allowed, 0.0, masked_fill)
    first, second, is_first = head_masks()

    def one_pair(p, carry):
        lanes = pl.ds(pl.multiple_of(p * PAIR, PAIR), PAIR)
        q2 = q_ref[:, lanes]
        k2 = k_ref[pl.ds(start, span), lanes]
        v2 = v_ref[pl.ds(start, span), lanes]
        outs, logs = [], []
        for mask in (first, second):
            s = mm_nt(q2 * mask, k2) + bias[...]
            top = jnp.max(s, axis=1, keepdims=True)
            e = jnp.exp(s - top)
            total = jnp.sum(e, axis=1, keepdims=True)
            outs.append(mm(e.astype(low), v2) / total)
            logs.append(top + jnp.log(total))
        o_ref[:, lanes] = jnp.where(is_first, outs[0], outs[1]).astype(low)
        stats = jnp.where(is_first, logs[0], logs[1])
        turned = jnp.transpose(stats)
        lse_ref[p, 0:1, :] = turned[0:1]
        lse_ref[p, 1:2, :] = turned[HEAD_DIM : HEAD_DIM + 1]
        return carry

    lax.fori_loop(0, pairs, one_pair, 0)


def attend(q, k, v, qid, kid, windowed):
    tokens, width = q.shape
    keys = k.shape[0]
    pairs = width // PAIR
    rows = QUERY_ROWS
    span = WIN + rows if windowed else keys
    return pl.pallas_call(
        functools.partial(attend_kernel, span=span, windowed=windowed),
        grid=(tokens // rows,),
        in_specs=[
            pl.BlockSpec((rows, width), lambda i: (i, 0)),
            pl.BlockSpec((keys, width), lambda i: (0, 0)),
            pl.BlockSpec((keys, width), lambda i: (0, 0)),
            pl.BlockSpec((rows, 1), lambda i: (i, 0)),
            pl.BlockSpec((1, keys), lambda i: (0, 0)),
        ],
        out_specs=[
            pl.BlockSpec((rows, width), lambda i: (i, 0)),
            pl.BlockSpec((pairs, 8, rows), lambda i: (0, 0, i)),
        ],
        out_shape=[
            jax.ShapeDtypeStruct((tokens, width), low),
            jax.ShapeDtypeStruct((pairs, 8, tokens), f32),
        ],
        scratch_shapes=[pltpu.VMEM((rows, span), f32)],
        compiler_params=pltpu.CompilerParams(vmem_limit_bytes=VMEM),
        cost_estimate=pl.CostEstimate(
            flops=16 * tokens * span * width, bytes_accessed=4 * keys * width, transcendentals=0
        ),
        name="attend",
    )(q, k, v, qid[:, None], kid[None, :])


def attend_back_kernel(
    q_ref, k_ref, v_ref, do_ref, o_ref, lse_ref, qid_ref, kid_ref, dq_ref, dk_ref, dv_ref,
    bias, dk_sum, dv_sum, *, span, windowed,
):
    rows = q_ref.shape[0]
    pairs = q_ref.shape[1] // PAIR
    step = pl.program_id(0)
    start = pl.multiple_of(step * rows, rows) if windowed else 0
    keys = pl.ds(start, span)

    @pl.when(step == 0)
    def _():
        dk_sum[...] = jnp.zeros_like(dk_sum)
        dv_sum[...] = jnp.zeros_like(dv_sum)

    allowed = kid_ref[keys, :] == qid_ref[...]
    if windowed:
        at_key = lax.broadcasted_iota(jnp.int32, (span, rows), 0)
        at_row = lax.broadcasted_iota(jnp.int32, (span, rows), 1)
        allowed = allowed & (at_key > at_row) & (at_key <= at_row + WIN)
    bias[...] = jnp.where(allowed, 0.0, masked_fill)
    first, second, is_first = head_masks()

    def one_pair(p, carry):
        lanes = pl.ds(pl.multiple_of(p * PAIR, PAIR), PAIR)
        q2 = q_ref[:, lanes]
        k2 = k_ref[keys, lanes]
        v2 = v_ref[keys, lanes]
        do2 = do_ref[:, lanes]
        turned = jnp.transpose(do2.astype(f32) * o_ref[:, lanes].astype(f32))
        dk, dv, dqs = 0.0, 0.0, []
        for h, mask in enumerate((first, second)):
            qm, dom = q2 * mask, do2 * mask
            inner = jnp.sum(turned[h * HEAD_DIM : (h + 1) * HEAD_DIM], axis=0, keepdims=True)
            s = mm_nt(k2, qm) + bias[...]
            share = jnp.exp(s - lse_ref[p, h : h + 1, :])
            ds = (share * (mm_nt(v2, dom) - inner)).astype(low)
            dv = dv + mm(share.astype(low), dom)
            dk = dk + mm(ds, qm)
            dqs.append(mm_tn(ds, k2))
        dk_sum[keys, lanes] += dk
        dv_sum[keys, lanes] += dv
        dq_ref[:, lanes] = (jnp.where(is_first, dqs[0], dqs[1]) * HEAD_DIM**-0.5).astype(low)
        return carry

    lax.fori_loop(0, pairs, one_pair, 0)

    @pl.when(step == pl.num_programs(0) - 1)
    def _():
        dk_ref[...] = dk_sum[...].astype(low)
        dv_ref[...] = dv_sum[...].astype(low)


def attend_back(q, k, v, do, o, lse, qid, kid, windowed):
    tokens, width = q.shape
    keys = k.shape[0]
    pairs = width // PAIR
    rows = QUERY_ROWS
    span = WIN + rows if windowed else keys
    by_row = pl.BlockSpec((rows, width), lambda i: (i, 0))
    whole = pl.BlockSpec((keys, width), lambda i: (0, 0))
    return pl.pallas_call(
        functools.partial(attend_back_kernel, span=span, windowed=windowed),
        grid=(tokens // rows,),
        in_specs=[
            by_row,
            whole,
            whole,
            by_row,
            by_row,
            pl.BlockSpec((pairs, 8, rows), lambda i: (0, 0, i)),
            pl.BlockSpec((1, rows), lambda i: (0, i)),
            pl.BlockSpec((keys, 1), lambda i: (0, 0)),
        ],
        out_specs=[by_row, whole, whole],
        out_shape=[
            jax.ShapeDtypeStruct((tokens, width), low),
            jax.ShapeDtypeStruct((keys, width), low),
            jax.ShapeDtypeStruct((keys, width), low),
        ],
        scratch_shapes=[
            pltpu.VMEM((span, rows), f32),
            pltpu.VMEM((keys, width), f32),
            pltpu.VMEM((keys, width), f32),
        ],
        compiler_params=pltpu.CompilerParams(vmem_limit_bytes=VMEM),
        cost_estimate=pl.CostEstimate(
            flops=40 * tokens * span * width, bytes_accessed=8 * keys * width, transcendentals=0
        ),
        name="attend_back",
    )(q, k, v, do, o, lse, qid[None, :], kid[:, None])


ROOT = 0.7978845608028654
CUBE = 0.044715


def hidden_kernel(f_ref, w1_ref, b1_ref, w2_ref, act_ref, slope_ref, out_ref, total):
    step = pl.program_id(0) * pl.num_programs(1) + pl.program_id(1)
    last = pl.num_programs(0) * pl.num_programs(1) - 1

    @pl.when(step == 0)
    def _():
        total[...] = jnp.zeros_like(total)

    def one_part(t, carry):
        rows = pl.ds(pl.multiple_of(t * 256, 256), 256)
        h = mm(f_ref[rows, :], w1_ref[0]) + b1_ref[0]
        square = h * h
        bend = jnp.tanh(h * (ROOT + (ROOT * CUBE) * square))
        half = 0.5 + 0.5 * bend
        act = (h * half).astype(low)
        act_ref[0, rows, :] = act
        slope = half + (0.5 * h) * (1.0 - bend * bend) * (ROOT + (3.0 * ROOT * CUBE) * square)
        slope_ref[0, rows, :] = slope.astype(low)
        total[rows, :] += mm_nt(act, w2_ref[0])
        return carry

    lax.fori_loop(0, f_ref.shape[0] // 256, one_part, 0)

    @pl.when(step == last)
    def _():
        out_ref[...] = total[...].astype(low)


def hidden_forward(f, w1, b1, w2):
    parts, width, inner = w1.shape
    tokens = f.shape[0]
    block = min(512, inner)
    grid = (parts, inner // block)
    weight = pl.BlockSpec((1, width, block), lambda j, n: (j, 0, n))
    active = pl.BlockSpec((1, tokens, block), lambda j, n: (j, 0, n))
    return pl.pallas_call(
        hidden_kernel,
        grid=grid,
        in_specs=[
            pl.BlockSpec((tokens, width), lambda j, n: (0, 0)),
            weight,
            pl.BlockSpec((1, 1, block), lambda j, n: (j, 0, n)),
            weight,
        ],
        out_specs=[active, active, pl.BlockSpec((tokens, width), lambda j, n: (0, 0))],
        out_shape=[
            jax.ShapeDtypeStruct((parts, tokens, inner), low),
            jax.ShapeDtypeStruct((parts, tokens, inner), low),
            jax.ShapeDtypeStruct((tokens, width), low),
        ],
        scratch_shapes=[pltpu.VMEM((tokens, width), f32)],
        compiler_params=pltpu.CompilerParams(vmem_limit_bytes=VMEM),
        cost_estimate=pl.CostEstimate(
            flops=4 * tokens * width * parts * inner,
            bytes_accessed=8 * width * parts * inner,
            transcendentals=0,
        ),
        name="hidden_forward",
    )(f, w1, b1, w2)


def hidden_back_kernel(
    dz_ref, dzt_ref, ft_ref, w1_ref, w2_ref, act_ref, slope_ref,
    g1_ref, g2_ref, gb_ref, df_ref, dh_low, total,
):
    step = pl.program_id(0) * pl.num_programs(1) + pl.program_id(1)
    last = pl.num_programs(0) * pl.num_programs(1) - 1

    @pl.when(step == 0)
    def _():
        total[...] = jnp.zeros_like(total)

    gb_ref[...] = jnp.zeros_like(gb_ref)

    def one_part(t, carry):
        rows = pl.ds(pl.multiple_of(t * 256, 256), 256)
        dh = (mm(dz_ref[rows, :], w2_ref[0]) * slope_ref[0, rows, :].astype(f32)).astype(low)
        dh_low[rows, :] = dh
        gb_ref[0] += jnp.sum(dh.astype(f32), axis=0, keepdims=True)
        total[rows, :] += mm_nt(dh, w1_ref[0])
        return carry

    lax.fori_loop(0, dz_ref.shape[0] // 256, one_part, 0)

    def one_grad(t, carry):
        rows = pl.ds(pl.multiple_of(t * 256, 256), 256)
        g2_ref[0, rows, :] = mm(dzt_ref[rows, :], act_ref[0]).astype(low)
        g1_ref[0, rows, :] = mm(ft_ref[rows, :], dh_low[...]).astype(low)
        return carry

    lax.fori_loop(0, ft_ref.shape[0] // 256, one_grad, 0)

    @pl.when(step == last)
    def _():
        df_ref[...] = total[...].astype(low)


def hidden_backward(dz, f, w1, w2, act, slope):
    parts, width, inner = w1.shape
    tokens = f.shape[0]
    block = min(512, inner)
    grid = (parts, inner // block)
    weight = pl.BlockSpec((1, width, block), lambda j, n: (j, 0, n))
    active = pl.BlockSpec((1, tokens, block), lambda j, n: (j, 0, n))
    whole = pl.BlockSpec((tokens, width), lambda j, n: (0, 0))
    turned = pl.BlockSpec((width, tokens), lambda j, n: (0, 0))
    return pl.pallas_call(
        hidden_back_kernel,
        grid=grid,
        in_specs=[whole, turned, turned, weight, weight, active, active],
        out_specs=[weight, weight, pl.BlockSpec((1, 1, block), lambda j, n: (j, 0, n)), whole],
        out_shape=[
            jax.ShapeDtypeStruct(w1.shape, low),
            jax.ShapeDtypeStruct(w1.shape, low),
            jax.ShapeDtypeStruct((parts, 1, inner), f32),
            jax.ShapeDtypeStruct((tokens, width), low),
        ],
        scratch_shapes=[pltpu.VMEM((tokens, block), low), pltpu.VMEM((tokens, width), f32)],
        compiler_params=pltpu.CompilerParams(vmem_limit_bytes=VMEM),
        cost_estimate=pl.CostEstimate(
            flops=8 * tokens * width * parts * inner,
            bytes_accessed=16 * width * parts * inner,
            transcendentals=0,
        ),
        name="hidden_backward",
    )(dz, dz.T, f.T, w1, w2, act, slope)


MESH = pl.DeviceIdType.MESH
ANYWHERE = pl.BlockSpec(memory_space=pl.ANY)
IN_VMEM = pl.BlockSpec(memory_space=pltpu.VMEM)


def here():
    return lax.axis_index("dp"), lax.axis_index("row"), lax.axis_index("col")


def meet(partners):
    barrier = pltpu.get_barrier_semaphore()
    for partner in partners:
        pl.semaphore_signal(barrier, inc=1, device_id=partner, device_id_type=MESH)
    pl.semaphore_wait(barrier, len(partners))


def remote(src, dst, sends, recvs, device):
    return pltpu.make_async_remote_copy(
        src_ref=src, dst_ref=dst, send_sem=sends, recv_sem=recvs, device_id=device,
        device_id_type=MESH,
    )


def start_kernel(
    tokens, encoder, vec_f, vec_c, *refs, n_col,
):
    weights, (x_ext, enc, all_f, all_c), full = refs[:8], refs[8:12], refs[12:20]
    zeros, w_send, w_recv, w_own, t_send, t_recv, e_send, e_recv, v_send, v_recv, z_sem = refs[20:]
    dp, row, col = here()
    part = lax.rem(dp, PARTS)
    twin = (dp, 1 - row, col)
    flip = [
        dp + 1 - 2 * lax.rem(dp, 2),
        dp + 2 - 4 * lax.rem(dp // 2, 2),
    ]
    by_x, by_y = (flip[0], row, col), (flip[1], row, col)
    part_x, part_y = lax.rem(flip[0], PARTS), lax.rem(flip[1], PARTS)
    shift = [lax.rem(col + k, n_col) for k in range(n_col)]
    group = [(dp, r, c) for r in (row, 1 - row) for c in shift][1:]
    meet(group + [by_x, by_y])

    wide = tokens.shape[1]
    deep = n_col * wide
    rest = deep - wide

    def chunk(index, size):
        return pl.ds(pl.multiple_of(index * size, size), size)

    def weight_z(i, k):
        w, to = weights[i], (dp, row, lax.rem(col + n_col - k, n_col))
        if i % 4 < 3:
            size = w.shape[1] // PARTS
            src = w.at[:, chunk(part, size)]
            dst = full[i].at[pl.ds(k * wide, wide), chunk(part, size)]
        else:
            size = w.shape[0] // PARTS
            src = w.at[chunk(part, size), :]
            dst = full[i].at[chunk(part, size), pl.ds(k * wide, wide)]
        return remote(src, dst, w_send.at[i, k - 1], w_recv.at[i, k - 1], to)

    def weight_own(i):
        w = weights[i]
        place = full[i].at[pl.ds(0, wide), :] if i % 4 < 3 else full[i].at[:, pl.ds(0, wide)]
        return pltpu.make_async_copy(w, place, w_own.at[i])

    def weight_part(i, which, begin, size):
        if i % 4 < 3:
            return full[i].at[pl.ds(begin, size), chunk(which, weights[i].shape[1] // PARTS)]
        return full[i].at[chunk(which, weights[i].shape[0] // PARTS), pl.ds(begin, size)]

    def weight_plane(i, stage):
        half = rest // 2
        which, begin, size, to = [
            (part, wide, rest, by_x),
            (part, wide, rest, by_y),
            (part_x, wide, half, by_y),
            (part_y, wide + half, half, by_x),
        ][stage]
        ref = weight_part(i, which, begin, size)
        return remote(ref, ref, w_send.at[i, 3 + stage], w_recv.at[i, 3 + stage], to)

    def token_piece(j, slot):
        rows = tokens.shape[0] // n_col
        to_col = 2 * row + j // 2 + (1 - slot)
        k = lax.rem(col + n_col - lax.rem(to_col, n_col), n_col)
        src = tokens.at[pl.ds(j * rows, rows), :]
        dst = x_ext.at[slot, :, chunk(k, wide)]
        local = (row == j % 2) & (col == to_col)
        valid = to_col < n_col
        return src, dst, k, local, valid, (dp, j % 2, to_col)

    def send_tokens(slot):
        for j in range(n_col):
            src, dst, k, local, valid, to = token_piece(j, slot)

            @pl.when(valid & local)
            def _():
                pltpu.make_async_copy(src, dst, t_recv.at[slot, k]).start()

            @pl.when(valid & jnp.logical_not(local))
            def _():
                remote(src, dst, t_send.at[slot, j], t_recv.at[slot, k], to).start()

    def enc_z(k):
        ref = enc.at[chunk(row, encoder.shape[0]), pl.ds(k * wide, wide)]
        to = (dp, row, lax.rem(col + n_col - k, n_col))
        return remote(encoder, ref, e_send.at[0, k], e_recv.at[0, k], to)

    def enc_twin(k):
        ref = enc.at[chunk(row, encoder.shape[0]), pl.ds(k * wide, wide)]
        return remote(encoder if k == 0 else ref, ref, e_send.at[1, k], e_recv.at[1, k], twin)

    def vectors(k):
        to = (dp, row, lax.rem(col + n_col - k, n_col))
        return [
            remote(vec_f, all_f.at[:, pl.ds(k * wide, wide)], v_send.at[0, k], v_recv.at[0, k], to),
            remote(vec_c, all_c.at[col], v_send.at[1, k], v_recv.at[1, k], to),
        ]

    own_vectors = [
        pltpu.make_async_copy(vec_f, all_f.at[:, pl.ds(0, wide)], v_recv.at[0, 0]),
        pltpu.make_async_copy(vec_c, all_c.at[col], v_recv.at[1, 0]),
        pltpu.make_async_copy(
            encoder, enc.at[chunk(row, encoder.shape[0]), pl.ds(0, wide)], e_recv.at[0, 0]
        ),
    ]
    ks = range(1, n_col)
    for i in range(4):
        for k in ks:
            weight_z(i, k).start()
    send_tokens(1)
    for k in ks:
        for copy in vectors(k):
            copy.start()
    for i in range(4, 8):
        for k in ks:
            weight_z(i, k).start()
    send_tokens(0)
    enc_twin(0).start()
    for k in ks:
        enc_z(k).start()
    for i in range(8):
        weight_own(i).start()
    for copy in own_vectors:
        copy.start()

    @pl.when(col == 0)
    def _():
        zeros[...] = jnp.zeros_like(zeros)
        clear = pltpu.make_async_copy(zeros, x_ext.at[0], z_sem)
        clear.start()
        clear.wait()

    for base in (0, 4):
        for i in range(base, base + 4):
            for k in ks:
                weight_z(i, k).wait_recv()
            weight_plane(i, 0).start()
            weight_plane(i, 1).start()
        for i in range(base, base + 4):
            weight_plane(i, 0).wait_recv()
            weight_plane(i, 2).start()
            weight_plane(i, 1).wait_recv()
            weight_plane(i, 3).start()
    for k in ks:
        enc_z(k).wait_recv()
        enc_twin(k).start()
    for i in range(8):
        weight_plane(i, 2).wait_recv()
        weight_plane(i, 3).wait_recv()
        weight_own(i).wait()
        for k in ks:
            weight_z(i, k).wait_send()
        for stage in range(4):
            weight_plane(i, stage).wait_send()
    for copy in own_vectors:
        copy.wait()
    for k in ks:
        for copy in vectors(k):
            copy.wait()
        enc_z(k).wait_send()
    for k in range(n_col):
        enc_twin(k).wait()
    for slot in (1, 0):
        for j in range(n_col):
            src, dst, k, local, valid, to = token_piece(j, slot)

            @pl.when(valid & jnp.logical_not(local))
            def _():
                remote(src, dst, t_send.at[slot, j], t_recv.at[slot, k], to).wait_send()

        for k in range(n_col):
            rows = tokens.shape[0] // n_col
            came = pltpu.make_async_copy(
                tokens.at[pl.ds(0, rows), :],
                x_ext.at[slot, :, pl.ds(k * wide, wide)],
                t_recv.at[slot, k],
            )
            if slot == 1:
                came.wait()
            else:

                @pl.when(col > 0)
                def _():
                    came.wait()


def start(tokens, encoder, vec_f, vec_c, weights, n_col):
    wide = tokens.shape[1]
    deep = n_col * wide
    rows = tokens.shape[0] // n_col
    shapes = [
        jax.ShapeDtypeStruct((2, rows, deep), low),
        jax.ShapeDtypeStruct((2 * encoder.shape[0], deep), low),
        jax.ShapeDtypeStruct((vec_f.shape[0], deep), f32),
        jax.ShapeDtypeStruct((n_col,) + vec_c.shape, f32),
    ]
    for i, w in enumerate(weights):
        shapes.append(
            jax.ShapeDtypeStruct((deep, w.shape[1]) if i % 4 < 3 else (w.shape[0], deep), low)
        )
    dma = pltpu.SemaphoreType.DMA
    return pl.pallas_call(
        functools.partial(start_kernel, n_col=n_col),
        in_specs=[ANYWHERE] * 12,
        out_specs=[ANYWHERE] * 12,
        out_shape=shapes,
        scratch_shapes=[
            pltpu.VMEM((rows, deep), low),
            dma((8, 7)), dma((8, 7)), dma((8,)),
            dma((2, n_col)), dma((2, n_col)),
            dma((2, n_col)), dma((2, n_col)),
            dma((2, n_col)), dma((2, n_col)),
            dma,
        ],
        compiler_params=pltpu.CompilerParams(
            collective_id=1, has_side_effects=True, vmem_limit_bytes=VMEM
        ),
        name="start",
    )(tokens, encoder, vec_f, vec_c, *weights)


def norm_rows(x):
    center = jnp.mean(x, axis=1, keepdims=True)
    spread = jnp.mean(x * x, axis=1, keepdims=True) - center * center
    scaling = lax.rsqrt(spread + norm_epsilon)
    return (x - center) * scaling, scaling


CUT = 256


def enter_kernel(x_ref, gain, shift, a_ref, sends, recvs):
    dp, row, col = here()
    twin = (dp, 1 - row, col)
    meet([twin])
    slots, rows = x_ref.shape[:2]

    def place(slot):
        return a_ref.at[slot, pl.ds(pl.multiple_of(row * rows, rows), rows), :]

    copies = []
    for slot in reversed(range(slots)):
        for t in range(rows // CUT):
            normed, _ = norm_rows(x_ref[slot, pl.ds(t * CUT, CUT), :].astype(f32))
            begin = pl.multiple_of(row * rows + t * CUT, CUT)
            a_ref[slot, pl.ds(begin, CUT), :] = (normed * gain[...] + shift[...]).astype(low)
        copy = remote(place(slot), place(slot), sends.at[slot], recvs.at[slot], twin)
        copy.start()
        copies.append(copy)
    for copy in copies:
        copy.wait()


def enter(x_ext, gain, shift, number):
    slots, rows, deep = x_ext.shape
    return pl.pallas_call(
        enter_kernel,
        in_specs=[IN_VMEM] * 3,
        out_specs=IN_VMEM,
        out_shape=jax.ShapeDtypeStruct((slots, 2 * rows, deep), low),
        scratch_shapes=[pltpu.SemaphoreType.DMA((slots,)), pltpu.SemaphoreType.DMA((slots,))],
        compiler_params=pltpu.CompilerParams(
            collective_id=number, has_side_effects=True, vmem_limit_bytes=VMEM
        ),
        name="enter",
    )(x_ext, gain[None], shift[None])


def junction_kernel(*refs, kinds, mode):
    dp, row, col = here()
    twin = (dp, 1 - row, col)
    meet([twin])
    refs = list(refs)
    sources = []
    for kind in kinds:
        sources.append((kind, refs.pop(0), refs.pop(0) if kind != "sum" else None))
    if mode == "forward":
        x_ref, bias, gain, shift, x_out, full, away, came, s1, r1, s2, r2 = refs
    elif mode == "backward":
        res_ref, x_ref, gain, dx_out, full, stats, away, came, s1, r1, s2, r2 = refs
    else:
        out, away, came, s1, r1 = refs
    rows = came.shape[0]
    cuts = rows // CUT

    def partial(begin):
        total = None
        for kind, g, w in sources:
            part = g[pl.ds(begin, CUT), :]
            if kind == "sum":
                part = part.astype(f32)
            elif kind == "nt":
                part = mm_nt(part, w[...])
            else:
                part = mm(part, w[...])
            total = part if total is None else total + part
        return total

    sent = []
    for t in range(cuts):
        at = pl.ds(t * CUT, CUT)
        away[at, :] = partial(pl.multiple_of((1 - row) * rows + t * CUT, CUT)).astype(low)
        copy = remote(away.at[at, :], came.at[at, :], s1.at[t], r1.at[t], twin)
        copy.start()
        sent.append(copy)
    gathered = []
    sums = [0.0, 0.0, 0.0]
    for t in range(cuts):
        at = pl.ds(t * CUT, CUT)
        begin = pl.multiple_of(row * rows + t * CUT, CUT)
        own = partial(begin)
        sent[t].wait_recv()
        total = own + came[at, :].astype(f32)
        if mode == "sum":
            out[at, :] = total
            continue
        if mode == "forward":
            x = x_ref[at, :].astype(f32) + (total + bias[...])
            x_out[at, :] = x
            normed, _ = norm_rows(x)
            result = (normed * gain[...] + shift[...]).astype(low)
        else:
            normed, scaling = norm_rows(x_ref[at, :].astype(f32))
            upstream = total * gain[...]
            mean_up = jnp.mean(upstream, axis=1, keepdims=True)
            mean_both = jnp.mean(upstream * normed, axis=1, keepdims=True)
            dx = res_ref[at, :].astype(f32) + scaling * (upstream - mean_up - normed * mean_both)
            dx_out[at, :] = dx
            result = dx.astype(low)
            for i, value in enumerate((total * normed, total, result.astype(f32))):
                sums[i] = sums[i] + jnp.sum(value, axis=0, keepdims=True)
        if full is None:
            continue
        full[pl.ds(begin, CUT), :] = result
        place = full.at[pl.ds(begin, CUT), :]
        copy = remote(place, place, s2.at[t], r2.at[t], twin)
        copy.start()
        gathered.append(copy)
    if mode == "backward":
        for i in range(3):
            stats[i : i + 1, :] = sums[i]
    for copy in sent:
        copy.wait_send()
    for copy in gathered:
        copy.wait()


def junction(mode, sources, others, number):
    kinds = [x[0] for x in sources]
    first = sources[0]
    tokens = first[1].shape[0]
    deep = first[1].shape[1]
    if first[0] != "sum":
        deep = first[2].shape[0 if first[0] == "nt" else 1]
    rows = tokens // 2
    flat = [x for source in sources for x in source[1:]]
    dma = pltpu.SemaphoreType.DMA((rows // CUT,))
    wide_rows = jax.ShapeDtypeStruct((rows, deep), f32)
    every = jax.ShapeDtypeStruct((tokens, deep), low)
    shapes = {
        "forward": [wide_rows, every],
        "backward": [wide_rows, every, jax.ShapeDtypeStruct((8, deep), f32)],
        "sum": [wide_rows],
    }[mode]
    scratch = [pltpu.VMEM((rows, deep), low), pltpu.VMEM((rows, deep), low), dma, dma]
    if mode != "sum":
        scratch += [dma, dma]
    args = flat + [x[None] if x.ndim == 1 else x for x in others]
    out = pl.pallas_call(
        functools.partial(junction_kernel, kinds=kinds, mode=mode),
        in_specs=[IN_VMEM] * len(args),
        out_specs=[IN_VMEM] * len(shapes),
        out_shape=shapes,
        scratch_shapes=scratch,
        compiler_params=pltpu.CompilerParams(
            collective_id=number, has_side_effects=True, vmem_limit_bytes=VMEM
        ),
        name="junction_" + mode,
    )(*args)
    return out if len(out) > 1 else out[0]


def norm_backward(incoming, normed, scaling, gain):
    gain_grad = jnp.sum(incoming * normed, axis=0)
    bias_grad = jnp.sum(incoming, axis=0)
    upstream = incoming * gain
    mean_up = jnp.mean(upstream, axis=1, keepdims=True)
    mean_both = jnp.mean(upstream * normed, axis=1, keepdims=True)
    return scaling * (upstream - mean_up - normed * mean_both), gain_grad, bias_grad


def build_local(mesh):
    n_dp, n_col = mesh.shape["dp"], mesh.shape["col"]

    def swap(x):
        return lax.ppermute(x, "row", [(0, 1), (1, 0)])

    def from_col(x, k):
        return lax.ppermute(x, "col", [(i, (i - k) % n_col) for i in range(n_col)])

    def to_col(x, k):
        return lax.ppermute(x, "col", [(i, (i + k) % n_col) for i in range(n_col)])

    def across(x, bit):
        return lax.ppermute(x, "dp", [(i, i ^ bit) for i in range(n_dp)])

    def plane_gather(x):
        half = x.shape[0] // 2
        by_x, by_y = across(x, 1), across(x, 2)
        far = jnp.concatenate([across(by_x[:half], 2), across(by_y[half:], 1)], axis=0)
        return [x, by_x, by_y, far]

    def plane_scatter(parts):
        half = parts[0].shape[0] // 2
        a, b = [p[:half] for p in parts], [p[half:] for p in parts]
        got = across(jnp.stack([a[1], a[3]]), 1)
        a0, a2 = a[0] + got[0], a[2] + got[1]
        got = across(jnp.stack([b[2], b[3]]), 2)
        b0, b1 = b[0] + got[0], b[1] + got[1]
        a0 = a0 + across(a2, 2)
        b0 = b0 + across(b1, 1)
        return jnp.concatenate([a0, b0], axis=0)

    def local(
        tokens, encoder, cotangent, dec_lengths, src_lengths,
        self_norm_gain, self_norm_bias, self_query, self_key, self_value,
        self_query_bias, self_value_bias, self_out, self_out_bias,
        cross_norm_gain, cross_norm_bias, cross_query, cross_key, cross_value,
        cross_query_bias, cross_value_bias, cross_out, cross_out_bias,
        hidden_norm_gain, hidden_norm_bias, hidden_in, hidden_in_bias,
        hidden_out, hidden_out_bias,
    ):
        row, col = lax.axis_index("row"), lax.axis_index("col")
        place = lax.axis_index("dp") % PARTS
        wide = tokens.shape[1]
        chunk = tokens.shape[0] // n_col
        span = 2 * chunk

        def by_row(own, other):
            return jnp.where(
                row == 0,
                jnp.concatenate([own, other], axis=0),
                jnp.concatenate([other, own], axis=0),
            )

        def row_gather(own):
            return by_row(own, swap(own))

        def row_scatter(partial):
            half = partial.shape[0] // 2
            away = lax.dynamic_slice_in_dim(partial, (1 - row) * half, half, 0)
            mine = lax.dynamic_slice_in_dim(partial, row * half, half, 0)
            return mine.astype(f32) + swap(away.astype(low)).astype(f32)

        def spread_rows(x):
            cut = x.reshape(2, 2, chunk, wide)
            own = lax.dynamic_index_in_dim(cut, row, 1, keepdims=False)
            other = swap(lax.dynamic_index_in_dim(cut, 1 - row, 1, keepdims=False))
            every = by_row(own, other)
            pieces = []
            for k in range(n_col):
                piece = lax.dynamic_index_in_dim(every, (col - k) % n_col, 0, keepdims=False)
                pieces.append(from_col(piece, k) if k else piece)
            return jnp.concatenate(pieces, axis=1)

        def collect_rows(x):
            every = jnp.zeros((n_col, chunk, wide), x.dtype)
            for k in range(n_col):
                piece = x[:, k * wide : (k + 1) * wide]
                piece = to_col(piece, k) if k else piece
                every = lax.dynamic_update_index_in_dim(every, piece, (col - k) % n_col, 0)
            own = lax.dynamic_slice_in_dim(every, 2 * row, 2, 0)
            other = swap(lax.dynamic_slice_in_dim(every, 2 * (1 - row), 2, 0))
            both = jnp.where(
                row == 0, jnp.stack([own, other], axis=1), jnp.stack([other, own], axis=1)
            )
            return both.reshape(n_col * chunk, wide)

        def in_order(parts):
            stacked = jnp.stack(parts)
            return [
                lax.dynamic_index_in_dim(stacked, i ^ place, 0, keepdims=False)
                for i in range(PARTS)
            ]

        def weights_of(arrays):
            def own(j):
                cuts = []
                for w in arrays:
                    size = w.shape[1] // PARTS
                    cuts.append(lax.dynamic_slice_in_dim(w, (place ^ j) * size, size, 1))
                return jnp.concatenate(cuts, axis=1)

            mine = own(0)
            rest = jnp.concatenate([from_col(mine, k) for k in range(1, n_col)], axis=0)
            return [
                jnp.concatenate([own(j), part], axis=0)
                for j, part in enumerate(plane_gather(rest))
            ]

        def grads_of(parts):
            mine = plane_scatter(parts)
            total = mine[:wide].astype(f32)
            for k in range(1, n_col):
                total = total + to_col(mine[k * wide : (k + 1) * wide], k).astype(f32)
            bit = PARTS
            while bit < n_dp:
                total = total + across(total.astype(low), bit).astype(f32)
                bit *= 2
            return in_order(plane_gather(total.astype(low)))

        vec_f = jnp.stack([
            self_norm_gain, self_norm_bias, self_out_bias, cross_norm_gain, cross_norm_bias,
            cross_out_bias, hidden_norm_gain, hidden_norm_bias, hidden_out_bias,
        ])
        vec_f = jnp.pad(vec_f, ((0, 7), (0, 0)))
        vec_c = jnp.concatenate(
            [self_query_bias, self_value_bias, cross_query_bias, cross_value_bias, hidden_in_bias]
        ).reshape(-1, 128)
        vec_c = jnp.pad(vec_c, ((0, -vec_c.shape[0] % 8), (0, 0)))
        weights = [
            self_query, self_key, self_value, self_out,
            cross_query, cross_key, cross_value, cross_out,
        ]
        x_ext, enc, vectors, columns, *full = start(
            tokens, encoder, vec_f, vec_c, weights, n_col
        )
        wq1, wk1, wv1, wo1, wq2, wk2, wv2, wo2 = full
        (gain1, shift1, out_bias1, gain2, shift2, out_bias2, gain3, shift3, out_bias3) = vectors[:9]
        size = self_query_bias.shape[0]

        def column_vector(start, size):
            return columns.reshape(n_col, -1)[:, start : start + size].reshape(-1)

        q_bias1 = column_vector(0, size)
        v_bias1 = column_vector(size, size)
        q_bias2 = column_vector(2 * size, size)
        v_bias2 = column_vector(3 * size, size)
        hidden_bias = column_vector(4 * size, hidden_in_bias.shape[0]).reshape(PARTS, -1)
        hidden_bias = jnp.stack(
            [lax.dynamic_index_in_dim(hidden_bias, place ^ j, 0) for j in range(PARTS)]
        )

        hidden_in, hidden_out, cotangent, x_ext = lax.optimization_barrier(
            (hidden_in, hidden_out, cotangent, x_ext)
        )
        w1 = jnp.stack(weights_of([hidden_in]))
        w2 = jnp.stack(weights_of([hidden_out.T]))
        step = self_query.shape[1] // PARTS

        dec_ids = doc_numbers(dec_lengths, SEQ_LEN)[0]
        src_ids = doc_numbers(src_lengths, ENC)[0]
        padded = jnp.pad(dec_ids, (WIN, 0), constant_values=-1)
        key_ids = lax.dynamic_slice_in_dim(padded, col * span, WIN + span, 0)
        query_ids = key_ids[WIN:]

        scale = low(HEAD_DIM**-0.5)
        x0 = x_ext[1]
        a_ext = enter(x_ext, gain1, shift1, 2).reshape(WIN + span, -1)
        a = a_ext[WIN:]
        q1 = (mm(a, wq1) + q_bias1).astype(low) * scale
        k1 = mm(a_ext, wk1).astype(low)
        v1 = (mm(a_ext, wv1) + v_bias1).astype(low)
        o1, lse1 = attend(q1, k1, v1, query_ids, key_ids, True)
        x1, c = junction("forward", [("nn", o1, wo1)], [x0, out_bias1, gain2, shift2], 3)

        q2 = (mm(c, wq2) + q_bias2).astype(low) * scale
        k2 = mm(enc, wk2).astype(low)
        v2 = (mm(enc, wv2) + v_bias2).astype(low)
        o2, lse2 = attend(q2, k2, v2, query_ids, src_ids, False)
        x2, f = junction("forward", [("nn", o2, wo2)], [x1, out_bias2, gain3, shift3], 4)

        act, slope, branch = hidden_forward(f, w1, hidden_bias, w2)
        layer_out = collect_rows(
            (x2 + (junction("sum", [("sum", branch)], [], 5) + out_bias3)).astype(low)
        )

        dz_own = spread_rows(cotangent)
        dz = row_gather(dz_own)
        g1, g2, hidden_bias_grad, df = hidden_backward(dz, f, w1, w2, act, slope)
        g1_parts = grads_of([g1[j] for j in range(PARTS)])
        g2_parts = grads_of([g2[j] for j in range(PARTS)])
        dx2, dyc, stats3 = junction("backward", [("sum", df)], [dz_own, x2, gain3], 6)

        doc = mm_nt(dyc, wo2).astype(low)
        dq2, dk2, dv2 = attend_back(q2, k2, v2, doc, o2, lse2, query_ids, src_ids, False)
        grads = [
            mm_tn(c, dq2).astype(low),
            mm_tn(enc, dk2).astype(low),
            mm_tn(enc, dv2).astype(low),
            mm_tn(dyc, o2).astype(low),
        ]

        def by_part(arrays):
            return [
                jnp.concatenate(
                    [
                        lax.dynamic_slice_in_dim(g, (place ^ j) * step, step, 1)
                        for g in arrays
                    ],
                    axis=1,
                )
                for j in range(PARTS)
            ]

        cross_grads = grads_of(by_part(grads))
        enc_back = junction("sum", [("nt", dk2, wk2), ("nt", dv2, wv2)], [], 7)
        encoder_grad = enc_back[:, :wide]
        for k in range(1, n_col):
            encoder_grad = encoder_grad + to_col(
                enc_back[:, k * wide : (k + 1) * wide].astype(low), k
            ).astype(f32)
        dx1, dy, stats2 = junction("backward", [("nt", dq2, wq2)], [dx2, x1, gain2], 8)

        do = mm_nt(dy, wo1).astype(low)
        dq1, dk1, dv1 = attend_back(q1, k1, v1, do, o1, lse1, query_ids, key_ids, True)
        da_before = junction("sum", [("nt", dk1[:WIN], wk1), ("nt", dv1[:WIN], wv1)], [], 9)
        da_after = lax.ppermute(
            da_before.astype(low), "col", [(i + 1, i) for i in range(n_col - 1)]
        )
        da_after = jnp.concatenate([da_after[:, -wide:], da_after[:, :-wide]], axis=1)
        da = junction(
            "sum", [("nt", dq1, wq1), ("nt", dk1[WIN:], wk1), ("nt", dv1[WIN:], wv1)], [], 10
        ) + da_after.astype(f32)
        grads = [
            mm_tn(a, dq1).astype(low),
            mm_tn(a_ext, dk1).astype(low),
            mm_tn(a_ext, dv1).astype(low),
            mm_tn(dy, o1).astype(low),
        ]
        self_grads = grads_of(by_part(grads))
        normed1, scaling1 = norm_rows(x0.astype(f32))
        back1, gain_grad1, shift_grad1 = norm_backward(da, normed1, scaling1, gain1)
        tokens_grad = collect_rows((dx1 + back1).astype(low)).astype(f32)

        def total(x):
            return jnp.sum(x, axis=0, dtype=f32)

        feature_grads = jnp.concatenate([
            jnp.stack([gain_grad1, shift_grad1]), stats2[2:3], stats2[:2], stats3[2:3], stats3[:2],
            total(dz_own)[None],
        ])
        count = feature_grads.shape[0]
        chunks = jnp.moveaxis(feature_grads.reshape(count, n_col, wide), 1, 0)
        chunks = lax.dynamic_slice_in_dim(
            jnp.concatenate([chunks, chunks]), (n_col - col) % n_col, n_col, 0
        )
        chunks = lax.psum(chunks, ("dp", "row", "col"))
        feature_grads = lax.dynamic_index_in_dim(chunks, col, 0, keepdims=False)
        column_grads = []
        for vector in (total(dq1), total(dv1), total(dq2), total(dv2), hidden_bias_grad):
            parts = vector.reshape(PARTS, -1)
            if vector is hidden_bias_grad:
                parts = jnp.stack(in_order([parts[j] for j in range(PARTS)]))
            column_grads.append(parts.reshape(n_col, -1))
        column_grads = lax.psum(jnp.concatenate(column_grads, axis=1), ("dp", "col"))
        column_grads = lax.dynamic_index_in_dim(column_grads, col, 0, keepdims=False)

        def whole(parts, index=None):
            if index is not None:
                parts = [p[:, index * step : (index + 1) * step] for p in parts]
            return jnp.concatenate(parts, axis=1).astype(f32)

        return (
            layer_out,
            tokens_grad,
            encoder_grad,
            feature_grads[0],
            feature_grads[1],
            whole(self_grads, 0),
            whole(self_grads, 1),
            whole(self_grads, 2),
            column_grads[:size],
            column_grads[size : 2 * size],
            whole(self_grads, 3).T,
            feature_grads[2],
            feature_grads[3],
            feature_grads[4],
            whole(cross_grads, 0),
            whole(cross_grads, 1),
            whole(cross_grads, 2),
            column_grads[2 * size : 3 * size],
            column_grads[3 * size : 4 * size],
            whole(cross_grads, 3).T,
            feature_grads[5],
            feature_grads[6],
            feature_grads[7],
            whole(g1_parts),
            column_grads[4 * size :],
            whole(g2_parts).T,
            feature_grads[8],
        )

    return local


def solution(mesh):
    rows = P(("dp", "row"), "col")
    features = P("col")
    columns = P(("row", "col"))
    into, out_of = P("col", "row"), P("row", "col")
    attention = (into, into, into, columns, columns, out_of, features)
    norm = (features, features)
    weights = (
        norm
        + attention
        + norm
        + attention
        + norm
        + (into, columns, out_of, features)
    )
    return jax.shard_map(
        build_local(mesh),
        mesh=mesh,
        in_specs=(rows, rows, rows, P("dp", None), P("dp", None)) + weights,
        out_specs=(rows, rows, rows) + weights,
        check_vma=False,
    )
```

```python
import functools

import jax
import jax.numpy as jnp
from jax import lax
from jax.experimental import pallas as pl
from jax.experimental.pallas import tpu as pltpu
from jax.sharding import PartitionSpec as P

D = 1024
HEAD_DIM = 64
SEQ_LEN = 4096
ENC = 1024
WIN = 1024

norm_epsilon = 1e-05
masked_fill = -1e30
low = jnp.bfloat16
f32 = jnp.float32
PARTS = 4
PAIR = 2 * HEAD_DIM
QUERY_ROWS = 256
VMEM = 56 * 1024 * 1024


def doc_numbers(lengths, positions):
    bounds = jnp.cumsum(lengths, axis=1, dtype=jnp.int32)
    places = jnp.arange(positions, dtype=jnp.int32)
    return jnp.sum(
        (places[None, :, None] >= bounds[:, None, :]).astype(jnp.int32), axis=2, dtype=jnp.int32
    )


def mm(a, b):
    return lax.dot_general(a, b, (((1,), (0,)), ((), ())), preferred_element_type=f32)


def mm_nt(a, b):
    return lax.dot_general(a, b, (((1,), (1,)), ((), ())), preferred_element_type=f32)


def mm_tn(a, b):
    return lax.dot_general(a, b, (((0,), (0,)), ((), ())), preferred_element_type=f32)


MESH = pl.DeviceIdType.MESH
ANYWHERE = pl.BlockSpec(memory_space=pl.ANY)
IN_VMEM = pl.BlockSpec(memory_space=pltpu.VMEM)


def here():
    return lax.axis_index("dp"), lax.axis_index("row"), lax.axis_index("col")


def meet(partners):
    barrier = pltpu.get_barrier_semaphore()
    for partner in partners:
        pl.semaphore_signal(barrier, inc=1, device_id=partner, device_id_type=MESH)
    pl.semaphore_wait(barrier, len(partners))


def remote(src, dst, sends, recvs, device):
    return pltpu.make_async_remote_copy(
        src_ref=src, dst_ref=dst, send_sem=sends, recv_sem=recvs, device_id=device,
        device_id_type=MESH,
    )


def plane():
    dp, row, col = here()
    flips = [dp + b - 2 * b * lax.rem(dp // b, 2) for b in (1, 2)]
    return (flips[0], row, col), (flips[1], row, col)


def head_masks():
    lane = lax.broadcasted_iota(jnp.int32, (1, PAIR), 1)
    first = jnp.where(lane < HEAD_DIM, 1.0, 0.0)
    return first.astype(low), (1.0 - first).astype(low), lane < HEAD_DIM


def attend_kernel(q_ref, k_ref, v_ref, qid_ref, kid_ref, o_ref, lse_ref, bias, *, span, windowed):
    rows = q_ref.shape[0]
    pairs = q_ref.shape[1] // PAIR
    start = pl.program_id(0) * rows if windowed else 0
    if windowed:
        start = pl.multiple_of(start, rows)
    allowed = qid_ref[...] == kid_ref[0:1, pl.ds(start, span)]
    if windowed:
        at_row = lax.broadcasted_iota(jnp.int32, (rows, span), 0)
        at_key = lax.broadcasted_iota(jnp.int32, (rows, span), 1)
        allowed = allowed & (at_key > at_row) & (at_key <= at_row + WIN)
    bias[...] = jnp.where(allowed, 0.0, masked_fill)
    first, second, is_first = head_masks()

    def one_pair(p, carry):
        lanes = pl.ds(pl.multiple_of(p * PAIR, PAIR), PAIR)
        q2 = q_ref[:, lanes]
        k2 = k_ref[pl.ds(start, span), lanes]
        v2 = v_ref[pl.ds(start, span), lanes]
        outs, logs = [], []
        for mask in (first, second):
            s = mm_nt(q2 * mask, k2) + bias[...]
            top = jnp.max(s, axis=1, keepdims=True)
            e = jnp.exp(s - top)
            total = jnp.sum(e, axis=1, keepdims=True)
            outs.append(mm(e.astype(low), v2) / total)
            logs.append(top + jnp.log(total))
        o_ref[:, lanes] = jnp.where(is_first, outs[0], outs[1]).astype(low)
        stats = jnp.where(is_first, logs[0], logs[1])
        turned = jnp.transpose(stats)
        lse_ref[p, 0:1, :] = turned[0:1]
        lse_ref[p, 1:2, :] = turned[HEAD_DIM : HEAD_DIM + 1]
        return carry

    lax.fori_loop(0, pairs, one_pair, 0)


def attend(q, k, v, qid, kid, windowed):
    tokens, width = q.shape
    keys = k.shape[0]
    pairs = width // PAIR
    rows = QUERY_ROWS
    span = WIN + rows if windowed else keys
    return pl.pallas_call(
        functools.partial(attend_kernel, span=span, windowed=windowed),
        grid=(tokens // rows,),
        in_specs=[
            pl.BlockSpec((rows, width), lambda i: (i, 0)),
            pl.BlockSpec((keys, width), lambda i: (0, 0)),
            pl.BlockSpec((keys, width), lambda i: (0, 0)),
            pl.BlockSpec((rows, 1), lambda i: (i, 0)),
            pl.BlockSpec((1, keys), lambda i: (0, 0)),
        ],
        out_specs=[
            pl.BlockSpec((rows, width), lambda i: (i, 0)),
            pl.BlockSpec((pairs, 8, rows), lambda i: (0, 0, i)),
        ],
        out_shape=[
            jax.ShapeDtypeStruct((tokens, width), low),
            jax.ShapeDtypeStruct((pairs, 8, tokens), f32),
        ],
        scratch_shapes=[pltpu.VMEM((rows, span), f32)],
        compiler_params=pltpu.CompilerParams(vmem_limit_bytes=VMEM),
        name="attend",
    )(q, k, v, qid[:, None], kid[None, :])


def attend_back_kernel(*refs, span, windowed, rider, n_ins, n_outs):
    refs = list(refs)
    q_ref, k_ref, v_ref, do_ref, o_ref, lse_ref, qid_ref, kid_ref = refs[:8]
    rider_refs = refs[8 : 8 + n_ins]
    refs = refs[8 + n_ins :]
    dq_ref, dk_ref, dv_ref = refs[:3]
    rider_refs += refs[3 : 3 + n_outs]
    bias, dk_sum, dv_sum = refs[3 + n_outs : 6 + n_outs]
    rider_refs += refs[6 + n_outs :]
    rows = q_ref.shape[0]
    pairs = q_ref.shape[1] // PAIR
    step = pl.program_id(0)
    start = pl.multiple_of(step * rows, rows) if windowed else 0
    keys = pl.ds(start, span)
    begin, middle, end = rider(*rider_refs)

    @pl.when(step == 0)
    def _():
        begin()
        dk_sum[...] = jnp.zeros_like(dk_sum)
        dv_sum[...] = jnp.zeros_like(dv_sum)

    @pl.when(step == 1)
    def _():
        middle()

    allowed = kid_ref[keys, :] == qid_ref[...]
    if windowed:
        at_key = lax.broadcasted_iota(jnp.int32, (span, rows), 0)
        at_row = lax.broadcasted_iota(jnp.int32, (span, rows), 1)
        allowed = allowed & (at_key > at_row) & (at_key <= at_row + WIN)
    bias[...] = jnp.where(allowed, 0.0, masked_fill)
    first, second, is_first = head_masks()

    def one_pair(p, carry):
        lanes = pl.ds(pl.multiple_of(p * PAIR, PAIR), PAIR)
        q2 = q_ref[:, lanes]
        k2 = k_ref[keys, lanes]
        v2 = v_ref[keys, lanes]
        do2 = do_ref[:, lanes]
        turned = jnp.transpose(do2.astype(f32) * o_ref[:, lanes].astype(f32))
        dk, dv, dqs = 0.0, 0.0, []
        for h, mask in enumerate((first, second)):
            qm, dom = q2 * mask, do2 * mask
            inner = jnp.sum(turned[h * HEAD_DIM : (h + 1) * HEAD_DIM], axis=0, keepdims=True)
            s = mm_nt(k2, qm) + bias[...]
            share = jnp.exp(s - lse_ref[p, h : h + 1, :])
            ds = (share * (mm_nt(v2, dom) - inner)).astype(low)
            dv = dv + mm(share.astype(low), dom)
            dk = dk + mm(ds, qm)
            dqs.append(mm_tn(ds, k2))
        dk_sum[keys, lanes] += dk
        dv_sum[keys, lanes] += dv
        dq_ref[:, lanes] = (jnp.where(is_first, dqs[0], dqs[1]) * HEAD_DIM**-0.5).astype(low)
        return carry

    lax.fori_loop(0, pairs, one_pair, 0)

    @pl.when(step == pl.num_programs(0) - 1)
    def _():
        dk_ref[...] = dk_sum[...].astype(low)
        dv_ref[...] = dv_sum[...].astype(low)
        end()


def attend_back(q, k, v, do, o, lse, qid, kid, windowed, rider, riding, shapes, scratch, number):
    tokens, width = q.shape
    keys = k.shape[0]
    pairs = width // PAIR
    rows = QUERY_ROWS
    span = WIN + rows if windowed else keys
    by_row = pl.BlockSpec((rows, width), lambda i: (i, 0))
    whole = pl.BlockSpec((keys, width), lambda i: (0, 0))
    return pl.pallas_call(
        functools.partial(
            attend_back_kernel, span=span, windowed=windowed, rider=rider, n_ins=len(riding),
            n_outs=len(shapes),
        ),
        grid=(tokens // rows,),
        in_specs=[
            by_row,
            whole,
            whole,
            by_row,
            by_row,
            pl.BlockSpec((pairs, 8, rows), lambda i: (0, 0, i)),
            pl.BlockSpec((1, rows), lambda i: (0, i)),
            pl.BlockSpec((keys, 1), lambda i: (0, 0)),
        ]
        + [ANYWHERE] * len(riding),
        out_specs=[by_row, whole, whole] + [ANYWHERE] * len(shapes),
        out_shape=[
            jax.ShapeDtypeStruct((tokens, width), low),
            jax.ShapeDtypeStruct((keys, width), low),
            jax.ShapeDtypeStruct((keys, width), low),
        ]
        + [jax.ShapeDtypeStruct(*x) for x in shapes],
        scratch_shapes=[
            pltpu.VMEM((span, rows), f32),
            pltpu.VMEM((keys, width), f32),
            pltpu.VMEM((keys, width), f32),
        ]
        + scratch,
        compiler_params=pltpu.CompilerParams(
            vmem_limit_bytes=VMEM, collective_id=number, has_side_effects=True
        ),
        name="attend_back",
    )(q, k, v, do, o, lse, qid[None, :], kid[:, None], *riding)


def first_rider(
    g1, g2, got_a, got_b, back_a, back_b, far_a, far_b,
    load, mid, l_s, s_s, r_s,
):
    by_x, by_y = plane()
    half = back_a.shape[0]
    up, down = pl.ds(0, half), pl.ds(half, half)
    loads = [
        pltpu.make_async_copy(src, load.at[i], l_s.at[i])
        for i, src in enumerate((g1.at[2, up, :], got_a.at[0], g1.at[1, down, :], got_b.at[0]))
    ]
    hops = [
        remote(g2.at[3, up, :], far_a, s_s.at[0], r_s.at[0], by_x),
        remote(g2.at[3, down, :], far_b, s_s.at[1], r_s.at[1], by_y),
        remote(mid.at[0], back_a, s_s.at[2], r_s.at[2], by_y),
        remote(mid.at[1], back_b, s_s.at[3], r_s.at[3], by_x),
    ]

    def begin():
        meet([by_x, by_y])
        for copy in loads + hops[:2]:
            copy.start()

    def middle():
        for i in range(2):
            loads[2 * i].wait()
            loads[2 * i + 1].wait()
            mid[i] = (load[2 * i].astype(f32) + load[2 * i + 1].astype(f32)).astype(low)
            hops[2 + i].start()

    def end():
        for copy in hops:
            copy.wait()

    return begin, middle, end


def second_rider(
    g1, g2, got_a, got_b, back_a, back_b, far_a, far_b,
    near_a, near_b, far_back_a, far_back_b, z_got, own,
    load, mid, load_z, out_z, l_s, lz_s, s_s, r_s, z_s, z_r, o_s,
    *, n_col,
):
    dp, row, col = here()
    by_x, by_y = plane()
    half = back_a.shape[0]
    wide = own.shape[0]
    up, down = pl.ds(0, half), pl.ds(half, half)
    loads = [
        pltpu.make_async_copy(src, load.at[i], l_s.at[i])
        for i, src in enumerate((g2.at[2, up, :], far_a, g2.at[1, down, :], far_b))
    ]
    loads_z = []
    for i, (source, got, back) in enumerate(((up, got_a, back_a), (down, got_b, back_b))):
        for n, src in enumerate((g1.at[0, source, :], got.at[1], back)):
            loads_z.append(
                pltpu.make_async_copy(src, load_z.at[n, source, :], lz_s.at[i, n])
            )
    hops = [
        remote(g2.at[1, up, :], near_a, s_s.at[0], r_s.at[0], by_x),
        remote(g2.at[2, down, :], near_b, s_s.at[1], r_s.at[1], by_y),
        remote(mid.at[0], far_back_a, s_s.at[2], r_s.at[2], by_y),
        remote(mid.at[1], far_back_b, s_s.at[3], r_s.at[3], by_x),
    ]
    cols = [(dp, row, lax.rem(col + k, n_col)) for k in range(n_col)]
    over = [
        remote(out_z.at[k], z_got.at[k - 1], z_s.at[k - 1], z_r.at[k - 1], cols[k])
        for k in range(1, n_col)
    ]
    keep = pltpu.make_async_copy(out_z.at[0], own, o_s)

    def begin():
        meet([by_x, by_y] + cols[1:])
        for copy in loads + loads_z + hops[:2]:
            copy.start()

    def middle():
        for i in range(2):
            loads[2 * i].wait()
            loads[2 * i + 1].wait()
            mid[i] = (load[2 * i].astype(f32) + load[2 * i + 1].astype(f32)).astype(low)
            hops[2 + i].start()
        for copy in loads_z:
            copy.wait()
        for k in list(range(1, n_col)) + [0]:
            at = pl.ds(k * wide, wide)
            value = load_z[0, at, :].astype(f32) + load_z[1, at, :].astype(f32)
            out_z[k] = (value + load_z[2, at, :].astype(f32)).astype(low)
            if k:
                over[k - 1].start()
        keep.start()

    def end():
        for copy in hops + over + [keep]:
            copy.wait()

    return begin, middle, end


ROOT = 0.7978845608028654
CUBE = 0.044715


def hidden_kernel(f_ref, w1_ref, b1_ref, w2_ref, act_ref, slope_ref, out_ref, total):
    step = pl.program_id(0) * pl.num_programs(1) + pl.program_id(1)
    last = pl.num_programs(0) * pl.num_programs(1) - 1

    @pl.when(step == 0)
    def _():
        total[...] = jnp.zeros_like(total)

    def one_part(t, carry):
        rows = pl.ds(pl.multiple_of(t * 256, 256), 256)
        h = mm(f_ref[rows, :], w1_ref[0]) + b1_ref[0]
        square = h * h
        bend = jnp.tanh(h * (ROOT + (ROOT * CUBE) * square))
        half = 0.5 + 0.5 * bend
        act = (h * half).astype(low)
        act_ref[0, rows, :] = act
        slope = half + (0.5 * h) * (1.0 - bend * bend) * (ROOT + (3.0 * ROOT * CUBE) * square)
        slope_ref[0, rows, :] = slope.astype(low)
        total[rows, :] += mm_nt(act, w2_ref[0])
        return carry

    lax.fori_loop(0, f_ref.shape[0] // 256, one_part, 0)

    @pl.when(step == last)
    def _():
        out_ref[...] = total[...].astype(low)


def hidden_forward(f, w1, b1, w2):
    parts, width, inner = w1.shape
    tokens = f.shape[0]
    block = min(512, inner)
    grid = (parts, inner // block)
    weight = pl.BlockSpec((1, width, block), lambda j, n: (j, 0, n))
    active = pl.BlockSpec((1, tokens, block), lambda j, n: (j, 0, n))
    return pl.pallas_call(
        hidden_kernel,
        grid=grid,
        in_specs=[
            pl.BlockSpec((tokens, width), lambda j, n: (0, 0)),
            weight,
            pl.BlockSpec((1, 1, block), lambda j, n: (j, 0, n)),
            weight,
        ],
        out_specs=[active, active, pl.BlockSpec((tokens, width), lambda j, n: (0, 0))],
        out_shape=[
            jax.ShapeDtypeStruct((parts, tokens, inner), low),
            jax.ShapeDtypeStruct((parts, tokens, inner), low),
            jax.ShapeDtypeStruct((tokens, width), low),
        ],
        scratch_shapes=[pltpu.VMEM((tokens, width), f32)],
        compiler_params=pltpu.CompilerParams(vmem_limit_bytes=VMEM),
        name="hidden_forward",
    )(f, w1, b1, w2)


def hidden_back_kernel(
    dz_ref, dzt_ref, ft_ref, w1_ref, w2_ref, act_ref, slope_ref,
    g1_ref, g2_ref, gb_ref, df_ref, got_a, got_b, dh_low, total, away_a, away_b, s_s, r_s,
):
    inner, inners = pl.program_id(1), pl.num_programs(1)
    order = pl.program_id(0)
    step = order * inners + inner
    last = pl.num_programs(0) * inners - 1
    by_x, by_y = plane()
    half = got_a.shape[1]

    @pl.when(step == 0)
    def _():
        meet([by_x, by_y])
        total[...] = jnp.zeros_like(total)

    gb_ref[...] = jnp.zeros_like(gb_ref)

    def one_part(t, carry):
        rows = pl.ds(pl.multiple_of(t * 256, 256), 256)
        dh = (mm(dz_ref[rows, :], w2_ref[0]) * slope_ref[0, rows, :].astype(f32)).astype(low)
        dh_low[rows, :] = dh
        gb_ref[0] += jnp.sum(dh.astype(f32), axis=0, keepdims=True)
        total[rows, :] += mm_nt(dh, w1_ref[0])
        return carry

    lax.fori_loop(0, dz_ref.shape[0] // 256, one_part, 0)

    def one_grad(t, carry):
        rows = pl.ds(pl.multiple_of(t * 256, 256), 256)
        g2_ref[0, rows, :] = mm(dzt_ref[rows, :], act_ref[0]).astype(low)
        g1_ref[0, rows, :] = mm(ft_ref[rows, :], dh_low[...]).astype(low)
        return carry

    lax.fori_loop(0, ft_ref.shape[0] // 256, one_grad, 0)

    block = g1_ref.shape[2]
    lanes = pl.ds(pl.multiple_of(inner * block, block), block)

    def hop(which, slot):
        away, got, to = [(away_a, got_a, by_x), (away_b, got_b, by_y)][which]
        return remote(
            away.at[slot], got.at[slot], s_s.at[which, slot], r_s.at[which, slot], to
        )

    for at, which, slot in ((0, 0, 0), (0, 1, 0), (1, 0, 1), (2, 1, 1)):

        @pl.when(order == at)
        def _():
            away = (away_a, away_b)[which]
            away[slot, :, lanes] = g1_ref[0, which * half : (which + 1) * half, :]

        @pl.when((order == at) & (inner == inners - 1))
        def _():
            hop(which, slot).start()

    @pl.when(step == last)
    def _():
        df_ref[...] = total[...].astype(low)
        for which in range(2):
            for slot in range(2):
                hop(which, slot).wait()


def hidden_backward(dz, f, w1, w2, act, slope, number):
    parts, width, inner = w1.shape
    tokens = f.shape[0]
    block = min(512, inner)
    grid = (parts, inner // block)

    def number_of(j):
        return jnp.where(j == 0, parts - 1, jnp.where(j == parts - 1, 0, j))

    weight = pl.BlockSpec((1, width, block), lambda j, n: (number_of(j), 0, n))
    active = pl.BlockSpec((1, tokens, block), lambda j, n: (number_of(j), 0, n))
    whole = pl.BlockSpec((tokens, width), lambda j, n: (0, 0))
    turned = pl.BlockSpec((width, tokens), lambda j, n: (0, 0))
    landing = jax.ShapeDtypeStruct((2, width // 2, inner), low)
    return pl.pallas_call(
        hidden_back_kernel,
        grid=grid,
        in_specs=[whole, turned, turned, weight, weight, active, active],
        out_specs=[
            weight, weight, pl.BlockSpec((1, 1, block), lambda j, n: (number_of(j), 0, n)), whole,
            ANYWHERE, ANYWHERE,
        ],
        out_shape=[
            jax.ShapeDtypeStruct(w1.shape, low),
            jax.ShapeDtypeStruct(w1.shape, low),
            jax.ShapeDtypeStruct((parts, 1, inner), f32),
            jax.ShapeDtypeStruct((tokens, width), low),
            landing,
            landing,
        ],
        scratch_shapes=[
            pltpu.VMEM((tokens, block), low),
            pltpu.VMEM((tokens, width), f32),
            pltpu.VMEM(landing.shape, low),
            pltpu.VMEM(landing.shape, low),
            pltpu.SemaphoreType.DMA((2, 2)),
            pltpu.SemaphoreType.DMA((2, 2)),
        ],
        compiler_params=pltpu.CompilerParams(
            vmem_limit_bytes=VMEM, collective_id=number, has_side_effects=True
        ),
        name="hidden_backward",
    )(dz, dz.T, f.T, w1, w2, act, slope)


def start_kernel(
    tokens, encoder, vec_f, vec_c, *refs, n_col,
):
    weights, (x_ext, enc, all_f, all_c), full = refs[:8], refs[8:12], refs[12:20]
    zeros, w_send, w_recv, w_own, t_send, t_recv, e_send, e_recv, v_send, v_recv, z_sem = refs[20:]
    dp, row, col = here()
    part = lax.rem(dp, PARTS)
    twin = (dp, 1 - row, col)
    flip = [
        dp + 1 - 2 * lax.rem(dp, 2),
        dp + 2 - 4 * lax.rem(dp // 2, 2),
    ]
    by_x, by_y = (flip[0], row, col), (flip[1], row, col)
    part_x, part_y = lax.rem(flip[0], PARTS), lax.rem(flip[1], PARTS)
    shift = [lax.rem(col + k, n_col) for k in range(n_col)]
    group = [(dp, r, c) for r in (row, 1 - row) for c in shift][1:]
    meet(group + [by_x, by_y])

    wide = tokens.shape[1]
    deep = n_col * wide
    rest = deep - wide

    def chunk(index, size):
        return pl.ds(pl.multiple_of(index * size, size), size)

    def weight_z(i, k):
        w, to = weights[i], (dp, row, lax.rem(col + n_col - k, n_col))
        if i % 4 < 3:
            size = w.shape[1] // PARTS
            src = w.at[:, chunk(part, size)]
            dst = full[i].at[pl.ds(k * wide, wide), chunk(part, size)]
        else:
            size = w.shape[0] // PARTS
            src = w.at[chunk(part, size), :]
            dst = full[i].at[chunk(part, size), pl.ds(k * wide, wide)]
        return remote(src, dst, w_send.at[i, k - 1], w_recv.at[i, k - 1], to)

    def weight_own(i):
        w = weights[i]
        place = full[i].at[pl.ds(0, wide), :] if i % 4 < 3 else full[i].at[:, pl.ds(0, wide)]
        return pltpu.make_async_copy(w, place, w_own.at[i])

    def weight_part(i, which, begin, size):
        if i % 4 < 3:
            return full[i].at[pl.ds(begin, size), chunk(which, weights[i].shape[1] // PARTS)]
        return full[i].at[chunk(which, weights[i].shape[0] // PARTS), pl.ds(begin, size)]

    def weight_plane(i, stage):
        half = rest // 2
        which, begin, size, to = [
            (part, wide, rest, by_x),
            (part, wide, rest, by_y),
            (part_x, wide, half, by_y),
            (part_y, wide + half, half, by_x),
        ][stage]
        ref = weight_part(i, which, begin, size)
        return remote(ref, ref, w_send.at[i, 3 + stage], w_recv.at[i, 3 + stage], to)

    def token_piece(j, slot):
        rows = tokens.shape[0] // n_col
        to_col = 2 * row + j // 2 + (1 - slot)
        k = lax.rem(col + n_col - lax.rem(to_col, n_col), n_col)
        src = tokens.at[pl.ds(j * rows, rows), :]
        dst = x_ext.at[slot, :, chunk(k, wide)]
        local = (row == j % 2) & (col == to_col)
        valid = to_col < n_col
        return src, dst, k, local, valid, (dp, j % 2, to_col)

    def send_tokens(slot):
        for j in range(n_col):
            src, dst, k, local, valid, to = token_piece(j, slot)

            @pl.when(valid & local)
            def _():
                pltpu.make_async_copy(src, dst, t_recv.at[slot, k]).start()

            @pl.when(valid & jnp.logical_not(local))
            def _():
                remote(src, dst, t_send.at[slot, j], t_recv.at[slot, k], to).start()

    def enc_z(k):
        ref = enc.at[chunk(row, encoder.shape[0]), pl.ds(k * wide, wide)]
        to = (dp, row, lax.rem(col + n_col - k, n_col))
        return remote(encoder, ref, e_send.at[0, k], e_recv.at[0, k], to)

    def enc_twin(k):
        ref = enc.at[chunk(row, encoder.shape[0]), pl.ds(k * wide, wide)]
        return remote(encoder if k == 0 else ref, ref, e_send.at[1, k], e_recv.at[1, k], twin)

    def vectors(k):
        to = (dp, row, lax.rem(col + n_col - k, n_col))
        return [
            remote(vec_f, all_f.at[:, pl.ds(k * wide, wide)], v_send.at[0, k], v_recv.at[0, k], to),
            remote(vec_c, all_c.at[col], v_send.at[1, k], v_recv.at[1, k], to),
        ]

    own_vectors = [
        pltpu.make_async_copy(vec_f, all_f.at[:, pl.ds(0, wide)], v_recv.at[0, 0]),
        pltpu.make_async_copy(vec_c, all_c.at[col], v_recv.at[1, 0]),
        pltpu.make_async_copy(
            encoder, enc.at[chunk(row, encoder.shape[0]), pl.ds(0, wide)], e_recv.at[0, 0]
        ),
    ]
    ks = range(1, n_col)
    for i in range(4):
        for k in ks:
            weight_z(i, k).start()
    send_tokens(1)
    for k in ks:
        for copy in vectors(k):
            copy.start()
    for i in range(4, 8):
        for k in ks:
            weight_z(i, k).start()
    send_tokens(0)
    enc_twin(0).start()
    for k in ks:
        enc_z(k).start()
    for i in range(8):
        weight_own(i).start()
    for copy in own_vectors:
        copy.start()

    @pl.when(col == 0)
    def _():
        zeros[...] = jnp.zeros_like(zeros)
        clear = pltpu.make_async_copy(zeros, x_ext.at[0], z_sem)
        clear.start()
        clear.wait()

    for base in (0, 4):
        for i in range(base, base + 4):
            for k in ks:
                weight_z(i, k).wait_recv()
            weight_plane(i, 0).start()
            weight_plane(i, 1).start()
        for i in range(base, base + 4):
            weight_plane(i, 0).wait_recv()
            weight_plane(i, 2).start()
            weight_plane(i, 1).wait_recv()
            weight_plane(i, 3).start()
    for k in ks:
        enc_z(k).wait_recv()
        enc_twin(k).start()
    for i in range(8):
        weight_plane(i, 2).wait_recv()
        weight_plane(i, 3).wait_recv()
        weight_own(i).wait()
        for k in ks:
            weight_z(i, k).wait_send()
        for stage in range(4):
            weight_plane(i, stage).wait_send()
    for copy in own_vectors:
        copy.wait()
    for k in ks:
        for copy in vectors(k):
            copy.wait()
        enc_z(k).wait_send()
    for k in range(n_col):
        enc_twin(k).wait()
    for slot in (1, 0):
        for j in range(n_col):
            src, dst, k, local, valid, to = token_piece(j, slot)

            @pl.when(valid & jnp.logical_not(local))
            def _():
                remote(src, dst, t_send.at[slot, j], t_recv.at[slot, k], to).wait_send()

        for k in range(n_col):
            rows = tokens.shape[0] // n_col
            came = pltpu.make_async_copy(
                tokens.at[pl.ds(0, rows), :],
                x_ext.at[slot, :, pl.ds(k * wide, wide)],
                t_recv.at[slot, k],
            )
            if slot == 1:
                came.wait()
            else:

                @pl.when(col > 0)
                def _():
                    came.wait()


def start(tokens, encoder, vec_f, vec_c, weights, n_col):
    wide = tokens.shape[1]
    deep = n_col * wide
    rows = tokens.shape[0] // n_col
    shapes = [
        jax.ShapeDtypeStruct((2, rows, deep), low),
        jax.ShapeDtypeStruct((2 * encoder.shape[0], deep), low),
        jax.ShapeDtypeStruct((vec_f.shape[0], deep), f32),
        jax.ShapeDtypeStruct((n_col,) + vec_c.shape, f32),
    ]
    for i, w in enumerate(weights):
        shapes.append(
            jax.ShapeDtypeStruct((deep, w.shape[1]) if i % 4 < 3 else (w.shape[0], deep), low)
        )
    dma = pltpu.SemaphoreType.DMA
    return pl.pallas_call(
        functools.partial(start_kernel, n_col=n_col),
        in_specs=[ANYWHERE] * 12,
        out_specs=[ANYWHERE] * 12,
        out_shape=shapes,
        scratch_shapes=[
            pltpu.VMEM((rows, deep), low),
            dma((8, 7)), dma((8, 7)), dma((8,)),
            dma((2, n_col)), dma((2, n_col)),
            dma((2, n_col)), dma((2, n_col)),
            dma((2, n_col)), dma((2, n_col)),
            dma,
        ],
        compiler_params=pltpu.CompilerParams(
            collective_id=1, has_side_effects=True, vmem_limit_bytes=VMEM
        ),
        name="start",
    )(tokens, encoder, vec_f, vec_c, *weights)


def norm_rows(x):
    center = jnp.mean(x, axis=1, keepdims=True)
    spread = jnp.mean(x * x, axis=1, keepdims=True) - center * center
    scaling = lax.rsqrt(spread + norm_epsilon)
    return (x - center) * scaling, scaling


CUT = 256


def enter_kernel(x_ref, gain, shift, a_ref, sends, recvs):
    dp, row, col = here()
    twin = (dp, 1 - row, col)
    meet([twin])
    slots, rows = x_ref.shape[:2]

    def place(slot):
        return a_ref.at[slot, pl.ds(pl.multiple_of(row * rows, rows), rows), :]

    copies = []
    for slot in reversed(range(slots)):
        for t in range(rows // CUT):
            normed, _ = norm_rows(x_ref[slot, pl.ds(t * CUT, CUT), :].astype(f32))
            begin = pl.multiple_of(row * rows + t * CUT, CUT)
            a_ref[slot, pl.ds(begin, CUT), :] = (normed * gain[...] + shift[...]).astype(low)
        copy = remote(place(slot), place(slot), sends.at[slot], recvs.at[slot], twin)
        copy.start()
        copies.append(copy)
    for copy in copies:
        copy.wait()


def enter(x_ext, gain, shift, number):
    slots, rows, deep = x_ext.shape
    return pl.pallas_call(
        enter_kernel,
        in_specs=[IN_VMEM] * 3,
        out_specs=IN_VMEM,
        out_shape=jax.ShapeDtypeStruct((slots, 2 * rows, deep), low),
        scratch_shapes=[pltpu.SemaphoreType.DMA((slots,)), pltpu.SemaphoreType.DMA((slots,))],
        compiler_params=pltpu.CompilerParams(
            collective_id=number, has_side_effects=True, vmem_limit_bytes=VMEM
        ),
        name="enter",
    )(x_ext, gain[None], shift[None])


def junction_kernel(*refs, kinds, mode):
    dp, row, col = here()
    twin = (dp, 1 - row, col)
    meet([twin])
    refs = list(refs)
    sources = []
    for kind in kinds:
        sources.append((kind, refs.pop(0), refs.pop(0) if kind != "sum" else None))
    if mode == "forward":
        x_ref, bias, gain, shift, x_out, full, away, came, s1, r1, s2, r2 = refs
    elif mode == "backward":
        res_ref, x_ref, gain, dx_out, full, stats, away, came, s1, r1, s2, r2 = refs
    else:
        out, away, came, s1, r1 = refs
    rows = came.shape[0]
    cuts = rows // CUT

    def partial(begin):
        total = None
        for kind, g, w in sources:
            part = g[pl.ds(begin, CUT), :]
            if kind == "sum":
                part = part.astype(f32)
            elif kind == "nt":
                part = mm_nt(part, w[...])
            else:
                part = mm(part, w[...])
            total = part if total is None else total + part
        return total

    sent = []
    for t in range(cuts):
        at = pl.ds(t * CUT, CUT)
        away[at, :] = partial(pl.multiple_of((1 - row) * rows + t * CUT, CUT)).astype(low)
        copy = remote(away.at[at, :], came.at[at, :], s1.at[t], r1.at[t], twin)
        copy.start()
        sent.append(copy)
    gathered = []
    sums = [0.0, 0.0, 0.0]
    for t in range(cuts):
        at = pl.ds(t * CUT, CUT)
        begin = pl.multiple_of(row * rows + t * CUT, CUT)
        own = partial(begin)
        sent[t].wait_recv()
        total = own + came[at, :].astype(f32)
        if mode == "sum":
            out[at, :] = total
            continue
        if mode == "forward":
            x = x_ref[at, :].astype(f32) + (total + bias[...])
            x_out[at, :] = x
            normed, _ = norm_rows(x)
            result = (normed * gain[...] + shift[...]).astype(low)
        else:
            normed, scaling = norm_rows(x_ref[at, :].astype(f32))
            upstream = total * gain[...]
            mean_up = jnp.mean(upstream, axis=1, keepdims=True)
            mean_both = jnp.mean(upstream * normed, axis=1, keepdims=True)
            dx = res_ref[at, :].astype(f32) + scaling * (upstream - mean_up - normed * mean_both)
            dx_out[at, :] = dx
            result = dx.astype(low)
            for i, value in enumerate((total * normed, total, result.astype(f32))):
                sums[i] = sums[i] + jnp.sum(value, axis=0, keepdims=True)
        if full is None:
            continue
        full[pl.ds(begin, CUT), :] = result
        place = full.at[pl.ds(begin, CUT), :]
        copy = remote(place, place, s2.at[t], r2.at[t], twin)
        copy.start()
        gathered.append(copy)
    if mode == "backward":
        for i in range(3):
            stats[i : i + 1, :] = sums[i]
    for copy in sent:
        copy.wait_send()
    for copy in gathered:
        copy.wait()


def junction(mode, sources, others, number):
    kinds = [x[0] for x in sources]
    first = sources[0]
    tokens = first[1].shape[0]
    deep = first[1].shape[1]
    if first[0] != "sum":
        deep = first[2].shape[0 if first[0] == "nt" else 1]
    rows = tokens // 2
    flat = [x for source in sources for x in source[1:]]
    dma = pltpu.SemaphoreType.DMA((rows // CUT,))
    wide_rows = jax.ShapeDtypeStruct((rows, deep), f32)
    every = jax.ShapeDtypeStruct((tokens, deep), low)
    shapes = {
        "forward": [wide_rows, every],
        "backward": [wide_rows, every, jax.ShapeDtypeStruct((8, deep), f32)],
        "sum": [wide_rows],
    }[mode]
    scratch = [pltpu.VMEM((rows, deep), low), pltpu.VMEM((rows, deep), low), dma, dma]
    if mode != "sum":
        scratch += [dma, dma]
    args = flat + [x[None] if x.ndim == 1 else x for x in others]
    out = pl.pallas_call(
        functools.partial(junction_kernel, kinds=kinds, mode=mode),
        in_specs=[IN_VMEM] * len(args),
        out_specs=[IN_VMEM] * len(shapes),
        out_shape=shapes,
        scratch_shapes=scratch,
        compiler_params=pltpu.CompilerParams(
            collective_id=number, has_side_effects=True, vmem_limit_bytes=VMEM
        ),
        name="junction_" + mode,
    )(*args)
    return out if len(out) > 1 else out[0]


def finish_kernel(
    ga, gb, small, enc_in, tg, g2, near_a, near_b, far_back_a, far_back_b, z_got, own1,
    full, hidden_full, small_out, enc_out, tg_out,
    load, load_own, load_got, h_out, h_in, l_s, lo_s, hz_s, hz_r, h_extra, hx_s, hx_r, hg_s, hg_r,
    first, second, mid, zout, zin, tot, enc_got, s_cur, s_got, s_z, extra,
    f_s, f_r, m_s, m_r, z_s, z_r, g_s, g_r, e_s, e_r, s_s, s_r, sz_s, sz_r, t_s, t_r, x_s, x_r,
    *, n_col, n_dp,
):
    dp, row, col = here()
    part = lax.rem(dp, PARTS)
    twin = (dp, 1 - row, col)
    bits = [1 << b for b in range(n_dp.bit_length() - 1)]
    flips = [dp + b - 2 * b * lax.rem(dp // b, 2) for b in bits]
    by_bit = [(f, row, col) for f in flips]
    shift = [lax.rem(col + k, n_col) for k in range(n_col)]
    group = [(dp, r, c) for r in (row, 1 - row) for c in shift][1:]
    meet(group + by_bit)
    wide = enc_out.shape[1]
    ks = range(1, n_col)
    ways = [(ga, 0, (1, 3), 2), (gb, 1, (2, 3), 1)]
    h_half = near_a.shape[0]
    loads = []
    for i, sources in enumerate(((near_a, far_back_a), (near_b, far_back_b))):
        at = pl.ds(i * h_half, h_half)
        for n, src in enumerate((g2.at[0, at, :],) + sources):
            loads.append(pltpu.make_async_copy(src, load.at[n, at, :], l_s.at[i, n]))
    loads_own = [
        pltpu.make_async_copy(own1, load_own, lo_s.at[0]),
        pltpu.make_async_copy(z_got, load_got, lo_s.at[1]),
    ]

    def hidden_hop(k):
        return remote(h_out.at[k], h_in.at[k - 1], hz_s.at[k - 1], hz_r.at[k - 1], z_to(k))

    def hidden_total(k):
        at = rows(k)
        value = load[0, at, :].astype(f32) + load[1, at, :].astype(f32)
        return value + load[2, at, :].astype(f32)

    def other_bits(value, g, store, s_x, r_x):
        for i in range(len(bits) - 2):
            store[g, i, 0] = value.astype(low)
            copy = remote(
                store.at[g, i, 0], store.at[g, i, 1], s_x.at[g, i], r_x.at[g, i], by_bit[2 + i]
            )
            copy.start()
            copy.wait()
            value = value + store[g, i, 1].astype(f32)
        return value

    def rows(q):
        return pl.ds(q * wide, wide)

    def z_to(k):
        return (dp, row, shift[k])

    def hop(g, a, q):
        src, way, away, _ = ways[g]
        return remote(
            src.at[away[a], rows(q), :], first.at[g, a, rows(q), :], f_s.at[g, a, q],
            f_r.at[g, a, q], by_bit[way],
        )

    def hop2(g, q):
        ref = mid.at[g, rows(q), :]
        return remote(
            ref, second.at[g, rows(q), :], m_s.at[g, q], m_r.at[g, q], by_bit[1 - ways[g][1]]
        )

    def z_hop(g, q):
        return remote(zout.at[g, q - 1], zin.at[g, q - 1], z_s.at[g, q - 1], z_r.at[g, q - 1], z_to(q))

    def enc_hop(k):
        src = enc_in.at[:, pl.ds(k * wide, wide)]
        return remote(src, enc_got.at[k - 1], e_s.at[k - 1], e_r.at[k - 1], z_to(k))

    partners = [twin] + by_bit

    def small_hop(i):
        return remote(s_cur.at[i], s_got.at[i], s_s.at[i], s_r.at[i], partners[i])

    def small_z(k):
        return remote(s_cur.at[len(partners), k], s_z.at[k - 1], sz_s.at[k - 1], sz_r.at[k - 1], z_to(k))

    def small_step(i):
        if i == 0:
            s_cur[0] = small[...]
        elif i <= len(partners):
            small_hop(i - 1).wait_recv()
            got = s_got[i - 1]
            if i == 1:
                lane = lax.broadcasted_iota(jnp.int32, got.shape, 2)
                got = jnp.where(lane < wide, got, 0.0)
            s_cur[i] = s_cur[i - 1] + got
        if i < len(partners):
            small_hop(i).start()
        elif i == len(partners):
            for k in ks:
                small_z(k).start()
        else:
            value = s_cur[len(partners), 0]
            for k in ks:
                small_z(k).wait_recv()
                value = value + s_z[k - 1]
            small_out[...] = value

    t_rows = tg.shape[0]
    home = col // 2
    at_home = 2 * lax.rem(col, 2) + row

    def tg_hop(k):
        src = tg.at[:, pl.ds(k * wide, wide)]
        dst = tg_out.at[pl.ds(pl.multiple_of(at_home * t_rows, t_rows), t_rows), :]
        return src, dst, (dp, home, shift[k])

    part_x, part_y = lax.rem(flips[0], PARTS), lax.rem(flips[1], PARTS)
    half = wide // 2

    def plane_hop(full, g, stage, sends, recvs):
        which, begin, size, way = [
            (part, 0, wide, 0), (part, 0, wide, 1), (part_x, 0, half, 1), (part_y, half, half, 0),
        ][stage]
        ref = full.at[g, which, pl.ds(begin, size), :]
        return remote(ref, ref, sends.at[g, stage], recvs.at[g, stage], by_bit[way])

    def plane_to(g, stage):
        return plane_hop(full, g, stage, g_s, g_r)

    def hidden_plane(g, stage):
        return plane_hop(hidden_full, g, stage, hg_s, hg_r)

    small_step(0)
    for copy in loads + loads_own:
        copy.start()
    for q in range(n_col):
        for g in range(2):
            hop(g, 1, q).start()
    for k in ks:
        enc_hop(k).start()
    for q in range(n_col):
        for g in range(2):
            hop(g, 0, q).start()
    for k in range(n_col):
        src, dst, to = tg_hop(k)
        if k == 0:

            @pl.when(home == row)
            def _():
                pltpu.make_async_copy(src, dst, t_r.at[at_home]).start()

            @pl.when(home != row)
            def _():
                remote(src, dst, t_s.at[k], t_r.at[at_home], to).start()
        else:
            remote(src, dst, t_s.at[k], t_r.at[at_home], to).start()
    for copy in loads:
        copy.wait()
    for k in ks:
        h_out[k] = hidden_total(k).astype(low)
        hidden_hop(k).start()
    for copy in loads_own:
        copy.wait()
    value = load_own[...].astype(f32)
    for k in ks:
        value = value + load_got[k - 1].astype(f32)
    hidden_full[0, part] = other_bits(value, 0, h_extra, hx_s, hx_r).astype(low)
    hidden_plane(0, 0).start()
    hidden_plane(0, 1).start()
    done = 1
    for q in range(n_col):
        for g in range(2):
            src, _, _, keep = ways[g]
            hop(g, 1, q).wait_recv()
            value = src[keep, rows(q), :].astype(f32) + first[g, 1, rows(q), :].astype(f32)
            mid[g, rows(q), :] = value.astype(low)
            hop2(g, q).start()
        if done < len(partners) + 2:
            small_step(done)
            done += 1
    for q in (1, 2, 3, 0):
        for g in range(2):
            src = ways[g][0]
            hop(g, 0, q).wait_recv()
            hop2(g, q).wait_recv()
            value = src[0, rows(q), :].astype(f32) + first[g, 0, rows(q), :].astype(f32)
            value = value + second[g, rows(q), :].astype(f32)
            if q:
                zout[g, q - 1] = value.astype(low)
                z_hop(g, q).start()
            else:
                tot[g] = value
        if done < len(partners) + 2:
            small_step(done)
            done += 1
    for stage in range(2):
        hidden_plane(0, stage).wait_recv()
        hidden_plane(0, 2 + stage).start()
    value = enc_in[:, pl.ds(0, wide)].astype(f32)
    for k in ks:
        enc_hop(k).wait_recv()
        value = value + enc_got[k - 1].astype(f32)
    enc_out[...] = value
    while done < len(partners) + 2:
        small_step(done)
        done += 1
    for g in range(2):
        value = tot[g]
        for q in ks:
            z_hop(g, q).wait_recv()
            value = value + zin[g, q - 1].astype(f32)
        value = other_bits(value, g, extra, x_s, x_r)
        full[g, part] = value.astype(low)
    for g in range(2):
        plane_to(g, 0).start()
        plane_to(g, 1).start()
    value = hidden_total(0)
    for k in ks:
        hidden_hop(k).wait_recv()
        value = value + h_in[k - 1].astype(f32)
    hidden_full[1, part] = other_bits(value, 1, h_extra, hx_s, hx_r).astype(low)
    hidden_plane(1, 0).start()
    hidden_plane(1, 1).start()
    for g in range(2):
        for stage in range(2):
            plane_to(g, stage).wait_recv()
            plane_to(g, 2 + stage).start()
    for stage in range(2):
        hidden_plane(1, stage).wait_recv()
        hidden_plane(1, 2 + stage).start()
    for k in ks:
        hidden_hop(k).wait_send()
    for g in range(2):
        for ways_out in (plane_to, hidden_plane):
            ways_out(g, 2).wait_recv()
            ways_out(g, 3).wait_recv()
            for stage in range(4):
                ways_out(g, stage).wait_send()
        for q in range(n_col):
            hop(g, 0, q).wait_send()
            hop(g, 1, q).wait_send()
            hop2(g, q).wait_send()
            if q:
                z_hop(g, q).wait_send()
    for k in ks:
        enc_hop(k).wait_send()
        small_z(k).wait_send()
    for i in range(len(partners)):
        small_hop(i).wait_send()
    for k in range(n_col):
        src, dst, to = tg_hop(k)

        @pl.when((home != row) | (k > 0))
        def _():
            remote(src, dst, t_s.at[k], t_r.at[at_home], to).wait_send()

        place = tg_out.at[pl.ds(k * t_rows, t_rows), :]
        pltpu.make_async_copy(src, place, t_r.at[k]).wait()


def finish(ga, gb, small, enc_in, tg, riding, n_col, n_dp):
    parts, deep, columns = ga.shape
    wide = deep // n_col
    steps = n_dp.bit_length()
    sd, vm, dma = jax.ShapeDtypeStruct, pltpu.VMEM, pltpu.SemaphoreType.DMA
    more = max(n_dp.bit_length() - 3, 1)
    others = n_col - 1
    hidden = riding[0].shape[2]
    return pl.pallas_call(
        functools.partial(finish_kernel, n_col=n_col, n_dp=n_dp),
        in_specs=[IN_VMEM] * 4 + [ANYWHERE] * 8,
        out_specs=[IN_VMEM] * 4 + [ANYWHERE],
        out_shape=[
            sd((2, parts, wide, columns), low),
            sd((2, parts, wide, hidden), low),
            sd(small.shape[1:], f32),
            sd((enc_in.shape[0], wide), f32),
            sd((n_col * tg.shape[0], wide), low),
        ],
        scratch_shapes=[
            vm((3, deep, hidden), low),
            vm((wide, hidden), low),
            vm((others, wide, hidden), low),
            vm((n_col, wide, hidden), low),
            vm((others, wide, hidden), low),
            dma((2, 3)), dma((2,)),
            dma((others,)), dma((others,)),
            vm((2, more, 2, wide, hidden), low),
            dma((2, more)), dma((2, more)),
            dma((2, 4)), dma((2, 4)),
            vm((2, 2, deep, columns), low),
            vm((2, deep, columns), low),
            vm((2, deep, columns), low),
            vm((2, others, wide, columns), low),
            vm((2, others, wide, columns), low),
            vm((2, wide, columns), f32),
            vm((others, enc_in.shape[0], wide), low),
            vm((steps + 1,) + small.shape, f32),
            vm((steps,) + small.shape, f32),
            vm((others,) + small.shape[1:], f32),
            vm((2, more, 2, wide, columns), low),
            dma((2, 2, n_col)), dma((2, 2, n_col)),
            dma((2, n_col)), dma((2, n_col)),
            dma((2, others)), dma((2, others)),
            dma((2, 4)), dma((2, 4)),
            dma((others,)), dma((others,)),
            dma((steps,)), dma((steps,)),
            dma((others,)), dma((others,)),
            dma((n_col,)), dma((n_col,)),
            dma((2, more)), dma((2, more)),
        ],
        compiler_params=pltpu.CompilerParams(
            collective_id=20, has_side_effects=True, vmem_limit_bytes=VMEM
        ),
        name="finish",
    )(ga, gb, small, enc_in, tg, *riding)


def norm_backward(incoming, normed, scaling, gain):
    gain_grad = jnp.sum(incoming * normed, axis=0)
    bias_grad = jnp.sum(incoming, axis=0)
    upstream = incoming * gain
    mean_up = jnp.mean(upstream, axis=1, keepdims=True)
    mean_both = jnp.mean(upstream * normed, axis=1, keepdims=True)
    return scaling * (upstream - mean_up - normed * mean_both), gain_grad, bias_grad


def build_local(mesh):
    n_dp, n_col = mesh.shape["dp"], mesh.shape["col"]

    def swap(x):
        return lax.ppermute(x, "row", [(0, 1), (1, 0)])

    def from_col(x, k):
        return lax.ppermute(x, "col", [(i, (i - k) % n_col) for i in range(n_col)])

    def to_col(x, k):
        return lax.ppermute(x, "col", [(i, (i + k) % n_col) for i in range(n_col)])

    def across(x, bit):
        return lax.ppermute(x, "dp", [(i, i ^ bit) for i in range(n_dp)])

    def plane_gather(x):
        half = x.shape[0] // 2
        by_x, by_y = across(x, 1), across(x, 2)
        far = jnp.concatenate([across(by_x[:half], 2), across(by_y[half:], 1)], axis=0)
        return [x, by_x, by_y, far]

    def local(
        tokens, encoder, cotangent, dec_lengths, src_lengths,
        self_norm_gain, self_norm_bias, self_query, self_key, self_value,
        self_query_bias, self_value_bias, self_out, self_out_bias,
        cross_norm_gain, cross_norm_bias, cross_query, cross_key, cross_value,
        cross_query_bias, cross_value_bias, cross_out, cross_out_bias,
        hidden_norm_gain, hidden_norm_bias, hidden_in, hidden_in_bias,
        hidden_out, hidden_out_bias,
    ):
        row, col = lax.axis_index("row"), lax.axis_index("col")
        place = lax.axis_index("dp") % PARTS
        wide = tokens.shape[1]
        chunk = tokens.shape[0] // n_col
        span = 2 * chunk

        def by_row(own, other):
            return jnp.where(
                row == 0,
                jnp.concatenate([own, other], axis=0),
                jnp.concatenate([other, own], axis=0),
            )

        def row_gather(own):
            return by_row(own, swap(own))

        def row_scatter(partial):
            half = partial.shape[0] // 2
            away = lax.dynamic_slice_in_dim(partial, (1 - row) * half, half, 0)
            mine = lax.dynamic_slice_in_dim(partial, row * half, half, 0)
            return mine.astype(f32) + swap(away.astype(low)).astype(f32)

        def spread_rows(x):
            cut = x.reshape(2, 2, chunk, wide)
            own = lax.dynamic_index_in_dim(cut, row, 1, keepdims=False)
            other = swap(lax.dynamic_index_in_dim(cut, 1 - row, 1, keepdims=False))
            every = by_row(own, other)
            pieces = []
            for k in range(n_col):
                piece = lax.dynamic_index_in_dim(every, (col - k) % n_col, 0, keepdims=False)
                pieces.append(from_col(piece, k) if k else piece)
            return jnp.concatenate(pieces, axis=1)

        def collect_rows(x):
            every = jnp.zeros((n_col, chunk, wide), x.dtype)
            for k in range(n_col):
                piece = x[:, k * wide : (k + 1) * wide]
                piece = to_col(piece, k) if k else piece
                every = lax.dynamic_update_index_in_dim(every, piece, (col - k) % n_col, 0)
            own = lax.dynamic_slice_in_dim(every, 2 * row, 2, 0)
            other = swap(lax.dynamic_slice_in_dim(every, 2 * (1 - row), 2, 0))
            both = jnp.where(
                row == 0, jnp.stack([own, other], axis=1), jnp.stack([other, own], axis=1)
            )
            return both.reshape(n_col * chunk, wide)

        def in_order(parts):
            stacked = jnp.stack(parts)
            return [
                lax.dynamic_index_in_dim(stacked, i ^ place, 0, keepdims=False)
                for i in range(PARTS)
            ]

        def weights_of(arrays):
            def own(j):
                cuts = []
                for w in arrays:
                    size = w.shape[1] // PARTS
                    cuts.append(lax.dynamic_slice_in_dim(w, (place ^ j) * size, size, 1))
                return jnp.concatenate(cuts, axis=1)

            mine = own(0)
            rest = jnp.concatenate([from_col(mine, k) for k in range(1, n_col)], axis=0)
            return [
                jnp.concatenate([own(j), part], axis=0)
                for j, part in enumerate(plane_gather(rest))
            ]

        vec_f = jnp.stack([
            self_norm_gain, self_norm_bias, self_out_bias, cross_norm_gain, cross_norm_bias,
            cross_out_bias, hidden_norm_gain, hidden_norm_bias, hidden_out_bias,
        ])
        vec_f = jnp.pad(vec_f, ((0, 7), (0, 0)))
        vec_c = jnp.concatenate(
            [self_query_bias, self_value_bias, cross_query_bias, cross_value_bias, hidden_in_bias]
        ).reshape(-1, 128)
        vec_c = jnp.pad(vec_c, ((0, -vec_c.shape[0] % 8), (0, 0)))
        weights = [
            self_query, self_key, self_value, self_out,
            cross_query, cross_key, cross_value, cross_out,
        ]
        x_ext, enc, vectors, columns, *full = start(
            tokens, encoder, vec_f, vec_c, weights, n_col
        )
        wq1, wk1, wv1, wo1, wq2, wk2, wv2, wo2 = full
        (gain1, shift1, out_bias1, gain2, shift2, out_bias2, gain3, shift3, out_bias3) = vectors[:9]
        size = self_query_bias.shape[0]

        def column_vector(start, size):
            return columns.reshape(n_col, -1)[:, start : start + size].reshape(-1)

        q_bias1 = column_vector(0, size)
        v_bias1 = column_vector(size, size)
        q_bias2 = column_vector(2 * size, size)
        v_bias2 = column_vector(3 * size, size)
        hidden_bias = column_vector(4 * size, hidden_in_bias.shape[0]).reshape(PARTS, -1)
        hidden_bias = jnp.stack(
            [lax.dynamic_index_in_dim(hidden_bias, place ^ j, 0) for j in range(PARTS)]
        )

        hidden_in, hidden_out, cotangent, x_ext = lax.optimization_barrier(
            (hidden_in, hidden_out, cotangent, x_ext)
        )
        w1 = jnp.stack(weights_of([hidden_in]))
        w2 = jnp.stack(weights_of([hidden_out.T]))
        step = self_query.shape[1] // PARTS

        dec_ids = doc_numbers(dec_lengths, SEQ_LEN)[0]
        src_ids = doc_numbers(src_lengths, ENC)[0]
        padded = jnp.pad(dec_ids, (WIN, 0), constant_values=-1)
        key_ids = lax.dynamic_slice_in_dim(padded, col * span, WIN + span, 0)
        query_ids = key_ids[WIN:]

        scale = low(HEAD_DIM**-0.5)
        x0 = x_ext[1]
        a_ext = enter(x_ext, gain1, shift1, 2).reshape(WIN + span, -1)
        a = a_ext[WIN:]
        q1 = (mm(a, wq1) + q_bias1).astype(low) * scale
        k1 = mm(a_ext, wk1).astype(low)
        v1 = (mm(a_ext, wv1) + v_bias1).astype(low)
        o1, lse1 = attend(q1, k1, v1, query_ids, key_ids, True)
        x1, c = junction("forward", [("nn", o1, wo1)], [x0, out_bias1, gain2, shift2], 3)

        q2 = (mm(c, wq2) + q_bias2).astype(low) * scale
        k2 = mm(enc, wk2).astype(low)
        v2 = (mm(enc, wv2) + v_bias2).astype(low)
        o2, lse2 = attend(q2, k2, v2, query_ids, src_ids, False)
        x2, f = junction("forward", [("nn", o2, wo2)], [x1, out_bias2, gain3, shift3], 4)

        act, slope, branch = hidden_forward(f, w1, hidden_bias, w2)
        layer_out = collect_rows(
            (x2 + (junction("sum", [("sum", branch)], [], 5) + out_bias3)).astype(low)
        )

        dz_own = spread_rows(cotangent)
        dz = row_gather(dz_own)
        g1, g2, hidden_bias_grad, df, got_a, got_b = hidden_backward(
            dz, f, w1, w2, act, slope, 11
        )
        inner = g1.shape[2]
        half = g1.shape[1] // 2
        dma, one = pltpu.SemaphoreType.DMA, ((half, inner), low)
        dx2, dyc, stats3 = junction("backward", [("sum", df)], [dz_own, x2, gain3], 6)

        doc = mm_nt(dyc, wo2).astype(low)
        dq2, dk2, dv2, back_a, back_b, far_a, far_b = attend_back(
            q2, k2, v2, doc, o2, lse2, query_ids, src_ids, False,
            first_rider, [g1, g2, got_a, got_b], [one] * 4,
            [
                pltpu.VMEM((4, half, inner), low), pltpu.VMEM((2, half, inner), low),
                dma((4,)), dma((4,)), dma((4,)),
            ],
            12,
        )
        grads = [
            mm_tn(c, dq2).astype(low),
            mm_tn(enc, dk2).astype(low),
            mm_tn(enc, dv2).astype(low),
            mm_tn(dyc, o2).astype(low),
        ]

        def by_part(arrays):
            return [
                jnp.concatenate(
                    [
                        lax.dynamic_slice_in_dim(g, (place ^ j) * step, step, 1)
                        for g in arrays
                    ],
                    axis=1,
                )
                for j in range(PARTS)
            ]

        cross_grads = jnp.stack(by_part(grads))
        enc_back = junction("sum", [("nt", dk2, wk2), ("nt", dv2, wv2)], [], 7)
        dx1, dy, stats2 = junction("backward", [("nt", dq2, wq2)], [dx2, x1, gain2], 8)

        do = mm_nt(dy, wo1).astype(low)
        dq1, dk1, dv1, near_a, near_b, far_back_a, far_back_b, z_got, own1 = attend_back(
            q1, k1, v1, do, o1, lse1, query_ids, key_ids, True,
            functools.partial(second_rider, n_col=n_col),
            [g1, g2, got_a, got_b, back_a, back_b, far_a, far_b],
            [one] * 4 + [((n_col - 1, wide, inner), low), ((wide, inner), low)],
            [
                pltpu.VMEM((4, half, inner), low), pltpu.VMEM((2, half, inner), low),
                pltpu.VMEM((3, 2 * half, inner), low), pltpu.VMEM((n_col, wide, inner), low),
                dma((4,)), dma((2, 3)), dma((4,)), dma((4,)),
                dma((n_col - 1,)), dma((n_col - 1,)), dma,
            ],
            13,
        )
        da_before = junction("sum", [("nt", dk1[:WIN], wk1), ("nt", dv1[:WIN], wv1)], [], 9)
        da_after = lax.ppermute(
            da_before.astype(low), "col", [(i + 1, i) for i in range(n_col - 1)]
        )
        da_after = jnp.concatenate([da_after[:, -wide:], da_after[:, :-wide]], axis=1)
        da = junction(
            "sum", [("nt", dq1, wq1), ("nt", dk1[WIN:], wk1), ("nt", dv1[WIN:], wv1)], [], 10
        ) + da_after.astype(f32)
        grads = [
            mm_tn(a, dq1).astype(low),
            mm_tn(a_ext, dk1).astype(low),
            mm_tn(a_ext, dv1).astype(low),
            mm_tn(dy, o1).astype(low),
        ]
        self_grads = jnp.stack(by_part(grads))
        normed1, scaling1 = norm_rows(x0.astype(f32))
        back1, gain_grad1, shift_grad1 = norm_backward(da, normed1, scaling1, gain1)
        def total(x):
            return jnp.sum(x, axis=0, dtype=f32)

        feature_grads = jnp.concatenate([
            jnp.stack([gain_grad1, shift_grad1]), stats2[2:3], stats2[:2], stats3[2:3], stats3[:2],
            total(dz_own)[None],
        ])
        feature_grads = jnp.moveaxis(feature_grads.reshape(-1, n_col, wide), 1, 0)
        column_grads = []
        for vector in (total(dq1), total(dv1), total(dq2), total(dv2), hidden_bias_grad):
            parts = vector.reshape(PARTS, -1)
            if vector is hidden_bias_grad:
                parts = jnp.stack(in_order([parts[j] for j in range(PARTS)]))
            column_grads.append(parts.reshape(n_col, -1))
        column_grads = jnp.concatenate(column_grads, axis=1).reshape(n_col, -1, 128)
        column_grads = lax.dynamic_slice_in_dim(
            jnp.concatenate([column_grads, column_grads]), col, n_col, 0
        )
        lines = -(-max(feature_grads.shape[1], column_grads.shape[1]) // 8) * 8
        small = jnp.concatenate(
            [
                jnp.pad(x, ((0, 0), (0, lines - x.shape[1]), (0, 0)))
                for x in (feature_grads, column_grads)
            ],
            axis=2,
        )
        sums, hidden_sums, small, encoder_grad, tokens_grad = finish(
            cross_grads, self_grads, small, enc_back.astype(low), (dx1 + back1).astype(low),
            [g2, near_a, near_b, far_back_a, far_back_b, z_got, own1],
            n_col, n_dp,
        )
        g1_parts, g2_parts = [[hidden_sums[i, j] for j in range(PARTS)] for i in range(2)]
        tokens_grad = tokens_grad.astype(f32)
        cross_grads = [sums[0, i] for i in range(PARTS)]
        self_grads = [sums[1, i] for i in range(PARTS)]
        feature_grads = small[:, :wide]
        column_grads = small[:, wide:].reshape(-1)

        def whole(parts, index=None):
            if index is not None:
                parts = [p[:, index * step : (index + 1) * step] for p in parts]
            return jnp.concatenate(parts, axis=1).astype(f32)

        return (
            layer_out,
            tokens_grad,
            encoder_grad,
            feature_grads[0],
            feature_grads[1],
            whole(self_grads, 0),
            whole(self_grads, 1),
            whole(self_grads, 2),
            column_grads[:size],
            column_grads[size : 2 * size],
            whole(self_grads, 3).T,
            feature_grads[2],
            feature_grads[3],
            feature_grads[4],
            whole(cross_grads, 0),
            whole(cross_grads, 1),
            whole(cross_grads, 2),
            column_grads[2 * size : 3 * size],
            column_grads[3 * size : 4 * size],
            whole(cross_grads, 3).T,
            feature_grads[5],
            feature_grads[6],
            feature_grads[7],
            whole(g1_parts),
            column_grads[4 * size : 4 * size + hidden_in_bias.shape[0]],
            whole(g2_parts).T,
            feature_grads[8],
        )

    return local


def solution(mesh):
    rows = P(("dp", "row"), "col")
    features = P("col")
    columns = P(("row", "col"))
    into, out_of = P("col", "row"), P("row", "col")
    attention = (into, into, into, columns, columns, out_of, features)
    norm = (features, features)
    weights = (
        norm
        + attention
        + norm
        + attention
        + norm
        + (into, columns, out_of, features)
    )
    return jax.shard_map(
        build_local(mesh),
        mesh=mesh,
        in_specs=(rows, rows, rows, P("dp", None), P("dp", None)) + weights,
        out_specs=(rows, rows, rows) + weights,
        check_vma=False,
    )
```

```python
import functools

import jax
import jax.numpy as jnp
from jax import lax
from jax.experimental import pallas as pl
from jax.experimental.pallas import tpu as pltpu
from jax.sharding import PartitionSpec as P

D = 1024
HEAD_DIM = 64
SEQ_LEN = 4096
ENC = 1024
WIN = 1024

norm_epsilon = 1e-05
masked_fill = -1e30
low = jnp.bfloat16
f32 = jnp.float32
PARTS = 4
PAIR = 2 * HEAD_DIM
QUERY_ROWS = 256
VMEM = 56 * 1024 * 1024


def doc_numbers(lengths, positions):
    bounds = jnp.cumsum(lengths, axis=1, dtype=jnp.int32)
    places = jnp.arange(positions, dtype=jnp.int32)
    return jnp.sum(
        (places[None, :, None] >= bounds[:, None, :]).astype(jnp.int32), axis=2, dtype=jnp.int32
    )


def mm(a, b):
    return lax.dot_general(a, b, (((1,), (0,)), ((), ())), preferred_element_type=f32)


def mm_nt(a, b):
    return lax.dot_general(a, b, (((1,), (1,)), ((), ())), preferred_element_type=f32)


def mm_tn(a, b):
    return lax.dot_general(a, b, (((0,), (0,)), ((), ())), preferred_element_type=f32)


MESH = pl.DeviceIdType.MESH
ANYWHERE = pl.BlockSpec(memory_space=pl.ANY)
IN_VMEM = pl.BlockSpec(memory_space=pltpu.VMEM)


def here():
    return lax.axis_index("dp"), lax.axis_index("row"), lax.axis_index("col")


def meet(partners):
    barrier = pltpu.get_barrier_semaphore()
    for partner in partners:
        pl.semaphore_signal(barrier, inc=1, device_id=partner, device_id_type=MESH)
    pl.semaphore_wait(barrier, len(partners))


def remote(src, dst, sends, recvs, device):
    return pltpu.make_async_remote_copy(
        src_ref=src, dst_ref=dst, send_sem=sends, recv_sem=recvs, device_id=device,
        device_id_type=MESH,
    )


def home_hop(rows, home, sends, recvs, n_col, k):
    dp, row, col = here()
    wide, count = home.shape[1], rows.shape[0]
    to_row, at = col // 2, 2 * lax.rem(col, 2) + row
    src = rows.at[:, pl.ds(k * wide, wide)]
    dst = home.at[pl.ds(pl.multiple_of(at * count, count), count), :]
    copy = remote(src, dst, sends.at[k], recvs.at[at], (dp, to_row, lax.rem(col + k, n_col)))
    return copy, pltpu.make_async_copy(src, dst, recvs.at[at]), to_row == row


def send_home(rows, home, sends, recvs, n_col):
    for k in range(n_col):
        away, here_copy, same = home_hop(rows, home, sends, recvs, n_col, k)
        if k:
            away.start()
            continue

        @pl.when(same)
        def _():
            here_copy.start()

        @pl.when(jnp.logical_not(same))
        def _():
            away.start()


def wait_home(rows, home, sends, recvs, n_col):
    wide, count = home.shape[1], rows.shape[0]
    for k in range(n_col):
        away, _, same = home_hop(rows, home, sends, recvs, n_col, k)
        if k:
            away.wait_send()
        else:

            @pl.when(jnp.logical_not(same))
            def _():
                away.wait_send()

        src = rows.at[:, pl.ds(k * wide, wide)]
        pltpu.make_async_copy(src, home.at[pl.ds(k * count, count), :], recvs.at[k]).wait()


def plane():
    dp, row, col = here()
    flips = [dp + b - 2 * b * lax.rem(dp // b, 2) for b in (1, 2)]
    return (flips[0], row, col), (flips[1], row, col)


def head_masks():
    lane = lax.broadcasted_iota(jnp.int32, (1, PAIR), 1)
    first = jnp.where(lane < HEAD_DIM, 1.0, 0.0)
    return first.astype(low), (1.0 - first).astype(low), lane < HEAD_DIM


def attend_kernel(*refs, span, windowed, rider, n_ins, n_outs):
    refs = list(refs)
    q_ref, k_ref, v_ref, qid_ref, kid_ref = refs[:5]
    rider_refs = refs[5 : 5 + n_ins]
    refs = refs[5 + n_ins :]
    o_ref, lse_ref = refs[:2]
    rider_refs += refs[2 : 2 + n_outs]
    bias = refs[2 + n_outs]
    rider_refs += refs[3 + n_outs :]
    rows = q_ref.shape[0]
    pairs = q_ref.shape[1] // PAIR
    step = pl.program_id(0)
    if rider is not None:
        hooks = rider(*rider_refs)
        for at, hook in hooks:

            @pl.when(step == at)
            def _():
                hook()

    start = step * rows if windowed else 0
    if windowed:
        start = pl.multiple_of(start, rows)
    allowed = qid_ref[...] == kid_ref[0:1, pl.ds(start, span)]
    if windowed:
        at_row = lax.broadcasted_iota(jnp.int32, (rows, span), 0)
        at_key = lax.broadcasted_iota(jnp.int32, (rows, span), 1)
        allowed = allowed & (at_key > at_row) & (at_key <= at_row + WIN)
    bias[...] = jnp.where(allowed, 0.0, masked_fill)
    first, second, is_first = head_masks()

    def one_pair(p, carry):
        lanes = pl.ds(pl.multiple_of(p * PAIR, PAIR), PAIR)
        q2 = q_ref[:, lanes]
        k2 = k_ref[pl.ds(start, span), lanes]
        v2 = v_ref[pl.ds(start, span), lanes]
        outs, logs = [], []
        for mask in (first, second):
            s = mm_nt(q2 * mask, k2) + bias[...]
            top = jnp.max(s, axis=1, keepdims=True)
            e = jnp.exp(s - top)
            total = jnp.sum(e, axis=1, keepdims=True)
            outs.append(mm(e.astype(low), v2) / total)
            logs.append(top + jnp.log(total))
        o_ref[:, lanes] = jnp.where(is_first, outs[0], outs[1]).astype(low)
        stats = jnp.where(is_first, logs[0], logs[1])
        turned = jnp.transpose(stats)
        lse_ref[p, 0:1, :] = turned[0:1]
        lse_ref[p, 1:2, :] = turned[HEAD_DIM : HEAD_DIM + 1]
        return carry

    lax.fori_loop(0, pairs, one_pair, 0)

    if rider is not None:

        @pl.when(step == pl.num_programs(0) - 1)
        def _():
            hooks.end()


class Hooks(list):
    end = None


def attend(q, k, v, qid, kid, windowed, rider=None, riding=(), shapes=(), scratch=(), number=0):
    tokens, width = q.shape
    keys = k.shape[0]
    pairs = width // PAIR
    rows = QUERY_ROWS
    span = WIN + rows if windowed else keys
    params = dict(vmem_limit_bytes=VMEM)
    if rider is not None:
        params.update(collective_id=number, has_side_effects=True)
    return pl.pallas_call(
        functools.partial(
            attend_kernel, span=span, windowed=windowed, rider=rider, n_ins=len(riding),
            n_outs=len(shapes),
        ),
        grid=(tokens // rows,),
        in_specs=[
            pl.BlockSpec((rows, width), lambda i: (i, 0)),
            pl.BlockSpec((keys, width), lambda i: (0, 0)),
            pl.BlockSpec((keys, width), lambda i: (0, 0)),
            pl.BlockSpec((rows, 1), lambda i: (i, 0)),
            pl.BlockSpec((1, keys), lambda i: (0, 0)),
        ]
        + [pl.BlockSpec(x.shape, lambda i: (0, 0)) for x in riding],
        out_specs=[
            pl.BlockSpec((rows, width), lambda i: (i, 0)),
            pl.BlockSpec((pairs, 8, rows), lambda i: (0, 0, i)),
        ]
        + [ANYWHERE] * len(shapes),
        out_shape=[
            jax.ShapeDtypeStruct((tokens, width), low),
            jax.ShapeDtypeStruct((pairs, 8, tokens), f32),
        ]
        + [jax.ShapeDtypeStruct(*x) for x in shapes],
        scratch_shapes=[pltpu.VMEM((rows, span), f32)] + list(scratch),
        compiler_params=pltpu.CompilerParams(**params),
        name="attend",
    )(q, k, v, qid[:, None], kid[None, :], *riding)


def cross_rider(*refs, n_col):
    raw, slices, full = refs[:4], refs[4:8], refs[8:12]
    w_s, w_r, own_s = refs[12:]
    dp, row, col = here()
    part = lax.rem(dp, PARTS)
    part_x, part_y = part + 1 - 2 * lax.rem(part, 2), part + 2 - 4 * (part // 2)
    by_x, by_y = plane()
    wide = raw[0].shape[0]
    rest = (n_col - 1) * wide
    half = rest // 2

    def spot(i, which, begin, size):
        if i < 3:
            count = raw[i].shape[1] // PARTS
            return full[i].at[pl.ds(begin, size), pl.ds(pl.multiple_of(which * count, count), count)]
        count = raw[i].shape[0] // PARTS
        return full[i].at[pl.ds(pl.multiple_of(which * count, count), count), pl.ds(begin, size)]

    def hop(i, stage):
        which, begin, size, to = [
            (part, wide, rest, by_x), (part, wide, rest, by_y),
            (part_x, wide, half, by_y), (part_y, wide + half, half, by_x),
        ][stage]
        dst = spot(i, which, begin, size)
        return remote(slices[i] if stage < 2 else dst, dst, w_s.at[i, stage], w_r.at[i, stage], to)

    def own(i):
        place = full[i].at[pl.ds(0, wide), :] if i < 3 else full[i].at[:, pl.ds(0, wide)]
        return [
            pltpu.make_async_copy(raw[i], place, own_s.at[i, 0]),
            pltpu.make_async_copy(slices[i], spot(i, part, wide, rest), own_s.at[i, 1]),
        ]

    def begin():
        meet([by_x, by_y])
        for i in range(4):
            hop(i, 0).start()
            hop(i, 1).start()
        for i in range(4):
            for copy in own(i):
                copy.start()

    def later():
        for i in range(4):
            for stage in range(2):
                hop(i, stage).wait_recv()
                hop(i, 2 + stage).start()

    def end():
        for i in range(4):
            hop(i, 2).wait_recv()
            hop(i, 3).wait_recv()
            for stage in range(4):
                hop(i, stage).wait_send()
            for copy in own(i):
                copy.wait()

    hooks = Hooks([(0, begin), (2, later)])
    hooks.end = end
    return hooks


def attend_back_kernel(*refs, span, windowed, rider, n_ins, n_outs):
    refs = list(refs)
    q_ref, k_ref, v_ref, do_ref, o_ref, lse_ref, qid_ref, kid_ref = refs[:8]
    rider_refs = refs[8 : 8 + n_ins]
    refs = refs[8 + n_ins :]
    dq_ref, dk_ref, dv_ref = refs[:3]
    rider_refs += refs[3 : 3 + n_outs]
    bias, dk_sum, dv_sum = refs[3 + n_outs : 6 + n_outs]
    rider_refs += refs[6 + n_outs :]
    rows = q_ref.shape[0]
    pairs = q_ref.shape[1] // PAIR
    step = pl.program_id(0)
    start = pl.multiple_of(step * rows, rows) if windowed else 0
    keys = pl.ds(start, span)
    begin, middle, end = rider(*rider_refs)

    @pl.when(step == 0)
    def _():
        begin()
        dk_sum[...] = jnp.zeros_like(dk_sum)
        dv_sum[...] = jnp.zeros_like(dv_sum)

    allowed = kid_ref[keys, :] == qid_ref[...]
    if windowed:
        at_key = lax.broadcasted_iota(jnp.int32, (span, rows), 0)
        at_row = lax.broadcasted_iota(jnp.int32, (span, rows), 1)
        allowed = allowed & (at_key > at_row) & (at_key <= at_row + WIN)
    bias[...] = jnp.where(allowed, 0.0, masked_fill)
    first, second, is_first = head_masks()

    def one_pair(p, carry):
        lanes = pl.ds(pl.multiple_of(p * PAIR, PAIR), PAIR)
        q2 = q_ref[:, lanes]
        k2 = k_ref[keys, lanes]
        v2 = v_ref[keys, lanes]
        do2 = do_ref[:, lanes]
        turned = jnp.transpose(do2.astype(f32) * o_ref[:, lanes].astype(f32))
        dk, dv, dqs = 0.0, 0.0, []
        for h, mask in enumerate((first, second)):
            qm, dom = q2 * mask, do2 * mask
            inner = jnp.sum(turned[h * HEAD_DIM : (h + 1) * HEAD_DIM], axis=0, keepdims=True)
            s = mm_nt(k2, qm) + bias[...]
            share = jnp.exp(s - lse_ref[p, h : h + 1, :])
            ds = (share * (mm_nt(v2, dom) - inner)).astype(low)
            dv = dv + mm(share.astype(low), dom)
            dk = dk + mm(ds, qm)
            dqs.append(mm_tn(ds, k2))
        dk_sum[keys, lanes] += dk
        dv_sum[keys, lanes] += dv
        dq_ref[:, lanes] = (jnp.where(is_first, dqs[0], dqs[1]) * HEAD_DIM**-0.5).astype(low)

        @pl.when((step == 0) & (p == 0))
        def _():
            middle()

        return carry

    lax.fori_loop(0, pairs, one_pair, 0)

    @pl.when(step == pl.num_programs(0) - 1)
    def _():
        dk_ref[...] = dk_sum[...].astype(low)
        dv_ref[...] = dv_sum[...].astype(low)
        end()


def attend_back(q, k, v, do, o, lse, qid, kid, windowed, rider, riding, shapes, scratch, number):
    tokens, width = q.shape
    keys = k.shape[0]
    pairs = width // PAIR
    rows = QUERY_ROWS
    span = WIN + rows if windowed else keys
    by_row = pl.BlockSpec((rows, width), lambda i: (i, 0))
    whole = pl.BlockSpec((keys, width), lambda i: (0, 0))
    return pl.pallas_call(
        functools.partial(
            attend_back_kernel, span=span, windowed=windowed, rider=rider, n_ins=len(riding),
            n_outs=len(shapes),
        ),
        grid=(tokens // rows,),
        in_specs=[
            by_row,
            whole,
            whole,
            by_row,
            by_row,
            pl.BlockSpec((pairs, 8, rows), lambda i: (0, 0, i)),
            pl.BlockSpec((1, rows), lambda i: (0, i)),
            pl.BlockSpec((keys, 1), lambda i: (0, 0)),
        ]
        + [ANYWHERE] * len(riding),
        out_specs=[by_row, whole, whole] + [ANYWHERE] * len(shapes),
        out_shape=[
            jax.ShapeDtypeStruct((tokens, width), low),
            jax.ShapeDtypeStruct((keys, width), low),
            jax.ShapeDtypeStruct((keys, width), low),
        ]
        + [jax.ShapeDtypeStruct(*x) for x in shapes],
        scratch_shapes=[
            pltpu.VMEM((span, rows), f32),
            pltpu.VMEM((keys, width), f32),
            pltpu.VMEM((keys, width), f32),
        ]
        + scratch,
        compiler_params=pltpu.CompilerParams(
            vmem_limit_bytes=VMEM, collective_id=number, has_side_effects=True
        ),
        name="attend_back",
    )(q, k, v, do, o, lse, qid[None, :], kid[:, None], *riding)


def first_rider(
    g1, g2, got_a, got_b, back_a, back_b, far_a, far_b,
    load, mid, l_s, s_s, r_s,
):
    by_x, by_y = plane()
    half = back_a.shape[0]
    up, down = pl.ds(0, half), pl.ds(half, half)
    loads = [
        pltpu.make_async_copy(src, load.at[i], l_s.at[i])
        for i, src in enumerate((g1.at[2, up, :], got_a.at[0], g1.at[1, down, :], got_b.at[0]))
    ]
    hops = [
        remote(g2.at[3, up, :], far_a, s_s.at[0], r_s.at[0], by_x),
        remote(g2.at[3, down, :], far_b, s_s.at[1], r_s.at[1], by_y),
        remote(mid.at[0], back_a, s_s.at[2], r_s.at[2], by_y),
        remote(mid.at[1], back_b, s_s.at[3], r_s.at[3], by_x),
    ]

    def begin():
        meet([by_x, by_y])
        for copy in loads + hops[:2]:
            copy.start()

    def middle():
        for i in range(2):
            loads[2 * i].wait()
            loads[2 * i + 1].wait()
            mid[i] = (load[2 * i].astype(f32) + load[2 * i + 1].astype(f32)).astype(low)
            hops[2 + i].start()

    def end():
        for copy in hops:
            copy.wait()

    return begin, middle, end


def second_rider(
    g1, g2, got_a, got_b, back_a, back_b, far_a, far_b,
    near_a, near_b, far_back_a, far_back_b, z_got, own,
    load, mid, load_z, out_z, l_s, lz_s, s_s, r_s, z_s, z_r, o_s,
    *, n_col,
):
    dp, row, col = here()
    by_x, by_y = plane()
    half = back_a.shape[0]
    wide = own.shape[0]
    up, down = pl.ds(0, half), pl.ds(half, half)
    loads = [
        pltpu.make_async_copy(src, load.at[i], l_s.at[i])
        for i, src in enumerate((g2.at[2, up, :], far_a, g2.at[1, down, :], far_b))
    ]
    loads_z = []
    for i, (source, got, back) in enumerate(((up, got_a, back_a), (down, got_b, back_b))):
        for n, src in enumerate((g1.at[0, source, :], got.at[1], back)):
            loads_z.append(
                pltpu.make_async_copy(src, load_z.at[n, source, :], lz_s.at[i, n])
            )
    hops = [
        remote(g2.at[1, up, :], near_a, s_s.at[0], r_s.at[0], by_x),
        remote(g2.at[2, down, :], near_b, s_s.at[1], r_s.at[1], by_y),
        remote(mid.at[0], far_back_a, s_s.at[2], r_s.at[2], by_y),
        remote(mid.at[1], far_back_b, s_s.at[3], r_s.at[3], by_x),
    ]
    cols = [(dp, row, lax.rem(col + k, n_col)) for k in range(n_col)]
    over = [
        remote(out_z.at[k], z_got.at[k - 1], z_s.at[k - 1], z_r.at[k - 1], cols[k])
        for k in range(1, n_col)
    ]
    keep = pltpu.make_async_copy(out_z.at[0], own, o_s)

    def begin():
        meet([by_x, by_y] + cols[1:])
        for copy in loads + loads_z + hops[:2]:
            copy.start()

    def middle():
        for i in range(2):
            loads[2 * i].wait()
            loads[2 * i + 1].wait()
            mid[i] = (load[2 * i].astype(f32) + load[2 * i + 1].astype(f32)).astype(low)
            hops[2 + i].start()
        for copy in loads_z:
            copy.wait()
        for k in list(range(1, n_col)) + [0]:
            at = pl.ds(k * wide, wide)
            value = load_z[0, at, :].astype(f32) + load_z[1, at, :].astype(f32)
            out_z[k] = (value + load_z[2, at, :].astype(f32)).astype(low)
            if k:
                over[k - 1].start()
        keep.start()

    def end():
        for copy in hops + over + [keep]:
            copy.wait()

    return begin, middle, end


ROOT = 0.7978845608028654
CUBE = 0.044715


def hidden_kernel(
    f_ref, w1_ref, b1_ref, w2_ref, x_ref, bias, cot, act_ref, slope_ref, out_ref, dz,
    total, away, came, s_s, s_r, c_s, c_r, d_s, d_r,
    *, n_col,
):
    step = pl.program_id(0) * pl.num_programs(1) + pl.program_id(1)
    last = pl.num_programs(0) * pl.num_programs(1) - 1
    dp, row, col = here()
    twin = (dp, 1 - row, col)
    wide = cot.shape[1]
    rows_here = cot.shape[0] // n_col

    def cot_piece(j):
        to_col = 2 * row + j // 2
        k = lax.rem(col + n_col - to_col, n_col)
        src = cot.at[pl.ds(j * rows_here, rows_here), :]
        dst = dz.at[j % 2, :, pl.ds(pl.multiple_of(k * wide, wide), wide)]
        local = (row == j % 2) & (col == to_col)
        return src, dst, k, local, (dp, j % 2, to_col)

    def cot_twin(k):
        ref = dz.at[row, :, pl.ds(k * wide, wide)]
        return remote(ref, ref, d_s.at[k], d_r.at[k], twin)

    @pl.when(step == 0)
    def _():
        total[...] = jnp.zeros_like(total)
        group = [
            (dp, r, lax.rem(col + k, n_col)) for r in (row, 1 - row) for k in range(n_col)
        ]
        meet(group[1:])
        for j in range(n_col):
            src, dst, k, local, to = cot_piece(j)

            @pl.when(local)
            def _():
                pltpu.make_async_copy(src, dst, c_r.at[k]).start()

            @pl.when(jnp.logical_not(local))
            def _():
                remote(src, dst, c_s.at[j], c_r.at[k], to).start()

    def one_part(t, carry):
        rows = pl.ds(pl.multiple_of(t * 256, 256), 256)
        h = mm(f_ref[rows, :], w1_ref[0]) + b1_ref[0]
        square = h * h
        bend = jnp.tanh(h * (ROOT + (ROOT * CUBE) * square))
        half = 0.5 + 0.5 * bend
        act = (h * half).astype(low)
        act_ref[0, rows, :] = act
        slope = half + (0.5 * h) * (1.0 - bend * bend) * (ROOT + (3.0 * ROOT * CUBE) * square)
        slope_ref[0, rows, :] = slope.astype(low)
        total[rows, :] += mm_nt(act, w2_ref[0])
        return carry

    lax.fori_loop(0, f_ref.shape[0] // 256, one_part, 0)

    @pl.when(step == last - 1)
    def _():
        for k in range(n_col):
            pltpu.make_async_copy(
                cot.at[pl.ds(0, rows_here), :], dz.at[row, :, pl.ds(k * wide, wide)], c_r.at[k]
            ).wait()
            cot_twin(k).start()

    @pl.when(step == last)
    def _():
        rows = came.shape[0]
        sent = []
        for t in range(rows // CUT):
            at = pl.ds(t * CUT, CUT)
            begin = pl.multiple_of((1 - row) * rows + t * CUT, CUT)
            away[at, :] = total[pl.ds(begin, CUT), :].astype(low)
            copy = remote(away.at[at, :], came.at[at, :], s_s.at[t], s_r.at[t], twin)
            copy.start()
            sent.append(copy)
        for t in range(rows // CUT):
            at = pl.ds(t * CUT, CUT)
            begin = pl.multiple_of(row * rows + t * CUT, CUT)
            sent[t].wait()
            branch = total[pl.ds(begin, CUT), :] + came[at, :].astype(f32)
            out_ref[at, :] = (x_ref[at, :] + (branch + bias[...])).astype(low)
        for j in range(n_col):
            src, dst, k, local, to = cot_piece(j)

            @pl.when(jnp.logical_not(local))
            def _():
                remote(src, dst, c_s.at[j], c_r.at[k], to).wait_send()

        for k in range(n_col):
            cot_twin(k).wait()


def hidden_forward(f, w1, b1, w2, x, bias, cotangent, n_col, number):
    parts, width, inner = w1.shape
    tokens = f.shape[0]
    block = min(512, inner)
    grid = (parts, inner // block)
    weight = pl.BlockSpec((1, width, block), lambda j, n: (j, 0, n))
    active = pl.BlockSpec((1, tokens, block), lambda j, n: (j, 0, n))
    rows = tokens // 2
    dma = pltpu.SemaphoreType.DMA
    half = pl.BlockSpec((rows, width), lambda j, n: (0, 0))
    return pl.pallas_call(
        functools.partial(hidden_kernel, n_col=n_col),
        grid=grid,
        in_specs=[
            pl.BlockSpec((tokens, width), lambda j, n: (0, 0)),
            weight,
            pl.BlockSpec((1, 1, block), lambda j, n: (j, 0, n)),
            weight,
            half,
            pl.BlockSpec((1, width), lambda j, n: (0, 0)),
            pl.BlockSpec(cotangent.shape, lambda j, n: (0, 0)),
        ],
        out_specs=[active, active, half, ANYWHERE],
        out_shape=[
            jax.ShapeDtypeStruct((parts, tokens, inner), low),
            jax.ShapeDtypeStruct((parts, tokens, inner), low),
            jax.ShapeDtypeStruct((rows, width), low),
            jax.ShapeDtypeStruct((2, rows, width), low),
        ],
        scratch_shapes=[
            pltpu.VMEM((tokens, width), f32),
            pltpu.VMEM((rows, width), low),
            pltpu.VMEM((rows, width), low),
            dma((rows // CUT,)), dma((rows // CUT,)),
            dma((n_col,)), dma((n_col,)), dma((n_col,)), dma((n_col,)),
        ],
        compiler_params=pltpu.CompilerParams(
            vmem_limit_bytes=VMEM, collective_id=number, has_side_effects=True
        ),
        name="hidden_forward",
    )(f, w1, b1, w2, x, bias[None], cotangent)


def hidden_back_kernel(
    dz_ref, dzt_ref, ft_ref, w1_ref, w2_ref, act_ref, slope_ref, rows_out,
    g1_ref, g2_ref, gb_ref, df_ref, got_a, got_b, home, dh_low, total, away_a, away_b, s_s, r_s,
    h_s, h_r, *, n_col,
):
    inner, inners = pl.program_id(1), pl.num_programs(1)
    order = pl.program_id(0)
    step = order * inners + inner
    last = pl.num_programs(0) * inners - 1
    by_x, by_y = plane()
    half = got_a.shape[1]
    dp, row, col = here()

    @pl.when(step == 0)
    def _():
        group = [
            (dp, r, lax.rem(col + k, n_col)) for r in (row, 1 - row) for k in range(n_col)
        ]
        meet(group[1:] + [by_x, by_y])
        total[...] = jnp.zeros_like(total)
        send_home(rows_out, home, h_s, h_r, n_col)

    gb_ref[...] = jnp.zeros_like(gb_ref)

    def one_part(t, carry):
        rows = pl.ds(pl.multiple_of(t * 256, 256), 256)
        dh = (mm(dz_ref[rows, :], w2_ref[0]) * slope_ref[0, rows, :].astype(f32)).astype(low)
        dh_low[rows, :] = dh
        gb_ref[0] += jnp.sum(dh.astype(f32), axis=0, keepdims=True)
        total[rows, :] += mm_nt(dh, w1_ref[0])
        return carry

    lax.fori_loop(0, dz_ref.shape[0] // 256, one_part, 0)

    def one_grad(t, carry):
        rows = pl.ds(pl.multiple_of(t * 256, 256), 256)
        g2_ref[0, rows, :] = mm(dzt_ref[rows, :], act_ref[0]).astype(low)
        g1_ref[0, rows, :] = mm(ft_ref[rows, :], dh_low[...]).astype(low)
        return carry

    lax.fori_loop(0, ft_ref.shape[0] // 256, one_grad, 0)

    block = g1_ref.shape[2]
    lanes = pl.ds(pl.multiple_of(inner * block, block), block)

    def hop(which, slot, n):
        away, got, to = [(away_a, got_a, by_x), (away_b, got_b, by_y)][which]
        at = pl.ds(n * block, block)
        return remote(
            away.at[slot, :, at], got.at[slot, :, at], s_s.at[which, slot, n],
            r_s.at[which, slot, n], to,
        )

    for at, which, slot in ((0, 0, 0), (0, 1, 0), (1, 0, 1), (2, 1, 1)):

        @pl.when(order == at)
        def _():
            away = (away_a, away_b)[which]
            away[slot, :, lanes] = g1_ref[0, which * half : (which + 1) * half, :]

        for n in range(got_a.shape[2] // block):

            @pl.when((order == at) & (inner == n))
            def _():
                hop(which, slot, n).start()

    @pl.when(step == last)
    def _():
        df_ref[...] = total[...].astype(low)
        for which in range(2):
            for slot in range(2):
                for n in range(got_a.shape[2] // block):
                    hop(which, slot, n).wait()
        wait_home(rows_out, home, h_s, h_r, n_col)


def hidden_backward(dz, f, w1, w2, act, slope, rows_out, n_col, number):
    parts, width, inner = w1.shape
    tokens = f.shape[0]
    block = min(512, inner)
    grid = (parts, inner // block)

    def number_of(j):
        return jnp.where(j == 0, parts - 1, jnp.where(j == parts - 1, 0, j))

    weight = pl.BlockSpec((1, width, block), lambda j, n: (number_of(j), 0, n))
    active = pl.BlockSpec((1, tokens, block), lambda j, n: (number_of(j), 0, n))
    whole = pl.BlockSpec((tokens, width), lambda j, n: (0, 0))
    turned = pl.BlockSpec((width, tokens), lambda j, n: (0, 0))
    landing = jax.ShapeDtypeStruct((2, width // 2, inner), low)
    return pl.pallas_call(
        functools.partial(hidden_back_kernel, n_col=n_col),
        grid=grid,
        in_specs=[whole, turned, turned, weight, weight, active, active]
        + [pl.BlockSpec(rows_out.shape, lambda j, n: (0, 0))],
        out_specs=[
            weight, weight, pl.BlockSpec((1, 1, block), lambda j, n: (number_of(j), 0, n)), whole,
            ANYWHERE, ANYWHERE, ANYWHERE,
        ],
        out_shape=[
            jax.ShapeDtypeStruct(w1.shape, low),
            jax.ShapeDtypeStruct(w1.shape, low),
            jax.ShapeDtypeStruct((parts, 1, inner), f32),
            jax.ShapeDtypeStruct((tokens, width), low),
            landing,
            landing,
            jax.ShapeDtypeStruct((n_col * rows_out.shape[0], width // n_col), low),
        ],
        scratch_shapes=[
            pltpu.VMEM((tokens, block), low),
            pltpu.VMEM((tokens, width), f32),
            pltpu.VMEM(landing.shape, low),
            pltpu.VMEM(landing.shape, low),
            pltpu.SemaphoreType.DMA((2, 2, inner // block)),
            pltpu.SemaphoreType.DMA((2, 2, inner // block)),
            pltpu.SemaphoreType.DMA((n_col,)),
            pltpu.SemaphoreType.DMA((n_col,)),
        ],
        compiler_params=pltpu.CompilerParams(
            vmem_limit_bytes=VMEM, collective_id=number, has_side_effects=True
        ),
        name="hidden_backward",
    )(dz, dz.T, f.T, w1, w2, act, slope, rows_out)


def start_kernel(
    tokens, encoder, vec_f, vec_c, *refs, n_col,
):
    weights, (x_ext, enc, all_f, all_c), full = refs[:8], refs[8:12], refs[12:20]
    (zeros, w_send, w_recv, w_own, t_send, t_recv, v_send, v_recv, z_sem, z_send, z_recv, e_send,
     e_recv, o_sem) = refs[20:]
    dp, row, col = here()
    part = lax.rem(dp, PARTS)
    twin = (dp, 1 - row, col)
    flip = [
        dp + 1 - 2 * lax.rem(dp, 2),
        dp + 2 - 4 * lax.rem(dp // 2, 2),
    ]
    by_x, by_y = (flip[0], row, col), (flip[1], row, col)
    part_x, part_y = lax.rem(flip[0], PARTS), lax.rem(flip[1], PARTS)
    shift = [lax.rem(col + k, n_col) for k in range(n_col)]
    group = [(dp, r, c) for r in (row, 1 - row) for c in shift][1:]
    meet(group + [by_x, by_y])

    wide = tokens.shape[1]
    deep = n_col * wide
    rest = deep - wide

    def chunk(index, size):
        return pl.ds(pl.multiple_of(index * size, size), size)

    to_right, to_left = (dp, row, lax.rem(col + 1, n_col)), (dp, row, lax.rem(col + n_col - 1, n_col))

    def weight_chunk(i, k):
        w = weights[i]
        if i % 4 < 3:
            return full[i].at[pl.ds(k * wide, wide), chunk(part, w.shape[1] // PARTS)]
        return full[i].at[chunk(part, w.shape[0] // PARTS), pl.ds(k * wide, wide)]

    def weight_slice(i):
        w = weights[i]
        if i % 4 < 3:
            return w.at[:, chunk(part, w.shape[1] // PARTS)]
        return w.at[chunk(part, w.shape[0] // PARTS), :]

    def enc_chunk(k):
        return enc.at[chunk(row, encoder.shape[0]), pl.ds(k * wide, wide)]

    def piece(i, k):
        if i == 8:
            return enc_chunk(k)
        if i < 4:
            return weight_chunk(i, k)
        if i % 4 < 3:
            return full[i].at[pl.ds((k - 1) * wide, wide), :]
        return full[i].at[:, pl.ds((k - 1) * wide, wide)]

    def own_piece(i):
        return encoder if i == 8 else weight_slice(i)

    def enc_twin(k):
        return remote(own_piece(8) if k == 0 else enc_chunk(k), enc_chunk(k), e_send.at[k],
                      e_recv.at[k], twin)

    def rightward(i, h):
        src = own_piece(i) if h == 1 else piece(i, n_col + 1 - h)
        k = n_col - h
        return remote(src, piece(i, k), z_send.at[i, 0, h - 1], z_recv.at[i, k - 1], to_right)

    def leftward(i, h):
        src = own_piece(i) if h == 1 else piece(i, h - 1)
        return remote(src, piece(i, h), z_send.at[i, 1, h - 1], z_recv.at[i, h - 1], to_left)

    def right_valid(h):
        return (col >= h - 1) & (col < n_col - 1)

    def left_valid(h):
        return (col <= n_col - h) & (col > 0)

    def send_along(i, h):
        @pl.when(right_valid(h))
        def _():
            rightward(i, h).start()

        @pl.when(left_valid(h))
        def _():
            leftward(i, h).start()

    def take(i, h):
        @pl.when(col >= h)
        def _():
            rightward(i, h).wait_recv()

        @pl.when(col < n_col - h)
        def _():
            leftward(i, h).wait_recv()

    def weight_own(i):
        w = weights[i]
        place = full[i].at[pl.ds(0, wide), :] if i % 4 < 3 else full[i].at[:, pl.ds(0, wide)]
        return pltpu.make_async_copy(w, place, w_own.at[i])

    def weight_part(i, which, begin, size):
        if i % 4 < 3:
            return full[i].at[pl.ds(begin, size), chunk(which, weights[i].shape[1] // PARTS)]
        return full[i].at[chunk(which, weights[i].shape[0] // PARTS), pl.ds(begin, size)]

    def weight_plane(i, stage):
        half = rest // 2
        which, begin, size, to = [
            (part, wide, rest, by_x),
            (part, wide, rest, by_y),
            (part_x, wide, half, by_y),
            (part_y, wide + half, half, by_x),
        ][stage]
        ref = weight_part(i, which, begin, size)
        return remote(ref, ref, w_send.at[i, stage], w_recv.at[i, stage], to)

    def token_piece(j, slot):
        rows = tokens.shape[0] // n_col
        to_col = 2 * row + j // 2 + (1 - slot)
        k = lax.rem(col + n_col - lax.rem(to_col, n_col), n_col)
        src = tokens.at[pl.ds(j * rows, rows), :]
        dst = x_ext.at[slot, :, chunk(k, wide)]
        local = (row == j % 2) & (col == to_col)
        valid = to_col < n_col
        return src, dst, k, local, valid, (dp, j % 2, to_col)

    def send_tokens(slot):
        for j in range(n_col):
            src, dst, k, local, valid, to = token_piece(j, slot)

            @pl.when(valid & local)
            def _():
                pltpu.make_async_copy(src, dst, t_recv.at[slot, k]).start()

            @pl.when(valid & jnp.logical_not(local))
            def _():
                remote(src, dst, t_send.at[slot, j], t_recv.at[slot, k], to).start()

    def vectors(k):
        to = (dp, row, lax.rem(col + n_col - k, n_col))
        return [
            remote(vec_f, all_f.at[:, pl.ds(k * wide, wide)], v_send.at[0, k], v_recv.at[0, k], to),
            remote(vec_c, all_c.at[col], v_send.at[1, k], v_recv.at[1, k], to),
        ]

    own_vectors = [
        pltpu.make_async_copy(encoder, enc_chunk(0), o_sem),
        pltpu.make_async_copy(vec_f, all_f.at[:, pl.ds(0, wide)], v_recv.at[0, 0]),
        pltpu.make_async_copy(vec_c, all_c.at[col], v_recv.at[1, 0]),
    ]
    ks = range(1, n_col)
    for i in range(9):
        send_along(i, 1)
    for k in ks:
        for copy in vectors(k):
            copy.start()
    for i in range(4):
        weight_own(i).start()
    for copy in own_vectors:
        copy.start()
    enc_twin(0).start()
    for h in (1, 2):
        for i in range(9):
            take(i, h)
            send_along(i, h + 1)
    send_tokens(1)
    send_tokens(0)

    @pl.when(col == 0)
    def _():
        zeros[...] = jnp.zeros_like(zeros)
        clear = pltpu.make_async_copy(zeros, x_ext.at[0], z_sem)
        clear.start()
        clear.wait()

    for i in range(8):
        take(i, 3)
        if i < 4:
            weight_plane(i, 0).start()
            weight_plane(i, 1).start()
    take(8, 3)
    for k in ks:
        enc_twin(k).start()
    for i in range(4):
        weight_plane(i, 0).wait_recv()
        weight_plane(i, 2).start()
        weight_plane(i, 1).wait_recv()
        weight_plane(i, 3).start()
    for i in range(4):
        weight_plane(i, 2).wait_recv()
        weight_plane(i, 3).wait_recv()
        weight_own(i).wait()
        for stage in range(4):
            weight_plane(i, stage).wait_send()
    for k in range(n_col):
        enc_twin(k).wait()
    for i in range(9):
        for h in ks:

            @pl.when(right_valid(h))
            def _():
                rightward(i, h).wait_send()

            @pl.when(left_valid(h))
            def _():
                leftward(i, h).wait_send()

    for copy in own_vectors:
        copy.wait()
    for k in ks:
        for copy in vectors(k):
            copy.wait()
    for slot in (1, 0):
        for j in range(n_col):
            src, dst, k, local, valid, to = token_piece(j, slot)

            @pl.when(valid & jnp.logical_not(local))
            def _():
                remote(src, dst, t_send.at[slot, j], t_recv.at[slot, k], to).wait_send()

        for k in range(n_col):
            rows = tokens.shape[0] // n_col
            came = pltpu.make_async_copy(
                tokens.at[pl.ds(0, rows), :],
                x_ext.at[slot, :, pl.ds(k * wide, wide)],
                t_recv.at[slot, k],
            )
            if slot == 1:
                came.wait()
            else:

                @pl.when(col > 0)
                def _():
                    came.wait()


def start(tokens, encoder, vec_f, vec_c, weights, n_col):
    wide = tokens.shape[1]
    deep = n_col * wide
    rows = tokens.shape[0] // n_col
    shapes = [
        jax.ShapeDtypeStruct((2, rows, deep), low),
        jax.ShapeDtypeStruct((2 * encoder.shape[0], deep), low),
        jax.ShapeDtypeStruct((vec_f.shape[0], deep), f32),
        jax.ShapeDtypeStruct((n_col,) + vec_c.shape, f32),
    ]
    for i, w in enumerate(weights):
        at, length, size = (0, deep, w.shape[1]) if i % 4 < 3 else (1, deep, w.shape[0])
        if i >= 4:
            length, size = deep - wide, size // PARTS
        shapes.append(jax.ShapeDtypeStruct((size, length) if at else (length, size), low))
    dma = pltpu.SemaphoreType.DMA
    return pl.pallas_call(
        functools.partial(start_kernel, n_col=n_col),
        in_specs=[IN_VMEM] * 12,
        out_specs=[ANYWHERE] * 12,
        out_shape=shapes,
        scratch_shapes=[
            pltpu.VMEM((rows, deep), low),
            dma((4, 4)), dma((4, 4)), dma((4,)),
            dma((2, n_col)), dma((2, n_col)),
            dma((2, n_col)), dma((2, n_col)),
            dma, dma((9, 2, n_col - 1)), dma((9, n_col - 1)), dma((n_col,)), dma((n_col,)), dma,
        ],
        compiler_params=pltpu.CompilerParams(
            collective_id=1, has_side_effects=True, vmem_limit_bytes=VMEM
        ),
        name="start",
    )(tokens, encoder, vec_f, vec_c, *weights)


def norm_rows(x):
    center = jnp.mean(x, axis=1, keepdims=True)
    spread = jnp.mean(x * x, axis=1, keepdims=True) - center * center
    scaling = lax.rsqrt(spread + norm_epsilon)
    return (x - center) * scaling, scaling


CUT = 256
N_COL = 4


def enter_kernel(x_ref, gain, shift, a_ref, sends, recvs):
    dp, row, col = here()
    twin = (dp, 1 - row, col)
    meet([twin])
    slots, rows = x_ref.shape[:2]

    def place(slot):
        return a_ref.at[slot, pl.ds(pl.multiple_of(row * rows, rows), rows), :]

    copies = []
    for slot in reversed(range(slots)):
        for t in range(rows // CUT):
            normed, _ = norm_rows(x_ref[slot, pl.ds(t * CUT, CUT), :].astype(f32))
            begin = pl.multiple_of(row * rows + t * CUT, CUT)
            a_ref[slot, pl.ds(begin, CUT), :] = (normed * gain[...] + shift[...]).astype(low)
        copy = remote(place(slot), place(slot), sends.at[slot], recvs.at[slot], twin)
        copy.start()
        copies.append(copy)
    for copy in copies:
        copy.wait()


def enter(x_ext, gain, shift, number):
    slots, rows, deep = x_ext.shape
    return pl.pallas_call(
        enter_kernel,
        in_specs=[IN_VMEM] * 3,
        out_specs=IN_VMEM,
        out_shape=jax.ShapeDtypeStruct((slots, 2 * rows, deep), low),
        scratch_shapes=[pltpu.SemaphoreType.DMA((slots,)), pltpu.SemaphoreType.DMA((slots,))],
        compiler_params=pltpu.CompilerParams(
            collective_id=number, has_side_effects=True, vmem_limit_bytes=VMEM
        ),
        name="enter",
    )(x_ext, gain[None], shift[None])


def junction_kernel(*refs, kinds, mode):
    dp, row, col = here()
    twin = (dp, 1 - row, col)
    meet([twin])
    refs = list(refs)
    sources = []
    for kind in kinds:
        sources.append((kind, refs.pop(0), refs.pop(0) if kind != "sum" else None))
    if mode == "forward":
        x_ref, bias, gain, shift, x_out, full, away, came, s1, r1, s2, r2 = refs
    elif mode == "backward":
        res_ref, x_ref, gain, dx_out, full, stats, away, came, s1, r1, s2, r2 = refs
    elif mode == "last":
        res_ref, x_ref, gain, after, dx_out, stats, away, came, s1, r1 = refs
        full = None
    else:
        out, away, came, s1, r1 = refs
    rows = came.shape[0]
    cuts = rows // CUT

    def partial(begin):
        total = None
        for kind, g, w in sources:
            part = g[pl.ds(begin, CUT), :]
            if kind == "sum":
                part = part.astype(f32)
            elif kind == "nt":
                part = mm_nt(part, w[...])
            else:
                part = mm(part, w[...])
            total = part if total is None else total + part
        return total

    sent = []
    for t in range(cuts):
        at = pl.ds(t * CUT, CUT)
        away[at, :] = partial(pl.multiple_of((1 - row) * rows + t * CUT, CUT)).astype(low)
        copy = remote(away.at[at, :], came.at[at, :], s1.at[t], r1.at[t], twin)
        copy.start()
        sent.append(copy)
    gathered = []
    sums = [0.0] * 4
    for t in range(cuts):
        at = pl.ds(t * CUT, CUT)
        begin = pl.multiple_of(row * rows + t * CUT, CUT)
        own = partial(begin)
        sent[t].wait_recv()
        total = own + came[at, :].astype(f32)
        if mode == "sum":
            out[at, :] = total.astype(low)
            continue
        if mode == "last":
            deep = after.shape[1]
            wide = deep // N_COL
            moved = [after[at, pl.ds(deep - wide, wide)], after[at, pl.ds(0, deep - wide)]]
            total = total + jnp.concatenate(moved, axis=1).astype(f32)
        if mode == "forward":
            x = x_ref[at, :].astype(f32) + (total + bias[...])
            x_out[at, :] = x
            normed, _ = norm_rows(x)
            result = (normed * gain[...] + shift[...]).astype(low)
        else:
            normed, scaling = norm_rows(x_ref[at, :].astype(f32))
            upstream = total * gain[...]
            mean_up = jnp.mean(upstream, axis=1, keepdims=True)
            mean_both = jnp.mean(upstream * normed, axis=1, keepdims=True)
            res = res_ref[at if res_ref.shape[0] == rows else pl.ds(begin, CUT), :].astype(f32)
            dx = res + scaling * (upstream - mean_up - normed * mean_both)
            dx_out[at, :] = dx.astype(dx_out.dtype)
            result = dx.astype(low)
            for i, value in enumerate((total * normed, total, result.astype(f32), res)):
                sums[i] = sums[i] + jnp.sum(value, axis=0, keepdims=True)
        if full is None:
            continue
        full[pl.ds(begin, CUT), :] = result
        place = full.at[pl.ds(begin, CUT), :]
        copy = remote(place, place, s2.at[t], r2.at[t], twin)
        copy.start()
        gathered.append(copy)
    if mode in ("backward", "last"):
        for i in range(4):
            stats[i : i + 1, :] = sums[i]
    for copy in sent:
        copy.wait_send()
    for copy in gathered:
        copy.wait()


def junction(mode, sources, others, number):
    kinds = [x[0] for x in sources]
    first = sources[0]
    tokens = first[1].shape[0]
    deep = first[1].shape[1]
    if first[0] != "sum":
        deep = first[2].shape[0 if first[0] == "nt" else 1]
    rows = tokens // 2
    flat = [x for source in sources for x in source[1:]]
    dma = pltpu.SemaphoreType.DMA((rows // CUT,))
    wide_rows = jax.ShapeDtypeStruct((rows, deep), f32)
    every = jax.ShapeDtypeStruct((tokens, deep), low)
    shapes = {
        "forward": [wide_rows, every],
        "backward": [wide_rows, every, jax.ShapeDtypeStruct((8, deep), f32)],
        "last": [jax.ShapeDtypeStruct((rows, deep), low), jax.ShapeDtypeStruct((8, deep), f32)],
        "sum": [jax.ShapeDtypeStruct((rows, deep), low)],
    }[mode]
    scratch = [pltpu.VMEM((rows, deep), low), pltpu.VMEM((rows, deep), low), dma, dma]
    if mode in ("forward", "backward"):
        scratch += [dma, dma]
    args = flat + [x[None] if x.ndim == 1 else x for x in others]
    out = pl.pallas_call(
        functools.partial(junction_kernel, kinds=kinds, mode=mode),
        in_specs=[IN_VMEM] * len(args),
        out_specs=[IN_VMEM] * len(shapes),
        out_shape=shapes,
        scratch_shapes=scratch,
        compiler_params=pltpu.CompilerParams(
            collective_id=number, has_side_effects=True, vmem_limit_bytes=VMEM
        ),
        name="junction_" + mode,
    )(*args)
    return out if len(out) > 1 else out[0]


def finish_kernel(
    ga, gb, small, enc_in, tg, g2, near_a, near_b, far_back_a, far_back_b, z_got, own1,
    full, hidden_full, small_out, enc_out, tg_out,
    load, load_own, load_got, h_out, h_in, l_s, lo_s, hz_s, hz_r, h_extra, hx_s, hx_r, hg_s, hg_r,
    first, second, mid, zout, zin, tot, enc_got, s_cur, s_got, s_z, extra,
    f_s, f_r, m_s, m_r, z_s, z_r, g_s, g_r, e_s, e_r, s_s, s_r, sz_s, sz_r, t_s, t_r, x_s, x_r,
    *, n_col, n_dp,
):
    dp, row, col = here()
    part = lax.rem(dp, PARTS)
    twin = (dp, 1 - row, col)
    bits = [1 << b for b in range(n_dp.bit_length() - 1)]
    flips = [dp + b - 2 * b * lax.rem(dp // b, 2) for b in bits]
    by_bit = [(f, row, col) for f in flips]
    shift = [lax.rem(col + k, n_col) for k in range(n_col)]
    group = [(dp, r, c) for r in (row, 1 - row) for c in shift][1:]
    meet(group + by_bit)
    wide = ga.shape[1] // n_col
    ks = range(1, n_col)
    part_x, part_y, part_xy = part + 1 - 2 * lax.rem(part, 2), part + 2 - 4 * (part // 2), 3 - part
    ways = [(ga, 0, (part_x, part_xy), part_y), (gb, 1, (part_y, part_xy), part_x)]
    h_half = near_a.shape[0]
    loads = []
    for i, sources in enumerate(((near_a, far_back_a), (near_b, far_back_b))):
        at = pl.ds(i * h_half, h_half)
        for n, src in enumerate((g2.at[0, at, :],) + sources):
            loads.append(pltpu.make_async_copy(src, load.at[n, at, :], l_s.at[i, n]))
    loads_own = [
        pltpu.make_async_copy(own1, load_own, lo_s.at[0]),
        pltpu.make_async_copy(z_got, load_got, lo_s.at[1]),
    ]

    def hidden_hop(k):
        return remote(h_out.at[k], h_in.at[k - 1], hz_s.at[k - 1], hz_r.at[k - 1], z_to(k))

    def hidden_total(k):
        at = rows(k)
        value = load[0, at, :].astype(f32) + load[1, at, :].astype(f32)
        return value + load[2, at, :].astype(f32)

    def other_bits(value, g, store, s_x, r_x):
        for i in range(len(bits) - 2):
            store[g, i, 0] = value.astype(low)
            copy = remote(
                store.at[g, i, 0], store.at[g, i, 1], s_x.at[g, i], r_x.at[g, i], by_bit[2 + i]
            )
            copy.start()
            copy.wait()
            value = value + store[g, i, 1].astype(f32)
        return value

    def rows(q):
        return pl.ds(q * wide, wide)

    def z_to(k):
        return (dp, row, shift[k])

    def hop(g, a, q):
        src, way, away, _ = ways[g]
        return remote(
            src.at[away[a], rows(q), :], first.at[g, a, rows(q), :], f_s.at[g, a, q],
            f_r.at[g, a, q], by_bit[way],
        )

    def hop2(g, q):
        ref = mid.at[g, rows(q), :]
        return remote(
            ref, second.at[g, rows(q), :], m_s.at[g, q], m_r.at[g, q], by_bit[1 - ways[g][1]]
        )

    def z_hop(g, q):
        return remote(zout.at[g, q - 1], zin.at[g, q - 1], z_s.at[g, q - 1], z_r.at[g, q - 1], z_to(q))

    def enc_hop(k):
        src = enc_in.at[:, pl.ds(k * wide, wide)]
        return remote(src, enc_got.at[k - 1], e_s.at[k - 1], e_r.at[k - 1], z_to(k))

    partners = [twin] + by_bit

    def small_hop(i):
        return remote(s_cur.at[i], s_got.at[i], s_s.at[i], s_r.at[i], partners[i])

    def small_z(k):
        return remote(s_cur.at[len(partners), k], s_z.at[k - 1], sz_s.at[k - 1], sz_r.at[k - 1], z_to(k))

    def small_step(i):
        if i == 0:
            s_cur[0] = small[...]
        elif i <= len(partners):
            small_hop(i - 1).wait_recv()
            got = s_got[i - 1]
            if i == 1:
                lane = lax.broadcasted_iota(jnp.int32, got.shape, 2)
                got = jnp.where(lane < wide, got, 0.0)
            s_cur[i] = s_cur[i - 1] + got
        if i < len(partners):
            small_hop(i).start()
        elif i == len(partners):
            for k in ks:
                small_z(k).start()
        else:
            value = s_cur[len(partners), 0]
            for k in ks:
                small_z(k).wait_recv()
                value = value + s_z[k - 1]
            small_out[...] = value

    half = wide // 2

    def plane_hop(full, g, stage, sends, recvs):
        which, begin, size, way = [
            (part, 0, wide, 0), (part, 0, wide, 1), (part_x, 0, half, 1), (part_y, half, half, 0),
        ][stage]
        ref = full.at[g, which, pl.ds(begin, size), :]
        return remote(ref, ref, sends.at[g, stage], recvs.at[g, stage], by_bit[way])

    def plane_to(g, stage):
        return plane_hop(full, g, stage, g_s, g_r)

    def hidden_plane(g, stage):
        return plane_hop(hidden_full, g, stage, hg_s, hg_r)

    small_step(0)
    for copy in loads + loads_own:
        copy.start()
    for q in range(n_col):
        for g in range(2):
            hop(g, 1, q).start()
    for copy in loads:
        copy.wait()
    for k in ks:
        h_out[k] = hidden_total(k).astype(low)
        hidden_hop(k).start()
    small_step(1)
    done = 2
    for q in range(n_col):
        for g in range(2):
            src, _, _, keep = ways[g]
            hop(g, 1, q).wait_recv()
            value = src[keep, rows(q), :].astype(f32) + first[g, 1, rows(q), :].astype(f32)
            mid[g, rows(q), :] = value.astype(low)
            hop2(g, q).start()
            hop(g, 0, q).start()
        if done < len(partners) + 2:
            small_step(done)
            done += 1
    for copy in loads_own:
        copy.wait()
    value = load_own[...].astype(f32)
    for k in ks:
        value = value + load_got[k - 1].astype(f32)
    hidden_full[0, part] = other_bits(value, 0, h_extra, hx_s, hx_r).astype(low)
    hidden_plane(0, 0).start()
    hidden_plane(0, 1).start()
    for q in range(n_col):
        for g in range(2):
            src = ways[g][0]
            hop(g, 0, q).wait_recv()
            hop2(g, q).wait_recv()
            value = src[part, rows(q), :].astype(f32) + first[g, 0, rows(q), :].astype(f32)
            value = value + second[g, rows(q), :].astype(f32)
            if q:
                zout[g, q - 1] = value.astype(low)
                z_hop(g, q).start()
            else:
                tot[g] = value
        if done < len(partners) + 2:
            small_step(done)
            done += 1
    send_home(tg, tg_out, t_s, t_r, n_col)
    for k in ks:
        enc_hop(k).start()
    value = hidden_total(0)
    for k in ks:
        hidden_hop(k).wait_recv()
        value = value + h_in[k - 1].astype(f32)
    hidden_full[1, part] = other_bits(value, 1, h_extra, hx_s, hx_r).astype(low)
    hidden_plane(1, 0).start()
    hidden_plane(1, 1).start()
    for g in range(2):
        for stage in range(2):
            hidden_plane(g, stage).wait_recv()
            hidden_plane(g, 2 + stage).start()
    while done < len(partners) + 2:
        small_step(done)
        done += 1
    for g in range(2):
        value = tot[g]
        for q in ks:
            z_hop(g, q).wait_recv()
            value = value + zin[g, q - 1].astype(f32)
        value = other_bits(value, g, extra, x_s, x_r)
        full[g, part] = value.astype(low)
        plane_to(g, 0).start()
        plane_to(g, 1).start()
    for g in range(2):
        for stage in range(2):
            plane_to(g, stage).wait_recv()
            plane_to(g, 2 + stage).start()
    value = enc_in[:, pl.ds(0, wide)].astype(f32)
    for k in ks:
        enc_hop(k).wait()
        value = value + enc_got[k - 1].astype(f32)
    enc_out[...] = value
    for k in ks:
        hidden_hop(k).wait_send()
        small_z(k).wait_send()
    for g in range(2):
        for ways_out in (hidden_plane, plane_to):
            ways_out(g, 2).wait_recv()
            ways_out(g, 3).wait_recv()
            for stage in range(4):
                ways_out(g, stage).wait_send()
        for q in range(n_col):
            hop(g, 0, q).wait_send()
            hop(g, 1, q).wait_send()
            hop2(g, q).wait_send()
            if q:
                z_hop(g, q).wait_send()
    for i in range(len(partners)):
        small_hop(i).wait_send()
    wait_home(tg, tg_out, t_s, t_r, n_col)


def finish(ga, gb, small, enc_in, tg, riding, n_col, n_dp):
    parts, deep, columns = ga.shape
    wide = deep // n_col
    steps = n_dp.bit_length()
    sd, vm, dma = jax.ShapeDtypeStruct, pltpu.VMEM, pltpu.SemaphoreType.DMA
    more = max(n_dp.bit_length() - 3, 1)
    others = n_col - 1
    hidden = riding[0].shape[2]
    return pl.pallas_call(
        functools.partial(finish_kernel, n_col=n_col, n_dp=n_dp),
        in_specs=[IN_VMEM] * 5 + [ANYWHERE] * 7,
        out_specs=[IN_VMEM] * 4 + [ANYWHERE],
        out_shape=[
            sd((2, parts, wide, columns), low),
            sd((2, parts, wide, hidden), low),
            sd(small.shape[1:], f32),
            sd((enc_in.shape[0], wide), f32),
            sd((n_col * tg.shape[0], wide), low),
        ],
        scratch_shapes=[
            vm((3, deep, hidden), low),
            vm((wide, hidden), low),
            vm((others, wide, hidden), low),
            vm((n_col, wide, hidden), low),
            vm((others, wide, hidden), low),
            dma((2, 3)), dma((2,)),
            dma((others,)), dma((others,)),
            vm((2, more, 2, wide, hidden), low),
            dma((2, more)), dma((2, more)),
            dma((2, 4)), dma((2, 4)),
            vm((2, 2, deep, columns), low),
            vm((2, deep, columns), low),
            vm((2, deep, columns), low),
            vm((2, others, wide, columns), low),
            vm((2, others, wide, columns), low),
            vm((2, wide, columns), f32),
            vm((others, enc_in.shape[0], wide), low),
            vm((steps + 1,) + small.shape, f32),
            vm((steps,) + small.shape, f32),
            vm((others,) + small.shape[1:], f32),
            vm((2, more, 2, wide, columns), low),
            dma((2, 2, n_col)), dma((2, 2, n_col)),
            dma((2, n_col)), dma((2, n_col)),
            dma((2, others)), dma((2, others)),
            dma((2, 4)), dma((2, 4)),
            dma((others,)), dma((others,)),
            dma((steps,)), dma((steps,)),
            dma((others,)), dma((others,)),
            dma((n_col,)), dma((n_col,)),
            dma((2, more)), dma((2, more)),
        ],
        compiler_params=pltpu.CompilerParams(
            collective_id=20, has_side_effects=True, vmem_limit_bytes=VMEM
        ),
        name="finish",
    )(ga, gb, small, enc_in, tg, *riding)


def column_grads_kernel(*refs, pairs, firsts):
    count = len(pairs)
    firsts_refs, others = refs[:firsts], refs[firsts : firsts + count]
    out, sums = refs[firsts + count :]
    size = out.shape[2] // count
    for i, (which, begin) in enumerate(pairs):
        a, b = firsts_refs[which], others[i]
        value = mm_tn(a[pl.ds(begin, b.shape[0]), :], b[...]).astype(low)
        for p in range(out.shape[0]):
            out[p, :, i * size : (i + 1) * size] = value[:, p * size : (p + 1) * size]

    @pl.when(pl.program_id(0) == 0)
    def _():
        for i in range(count):
            sums[i : i + 1, :] = jnp.sum(others[i][...].astype(f32), axis=0, keepdims=True)


def column_grads_of(firsts, pairs, others):
    deep, width = firsts[0].shape[1], others[0].shape[1]
    block = 256
    return pl.pallas_call(
        functools.partial(column_grads_kernel, pairs=pairs, firsts=len(firsts)),
        grid=(deep // block,),
        in_specs=[pl.BlockSpec((x.shape[0], block), lambda i: (0, i)) for x in firsts]
        + [pl.BlockSpec(x.shape, lambda i: (0, 0)) for x in others],
        out_specs=[
            pl.BlockSpec((PARTS, block, width), lambda i: (0, i, 0)),
            pl.BlockSpec((8, width), lambda i: (0, 0)),
        ],
        out_shape=[
            jax.ShapeDtypeStruct((PARTS, deep, width), low),
            jax.ShapeDtypeStruct((8, width), f32),
        ],
        compiler_params=pltpu.CompilerParams(vmem_limit_bytes=VMEM),
        name="column_grads",
    )(*firsts, *others)


def unpack_kernel(sums, hidden, *outs):
    size = sums.shape[3] // 4
    for g in range(2):
        for i in range(4):
            value = sums[g, 0, :, i * size : (i + 1) * size].astype(f32)
            outs[4 * g + i][...] = value if i < 3 else jnp.transpose(value)
    outs[8][...] = hidden[0, 0].astype(f32)
    outs[9][...] = jnp.transpose(hidden[1, 0].astype(f32))


def unpack(sums, hidden):
    _, parts, wide, columns = sums.shape
    inner = hidden.shape[3]
    size = columns // 4
    into = (pl.BlockSpec((wide, size), lambda p: (0, p)), (wide, parts * size))
    out_of = (pl.BlockSpec((size, wide), lambda p: (p, 0)), (parts * size, wide))
    layouts = [into, into, into, out_of] * 2 + [
        (pl.BlockSpec((wide, inner), lambda p: (0, p)), (wide, parts * inner)),
        (pl.BlockSpec((inner, wide), lambda p: (p, 0)), (parts * inner, wide)),
    ]
    return pl.pallas_call(
        unpack_kernel,
        grid=(parts,),
        in_specs=[
            pl.BlockSpec((2, 1, wide, columns), lambda p: (0, p, 0, 0)),
            pl.BlockSpec((2, 1, wide, inner), lambda p: (0, p, 0, 0)),
        ],
        out_specs=[x[0] for x in layouts],
        out_shape=[jax.ShapeDtypeStruct(x[1], f32) for x in layouts],
        compiler_params=pltpu.CompilerParams(vmem_limit_bytes=VMEM),
        name="unpack",
    )(sums, hidden)


def build_local(mesh):
    n_dp, n_col = mesh.shape["dp"], mesh.shape["col"]

    def from_col(x, k):
        return lax.ppermute(x, "col", [(i, (i - k) % n_col) for i in range(n_col)])

    def across(x, bit):
        return lax.ppermute(x, "dp", [(i, i ^ bit) for i in range(n_dp)])

    def local(
        tokens, encoder, cotangent, dec_lengths, src_lengths,
        self_norm_gain, self_norm_bias, self_query, self_key, self_value,
        self_query_bias, self_value_bias, self_out, self_out_bias,
        cross_norm_gain, cross_norm_bias, cross_query, cross_key, cross_value,
        cross_query_bias, cross_value_bias, cross_out, cross_out_bias,
        hidden_norm_gain, hidden_norm_bias, hidden_in, hidden_in_bias,
        hidden_out, hidden_out_bias,
    ):
        row, col = lax.axis_index("row"), lax.axis_index("col")
        place = lax.axis_index("dp") % PARTS
        wide = tokens.shape[1]
        chunk = tokens.shape[0] // n_col
        span = 2 * chunk

        def in_order(parts):
            stacked = jnp.stack(parts)
            return [
                lax.dynamic_index_in_dim(stacked, i ^ place, 0, keepdims=False)
                for i in range(PARTS)
            ]

        def own_columns(w, j):
            size = w.shape[1] // PARTS
            return lax.dynamic_slice_in_dim(w, (place ^ j) * size, size, 1)

        def along_col(w):
            return [from_col(own_columns(w, 0), k) for k in range(1, n_col)]

        def whole_weight(w, parts):
            return jnp.stack(
                [jnp.concatenate([own_columns(w, j), p], axis=0) for j, p in enumerate(parts)]
            )

        vec_f = jnp.stack([
            self_norm_gain, self_norm_bias, self_out_bias, cross_norm_gain, cross_norm_bias,
            cross_out_bias, hidden_norm_gain, hidden_norm_bias, hidden_out_bias,
        ])
        vec_f = jnp.pad(vec_f, ((0, 7), (0, 0)))
        vec_c = jnp.concatenate(
            [self_query_bias, self_value_bias, cross_query_bias, cross_value_bias, hidden_in_bias]
        ).reshape(-1, 128)
        vec_c = jnp.pad(vec_c, ((0, -vec_c.shape[0] % 8), (0, 0)))
        weights = [
            self_query, self_key, self_value, self_out,
            cross_query, cross_key, cross_value, cross_out,
        ]
        x_ext, enc, vectors, columns, *full = start(tokens, encoder, vec_f, vec_c, weights, n_col)
        wq1, wk1, wv1, wo1 = full[:4]
        (gain1, shift1, out_bias1, gain2, shift2, out_bias2, gain3, shift3, out_bias3) = vectors[:9]
        size = self_query_bias.shape[0]

        def column_vector(start, size):
            return columns.reshape(n_col, -1)[:, start : start + size].reshape(-1)

        q_bias1 = column_vector(0, size)
        v_bias1 = column_vector(size, size)
        q_bias2 = column_vector(2 * size, size)
        v_bias2 = column_vector(3 * size, size)
        hidden_bias = column_vector(4 * size, hidden_in_bias.shape[0]).reshape(PARTS, -1)
        hidden_bias = jnp.stack(
            [lax.dynamic_index_in_dim(hidden_bias, place ^ j, 0) for j in range(PARTS)]
        )

        hidden_in, x_ext = lax.optimization_barrier((hidden_in, x_ext))
        hidden_out_t = hidden_out.T
        pieces1 = along_col(hidden_in)

        dec_ids = doc_numbers(dec_lengths, SEQ_LEN)[0]
        src_ids = doc_numbers(src_lengths, ENC)[0]
        padded = jnp.pad(dec_ids, (WIN, 0), constant_values=-1)
        key_ids = lax.dynamic_slice_in_dim(padded, col * span, WIN + span, 0)
        query_ids = key_ids[WIN:]

        scale = low(HEAD_DIM**-0.5)
        x0 = x_ext[1]
        a_ext = enter(x_ext, gain1, shift1, 2).reshape(WIN + span, -1)
        a = a_ext[WIN:]
        hidden_out_t, a_ext = lax.optimization_barrier((hidden_out_t, a_ext))
        pieces2 = along_col(hidden_out_t)
        q1 = (mm(a, wq1) + q_bias1).astype(low) * scale
        k1 = mm(a_ext, wk1).astype(low)
        v1 = (mm(a_ext, wv1) + v_bias1).astype(low)
        dma = pltpu.SemaphoreType.DMA
        o1, lse1, wq2, wk2, wv2, wo2 = attend(
            q1, k1, v1, query_ids, key_ids, True,
            functools.partial(cross_rider, n_col=n_col),
            weights[4:] + full[4:],
            [(x.shape, low) for x in full[:4]],
            [dma((4, 4)), dma((4, 4)), dma((4, 2))],
            14,
        )
        pieces1, o1 = lax.optimization_barrier((pieces1, o1))
        rest1 = jnp.concatenate(pieces1, axis=0)
        near1 = [across(rest1, 1), across(rest1, 2)]
        pieces2, o1 = lax.optimization_barrier((pieces2, o1))
        rest2 = jnp.concatenate(pieces2, axis=0)
        near2 = [across(rest2, 1), across(rest2, 2)]
        x1, c = junction("forward", [("nn", o1, wo1)], [x0, out_bias1, gain2, shift2], 3)

        near1, c = lax.optimization_barrier((near1, c))
        half = rest1.shape[0] // 2
        far1 = [across(near1[0][:half], 2), across(near1[1][half:], 1)]
        q2 = (mm(c, wq2) + q_bias2).astype(low) * scale
        k2 = mm(enc, wk2).astype(low)
        v2 = (mm(enc, wv2) + v_bias2).astype(low)
        o2, lse2 = attend(q2, k2, v2, query_ids, src_ids, False)
        near2, o2 = lax.optimization_barrier((near2, o2))
        far2 = [across(near2[0][:half], 2), across(near2[1][half:], 1)]
        x2, f = junction("forward", [("nn", o2, wo2)], [x1, out_bias2, gain3, shift3], 4)
        w1 = whole_weight(hidden_in, [rest1, *near1, jnp.concatenate(far1)])
        w2 = whole_weight(hidden_out_t, [rest2, *near2, jnp.concatenate(far2)])

        act, slope, rows_out, dz = hidden_forward(
            f, w1, hidden_bias, w2, x2, out_bias3, cotangent, n_col, 5
        )
        dz = dz.reshape(span, -1)

        g1, g2, hidden_bias_grad, df, got_a, got_b, layer_out = hidden_backward(
            dz, f, w1, w2, act, slope, rows_out, n_col, 11
        )
        inner = g1.shape[2]
        half = g1.shape[1] // 2
        one = ((half, inner), low)
        dx2, dyc, stats3 = junction("backward", [("sum", df)], [dz, x2, gain3], 6)

        doc = mm_nt(dyc, wo2).astype(low)
        dq2, dk2, dv2, back_a, back_b, far_a, far_b = attend_back(
            q2, k2, v2, doc, o2, lse2, query_ids, src_ids, False,
            first_rider, [g1, g2, got_a, got_b], [one] * 4,
            [
                pltpu.VMEM((4, half, inner), low), pltpu.VMEM((2, half, inner), low),
                dma((4,)), dma((4,)), dma((4,)),
            ],
            12,
        )
        cross_grads, cross_columns = column_grads_of(
            [c, enc, dyc], [(0, 0), (1, 0), (1, 0), (2, 0)], [dq2, dk2, dv2, o2]
        )
        enc_back = junction("sum", [("nt", dk2, wk2), ("nt", dv2, wv2)], [], 7)
        dx1, dy, stats2 = junction("backward", [("nt", dq2, wq2)], [dx2, x1, gain2], 8)

        do = mm_nt(dy, wo1).astype(low)
        (
            dq1, dk1, dv1, near_a, near_b, far_back_a, far_back_b, z_got, own1
        ) = attend_back(
            q1, k1, v1, do, o1, lse1, query_ids, key_ids, True,
            functools.partial(second_rider, n_col=n_col),
            [g1, g2, got_a, got_b, back_a, back_b, far_a, far_b],
            [one] * 4 + [((n_col - 1, wide, inner), low), ((wide, inner), low)],
            [
                pltpu.VMEM((4, half, inner), low), pltpu.VMEM((2, half, inner), low),
                pltpu.VMEM((3, 2 * half, inner), low), pltpu.VMEM((n_col, wide, inner), low),
                dma((4,)), dma((2, 3)), dma((4,)), dma((4,)),
                dma((n_col - 1,)), dma((n_col - 1,)), dma,
            ],
            13,
        )
        da_before = junction("sum", [("nt", dk1[:WIN], wk1), ("nt", dv1[:WIN], wv1)], [], 9)
        da_after = lax.ppermute(da_before, "col", [(i + 1, i) for i in range(n_col - 1)])
        self_grads, self_columns = column_grads_of(
            [a_ext, dy], [(0, WIN), (0, 0), (0, 0), (1, 0)], [dq1, dk1, dv1, o1]
        )
        x0_grad, stats1 = junction(
            "last",
            [("nt", dq1, wq1), ("nt", dk1[WIN:], wk1), ("nt", dv1[WIN:], wv1)],
            [dx1, x0, gain1, da_after],
            10,
        )

        feature_grads = jnp.concatenate([
            stats1[:2], stats2[2:3], stats2[:2], stats3[2:3], stats3[:2], stats3[3:4],
        ])
        feature_grads = jnp.moveaxis(feature_grads.reshape(-1, n_col, wide), 1, 0)
        column_grads = []
        for vector in (self_columns[0], self_columns[2], cross_columns[0], cross_columns[2]):
            column_grads.append(vector.reshape(n_col, -1))
        column_grads.append(
            jnp.stack(in_order([hidden_bias_grad[j] for j in range(PARTS)])).reshape(n_col, -1)
        )
        column_grads = jnp.concatenate(column_grads, axis=1).reshape(n_col, -1, 128)
        column_grads = lax.dynamic_slice_in_dim(
            jnp.concatenate([column_grads, column_grads]), col, n_col, 0
        )
        lines = -(-max(feature_grads.shape[1], column_grads.shape[1]) // 8) * 8
        small = jnp.concatenate(
            [
                jnp.pad(x, ((0, 0), (0, lines - x.shape[1]), (0, 0)))
                for x in (feature_grads, column_grads)
            ],
            axis=2,
        )
        sums, hidden_sums, small, encoder_grad, tokens_grad = finish(
            cross_grads, self_grads, small, enc_back, x0_grad,
            [g2, near_a, near_b, far_back_a, far_back_b, z_got, own1],
            n_col, n_dp,
        )
        grads = unpack(sums, hidden_sums)
        tokens_grad = tokens_grad.astype(f32)
        feature_grads = small[:, :wide]
        column_grads = small[:, wide:].reshape(-1)

        return (
            layer_out,
            tokens_grad,
            encoder_grad,
            feature_grads[0],
            feature_grads[1],
            grads[4],
            grads[5],
            grads[6],
            column_grads[:size],
            column_grads[size : 2 * size],
            grads[7],
            feature_grads[2],
            feature_grads[3],
            feature_grads[4],
            grads[0],
            grads[1],
            grads[2],
            column_grads[2 * size : 3 * size],
            column_grads[3 * size : 4 * size],
            grads[3],
            feature_grads[5],
            feature_grads[6],
            feature_grads[7],
            grads[8],
            column_grads[4 * size : 4 * size + hidden_in_bias.shape[0]],
            grads[9],
            feature_grads[8],
        )

    return local


def solution(mesh):
    rows = P(("dp", "row"), "col")
    features = P("col")
    columns = P(("row", "col"))
    into, out_of = P("col", "row"), P("row", "col")
    attention = (into, into, into, columns, columns, out_of, features)
    norm = (features, features)
    weights = (
        norm
        + attention
        + norm
        + attention
        + norm
        + (into, columns, out_of, features)
    )
    return jax.shard_map(
        build_local(mesh),
        mesh=mesh,
        in_specs=(rows, rows, rows, P("dp", None), P("dp", None)) + weights,
        out_specs=(rows, rows, rows) + weights,
        check_vma=False,
    )
```

```python
import functools

import jax
import jax.numpy as jnp
from jax import lax
from jax.experimental import pallas as pl
from jax.experimental.pallas import tpu as pltpu
from jax.sharding import PartitionSpec as P

D = 1024
HEAD_DIM = 64
SEQ_LEN = 4096
ENC = 1024
WIN = 1024

norm_epsilon = 1e-05
masked_fill = -1e30
low = jnp.bfloat16
f32 = jnp.float32
PARTS = 4
PAIR = 2 * HEAD_DIM
QUERY_ROWS = 256
VMEM = 56 * 1024 * 1024


def doc_numbers(lengths, positions):
    bounds = jnp.cumsum(lengths, axis=1, dtype=jnp.int32)
    places = jnp.arange(positions, dtype=jnp.int32)
    return jnp.sum(
        (places[None, :, None] >= bounds[:, None, :]).astype(jnp.int32), axis=2, dtype=jnp.int32
    )


def mm(a, b):
    return lax.dot_general(a, b, (((1,), (0,)), ((), ())), preferred_element_type=f32)


def mm_nt(a, b):
    return lax.dot_general(a, b, (((1,), (1,)), ((), ())), preferred_element_type=f32)


def mm_tn(a, b):
    return lax.dot_general(a, b, (((0,), (0,)), ((), ())), preferred_element_type=f32)


MESH = pl.DeviceIdType.MESH
ANYWHERE = pl.BlockSpec(memory_space=pl.ANY)
IN_VMEM = pl.BlockSpec(memory_space=pltpu.VMEM)


def here():
    return lax.axis_index("dp"), lax.axis_index("row"), lax.axis_index("col")


def meet(partners):
    barrier = pltpu.get_barrier_semaphore()
    for partner in partners:
        pl.semaphore_signal(barrier, inc=1, device_id=partner, device_id_type=MESH)
    pl.semaphore_wait(barrier, len(partners))


def remote(src, dst, sends, recvs, device):
    return pltpu.make_async_remote_copy(
        src_ref=src, dst_ref=dst, send_sem=sends, recv_sem=recvs, device_id=device,
        device_id_type=MESH,
    )


def home_hop(rows, home, sends, recvs, n_col, k):
    dp, row, col = here()
    wide, count = home.shape[1], rows.shape[0]
    to_row, at = col // 2, 2 * lax.rem(col, 2) + row
    src = rows.at[:, pl.ds(k * wide, wide)]
    dst = home.at[pl.ds(pl.multiple_of(at * count, count), count), :]
    copy = remote(src, dst, sends.at[k], recvs.at[at], (dp, to_row, lax.rem(col + k, n_col)))
    return copy, pltpu.make_async_copy(src, dst, recvs.at[at]), to_row == row


def send_home(rows, home, sends, recvs, n_col):
    for k in range(n_col):
        away, here_copy, same = home_hop(rows, home, sends, recvs, n_col, k)
        if k:
            away.start()
            continue

        @pl.when(same)
        def _():
            here_copy.start()

        @pl.when(jnp.logical_not(same))
        def _():
            away.start()


def wait_home(rows, home, sends, recvs, n_col):
    wide, count = home.shape[1], rows.shape[0]
    for k in range(n_col):
        away, _, same = home_hop(rows, home, sends, recvs, n_col, k)
        if k:
            away.wait_send()
        else:

            @pl.when(jnp.logical_not(same))
            def _():
                away.wait_send()

        src = rows.at[:, pl.ds(k * wide, wide)]
        pltpu.make_async_copy(src, home.at[pl.ds(k * count, count), :], recvs.at[k]).wait()


def plane():
    dp, row, col = here()
    flips = [dp + b - 2 * b * lax.rem(dp // b, 2) for b in (1, 2)]
    return (flips[0], row, col), (flips[1], row, col)


def head_masks():
    lane = lax.broadcasted_iota(jnp.int32, (1, PAIR), 1)
    first = jnp.where(lane < HEAD_DIM, 1.0, 0.0)
    return first.astype(low), (1.0 - first).astype(low), lane < HEAD_DIM


def attend_kernel(*refs, span, windowed, rider, n_ins, n_outs):
    refs = list(refs)
    q_ref, k_ref, v_ref, qid_ref, kid_ref = refs[:5]
    rider_refs = refs[5 : 5 + n_ins]
    refs = refs[5 + n_ins :]
    o_ref, lse_ref = refs[:2]
    rider_refs += refs[2 : 2 + n_outs]
    bias = refs[2 + n_outs]
    rider_refs += refs[3 + n_outs :]
    rows = q_ref.shape[0]
    pairs = q_ref.shape[1] // PAIR
    step = pl.program_id(0)
    if rider is not None:
        hooks = rider(*rider_refs)
        for at, hook in hooks:

            @pl.when(step == at)
            def _():
                hook()

    start = step * rows if windowed else 0
    if windowed:
        start = pl.multiple_of(start, rows)
    allowed = qid_ref[...] == kid_ref[0:1, pl.ds(start, span)]
    if windowed:
        at_row = lax.broadcasted_iota(jnp.int32, (rows, span), 0)
        at_key = lax.broadcasted_iota(jnp.int32, (rows, span), 1)
        allowed = allowed & (at_key > at_row) & (at_key <= at_row + WIN)
    bias[...] = jnp.where(allowed, 0.0, masked_fill)
    first, second, is_first = head_masks()

    def one_pair(p, carry):
        lanes = pl.ds(pl.multiple_of(p * PAIR, PAIR), PAIR)
        q2 = q_ref[:, lanes]
        k2 = k_ref[pl.ds(start, span), lanes]
        v2 = v_ref[pl.ds(start, span), lanes]
        outs, logs = [], []
        for mask in (first, second):
            s = mm_nt(q2 * mask, k2) + bias[...]
            top = jnp.max(s, axis=1, keepdims=True)
            e = jnp.exp(s - top)
            total = jnp.sum(e, axis=1, keepdims=True)
            outs.append(mm(e.astype(low), v2) / total)
            logs.append(top + jnp.log(total))
        o_ref[:, lanes] = jnp.where(is_first, outs[0], outs[1]).astype(low)
        stats = jnp.where(is_first, logs[0], logs[1])
        turned = jnp.transpose(stats)
        lse_ref[p, 0:1, :] = turned[0:1]
        lse_ref[p, 1:2, :] = turned[HEAD_DIM : HEAD_DIM + 1]
        return carry

    lax.fori_loop(0, pairs, one_pair, 0)

    if rider is not None:

        @pl.when(step == pl.num_programs(0) - 1)
        def _():
            hooks.end()


class Hooks(list):
    end = None


def attend(q, k, v, qid, kid, windowed, rider=None, riding=(), shapes=(), scratch=(), number=0):
    tokens, width = q.shape
    keys = k.shape[0]
    pairs = width // PAIR
    rows = QUERY_ROWS
    span = WIN + rows if windowed else keys
    params = dict(vmem_limit_bytes=VMEM)
    if rider is not None:
        params.update(collective_id=number, has_side_effects=True)
    return pl.pallas_call(
        functools.partial(
            attend_kernel, span=span, windowed=windowed, rider=rider, n_ins=len(riding),
            n_outs=len(shapes),
        ),
        grid=(tokens // rows,),
        in_specs=[
            pl.BlockSpec((rows, width), lambda i: (i, 0)),
            pl.BlockSpec((keys, width), lambda i: (0, 0)),
            pl.BlockSpec((keys, width), lambda i: (0, 0)),
            pl.BlockSpec((rows, 1), lambda i: (i, 0)),
            pl.BlockSpec((1, keys), lambda i: (0, 0)),
        ]
        + [pl.BlockSpec(x.shape, lambda i: (0, 0)) for x in riding],
        out_specs=[
            pl.BlockSpec((rows, width), lambda i: (i, 0)),
            pl.BlockSpec((pairs, 8, rows), lambda i: (0, 0, i)),
        ]
        + [ANYWHERE] * len(shapes),
        out_shape=[
            jax.ShapeDtypeStruct((tokens, width), low),
            jax.ShapeDtypeStruct((pairs, 8, tokens), f32),
        ]
        + [jax.ShapeDtypeStruct(*x) for x in shapes],
        scratch_shapes=[pltpu.VMEM((rows, span), f32)] + list(scratch),
        compiler_params=pltpu.CompilerParams(**params),
        name="attend",
    )(q, k, v, qid[:, None], kid[None, :], *riding)


def cotangent_rider(cot, dz, c_s, c_r, d_s, d_r, *, n_col):
    dp, row, col = here()
    wide = cot.shape[1]
    rows_here = cot.shape[0] // n_col

    def piece(j):
        to_col = 2 * row + j // 2
        k = lax.rem(col + n_col - to_col, n_col)
        src = cot.at[pl.ds(j * rows_here, rows_here), :]
        dst = dz.at[j % 2, :, pl.ds(pl.multiple_of(k * wide, wide), wide)]
        local = (row == j % 2) & (col == to_col)
        return src, dst, k, local, (dp, j % 2, to_col)

    def to_twin(k):
        ref = dz.at[row, :, pl.ds(k * wide, wide)]
        return remote(ref, ref, d_s.at[k], d_r.at[k], (dp, 1 - row, col))

    def begin():
        group = [
            (dp, r, lax.rem(col + k, n_col)) for r in (row, 1 - row) for k in range(n_col)
        ]
        meet(group[1:])
        for j in range(n_col):
            src, dst, k, local, to = piece(j)

            @pl.when(local)
            def _():
                pltpu.make_async_copy(src, dst, c_r.at[k]).start()

            @pl.when(jnp.logical_not(local))
            def _():
                remote(src, dst, c_s.at[j], c_r.at[k], to).start()

    def end():
        for k in range(n_col):
            pltpu.make_async_copy(
                cot.at[pl.ds(0, rows_here), :], dz.at[row, :, pl.ds(k * wide, wide)], c_r.at[k]
            ).wait()
            to_twin(k).start()
        for j in range(n_col):
            src, dst, k, local, to = piece(j)

            @pl.when(jnp.logical_not(local))
            def _():
                remote(src, dst, c_s.at[j], c_r.at[k], to).wait_send()

        for k in range(n_col):
            to_twin(k).wait()

    hooks = Hooks([(0, begin)])
    hooks.end = end
    return hooks


def attend_back_kernel(*refs, span, windowed, rider, n_ins, n_outs):
    refs = list(refs)
    q_ref, k_ref, v_ref, do_ref, o_ref, lse_ref, qid_ref, kid_ref = refs[:8]
    rider_refs = refs[8 : 8 + n_ins]
    refs = refs[8 + n_ins :]
    dq_ref, dk_ref, dv_ref = refs[:3]
    rider_refs += refs[3 : 3 + n_outs]
    bias, dk_sum, dv_sum = refs[3 + n_outs : 6 + n_outs]
    rider_refs += refs[6 + n_outs :]
    rows = q_ref.shape[0]
    pairs = q_ref.shape[1] // PAIR
    step = pl.program_id(0)
    start = pl.multiple_of(step * rows, rows) if windowed else 0
    keys = pl.ds(start, span)
    begin, middle, end = rider(*rider_refs)

    @pl.when(step == 0)
    def _():
        begin()
        dk_sum[...] = jnp.zeros_like(dk_sum)
        dv_sum[...] = jnp.zeros_like(dv_sum)

    allowed = kid_ref[keys, :] == qid_ref[...]
    if windowed:
        at_key = lax.broadcasted_iota(jnp.int32, (span, rows), 0)
        at_row = lax.broadcasted_iota(jnp.int32, (span, rows), 1)
        allowed = allowed & (at_key > at_row) & (at_key <= at_row + WIN)
    bias[...] = jnp.where(allowed, 0.0, masked_fill)
    first, second, is_first = head_masks()

    def one_pair(p, carry):
        lanes = pl.ds(pl.multiple_of(p * PAIR, PAIR), PAIR)
        q2 = q_ref[:, lanes]
        k2 = k_ref[keys, lanes]
        v2 = v_ref[keys, lanes]
        do2 = do_ref[:, lanes]
        turned = jnp.transpose(do2.astype(f32) * o_ref[:, lanes].astype(f32))
        dk, dv, dqs = 0.0, 0.0, []
        for h, mask in enumerate((first, second)):
            qm, dom = q2 * mask, do2 * mask
            inner = jnp.sum(turned[h * HEAD_DIM : (h + 1) * HEAD_DIM], axis=0, keepdims=True)
            s = mm_nt(k2, qm) + bias[...]
            share = jnp.exp(s - lse_ref[p, h : h + 1, :])
            ds = (share * (mm_nt(v2, dom) - inner)).astype(low)
            dv = dv + mm(share.astype(low), dom)
            dk = dk + mm(ds, qm)
            dqs.append(mm_tn(ds, k2))
        dk_sum[keys, lanes] += dk
        dv_sum[keys, lanes] += dv
        dq_ref[:, lanes] = (jnp.where(is_first, dqs[0], dqs[1]) * HEAD_DIM**-0.5).astype(low)

        @pl.when((step == 0) & (p == 0))
        def _():
            middle()

        return carry

    lax.fori_loop(0, pairs, one_pair, 0)

    @pl.when(step == pl.num_programs(0) - 1)
    def _():
        dk_ref[...] = dk_sum[...].astype(low)
        dv_ref[...] = dv_sum[...].astype(low)
        end()


def attend_back(q, k, v, do, o, lse, qid, kid, windowed, rider, riding, shapes, scratch, number):
    tokens, width = q.shape
    keys = k.shape[0]
    pairs = width // PAIR
    rows = QUERY_ROWS
    span = WIN + rows if windowed else keys
    by_row = pl.BlockSpec((rows, width), lambda i: (i, 0))
    whole = pl.BlockSpec((keys, width), lambda i: (0, 0))
    return pl.pallas_call(
        functools.partial(
            attend_back_kernel, span=span, windowed=windowed, rider=rider, n_ins=len(riding),
            n_outs=len(shapes),
        ),
        grid=(tokens // rows,),
        in_specs=[
            by_row,
            whole,
            whole,
            by_row,
            by_row,
            pl.BlockSpec((pairs, 8, rows), lambda i: (0, 0, i)),
            pl.BlockSpec((1, rows), lambda i: (0, i)),
            pl.BlockSpec((keys, 1), lambda i: (0, 0)),
        ]
        + [ANYWHERE] * len(riding),
        out_specs=[by_row, whole, whole] + [ANYWHERE] * len(shapes),
        out_shape=[
            jax.ShapeDtypeStruct((tokens, width), low),
            jax.ShapeDtypeStruct((keys, width), low),
            jax.ShapeDtypeStruct((keys, width), low),
        ]
        + [jax.ShapeDtypeStruct(*x) for x in shapes],
        scratch_shapes=[
            pltpu.VMEM((span, rows), f32),
            pltpu.VMEM((keys, width), f32),
            pltpu.VMEM((keys, width), f32),
        ]
        + scratch,
        compiler_params=pltpu.CompilerParams(
            vmem_limit_bytes=VMEM, collective_id=number, has_side_effects=True
        ),
        name="attend_back",
    )(q, k, v, do, o, lse, qid[None, :], kid[:, None], *riding)


def first_rider(
    g1, g2, got_a, got_b, back_a, back_b, far_a, far_b,
    load, mid, l_s, s_s, r_s,
):
    by_x, by_y = plane()
    half = back_a.shape[0]
    up, down = pl.ds(0, half), pl.ds(half, half)
    loads = [
        pltpu.make_async_copy(src, load.at[i], l_s.at[i])
        for i, src in enumerate((g1.at[2, up, :], got_a.at[0], g1.at[1, down, :], got_b.at[0]))
    ]
    hops = [
        remote(g2.at[3, up, :], far_a, s_s.at[0], r_s.at[0], by_x),
        remote(g2.at[3, down, :], far_b, s_s.at[1], r_s.at[1], by_y),
        remote(mid.at[0], back_a, s_s.at[2], r_s.at[2], by_y),
        remote(mid.at[1], back_b, s_s.at[3], r_s.at[3], by_x),
    ]

    def begin():
        meet([by_x, by_y])
        for copy in loads + hops[:2]:
            copy.start()

    def middle():
        for i in range(2):
            loads[2 * i].wait()
            loads[2 * i + 1].wait()
            mid[i] = (load[2 * i].astype(f32) + load[2 * i + 1].astype(f32)).astype(low)
            hops[2 + i].start()

    def end():
        for copy in hops:
            copy.wait()

    return begin, middle, end


def second_rider(
    g1, g2, got_a, got_b, back_a, back_b, far_a, far_b,
    near_a, near_b, far_back_a, far_back_b, z_got, own,
    load, mid, load_z, out_z, l_s, lz_s, s_s, r_s, z_s, z_r, o_s,
    *, n_col,
):
    dp, row, col = here()
    by_x, by_y = plane()
    half = back_a.shape[0]
    wide = own.shape[0]
    up, down = pl.ds(0, half), pl.ds(half, half)
    loads = [
        pltpu.make_async_copy(src, load.at[i], l_s.at[i])
        for i, src in enumerate((g2.at[2, up, :], far_a, g2.at[1, down, :], far_b))
    ]
    loads_z = []
    for i, (source, got, back) in enumerate(((up, got_a, back_a), (down, got_b, back_b))):
        for n, src in enumerate((g1.at[0, source, :], got.at[1], back)):
            loads_z.append(
                pltpu.make_async_copy(src, load_z.at[n, source, :], lz_s.at[i, n])
            )
    hops = [
        remote(g2.at[1, up, :], near_a, s_s.at[0], r_s.at[0], by_x),
        remote(g2.at[2, down, :], near_b, s_s.at[1], r_s.at[1], by_y),
        remote(mid.at[0], far_back_a, s_s.at[2], r_s.at[2], by_y),
        remote(mid.at[1], far_back_b, s_s.at[3], r_s.at[3], by_x),
    ]
    cols = [(dp, row, lax.rem(col + k, n_col)) for k in range(n_col)]
    over = [
        remote(out_z.at[k], z_got.at[k - 1], z_s.at[k - 1], z_r.at[k - 1], cols[k])
        for k in range(1, n_col)
    ]
    keep = pltpu.make_async_copy(out_z.at[0], own, o_s)

    def begin():
        meet([by_x, by_y] + cols[1:])
        for copy in loads + loads_z + hops[:2]:
            copy.start()

    def middle():
        for i in range(2):
            loads[2 * i].wait()
            loads[2 * i + 1].wait()
            mid[i] = (load[2 * i].astype(f32) + load[2 * i + 1].astype(f32)).astype(low)
            hops[2 + i].start()
        for copy in loads_z:
            copy.wait()
        for k in list(range(1, n_col)) + [0]:
            at = pl.ds(k * wide, wide)
            value = load_z[0, at, :].astype(f32) + load_z[1, at, :].astype(f32)
            out_z[k] = (value + load_z[2, at, :].astype(f32)).astype(low)
            if k:
                over[k - 1].start()
        keep.start()

    def end():
        for copy in hops + over + [keep]:
            copy.wait()

    return begin, middle, end


ROOT = 0.7978845608028654
CUBE = 0.044715


ORDER = (3, 1, 2, 0)


def part_numbers():
    part = lax.rem(lax.axis_index("dp"), PARTS)
    return part, part + 1 - 2 * lax.rem(part, 2), part + 2 - 4 * (part // 2), PARTS - 1 - part


def weight_copies(own, rest, j, n, to, sem):
    wide, block = own.shape[0], to.shape[1]
    inner = rest.shape[1]
    begin = pl.multiple_of(part_numbers()[j] * inner + n * block, block)
    return [
        pltpu.make_async_copy(own.at[:, pl.ds(begin, block)], to.at[pl.ds(0, wide), :], sem),
        pltpu.make_async_copy(
            rest.at[:, pl.ds(pl.multiple_of(n * block, block), block)],
            to.at[pl.ds(wide, rest.shape[0]), :],
            sem,
        ),
    ]


def hidden_kernel(*refs, numbers, opening, closing):
    count = len(numbers)
    refs = list(refs)

    def take(n):
        got, refs[:n] = refs[:n], []
        return got

    f_ref, b1_ref, own1, own2 = take(4)
    rest1, rest2 = take(count), take(count)
    if not opening:
        (sum_in,) = take(1)
    if closing:
        x_ref, bias = take(2)
    act_ref, slope_ref = take(2)
    (out_ref,) = take(1)
    total, w1, w2, w_sem = take(4)
    step, steps = pl.program_id(0), pl.num_programs(0)
    dp, row, col = here()
    twin = (dp, 1 - row, col)
    block = w1.shape[2]
    blocks = rest1[0].shape[1] // block
    slot = lax.rem(step, 2)

    def fetch(s):
        for i in range(count):

            @pl.when(s // blocks == i)
            def _():
                n = lax.rem(s, blocks)
                at = lax.rem(s, 2)
                for copy in weight_copies(
                    own1, rest1[i], numbers[i], n, w1.at[at], w_sem.at[0, at]
                ) + weight_copies(own2, rest2[i], numbers[i], n, w2.at[at], w_sem.at[1, at]):
                    copy.start()

    if closing:
        away, came, s_s, s_r = take(4)

    @pl.when(step == 0)
    def _():
        fetch(step)
        if opening:
            total[...] = jnp.zeros_like(total)
        else:
            total[...] = sum_in[...]
            if closing:
                meet([twin])

    @pl.when(step + 1 < steps)
    def _():
        fetch(step + 1)

    for i, w in enumerate((w1, w2)):
        pltpu.make_async_copy(w.at[slot], w.at[slot], w_sem.at[i, slot]).wait()

    def one_part(t, carry):
        rows = pl.ds(pl.multiple_of(t * 256, 256), 256)
        h = mm(f_ref[rows, :], w1[slot]) + b1_ref[0]
        square = h * h
        bend = jnp.tanh(h * (ROOT + (ROOT * CUBE) * square))
        half = 0.5 + 0.5 * bend
        act = (h * half).astype(low)
        act_ref[0, rows, :] = act
        slope = half + (0.5 * h) * (1.0 - bend * bend) * (ROOT + (3.0 * ROOT * CUBE) * square)
        slope_ref[0, rows, :] = slope.astype(low)
        total[rows, :] += mm_nt(act, w2[slot])
        return carry

    lax.fori_loop(0, f_ref.shape[0] // 256, one_part, 0)

    @pl.when(step == steps - 1)
    def _():
        if not closing:
            out_ref[...] = total[...]
        else:
            rows = came.shape[0]
            sent = []
            for t in range(rows // CUT):
                at = pl.ds(t * CUT, CUT)
                begin = pl.multiple_of((1 - row) * rows + t * CUT, CUT)
                away[at, :] = total[pl.ds(begin, CUT), :].astype(low)
                copy = remote(away.at[at, :], came.at[at, :], s_s.at[t], s_r.at[t], twin)
                copy.start()
                sent.append(copy)
            for t in range(rows // CUT):
                at = pl.ds(t * CUT, CUT)
                begin = pl.multiple_of(row * rows + t * CUT, CUT)
                sent[t].wait()
                branch = total[pl.ds(begin, CUT), :] + came[at, :].astype(f32)
                out_ref[at, :] = (x_ref[at, :] + (branch + bias[...])).astype(low)

def hidden_forward(f, b1, own1, own2, rest1, rest2, numbers, number, sum_in=None, x=None, bias=None):
    tokens, width = f.shape
    inner = rest1[0].shape[1]
    count = len(numbers)
    block = min(512, inner)
    blocks = inner // block
    rows = tokens // 2
    opening, closing = sum_in is None, x is not None
    dma = pltpu.SemaphoreType.DMA

    def still(shape):
        return pl.BlockSpec(shape, lambda s: (0,) * len(shape))

    active = pl.BlockSpec((1, tokens, block), lambda s: (s // blocks, 0, lax.rem(s, blocks)))
    args = [f, b1, own1, own2, *rest1, *rest2]
    in_specs = [
        still((tokens, width)),
        pl.BlockSpec((1, 1, block), lambda s: (s // blocks, 0, lax.rem(s, blocks))),
    ] + [ANYWHERE] * (2 + 2 * count)
    out_specs = [active, active]
    out_shape = [jax.ShapeDtypeStruct((count, tokens, inner), low)] * 2
    scratch = [
        pltpu.VMEM((tokens, width), f32),
        pltpu.VMEM((2, width, block), low),
        pltpu.VMEM((2, width, block), low),
        dma((2, 2)),
    ]
    if not opening:
        args.append(sum_in)
        in_specs.append(still((tokens, width)))
    if closing:
        args += [x, bias[None]]
        in_specs += [still((rows, width)), still((1, width))]
        out_shape.append(jax.ShapeDtypeStruct((rows, width), low))
        scratch += [pltpu.VMEM((rows, width), low), pltpu.VMEM((rows, width), low)]
        scratch += [dma((rows // CUT,)), dma((rows // CUT,))]
    else:
        out_shape.append(jax.ShapeDtypeStruct((tokens, width), f32))
    out_specs.append(still(out_shape[-1].shape))
    params = dict(vmem_limit_bytes=VMEM)
    if closing:
        params.update(collective_id=number, has_side_effects=True)
    return pl.pallas_call(
        functools.partial(
            hidden_kernel, numbers=numbers, opening=opening, closing=closing
        ),
        grid=(count * blocks,),
        in_specs=in_specs,
        out_specs=out_specs,
        out_shape=out_shape,
        scratch_shapes=scratch,
        compiler_params=pltpu.CompilerParams(**params),
        name="hidden_forward",
    )(*args)


def hidden_back_kernel(
    dz_ref, dzt_ref, ft_ref, rows_out, own1, own2, *refs, n_col, places,
):
    rest1, rest2 = refs[:PARTS], refs[PARTS : 2 * PARTS]
    calls = 1 + max(p[0] for p in places)
    acts, slopes = refs[2 * PARTS : 2 * PARTS + calls], refs[2 * PARTS + calls : 2 * (PARTS + calls)]
    (
        g1_ref, g2_ref, gb_ref, df_ref, got_a, got_b, home, dh_low, total, away_a, away_b, s_s,
        r_s, h_s, h_r, w1, w2, act_ref, slope_ref, w_sem,
    ) = refs[2 * (PARTS + calls) :]
    block = g1_ref.shape[2]
    inners = rest1[0].shape[1] // block
    step = pl.program_id(0)
    last = pl.num_programs(0) - 1
    order, inner = step // inners, lax.rem(step, inners)
    slot = lax.rem(step, 2)

    def fetch(s):
        for i, j in enumerate(ORDER):

            @pl.when(s // inners == i)
            def _():
                n, at = lax.rem(s, inners), lax.rem(s, 2)
                lanes = pl.ds(pl.multiple_of(n * block, block), block)
                call, index = places[j]
                copies = weight_copies(own1, rest1[j], j, n, w1.at[at], w_sem.at[0, at])
                copies += weight_copies(own2, rest2[j], j, n, w2.at[at], w_sem.at[1, at])
                for src, to, k in ((acts, act_ref, 2), (slopes, slope_ref, 3)):
                    copies.append(
                        pltpu.make_async_copy(
                            src[call].at[index, :, lanes], to.at[at], w_sem.at[k, at]
                        )
                    )
                for copy in copies:
                    copy.start()

    by_x, by_y = plane()
    half = got_a.shape[1]
    dp, row, col = here()

    @pl.when(step == 0)
    def _():
        group = [
            (dp, r, lax.rem(col + k, n_col)) for r in (row, 1 - row) for k in range(n_col)
        ]
        meet(group[1:] + [by_x, by_y])
        total[...] = jnp.zeros_like(total)
        send_home(rows_out, home, h_s, h_r, n_col)
        fetch(step)

    @pl.when(step < last)
    def _():
        fetch(step + 1)

    gb_ref[...] = jnp.zeros_like(gb_ref)
    for i, w in enumerate((w1, w2, act_ref, slope_ref)):
        pltpu.make_async_copy(w.at[slot], w.at[slot], w_sem.at[i, slot]).wait()

    def one_part(t, carry):
        rows = pl.ds(pl.multiple_of(t * 256, 256), 256)
        dh = (mm(dz_ref[rows, :], w2[slot]) * slope_ref[slot, rows, :].astype(f32)).astype(low)
        dh_low[rows, :] = dh
        gb_ref[0] += jnp.sum(dh.astype(f32), axis=0, keepdims=True)
        total[rows, :] += mm_nt(dh, w1[slot])
        return carry

    lax.fori_loop(0, dz_ref.shape[0] // 256, one_part, 0)

    def one_grad(t, carry):
        rows = pl.ds(pl.multiple_of(t * 256, 256), 256)
        g2_ref[0, rows, :] = mm(dzt_ref[rows, :], act_ref[slot]).astype(low)
        g1_ref[0, rows, :] = mm(ft_ref[rows, :], dh_low[...]).astype(low)
        return carry

    lax.fori_loop(0, ft_ref.shape[0] // 256, one_grad, 0)

    lanes = pl.ds(pl.multiple_of(inner * block, block), block)

    def hop(which, slot, n):
        away, got, to = [(away_a, got_a, by_x), (away_b, got_b, by_y)][which]
        at = pl.ds(n * block, block)
        return remote(
            away.at[slot, :, at], got.at[slot, :, at], s_s.at[which, slot, n],
            r_s.at[which, slot, n], to,
        )

    for at, which, slot in ((0, 0, 0), (0, 1, 0), (1, 0, 1), (2, 1, 1)):

        @pl.when(order == at)
        def _():
            away = (away_a, away_b)[which]
            away[slot, :, lanes] = g1_ref[0, which * half : (which + 1) * half, :]

        for n in range(got_a.shape[2] // block):

            @pl.when((order == at) & (inner == n))
            def _():
                hop(which, slot, n).start()

    @pl.when(step == last)
    def _():
        df_ref[...] = total[...].astype(low)
        for which in range(2):
            for slot in range(2):
                for n in range(got_a.shape[2] // block):
                    hop(which, slot, n).wait()
        wait_home(rows_out, home, h_s, h_r, n_col)


def hidden_backward(dz, f, own1, own2, rest1, rest2, acts, slopes, places, rows_out, n_col, number):
    tokens, width = f.shape
    inner = rest1[0].shape[1]
    block = min(512, inner)
    blocks = inner // block

    def number_of(s):
        j = s // blocks
        return jnp.where(j == 0, PARTS - 1, jnp.where(j == PARTS - 1, 0, j))

    def still(shape):
        return pl.BlockSpec(shape, lambda s: (0,) * len(shape))

    weight = pl.BlockSpec((1, width, block), lambda s: (number_of(s), 0, lax.rem(s, blocks)))
    landing = jax.ShapeDtypeStruct((2, width // 2, inner), low)
    grad = jax.ShapeDtypeStruct((PARTS, width, inner), low)
    vm, dma = pltpu.VMEM, pltpu.SemaphoreType.DMA
    return pl.pallas_call(
        functools.partial(hidden_back_kernel, n_col=n_col, places=places),
        grid=(PARTS * blocks,),
        in_specs=[still((tokens, width)), still((width, tokens)), still((width, tokens))]
        + [still(rows_out.shape)]
        + [ANYWHERE] * (2 + 2 * PARTS + 2 * len(acts)),
        out_specs=[
            weight,
            weight,
            pl.BlockSpec((1, 1, block), lambda s: (number_of(s), 0, lax.rem(s, blocks))),
            still((tokens, width)),
            ANYWHERE, ANYWHERE, ANYWHERE,
        ],
        out_shape=[
            grad,
            grad,
            jax.ShapeDtypeStruct((PARTS, 1, inner), f32),
            jax.ShapeDtypeStruct((tokens, width), low),
            landing,
            landing,
            jax.ShapeDtypeStruct((n_col * rows_out.shape[0], width // n_col), low),
        ],
        scratch_shapes=[
            vm((tokens, block), low),
            vm((tokens, width), f32),
            vm(landing.shape, low),
            vm(landing.shape, low),
            dma((2, 2, blocks)),
            dma((2, 2, blocks)),
            dma((n_col,)),
            dma((n_col,)),
            vm((2, width, block), low),
            vm((2, width, block), low),
            vm((2, tokens, block), low),
            vm((2, tokens, block), low),
            dma((4, 2)),
        ],
        compiler_params=pltpu.CompilerParams(
            vmem_limit_bytes=VMEM, collective_id=number, has_side_effects=True
        ),
        name="hidden_backward",
    )(dz, dz.T, f.T, rows_out, own1, own2, *rest1, *rest2, *acts, *slopes)


def start_kernel(
    tokens, encoder, vec_f, vec_c, *refs, n_col,
):
    weights, (x_ext, enc, all_f, all_c), full = refs[:8], refs[8:12], refs[12:20]
    (zeros, w_send, w_recv, w_own, t_send, t_recv, v_send, v_recv, z_sem, z_send, z_recv, e_send,
     e_recv, o_sem) = refs[20:]
    dp, row, col = here()
    part = lax.rem(dp, PARTS)
    twin = (dp, 1 - row, col)
    flip = [
        dp + 1 - 2 * lax.rem(dp, 2),
        dp + 2 - 4 * lax.rem(dp // 2, 2),
    ]
    by_x, by_y = (flip[0], row, col), (flip[1], row, col)
    part_x, part_y = lax.rem(flip[0], PARTS), lax.rem(flip[1], PARTS)
    shift = [lax.rem(col + k, n_col) for k in range(n_col)]
    group = [(dp, r, c) for r in (row, 1 - row) for c in shift][1:]
    meet(group + [by_x, by_y])

    wide = tokens.shape[1]
    deep = n_col * wide
    rest = deep - wide

    def chunk(index, size):
        return pl.ds(pl.multiple_of(index * size, size), size)

    to_right, to_left = (dp, row, lax.rem(col + 1, n_col)), (dp, row, lax.rem(col + n_col - 1, n_col))

    def weight_chunk(i, k):
        w = weights[i]
        if i % 4 < 3:
            return full[i].at[pl.ds(k * wide, wide), chunk(part, w.shape[1] // PARTS)]
        return full[i].at[chunk(part, w.shape[0] // PARTS), pl.ds(k * wide, wide)]

    def weight_slice(i):
        w = weights[i]
        if i % 4 < 3:
            return w.at[:, chunk(part, w.shape[1] // PARTS)]
        return w.at[chunk(part, w.shape[0] // PARTS), :]

    def enc_chunk(k):
        return enc.at[chunk(row, encoder.shape[0]), pl.ds(k * wide, wide)]

    def piece(i, k):
        if i == 8:
            return enc_chunk(k)
        return weight_chunk(i, k)

    def own_piece(i):
        return encoder if i == 8 else weight_slice(i)

    def enc_twin(k):
        return remote(own_piece(8) if k == 0 else enc_chunk(k), enc_chunk(k), e_send.at[k],
                      e_recv.at[k], twin)

    def rightward(i, h):
        src = own_piece(i) if h == 1 else piece(i, n_col + 1 - h)
        k = n_col - h
        return remote(src, piece(i, k), z_send.at[i, 0, h - 1], z_recv.at[i, k - 1], to_right)

    def leftward(i, h):
        src = own_piece(i) if h == 1 else piece(i, h - 1)
        return remote(src, piece(i, h), z_send.at[i, 1, h - 1], z_recv.at[i, h - 1], to_left)

    def right_valid(h):
        return (col >= h - 1) & (col < n_col - 1)

    def left_valid(h):
        return (col <= n_col - h) & (col > 0)

    def send_along(i, h):
        @pl.when(right_valid(h))
        def _():
            rightward(i, h).start()

        @pl.when(left_valid(h))
        def _():
            leftward(i, h).start()

    def take(i, h):
        @pl.when(col >= h)
        def _():
            rightward(i, h).wait_recv()

        @pl.when(col < n_col - h)
        def _():
            leftward(i, h).wait_recv()

    def weight_own(i):
        w = weights[i]
        place = full[i].at[pl.ds(0, wide), :] if i % 4 < 3 else full[i].at[:, pl.ds(0, wide)]
        return pltpu.make_async_copy(w, place, w_own.at[i])

    def weight_part(i, which, begin, size):
        if i % 4 < 3:
            return full[i].at[pl.ds(begin, size), chunk(which, weights[i].shape[1] // PARTS)]
        return full[i].at[chunk(which, weights[i].shape[0] // PARTS), pl.ds(begin, size)]

    def weight_plane(i, stage):
        half = rest // 2
        which, begin, size, to = [
            (part, wide, rest, by_x),
            (part, wide, rest, by_y),
            (part_x, wide, half, by_y),
            (part_y, wide + half, half, by_x),
        ][stage]
        ref = weight_part(i, which, begin, size)
        return remote(ref, ref, w_send.at[i, stage], w_recv.at[i, stage], to)

    def token_piece(j, slot):
        rows = tokens.shape[0] // n_col
        to_col = 2 * row + j // 2 + (1 - slot)
        k = lax.rem(col + n_col - lax.rem(to_col, n_col), n_col)
        src = tokens.at[pl.ds(j * rows, rows), :]
        dst = x_ext.at[slot, :, chunk(k, wide)]
        local = (row == j % 2) & (col == to_col)
        valid = to_col < n_col
        return src, dst, k, local, valid, (dp, j % 2, to_col)

    def send_tokens(slot):
        for j in range(n_col):
            src, dst, k, local, valid, to = token_piece(j, slot)

            @pl.when(valid & local)
            def _():
                pltpu.make_async_copy(src, dst, t_recv.at[slot, k]).start()

            @pl.when(valid & jnp.logical_not(local))
            def _():
                remote(src, dst, t_send.at[slot, j], t_recv.at[slot, k], to).start()

    def vectors(k):
        to = (dp, row, lax.rem(col + n_col - k, n_col))
        return [
            remote(vec_f, all_f.at[:, pl.ds(k * wide, wide)], v_send.at[0, k], v_recv.at[0, k], to),
            remote(vec_c, all_c.at[col], v_send.at[1, k], v_recv.at[1, k], to),
        ]

    own_vectors = [
        pltpu.make_async_copy(encoder, enc_chunk(0), o_sem),
        pltpu.make_async_copy(vec_f, all_f.at[:, pl.ds(0, wide)], v_recv.at[0, 0]),
        pltpu.make_async_copy(vec_c, all_c.at[col], v_recv.at[1, 0]),
    ]
    ks = range(1, n_col)
    for i in range(8):
        send_along(i, 1)
    for k in ks:
        for copy in vectors(k):
            copy.start()
    for i in range(8):
        weight_own(i).start()
    for copy in own_vectors:
        copy.start()
    enc_twin(0).start()
    for h in (1, 2):
        for i in range(8):
            take(i, h)
            send_along(i, h + 1)
    send_along(8, 1)
    send_tokens(1)
    for i in range(8):
        take(i, 3)
        weight_plane(i, 0).start()
        weight_plane(i, 1).start()
    take(8, 1)
    send_along(8, 2)
    send_tokens(0)

    @pl.when(col == 0)
    def _():
        zeros[...] = jnp.zeros_like(zeros)
        clear = pltpu.make_async_copy(zeros, x_ext.at[0], z_sem)
        clear.start()
        clear.wait()

    for i in range(8):
        weight_plane(i, 0).wait_recv()
        weight_plane(i, 2).start()
        weight_plane(i, 1).wait_recv()
        weight_plane(i, 3).start()
        if i == 3:
            take(8, 2)
            send_along(8, 3)
    take(8, 3)
    for k in ks:
        enc_twin(k).start()
    for i in range(8):
        weight_plane(i, 2).wait_recv()
        weight_plane(i, 3).wait_recv()
        weight_own(i).wait()
        for stage in range(4):
            weight_plane(i, stage).wait_send()
    for k in range(n_col):
        enc_twin(k).wait()
    for i in range(9):
        for h in ks:

            @pl.when(right_valid(h))
            def _():
                rightward(i, h).wait_send()

            @pl.when(left_valid(h))
            def _():
                leftward(i, h).wait_send()

    for copy in own_vectors:
        copy.wait()
    for k in ks:
        for copy in vectors(k):
            copy.wait()
    for slot in (1, 0):
        for j in range(n_col):
            src, dst, k, local, valid, to = token_piece(j, slot)

            @pl.when(valid & jnp.logical_not(local))
            def _():
                remote(src, dst, t_send.at[slot, j], t_recv.at[slot, k], to).wait_send()

        for k in range(n_col):
            rows = tokens.shape[0] // n_col
            came = pltpu.make_async_copy(
                tokens.at[pl.ds(0, rows), :],
                x_ext.at[slot, :, pl.ds(k * wide, wide)],
                t_recv.at[slot, k],
            )
            if slot == 1:
                came.wait()
            else:

                @pl.when(col > 0)
                def _():
                    came.wait()


def start(tokens, encoder, vec_f, vec_c, weights, n_col):
    wide = tokens.shape[1]
    deep = n_col * wide
    rows = tokens.shape[0] // n_col
    shapes = [
        jax.ShapeDtypeStruct((2, rows, deep), low),
        jax.ShapeDtypeStruct((2 * encoder.shape[0], deep), low),
        jax.ShapeDtypeStruct((vec_f.shape[0], deep), f32),
        jax.ShapeDtypeStruct((n_col,) + vec_c.shape, f32),
    ]
    for i, w in enumerate(weights):
        shapes.append(
            jax.ShapeDtypeStruct((deep, w.shape[1]) if i % 4 < 3 else (w.shape[0], deep), low)
        )
    dma = pltpu.SemaphoreType.DMA
    return pl.pallas_call(
        functools.partial(start_kernel, n_col=n_col),
        in_specs=[IN_VMEM] * 12,
        out_specs=[ANYWHERE] * 12,
        out_shape=shapes,
        scratch_shapes=[
            pltpu.VMEM((rows, deep), low),
            dma((8, 4)), dma((8, 4)), dma((8,)),
            dma((2, n_col)), dma((2, n_col)),
            dma((2, n_col)), dma((2, n_col)),
            dma, dma((9, 2, n_col - 1)), dma((9, n_col - 1)), dma((n_col,)), dma((n_col,)), dma,
        ],
        compiler_params=pltpu.CompilerParams(
            collective_id=1, has_side_effects=True, vmem_limit_bytes=VMEM
        ),
        name="start",
    )(tokens, encoder, vec_f, vec_c, *weights)


def norm_rows(x):
    center = jnp.mean(x, axis=1, keepdims=True)
    spread = jnp.mean(x * x, axis=1, keepdims=True) - center * center
    scaling = lax.rsqrt(spread + norm_epsilon)
    return (x - center) * scaling, scaling


CUT = 256


def enter_kernel(x_ref, gain, shift, a_ref, sends, recvs):
    dp, row, col = here()
    twin = (dp, 1 - row, col)
    meet([twin])
    slots, rows = x_ref.shape[:2]

    def place(slot):
        return a_ref.at[slot, pl.ds(pl.multiple_of(row * rows, rows), rows), :]

    copies = []
    for slot in reversed(range(slots)):
        for t in range(rows // CUT):
            normed, _ = norm_rows(x_ref[slot, pl.ds(t * CUT, CUT), :].astype(f32))
            begin = pl.multiple_of(row * rows + t * CUT, CUT)
            a_ref[slot, pl.ds(begin, CUT), :] = (normed * gain[...] + shift[...]).astype(low)
        copy = remote(place(slot), place(slot), sends.at[slot], recvs.at[slot], twin)
        copy.start()
        copies.append(copy)
    for copy in copies:
        copy.wait()


def enter(x_ext, gain, shift, number):
    slots, rows, deep = x_ext.shape
    return pl.pallas_call(
        enter_kernel,
        in_specs=[IN_VMEM] * 3,
        out_specs=IN_VMEM,
        out_shape=jax.ShapeDtypeStruct((slots, 2 * rows, deep), low),
        scratch_shapes=[pltpu.SemaphoreType.DMA((slots,)), pltpu.SemaphoreType.DMA((slots,))],
        compiler_params=pltpu.CompilerParams(
            collective_id=number, has_side_effects=True, vmem_limit_bytes=VMEM
        ),
        name="enter",
    )(x_ext, gain[None], shift[None])


def junction_kernel(*refs, kinds, mode):
    dp, row, col = here()
    twin = (dp, 1 - row, col)
    meet([twin])
    refs = list(refs)
    sources = []
    for kind in kinds:
        sources.append((kind, refs.pop(0), refs.pop(0) if kind != "sum" else None))
    if mode == "forward":
        x_ref, bias, gain, shift, x_out, full, away, came, s1, r1, s2, r2 = refs
    elif mode == "backward":
        res_ref, x_ref, gain, dx_out, full, stats, away, came, s1, r1, s2, r2 = refs
    else:
        out, away, came, s1, r1 = refs
    rows = came.shape[0]
    cuts = rows // CUT

    def partial(begin):
        total = None
        for kind, g, w in sources:
            part = g[pl.ds(begin, CUT), :]
            if kind == "sum":
                part = part.astype(f32)
            elif kind == "nt":
                part = mm_nt(part, w[...])
            else:
                part = mm(part, w[...])
            total = part if total is None else total + part
        return total

    sent = []
    for t in range(cuts):
        at = pl.ds(t * CUT, CUT)
        away[at, :] = partial(pl.multiple_of((1 - row) * rows + t * CUT, CUT)).astype(low)
        copy = remote(away.at[at, :], came.at[at, :], s1.at[t], r1.at[t], twin)
        copy.start()
        sent.append(copy)
    gathered = []
    sums = [0.0] * 4
    for t in range(cuts):
        at = pl.ds(t * CUT, CUT)
        begin = pl.multiple_of(row * rows + t * CUT, CUT)
        own = partial(begin)
        sent[t].wait_recv()
        total = own + came[at, :].astype(f32)
        if mode == "sum":
            out[at, :] = total.astype(low)
            continue
        if mode == "forward":
            x = x_ref[at, :].astype(f32) + (total + bias[...])
            x_out[at, :] = x
            normed, _ = norm_rows(x)
            result = (normed * gain[...] + shift[...]).astype(low)
        else:
            normed, scaling = norm_rows(x_ref[at, :].astype(f32))
            upstream = total * gain[...]
            mean_up = jnp.mean(upstream, axis=1, keepdims=True)
            mean_both = jnp.mean(upstream * normed, axis=1, keepdims=True)
            res = res_ref[at if res_ref.shape[0] == rows else pl.ds(begin, CUT), :].astype(f32)
            dx = res + scaling * (upstream - mean_up - normed * mean_both)
            dx_out[at, :] = dx.astype(dx_out.dtype)
            result = dx.astype(low)
            for i, value in enumerate((total * normed, total, result.astype(f32), res)):
                sums[i] = sums[i] + jnp.sum(value, axis=0, keepdims=True)
        full[pl.ds(begin, CUT), :] = result
        place = full.at[pl.ds(begin, CUT), :]
        copy = remote(place, place, s2.at[t], r2.at[t], twin)
        copy.start()
        gathered.append(copy)
    if mode == "backward":
        for i in range(4):
            stats[i : i + 1, :] = sums[i]
    for copy in sent:
        copy.wait_send()
    for copy in gathered:
        copy.wait()


def junction(mode, sources, others, number):
    kinds = [x[0] for x in sources]
    first = sources[0]
    tokens = first[1].shape[0]
    deep = first[1].shape[1]
    if first[0] != "sum":
        deep = first[2].shape[0 if first[0] == "nt" else 1]
    rows = tokens // 2
    flat = [x for source in sources for x in source[1:]]
    dma = pltpu.SemaphoreType.DMA((rows // CUT,))
    wide_rows = jax.ShapeDtypeStruct((rows, deep), f32)
    every = jax.ShapeDtypeStruct((tokens, deep), low)
    shapes = {
        "forward": [wide_rows, every],
        "backward": [wide_rows, every, jax.ShapeDtypeStruct((8, deep), f32)],
        "sum": [jax.ShapeDtypeStruct((rows, deep), low)],
    }[mode]
    scratch = [pltpu.VMEM((rows, deep), low), pltpu.VMEM((rows, deep), low), dma, dma]
    if mode in ("forward", "backward"):
        scratch += [dma, dma]
    args = flat + [x[None] if x.ndim == 1 else x for x in others]
    out = pl.pallas_call(
        functools.partial(junction_kernel, kinds=kinds, mode=mode),
        in_specs=[IN_VMEM] * len(args),
        out_specs=[IN_VMEM] * len(shapes),
        out_shape=shapes,
        scratch_shapes=scratch,
        compiler_params=pltpu.CompilerParams(
            collective_id=number, has_side_effects=True, vmem_limit_bytes=VMEM
        ),
        name="junction_" + mode,
    )(*args)
    return out if len(out) > 1 else out[0]


def plane_copies(full, part, parts, by_x, by_y, sends, recvs):
    size = full.shape[1]
    half = size // 2

    def copy(stage):
        which, begin, count, to = [
            (part, 0, size, by_x), (part, 0, size, by_y),
            (parts[1], 0, half, by_y), (parts[2], half, half, by_x),
        ][stage]
        ref = full.at[which, pl.ds(begin, count), :]
        return remote(ref, ref, sends.at[stage], recvs.at[stage], to)

    return copy


class LineSum:
    def __init__(self, buf, in_l, in_r, sends, recvs, cols):
        self.buf, self.in_l, self.in_r, self.sends, self.recvs = buf, in_l, in_r, sends, recvs
        self.cols, self.n, self.col = cols, len(cols), lax.axis_index("col")

    def right(self, d):
        return remote(
            self.buf.at[d - 1], self.in_l.at[d - 1], self.sends.at[0, d - 1],
            self.recvs.at[0, d - 1], self.cols[1],
        )

    def left(self, d):
        return remote(
            self.buf.at[self.n - d - 1], self.in_r.at[d - 1], self.sends.at[1, d - 1],
            self.recvs.at[1, d - 1], self.cols[self.n - 1],
        )

    def add(self, k, got):
        self.buf[k - 1] = (self.buf[k - 1].astype(f32) + got.astype(f32)).astype(low)

    def begin(self):
        @pl.when(self.col == 0)
        def _():
            self.in_l[0] = jnp.zeros(self.in_l.shape[1:], low)
            for d in range(self.n - 1, 0, -1):
                self.right(d).start()

        @pl.when(self.col == self.n - 1)
        def _():
            self.in_r[0] = jnp.zeros(self.in_r.shape[1:], low)
            for d in range(self.n - 1, 0, -1):
                self.left(d).start()

    def go(self, d):
        @pl.when((self.col > 0) & (self.col <= self.n - 1 - d))
        def _():
            self.right(d + 1).wait_recv()
            self.add(d, self.in_l[d])
            self.right(d).start()

        @pl.when((self.col < self.n - 1) & (self.col >= d))
        def _():
            self.left(d + 1).wait_recv()
            self.add(self.n - d, self.in_r[d])
            self.left(d).start()

    def total(self, value):
        @pl.when(self.col > 0)
        def _():
            self.right(1).wait_recv()

        @pl.when(self.col < self.n - 1)
        def _():
            self.left(1).wait_recv()

        return value + self.in_l[0].astype(f32) + self.in_r[0].astype(f32)

    def end(self):
        for d in range(1, self.n):

            @pl.when(self.col <= self.n - 1 - d)
            def _():
                self.right(d).wait_send()

            @pl.when(self.col >= d)
            def _():
                self.left(d).wait_send()


def with_other_bits(value, store, which, sends, recvs, partners):
    for i, partner in enumerate(partners):
        store[i, 0] = value.astype(low)
        copy = remote(
            store.at[i, 0], store.at[i, 1 + which], sends.at[which, i], recvs.at[which, i], partner
        )
        copy.start()
        copy.wait()
        value = value + store[i, 1 + which].astype(f32)
    return value


def bit_partners(n_dp):
    dp, row, col = here()
    bits = [1 << b for b in range(n_dp.bit_length() - 1)]
    return [(dp + b - 2 * b * lax.rem(dp // b, 2), row, col) for b in bits]


def fold_kernel(
    dq, dk, dv, a_ext, dy, o, wq, wk, wv, res, x0, gain, ga,
    g2, near_a, near_b, far_back_a, far_back_b, z_got, own1,
    gb, sums, tg, stats, a_sum, hidden0, q_own,
    load, load_own, load_got, h_out, h_l, h_r, first, second, mid, away_b, came_b, away_l, came_l,
    da_got, extra,
    l_s, lo_s, hz_s, hz_r, f_s, f_r, m_s, m_r, b_s, b_r, c_s, c_r, d_s, d_r, g_s, g_r, x_s, x_r,
    *, n_col, n_dp,
):
    dp, row, col = here()
    parts = part_numbers()
    part = parts[0]
    by_bit = bit_partners(n_dp)
    by_x, by_y = by_bit[:2]
    twin = (dp, 1 - row, col)
    cols = [(dp, row, lax.rem(col + k, n_col)) for k in range(n_col)]
    left = cols[n_col - 1]
    meet([twin] + by_bit + cols[1:])
    ks = range(1, n_col)
    deep = tg.shape[1]
    wide = deep // n_col
    half = near_a.shape[0]
    rows = tg.shape[0]
    cuts = rows // CUT
    window = dk.shape[0] - dq.shape[0]

    def at(q):
        return pl.ds(q * wide, wide)

    loads = []
    for i, sources in enumerate(((near_a, far_back_a), (near_b, far_back_b))):
        spot = pl.ds(i * half, half)
        for n, src in enumerate((g2.at[0, spot, :],) + sources):
            loads.append(pltpu.make_async_copy(src, load.at[n, spot, :], l_s.at[i, n]))
    loads_own = [
        pltpu.make_async_copy(own1, load_own, lo_s.at[0]),
        pltpu.make_async_copy(z_got, load_got, lo_s.at[1]),
    ]

    def hop(which, q):
        source = ga.at[parts[3] if which else parts[1], at(q), :]
        return remote(source, first.at[which, at(q), :], f_s.at[which, q], f_r.at[which, q], by_x)

    def hop2(q):
        return remote(mid.at[at(q), :], second.at[at(q), :], m_s.at[q], m_r.at[q], by_y)

    line = LineSum(h_out, h_l, h_r, hz_s, hz_r, cols)

    def hidden_total(k):
        value = load[0, at(k), :].astype(f32) + load[1, at(k), :].astype(f32)
        return value + load[2, at(k), :].astype(f32)

    for copy in loads + loads_own:
        copy.start()
    for which in (1, 0):
        for q in range(n_col):
            hop(which, q).start()

    for copy in loads:
        copy.wait()
    for k in ks:
        h_out[k - 1] = hidden_total(k).astype(low)
    line.begin()

    def before(begin):
        spot = pl.ds(begin, CUT)
        return mm_nt(dk[spot, :], wk[...]) + mm_nt(dv[spot, :], wv[...])

    def exchange(away, came, sends, recvs, t):
        spot = pl.ds(t * CUT, CUT)
        return remote(away.at[spot, :], came.at[spot, :], sends.at[t], recvs.at[t], twin)

    for t in range(cuts):
        spot = pl.ds(t * CUT, CUT)
        away_b[spot, :] = before(pl.multiple_of((1 - row) * rows + t * CUT, CUT)).astype(low)
        exchange(away_b, came_b, b_s, b_r, t).start()
    for t in range(cuts):
        spot = pl.ds(t * CUT, CUT)
        own = before(pl.multiple_of(row * rows + t * CUT, CUT))
        exchange(away_b, came_b, b_s, b_r, t).wait_recv()
        came_b[spot, :] = (own + came_b[spot, :].astype(f32)).astype(low)
    da_hop = remote(came_b, da_got, d_s, d_r, left)

    @pl.when(col > 0)
    def _():
        da_hop.start()

    @pl.when(col == n_col - 1)
    def _():
        da_got[...] = jnp.zeros_like(da_got)

    for q in range(n_col):
        hop(1, q).wait_recv()
        value = ga[parts[2], at(q), :].astype(f32) + first[1, at(q), :].astype(f32)
        mid[at(q), :] = value.astype(low)
        hop2(q).start()
    for copy in loads_own:
        copy.wait()
    value = load_own[...].astype(f32)
    for k in ks:
        value = value + load_got[k - 1].astype(f32)
    value = with_other_bits(value, extra, 0, x_s, x_r, by_bit[2:])
    hidden0[part] = value.astype(low)
    spread = plane_copies(hidden0, part, parts, by_x, by_y, g_s, g_r)
    spread(0).start()
    spread(1).start()

    line.go(2)

    def last(begin):
        spot = pl.ds(begin, CUT)
        later = pl.ds(window + begin, CUT)
        value = mm_nt(dq[spot, :], wq[...]) + mm_nt(dk[later, :], wk[...])
        return value + mm_nt(dv[later, :], wv[...])

    for t in range(cuts):
        spot = pl.ds(t * CUT, CUT)
        away_l[spot, :] = last(pl.multiple_of((1 - row) * rows + t * CUT, CUT)).astype(low)
        exchange(away_l, came_l, c_s, c_r, t).start()

    size = gb.shape[2] // 4
    pairs = ((window, dq), (0, dk), (0, dv), (None, o))

    def one_block(i, carry):
        lanes = pl.ds(pl.multiple_of(i * wide, wide), wide)
        for n, (begin, other) in enumerate(pairs):
            source = dy[:, lanes] if begin is None else a_ext[pl.ds(begin, other.shape[0]), lanes]
            value = mm_tn(source, other[...]).astype(low)
            for p in range(PARTS):
                gb[p, lanes, n * size : (n + 1) * size] = value[:, p * size : (p + 1) * size]
        return carry

    lax.fori_loop(0, n_col, one_block, 0)
    line.go(1)
    for n, (_, other) in enumerate(pairs):
        sums[n : n + 1, :] = jnp.sum(other[...].astype(f32), axis=0, keepdims=True)

    @pl.when(col < n_col - 1)
    def _():
        da_hop.wait_recv()

    totals = [0.0, 0.0]
    for t in range(cuts):
        spot = pl.ds(t * CUT, CUT)
        own = last(pl.multiple_of(row * rows + t * CUT, CUT))
        exchange(away_l, came_l, c_s, c_r, t).wait_recv()
        total = own + came_l[spot, :].astype(f32)
        after = [da_got[spot, pl.ds(deep - wide, wide)], da_got[spot, pl.ds(0, deep - wide)]]
        total = total + jnp.concatenate(after, axis=1).astype(f32)
        normed, scaling = norm_rows(x0[spot, :].astype(f32))
        upstream = total * gain[...]
        mean_up = jnp.mean(upstream, axis=1, keepdims=True)
        mean_both = jnp.mean(upstream * normed, axis=1, keepdims=True)
        dx = res[spot, :] + scaling * (upstream - mean_up - normed * mean_both)
        tg[spot, :] = dx.astype(low)
        for i, value in enumerate((total * normed, total)):
            totals[i] = totals[i] + jnp.sum(value, axis=0, keepdims=True)
    for i in range(2):
        stats[i : i + 1, :] = totals[i]
    for stage in range(2):
        spread(stage).wait_recv()
        spread(2 + stage).start()
    for q in range(n_col):
        hop(0, q).wait_recv()
        hop2(q).wait_recv()
        value = ga[part, at(q), :].astype(f32) + first[0, at(q), :].astype(f32)
        a_sum[at(q), :] = (value + second[at(q), :].astype(f32)).astype(low)
    value = line.total(hidden_total(0))
    value = with_other_bits(value, extra, 1, x_s, x_r, by_bit[2:])
    q_own[...] = value.astype(low)
    spread(2).wait_recv()
    spread(3).wait_recv()
    for stage in range(4):
        spread(stage).wait_send()
    line.end()
    for q in range(n_col):
        hop(0, q).wait_send()
        hop(1, q).wait_send()
        hop2(q).wait_send()
    for t in range(cuts):
        exchange(away_b, came_b, b_s, b_r, t).wait_send()
        exchange(away_l, came_l, c_s, c_r, t).wait_send()

    @pl.when(col > 0)
    def _():
        da_hop.wait_send()


def fold(dq, dk, dv, a_ext, dy, o, weights, res, x0, gain, ga, riding, n_col, n_dp):
    sd, vm, dma = jax.ShapeDtypeStruct, pltpu.VMEM, pltpu.SemaphoreType.DMA
    rows, deep = x0.shape
    wide = deep // n_col
    columns, hidden = ga.shape[2], riding[0].shape[2]
    others, cuts = n_col - 1, rows // CUT
    more = max(n_dp.bit_length() - 3, 1)
    by_rows = vm((rows, deep), low)
    return pl.pallas_call(
        functools.partial(fold_kernel, n_col=n_col, n_dp=n_dp),
        in_specs=[IN_VMEM] * 13 + [ANYWHERE] * 7,
        out_specs=[IN_VMEM] * 7,
        out_shape=[
            sd(ga.shape, low),
            sd((8, dq.shape[1]), f32),
            sd((rows, deep), low),
            sd((8, deep), f32),
            sd((deep, columns), low),
            sd((PARTS, wide, hidden), low),
            sd((wide, hidden), low),
        ],
        scratch_shapes=[
            vm((3, deep, hidden), low),
            vm((wide, hidden), low),
            vm((others, wide, hidden), low),
            vm((others, wide, hidden), low),
            vm((others, wide, hidden), low),
            vm((others, wide, hidden), low),
            vm((2, deep, columns), low),
            vm((deep, columns), low),
            vm((deep, columns), low),
            by_rows, by_rows, by_rows, by_rows, by_rows,
            vm((more, 3, wide, hidden), low),
            dma((2, 3)), dma((2,)),
            dma((2, others)), dma((2, others)),
            dma((2, n_col)), dma((2, n_col)),
            dma((n_col,)), dma((n_col,)),
            dma((cuts,)), dma((cuts,)), dma((cuts,)), dma((cuts,)),
            dma, dma,
            dma((4,)), dma((4,)),
            dma((2, more)), dma((2, more)),
        ],
        compiler_params=pltpu.CompilerParams(
            collective_id=21, has_side_effects=True, vmem_limit_bytes=60 * 1024 * 1024
        ),
        name="fold",
    )(dq, dk, dv, a_ext, dy, o, *weights, res, x0, gain[None], ga, *riding)


def finish_kernel(
    gb, a_sum, q_own, small, enc_in, tg,
    full_a, full_b, hidden1, small_out, enc_out, tg_out,
    first, second, mid, za, za_l, za_r, zb, zb_l, zb_r, enc_got, s_cur, s_got, s_z, extra,
    f_s, f_r, m_s, m_r, za_s, za_t, zb_s, zb_t, g_s, g_r, e_s, e_r, s_s, s_r, sz_s, sz_r, t_s, t_r, x_s, x_r,
    *, n_col, n_dp,
):
    dp, row, col = here()
    parts = part_numbers()
    part = parts[0]
    by_bit = bit_partners(n_dp)
    by_x, by_y = by_bit[:2]
    twin = (dp, 1 - row, col)
    cols = [(dp, row, lax.rem(col + k, n_col)) for k in range(n_col)]
    meet([twin] + [(dp, 1 - row, c[2]) for c in cols[1:]] + cols[1:] + by_bit)
    wide = gb.shape[1] // n_col
    ks = range(1, n_col)

    def rows(q):
        return pl.ds(q * wide, wide)

    def hop(which, q):
        to, side = (by_y, 2) if 2 * q < n_col else (by_x, 1)
        source = gb.at[parts[3] if which else parts[side], rows(q), :]
        return remote(source, first.at[which, rows(q), :], f_s.at[which, q], f_r.at[which, q], to)

    def hop2(q):
        to = by_x if 2 * q < n_col else by_y
        return remote(mid.at[rows(q), :], second.at[rows(q), :], m_s.at[q], m_r.at[q], to)

    turns = [q for pair in zip(range(n_col // 2), range(n_col // 2, n_col)) for q in pair]

    line_a = LineSum(za, za_l, za_r, za_s, za_t, cols)
    line_b = LineSum(zb, zb_l, zb_r, zb_s, zb_t, cols)

    def enc_hop(k):
        src = enc_in.at[:, pl.ds(k * wide, wide)]
        return remote(src, enc_got.at[k - 1], e_s.at[k - 1], e_r.at[k - 1], cols[k])

    partners = [twin] + by_bit

    def small_hop(i):
        return remote(s_cur.at[i], s_got.at[i], s_s.at[i], s_r.at[i], partners[i])

    def small_z(k):
        return remote(
            s_cur.at[len(partners), k], s_z.at[k - 1], sz_s.at[k - 1], sz_r.at[k - 1], cols[k]
        )

    def small_step(i):
        if i == 0:
            s_cur[0] = small[...]
        elif i <= len(partners):
            small_hop(i - 1).wait_recv()
            got = s_got[i - 1]
            if i == 1:
                lane = lax.broadcasted_iota(jnp.int32, got.shape, 2)
                got = jnp.where(lane < wide, got, 0.0)
            s_cur[i] = s_cur[i - 1] + got
        if i < len(partners):
            small_hop(i).start()
        elif i == len(partners):
            for k in ks:
                small_z(k).start()
        else:
            value = s_cur[len(partners), 0]
            for k in ks:
                small_z(k).wait_recv()
                value = value + s_z[k - 1]
            small_out[...] = value

    spread_q = plane_copies(hidden1, part, parts, by_x, by_y, g_s.at[0], g_r.at[0])
    spread_a = plane_copies(full_a, part, parts, by_x, by_y, g_s.at[1], g_r.at[1])
    spread_b = plane_copies(full_b, part, parts, by_x, by_y, g_s.at[2], g_r.at[2])

    small_step(0)
    for q in ks:
        za[q - 1] = a_sum[rows(q), :]
    hidden1[part] = q_own[...]
    for i in range(1, len(partners)):
        small_step(i)
    for q in turns:
        hop(1, q).start()
    small_step(len(partners))
    line_a.begin()
    send_home(tg, tg_out, t_s, t_r, n_col)
    spread_q(0).start()
    for q in turns:
        hop(1, q).wait_recv()
        keep = parts[1] if 2 * q < n_col else parts[2]
        value = gb[keep, rows(q), :].astype(f32) + first[1, rows(q), :].astype(f32)
        mid[rows(q), :] = value.astype(low)
        hop2(q).start()
        hop(0, q).start()
    spread_q(1).start()
    for q in list(ks) + [0]:
        hop(0, q).wait_recv()
        hop2(q).wait_recv()
        value = gb[part, rows(q), :].astype(f32) + first[0, rows(q), :].astype(f32)
        value = value + second[rows(q), :].astype(f32)
        if q:
            zb[q - 1] = value.astype(low)
    line_b.begin()
    line_a.go(2)
    line_b.go(2)
    line_a.go(1)
    line_b.go(1)
    for k in ks:
        enc_hop(k).start()
    for stage in range(2):
        spread_q(stage).wait_recv()
        spread_q(2 + stage).start()
    value_a = line_a.total(a_sum[rows(0), :].astype(f32))
    value_a = with_other_bits(value_a, extra, 0, x_s, x_r, by_bit[2:])
    full_a[part] = value_a.astype(low)
    spread_a(0).start()
    spread_a(1).start()
    value = line_b.total(value)
    value = with_other_bits(value, extra, 1, x_s, x_r, by_bit[2:])
    full_b[part] = value.astype(low)
    spread_b(0).start()
    spread_b(1).start()
    for stage in range(2):
        spread_a(stage).wait_recv()
        spread_a(2 + stage).start()
    small_step(len(partners) + 1)
    for stage in range(2):
        spread_b(stage).wait_recv()
        spread_b(2 + stage).start()
    value = enc_in[:, pl.ds(0, wide)].astype(f32)
    for k in ks:
        enc_hop(k).wait()
        value = value + enc_got[k - 1].astype(f32)
    enc_out[...] = value
    for spread in (spread_q, spread_a, spread_b):
        spread(2).wait_recv()
        spread(3).wait_recv()
        for stage in range(4):
            spread(stage).wait_send()
    for q in range(n_col):
        hop(0, q).wait_send()
        hop(1, q).wait_send()
        hop2(q).wait_send()
        if q:
            small_z(q).wait_send()
    line_a.end()
    line_b.end()
    for i in range(len(partners)):
        small_hop(i).wait_send()
    wait_home(tg, tg_out, t_s, t_r, n_col)


def finish(gb, a_sum, q_own, small, enc_in, tg, n_col, n_dp):
    parts, deep, columns = gb.shape
    wide, hidden = q_own.shape
    steps = n_dp.bit_length()
    sd, vm, dma = jax.ShapeDtypeStruct, pltpu.VMEM, pltpu.SemaphoreType.DMA
    more = max(n_dp.bit_length() - 3, 1)
    others = n_col - 1
    return pl.pallas_call(
        functools.partial(finish_kernel, n_col=n_col, n_dp=n_dp),
        in_specs=[IN_VMEM] * 6,
        out_specs=[IN_VMEM] * 5 + [ANYWHERE],
        out_shape=[
            sd((parts, wide, columns), low),
            sd((parts, wide, columns), low),
            sd((parts, wide, hidden), low),
            sd(small.shape[1:], f32),
            sd((enc_in.shape[0], wide), f32),
            sd((n_col * tg.shape[0], wide), low),
        ],
        scratch_shapes=[
            vm((2, deep, columns), low),
            vm((deep, columns), low),
            vm((deep, columns), low),
            *[vm((others, wide, columns), low)] * 6,
            vm((others, enc_in.shape[0], wide), low),
            vm((steps + 1,) + small.shape, f32),
            vm((steps,) + small.shape, f32),
            vm((others,) + small.shape[1:], f32),
            vm((more, 3, wide, columns), low),
            dma((2, n_col)), dma((2, n_col)),
            dma((n_col,)), dma((n_col,)),
            *[dma((2, others))] * 4,
            dma((3, 4)), dma((3, 4)),
            dma((others,)), dma((others,)),
            dma((steps,)), dma((steps,)),
            dma((others,)), dma((others,)),
            dma((n_col,)), dma((n_col,)),
            dma((2, more)), dma((2, more)),
        ],
        compiler_params=pltpu.CompilerParams(
            collective_id=20, has_side_effects=True, vmem_limit_bytes=VMEM
        ),
        name="finish",
    )(gb, a_sum, q_own, small, enc_in, tg)


def column_grads_kernel(*refs, pairs, firsts):
    count = len(pairs)
    firsts_refs, others = refs[:firsts], refs[firsts : firsts + count]
    out, sums = refs[firsts + count :]
    size = out.shape[2] // count
    for i, (which, begin) in enumerate(pairs):
        a, b = firsts_refs[which], others[i]
        value = mm_tn(a[pl.ds(begin, b.shape[0]), :], b[...]).astype(low)
        for p in range(out.shape[0]):
            out[p, :, i * size : (i + 1) * size] = value[:, p * size : (p + 1) * size]

    @pl.when(pl.program_id(0) == 0)
    def _():
        for i in range(count):
            sums[i : i + 1, :] = jnp.sum(others[i][...].astype(f32), axis=0, keepdims=True)


def column_grads_of(firsts, pairs, others):
    deep, width = firsts[0].shape[1], others[0].shape[1]
    block = 256
    return pl.pallas_call(
        functools.partial(column_grads_kernel, pairs=pairs, firsts=len(firsts)),
        grid=(deep // block,),
        in_specs=[pl.BlockSpec((x.shape[0], block), lambda i: (0, i)) for x in firsts]
        + [pl.BlockSpec(x.shape, lambda i: (0, 0)) for x in others],
        out_specs=[
            pl.BlockSpec((PARTS, block, width), lambda i: (0, i, 0)),
            pl.BlockSpec((8, width), lambda i: (0, 0)),
        ],
        out_shape=[
            jax.ShapeDtypeStruct((PARTS, deep, width), low),
            jax.ShapeDtypeStruct((8, width), f32),
        ],
        compiler_params=pltpu.CompilerParams(vmem_limit_bytes=VMEM),
        name="column_grads",
    )(*firsts, *others)


def unpack_kernel(full_a, full_b, hidden0, hidden1, *outs):
    size = full_a.shape[2] // 4
    for g, full in enumerate((full_a, full_b)):
        for i in range(4):
            value = full[0, :, i * size : (i + 1) * size].astype(f32)
            outs[4 * g + i][...] = value if i < 3 else jnp.transpose(value)
    outs[8][...] = hidden0[0].astype(f32)
    outs[9][...] = jnp.transpose(hidden1[0].astype(f32))


def unpack(full_a, full_b, hidden0, hidden1):
    parts, wide, columns = full_a.shape
    inner = hidden0.shape[2]
    size = columns // 4
    into = (pl.BlockSpec((wide, size), lambda p: (0, p)), (wide, parts * size))
    out_of = (pl.BlockSpec((size, wide), lambda p: (p, 0)), (parts * size, wide))
    layouts = [into, into, into, out_of] * 2 + [
        (pl.BlockSpec((wide, inner), lambda p: (0, p)), (wide, parts * inner)),
        (pl.BlockSpec((inner, wide), lambda p: (p, 0)), (parts * inner, wide)),
    ]
    return pl.pallas_call(
        unpack_kernel,
        grid=(parts,),
        in_specs=[
            pl.BlockSpec((1, wide, x.shape[2]), lambda p: (p, 0, 0))
            for x in (full_a, full_b, hidden0, hidden1)
        ],
        out_specs=[x[0] for x in layouts],
        out_shape=[jax.ShapeDtypeStruct(x[1], f32) for x in layouts],
        compiler_params=pltpu.CompilerParams(vmem_limit_bytes=VMEM),
        name="unpack",
    )(full_a, full_b, hidden0, hidden1)


def build_local(mesh):
    n_dp, n_col = mesh.shape["dp"], mesh.shape["col"]

    def from_col(x, k):
        return lax.ppermute(x, "col", [(i, (i - k) % n_col) for i in range(n_col)])

    def across(x, bit):
        return lax.ppermute(x, "dp", [(i, i ^ bit) for i in range(n_dp)])

    def local(
        tokens, encoder, cotangent, dec_lengths, src_lengths,
        self_norm_gain, self_norm_bias, self_query, self_key, self_value,
        self_query_bias, self_value_bias, self_out, self_out_bias,
        cross_norm_gain, cross_norm_bias, cross_query, cross_key, cross_value,
        cross_query_bias, cross_value_bias, cross_out, cross_out_bias,
        hidden_norm_gain, hidden_norm_bias, hidden_in, hidden_in_bias,
        hidden_out, hidden_out_bias,
    ):
        row, col = lax.axis_index("row"), lax.axis_index("col")
        place = lax.axis_index("dp") % PARTS
        wide = tokens.shape[1]
        chunk = tokens.shape[0] // n_col
        span = 2 * chunk

        def in_order(parts):
            stacked = jnp.stack(parts)
            return [
                lax.dynamic_index_in_dim(stacked, i ^ place, 0, keepdims=False)
                for i in range(PARTS)
            ]

        def own_columns(w, j):
            size = w.shape[1] // PARTS
            return lax.dynamic_slice_in_dim(w, (place ^ j) * size, size, 1)

        def along_col(w):
            return [from_col(own_columns(w, 0), k) for k in range(1, n_col)]

        vec_f = jnp.stack([
            self_norm_gain, self_norm_bias, self_out_bias, cross_norm_gain, cross_norm_bias,
            cross_out_bias, hidden_norm_gain, hidden_norm_bias, hidden_out_bias,
        ])
        vec_f = jnp.pad(vec_f, ((0, 7), (0, 0)))
        vec_c = jnp.concatenate(
            [self_query_bias, self_value_bias, cross_query_bias, cross_value_bias, hidden_in_bias]
        ).reshape(-1, 128)
        vec_c = jnp.pad(vec_c, ((0, -vec_c.shape[0] % 8), (0, 0)))
        weights = [
            self_query, self_key, self_value, self_out,
            cross_query, cross_key, cross_value, cross_out,
        ]
        x_ext, enc, vectors, columns, *full = start(tokens, encoder, vec_f, vec_c, weights, n_col)
        wq1, wk1, wv1, wo1, wq2, wk2, wv2, wo2 = full
        (gain1, shift1, out_bias1, gain2, shift2, out_bias2, gain3, shift3, out_bias3) = vectors[:9]
        size = self_query_bias.shape[0]

        def column_vector(start, size):
            return columns.reshape(n_col, -1)[:, start : start + size].reshape(-1)

        q_bias1 = column_vector(0, size)
        v_bias1 = column_vector(size, size)
        q_bias2 = column_vector(2 * size, size)
        v_bias2 = column_vector(3 * size, size)
        hidden_bias = column_vector(4 * size, hidden_in_bias.shape[0]).reshape(PARTS, -1)
        hidden_bias = jnp.stack(
            [lax.dynamic_index_in_dim(hidden_bias, place ^ j, 0) for j in range(PARTS)]
        )

        hidden_in, x_ext = lax.optimization_barrier((hidden_in, x_ext))
        hidden_out_t = hidden_out.T
        pieces1 = along_col(hidden_in)

        dec_ids = doc_numbers(dec_lengths, SEQ_LEN)[0]
        src_ids = doc_numbers(src_lengths, ENC)[0]
        padded = jnp.pad(dec_ids, (WIN, 0), constant_values=-1)
        key_ids = lax.dynamic_slice_in_dim(padded, col * span, WIN + span, 0)
        query_ids = key_ids[WIN:]

        scale = low(HEAD_DIM**-0.5)
        x0 = x_ext[1]
        a_ext = enter(x_ext, gain1, shift1, 2).reshape(WIN + span, -1)
        a = a_ext[WIN:]
        hidden_out_t, a_ext = lax.optimization_barrier((hidden_out_t, a_ext))
        pieces2 = along_col(hidden_out_t)
        q1 = (mm(a, wq1) + q_bias1).astype(low) * scale
        k1 = mm(a_ext, wk1).astype(low)
        v1 = (mm(a_ext, wv1) + v_bias1).astype(low)
        dma = pltpu.SemaphoreType.DMA
        dma = pltpu.SemaphoreType.DMA
        o1, lse1 = attend(q1, k1, v1, query_ids, key_ids, True)
        pieces1, o1 = lax.optimization_barrier((pieces1, o1))
        rest1 = jnp.concatenate(pieces1, axis=0)
        near1 = [across(rest1, 1), across(rest1, 2)]
        x1, c = junction("forward", [("nn", o1, wo1)], [x0, out_bias1, gain2, shift2], 3)

        pieces2, c = lax.optimization_barrier((pieces2, c))
        rest2 = jnp.concatenate(pieces2, axis=0)
        near2 = [across(rest2, 1), across(rest2, 2)]
        q2 = (mm(c, wq2) + q_bias2).astype(low) * scale
        k2 = mm(enc, wk2).astype(low)
        v2 = (mm(enc, wv2) + v_bias2).astype(low)
        o2, lse2, dz = attend(
            q2, k2, v2, query_ids, src_ids, False,
            functools.partial(cotangent_rider, n_col=n_col), [cotangent],
            [((2, chunk, n_col * wide), low)], [dma((n_col,))] * 4, 14,
        )
        near1, near2, o2 = lax.optimization_barrier((near1, near2, o2))
        far1 = across(near1[0], 2)
        far2 = across(near2[1], 1)
        x2, f = junction("forward", [("nn", o2, wo2)], [x1, out_bias2, gain3, shift3], 4)
        rests1, rests2 = [rest1, *near1], [rest2, *near2]
        act0, slope0, part_sum = hidden_forward(
            f, hidden_bias[:1], hidden_in, hidden_out_t, rests1[:1], rests2[:1], (0,), 0
        )
        rests1, rests2 = [rest1, *near1, far1], [rest2, *near2, far2]
        act1, slope1, part_sum = hidden_forward(
            f, hidden_bias[1:3], hidden_in, hidden_out_t, rests1[1:3], rests2[1:3], (1, 2), 0,
            sum_in=part_sum,
        )
        act2, slope2, rows_out = hidden_forward(
            f, hidden_bias[3:], hidden_in, hidden_out_t, rests1[3:], rests2[3:], (3,), 5,
            sum_in=part_sum, x=x2, bias=out_bias3,
        )
        dz = dz.reshape(span, -1)

        g1, g2, hidden_bias_grad, df, got_a, got_b, layer_out = hidden_backward(
            dz, f, hidden_in, hidden_out_t, rests1, rests2, [act0, act1, act2],
            [slope0, slope1, slope2], ((0, 0), (1, 0), (1, 1), (2, 0)), rows_out, n_col, 11,
        )
        inner = g1.shape[2]
        half = g1.shape[1] // 2
        one = ((half, inner), low)
        dx2, dyc, stats3 = junction("backward", [("sum", df)], [dz, x2, gain3], 6)

        doc = mm_nt(dyc, wo2).astype(low)
        dq2, dk2, dv2, back_a, back_b, far_a, far_b = attend_back(
            q2, k2, v2, doc, o2, lse2, query_ids, src_ids, False,
            first_rider, [g1, g2, got_a, got_b], [one] * 4,
            [
                pltpu.VMEM((4, half, inner), low), pltpu.VMEM((2, half, inner), low),
                dma((4,)), dma((4,)), dma((4,)),
            ],
            12,
        )
        cross_grads, cross_columns = column_grads_of(
            [c, enc, dyc], [(0, 0), (1, 0), (1, 0), (2, 0)], [dq2, dk2, dv2, o2]
        )
        enc_back = junction("sum", [("nt", dk2, wk2), ("nt", dv2, wv2)], [], 7)
        dx1, dy, stats2 = junction("backward", [("nt", dq2, wq2)], [dx2, x1, gain2], 8)

        cross_grads, enc_back, dy = lax.optimization_barrier((cross_grads, enc_back, dy))
        do = mm_nt(dy, wo1).astype(low)
        (
            dq1, dk1, dv1, near_a, near_b, far_back_a, far_back_b, z_got, own1
        ) = attend_back(
            q1, k1, v1, do, o1, lse1, query_ids, key_ids, True,
            functools.partial(second_rider, n_col=n_col),
            [g1, g2, got_a, got_b, back_a, back_b, far_a, far_b],
            [one] * 4 + [((n_col - 1, wide, inner), low), ((wide, inner), low)],
            [
                pltpu.VMEM((4, half, inner), low), pltpu.VMEM((2, half, inner), low),
                pltpu.VMEM((3, 2 * half, inner), low), pltpu.VMEM((n_col, wide, inner), low),
                dma((4,)), dma((2, 3)), dma((4,)), dma((4,)),
                dma((n_col - 1,)), dma((n_col - 1,)), dma,
            ],
            13,
        )
        gb, self_columns, x0_grad, stats1, a_sum, hidden0, q_own = fold(
            dq1, dk1, dv1, a_ext, dy, o1, [wq1, wk1, wv1], dx1, x0, gain1, cross_grads,
            [g2, near_a, near_b, far_back_a, far_back_b, z_got, own1], n_col, n_dp,
        )

        feature_grads = jnp.concatenate([
            stats1[:2], stats2[2:3], stats2[:2], stats3[2:3], stats3[:2], stats3[3:4],
        ])
        feature_grads = jnp.moveaxis(feature_grads.reshape(-1, n_col, wide), 1, 0)
        column_grads = []
        for vector in (self_columns[0], self_columns[2], cross_columns[0], cross_columns[2]):
            column_grads.append(vector.reshape(n_col, -1))
        column_grads.append(
            jnp.stack(in_order([hidden_bias_grad[j] for j in range(PARTS)])).reshape(n_col, -1)
        )
        column_grads = jnp.concatenate(column_grads, axis=1).reshape(n_col, -1, 128)
        column_grads = lax.dynamic_slice_in_dim(
            jnp.concatenate([column_grads, column_grads]), col, n_col, 0
        )
        lines = -(-max(feature_grads.shape[1], column_grads.shape[1]) // 8) * 8
        small = jnp.concatenate(
            [
                jnp.pad(x, ((0, 0), (0, lines - x.shape[1]), (0, 0)))
                for x in (feature_grads, column_grads)
            ],
            axis=2,
        )
        full_a, full_b, hidden1, small, encoder_grad, tokens_grad = finish(
            gb, a_sum, q_own, small, enc_back, x0_grad, n_col, n_dp
        )
        grads = unpack(full_a, full_b, hidden0, hidden1)
        tokens_grad = tokens_grad.astype(f32)
        feature_grads = small[:, :wide]
        column_grads = small[:, wide:].reshape(-1)

        return (
            layer_out,
            tokens_grad,
            encoder_grad,
            feature_grads[0],
            feature_grads[1],
            grads[4],
            grads[5],
            grads[6],
            column_grads[:size],
            column_grads[size : 2 * size],
            grads[7],
            feature_grads[2],
            feature_grads[3],
            feature_grads[4],
            grads[0],
            grads[1],
            grads[2],
            column_grads[2 * size : 3 * size],
            column_grads[3 * size : 4 * size],
            grads[3],
            feature_grads[5],
            feature_grads[6],
            feature_grads[7],
            grads[8],
            column_grads[4 * size : 4 * size + hidden_in_bias.shape[0]],
            grads[9],
            feature_grads[8],
        )

    return local


def solution(mesh):
    rows = P(("dp", "row"), "col")
    features = P("col")
    columns = P(("row", "col"))
    into, out_of = P("col", "row"), P("row", "col")
    attention = (into, into, into, columns, columns, out_of, features)
    norm = (features, features)
    weights = (
        norm
        + attention
        + norm
        + attention
        + norm
        + (into, columns, out_of, features)
    )
    return jax.shard_map(
        build_local(mesh),
        mesh=mesh,
        in_specs=(rows, rows, rows, P("dp", None), P("dp", None)) + weights,
        out_specs=(rows, rows, rows) + weights,
        check_vma=False,
    )
```

```python
import functools

import jax
import jax.numpy as jnp
from jax import lax
from jax.experimental import pallas as pl
from jax.experimental.pallas import tpu as pltpu
from jax.sharding import PartitionSpec as P

D = 1024
HEAD_DIM = 64
SEQ_LEN = 4096
ENC = 1024
WIN = 1024

norm_epsilon = 1e-05
masked_fill = -1e30
low = jnp.bfloat16
f32 = jnp.float32
PARTS = 4
PAIR = 2 * HEAD_DIM
QUERY_ROWS = 256
VMEM = 56 * 1024 * 1024


def doc_numbers(lengths, positions):
    bounds = jnp.cumsum(lengths, axis=1, dtype=jnp.int32)
    places = jnp.arange(positions, dtype=jnp.int32)
    return jnp.sum(
        (places[None, :, None] >= bounds[:, None, :]).astype(jnp.int32), axis=2, dtype=jnp.int32
    )


def mm(a, b):
    return lax.dot_general(a, b, (((1,), (0,)), ((), ())), preferred_element_type=f32)


def mm_nt(a, b):
    return lax.dot_general(a, b, (((1,), (1,)), ((), ())), preferred_element_type=f32)


def mm_tn(a, b):
    return lax.dot_general(a, b, (((0,), (0,)), ((), ())), preferred_element_type=f32)


MESH = pl.DeviceIdType.MESH
ANYWHERE = pl.BlockSpec(memory_space=pl.ANY)
IN_VMEM = pl.BlockSpec(memory_space=pltpu.VMEM)


def here():
    return lax.axis_index("dp"), lax.axis_index("row"), lax.axis_index("col")


def meet(partners):
    barrier = pltpu.get_barrier_semaphore()
    for partner in partners:
        pl.semaphore_signal(barrier, inc=1, device_id=partner, device_id_type=MESH)
    pl.semaphore_wait(barrier, len(partners))


def remote(src, dst, sends, recvs, device):
    return pltpu.make_async_remote_copy(
        src_ref=src, dst_ref=dst, send_sem=sends, recv_sem=recvs, device_id=device,
        device_id_type=MESH,
    )


def home_hop(rows, home, sends, recvs, n_col, k):
    dp, row, col = here()
    wide, count = home.shape[1], rows.shape[0]
    to_row, at = col // 2, 2 * lax.rem(col, 2) + row
    src = rows.at[:, pl.ds(k * wide, wide)]
    dst = home.at[pl.ds(pl.multiple_of(at * count, count), count), :]
    copy = remote(src, dst, sends.at[k], recvs.at[at], (dp, to_row, lax.rem(col + k, n_col)))
    return copy, pltpu.make_async_copy(src, dst, recvs.at[at]), to_row == row


def send_home(rows, home, sends, recvs, n_col):
    for k in range(n_col):
        away, here_copy, same = home_hop(rows, home, sends, recvs, n_col, k)
        if k:
            away.start()
            continue

        @pl.when(same)
        def _():
            here_copy.start()

        @pl.when(jnp.logical_not(same))
        def _():
            away.start()


def wait_home(rows, home, sends, recvs, n_col):
    wide, count = home.shape[1], rows.shape[0]
    for k in range(n_col):
        away, _, same = home_hop(rows, home, sends, recvs, n_col, k)
        if k:
            away.wait_send()
        else:

            @pl.when(jnp.logical_not(same))
            def _():
                away.wait_send()

        src = rows.at[:, pl.ds(k * wide, wide)]
        pltpu.make_async_copy(src, home.at[pl.ds(k * count, count), :], recvs.at[k]).wait()


class LineSum:
    def __init__(self, buf, in_l, in_r, sends, recvs, cols):
        self.buf, self.in_l, self.in_r, self.sends, self.recvs = buf, in_l, in_r, sends, recvs
        self.cols, self.n, self.col = cols, len(cols), lax.axis_index("col")

    def right(self, d):
        return remote(
            self.buf.at[d - 1], self.in_l.at[d - 1], self.sends.at[0, d - 1],
            self.recvs.at[0, d - 1], self.cols[1],
        )

    def left(self, d):
        return remote(
            self.buf.at[self.n - d - 1], self.in_r.at[d - 1], self.sends.at[1, d - 1],
            self.recvs.at[1, d - 1], self.cols[self.n - 1],
        )

    def add(self, k, got):
        self.buf[k - 1] = (self.buf[k - 1].astype(f32) + got.astype(f32)).astype(low)

    def begin(self):
        @pl.when(self.col == 0)
        def _():
            self.in_l[0] = jnp.zeros(self.in_l.shape[1:], low)
            for d in range(self.n - 1, 0, -1):
                self.right(d).start()

        @pl.when(self.col == self.n - 1)
        def _():
            self.in_r[0] = jnp.zeros(self.in_r.shape[1:], low)
            for d in range(self.n - 1, 0, -1):
                self.left(d).start()

    def go(self, d):
        @pl.when((self.col > 0) & (self.col <= self.n - 1 - d))
        def _():
            self.right(d + 1).wait_recv()
            self.add(d, self.in_l[d])
            self.right(d).start()

        @pl.when((self.col < self.n - 1) & (self.col >= d))
        def _():
            self.left(d + 1).wait_recv()
            self.add(self.n - d, self.in_r[d])
            self.left(d).start()

    def total(self, value):
        @pl.when(self.col > 0)
        def _():
            self.right(1).wait_recv()

        @pl.when(self.col < self.n - 1)
        def _():
            self.left(1).wait_recv()

        return value + self.in_l[0].astype(f32) + self.in_r[0].astype(f32)

    def end(self):
        for d in range(1, self.n):

            @pl.when(self.col <= self.n - 1 - d)
            def _():
                self.right(d).wait_send()

            @pl.when(self.col >= d)
            def _():
                self.left(d).wait_send()


def plane():
    dp, row, col = here()
    flips = [dp + b - 2 * b * lax.rem(dp // b, 2) for b in (1, 2)]
    return (flips[0], row, col), (flips[1], row, col)


def head_masks():
    lane = lax.broadcasted_iota(jnp.int32, (1, PAIR), 1)
    first = jnp.where(lane < HEAD_DIM, 1.0, 0.0)
    return first.astype(low), (1.0 - first).astype(low), lane < HEAD_DIM


def attend_kernel(q_ref, k_ref, v_ref, qid_ref, kid_ref, o_ref, lse_ref, bias, *, span, windowed):
    rows = q_ref.shape[0]
    pairs = q_ref.shape[1] // PAIR
    step = pl.program_id(0)
    start = step * rows if windowed else 0
    if windowed:
        start = pl.multiple_of(start, rows)
    allowed = qid_ref[...] == kid_ref[0:1, pl.ds(start, span)]
    if windowed:
        at_row = lax.broadcasted_iota(jnp.int32, (rows, span), 0)
        at_key = lax.broadcasted_iota(jnp.int32, (rows, span), 1)
        allowed = allowed & (at_key > at_row) & (at_key <= at_row + WIN)
    bias[...] = jnp.where(allowed, 0.0, masked_fill)
    first, second, is_first = head_masks()

    def one_pair(p, carry):
        lanes = pl.ds(pl.multiple_of(p * PAIR, PAIR), PAIR)
        q2 = q_ref[:, lanes]
        k2 = k_ref[pl.ds(start, span), lanes]
        v2 = v_ref[pl.ds(start, span), lanes]
        outs, logs = [], []
        for mask in (first, second):
            s = mm_nt(q2 * mask, k2) + bias[...]
            top = jnp.max(s, axis=1, keepdims=True)
            e = jnp.exp(s - top)
            total = jnp.sum(e, axis=1, keepdims=True)
            outs.append(mm(e.astype(low), v2) / total)
            logs.append(top + jnp.log(total))
        o_ref[:, lanes] = jnp.where(is_first, outs[0], outs[1]).astype(low)
        stats = jnp.where(is_first, logs[0], logs[1])
        turned = jnp.transpose(stats)
        lse_ref[p, 0:1, :] = turned[0:1]
        lse_ref[p, 1:2, :] = turned[HEAD_DIM : HEAD_DIM + 1]
        return carry

    lax.fori_loop(0, pairs, one_pair, 0)


def attend(q, k, v, qid, kid, windowed):
    tokens, width = q.shape
    keys = k.shape[0]
    pairs = width // PAIR
    rows = QUERY_ROWS
    span = WIN + rows if windowed else keys
    return pl.pallas_call(
        functools.partial(attend_kernel, span=span, windowed=windowed),
        grid=(tokens // rows,),
        in_specs=[
            pl.BlockSpec((rows, width), lambda i: (i, 0)),
            pl.BlockSpec((keys, width), lambda i: (0, 0)),
            pl.BlockSpec((keys, width), lambda i: (0, 0)),
            pl.BlockSpec((rows, 1), lambda i: (i, 0)),
            pl.BlockSpec((1, keys), lambda i: (0, 0)),
        ],
        out_specs=[
            pl.BlockSpec((rows, width), lambda i: (i, 0)),
            pl.BlockSpec((pairs, 8, rows), lambda i: (0, 0, i)),
        ],
        out_shape=[
            jax.ShapeDtypeStruct((tokens, width), low),
            jax.ShapeDtypeStruct((pairs, 8, tokens), f32),
        ],
        scratch_shapes=[pltpu.VMEM((rows, span), f32)],
        compiler_params=pltpu.CompilerParams(vmem_limit_bytes=VMEM),
        name="attend",
    )(q, k, v, qid[:, None], kid[None, :])


def attend_back_kernel(*refs, span, windowed, rider, n_ins, n_outs):
    refs = list(refs)
    q_ref, k_ref, v_ref, do_ref, o_ref, lse_ref, qid_ref, kid_ref = refs[:8]
    rider_refs = refs[8 : 8 + n_ins]
    refs = refs[8 + n_ins :]
    dq_ref, dk_ref, dv_ref = refs[:3]
    rider_refs += refs[3 : 3 + n_outs]
    bias, dk_sum, dv_sum = refs[3 + n_outs : 6 + n_outs]
    rider_refs += refs[6 + n_outs :]
    rows = q_ref.shape[0]
    pairs = q_ref.shape[1] // PAIR
    step = pl.program_id(0)
    start = pl.multiple_of(step * rows, rows) if windowed else 0
    keys = pl.ds(start, span)
    begin, middle, end, later = rider(*rider_refs)

    @pl.when(step == 0)
    def _():
        begin()
        dk_sum[...] = jnp.zeros_like(dk_sum)
        dv_sum[...] = jnp.zeros_like(dv_sum)

    for at, hook in later.items():

        @pl.when(step == at)
        def _():
            hook()

    allowed = kid_ref[keys, :] == qid_ref[...]
    if windowed:
        at_key = lax.broadcasted_iota(jnp.int32, (span, rows), 0)
        at_row = lax.broadcasted_iota(jnp.int32, (span, rows), 1)
        allowed = allowed & (at_key > at_row) & (at_key <= at_row + WIN)
    bias[...] = jnp.where(allowed, 0.0, masked_fill)
    first, second, is_first = head_masks()

    def one_pair(p, carry):
        lanes = pl.ds(pl.multiple_of(p * PAIR, PAIR), PAIR)
        q2 = q_ref[:, lanes]
        k2 = k_ref[keys, lanes]
        v2 = v_ref[keys, lanes]
        do2 = do_ref[:, lanes]
        turned = jnp.transpose(do2.astype(f32) * o_ref[:, lanes].astype(f32))
        dk, dv, dqs = 0.0, 0.0, []
        for h, mask in enumerate((first, second)):
            qm, dom = q2 * mask, do2 * mask
            inner = jnp.sum(turned[h * HEAD_DIM : (h + 1) * HEAD_DIM], axis=0, keepdims=True)
            s = mm_nt(k2, qm) + bias[...]
            share = jnp.exp(s - lse_ref[p, h : h + 1, :])
            ds = (share * (mm_nt(v2, dom) - inner)).astype(low)
            dv = dv + mm(share.astype(low), dom)
            dk = dk + mm(ds, qm)
            dqs.append(mm_tn(ds, k2))
        dk_sum[keys, lanes] += dk
        dv_sum[keys, lanes] += dv
        dq_ref[:, lanes] = (jnp.where(is_first, dqs[0], dqs[1]) * HEAD_DIM**-0.5).astype(low)

        @pl.when((step == 0) & (p == 0))
        def _():
            middle()

        return carry

    lax.fori_loop(0, pairs, one_pair, 0)

    @pl.when(step == pl.num_programs(0) - 1)
    def _():
        dk_ref[...] = dk_sum[...].astype(low)
        dv_ref[...] = dv_sum[...].astype(low)
        end()


def attend_back(q, k, v, do, o, lse, qid, kid, windowed, rider, riding, shapes, scratch, number):
    tokens, width = q.shape
    keys = k.shape[0]
    pairs = width // PAIR
    rows = QUERY_ROWS
    span = WIN + rows if windowed else keys
    by_row = pl.BlockSpec((rows, width), lambda i: (i, 0))
    whole = pl.BlockSpec((keys, width), lambda i: (0, 0))
    return pl.pallas_call(
        functools.partial(
            attend_back_kernel, span=span, windowed=windowed, rider=rider, n_ins=len(riding),
            n_outs=len(shapes),
        ),
        grid=(tokens // rows,),
        in_specs=[
            by_row,
            whole,
            whole,
            by_row,
            by_row,
            pl.BlockSpec((pairs, 8, rows), lambda i: (0, 0, i)),
            pl.BlockSpec((1, rows), lambda i: (0, i)),
            pl.BlockSpec((keys, 1), lambda i: (0, 0)),
        ]
        + [ANYWHERE] * len(riding),
        out_specs=[by_row, whole, whole] + [ANYWHERE] * len(shapes),
        out_shape=[
            jax.ShapeDtypeStruct((tokens, width), low),
            jax.ShapeDtypeStruct((keys, width), low),
            jax.ShapeDtypeStruct((keys, width), low),
        ]
        + [jax.ShapeDtypeStruct(*x) for x in shapes],
        scratch_shapes=[
            pltpu.VMEM((span, rows), f32),
            pltpu.VMEM((keys, width), f32),
            pltpu.VMEM((keys, width), f32),
        ]
        + scratch,
        compiler_params=pltpu.CompilerParams(
            vmem_limit_bytes=VMEM, collective_id=number, has_side_effects=True
        ),
        name="attend_back",
    )(q, k, v, do, o, lse, qid[None, :], kid[:, None], *riding)


def first_rider(g1, g2, got_a, got_b, back_a, back_b, far_a, far_b, load, mid, l_s, s_s, r_s):
    by_x, by_y = plane()
    half = back_a.shape[0]
    up, down = pl.ds(0, half), pl.ds(half, half)
    loads = [
        pltpu.make_async_copy(src, load.at[i], l_s.at[i])
        for i, src in enumerate((g1.at[2, up, :], got_a.at[0], g1.at[1, down, :], got_b.at[0]))
    ]
    hops = [
        remote(mid.at[0], back_a, s_s.at[0], r_s.at[0], by_y),
        remote(mid.at[1], back_b, s_s.at[1], r_s.at[1], by_x),
    ]
    count = far_a.shape[1]
    lanes = pl.ds(g2.shape[2] - count, count)
    far = [
        remote(g2.at[3, up, lanes], far_a, s_s.at[2], r_s.at[2], by_x),
        remote(g2.at[3, down, lanes], far_b, s_s.at[3], r_s.at[3], by_y),
    ]

    def begin():
        meet([by_x, by_y])
        for copy in loads + far:
            copy.start()

    def middle():
        for i in range(2):
            loads[2 * i].wait()
            loads[2 * i + 1].wait()
            mid[i] = (load[2 * i].astype(f32) + load[2 * i + 1].astype(f32)).astype(low)
            hops[i].start()

    def end():
        for copy in hops + far:
            copy.wait()

    return begin, middle, end, {}


def second_rider(
    g1, g2, got_a, got_b, back_a, back_b, far_a, far_b, far_c, far_d,
    near_a, near_b, far_back_a, far_back_b, own,
    load, mid, load_z, out_z, out_own, z_l, z_r, l_s, lz_s, s_s, r_s, zs_s, zr_s, o_s,
    *, n_col,
):
    dp, row, col = here()
    by_x, by_y = plane()
    half = back_a.shape[0]
    wide = own.shape[0]
    up, down = pl.ds(0, half), pl.ds(half, half)
    loads = [
        pltpu.make_async_copy(src, load.at[i], l_s.at[i])
        for i, src in ((0, g2.at[2, up, :]), (2, g2.at[1, down, :]))
    ]
    cut = far_a.shape[1]
    for i, (one, two) in ((1, (far_a, far_c)), (3, (far_b, far_d))):
        loads += [
            pltpu.make_async_copy(one, load.at[i, :, pl.ds(0, cut)], l_s.at[i]),
            pltpu.make_async_copy(
                two, load.at[i, :, pl.ds(cut, two.shape[1])], l_s.at[4 + i // 2]
            ),
        ]
    loads_z = []
    for i, (source, got, back) in enumerate(((up, got_a, back_a), (down, got_b, back_b))):
        for n, src in enumerate((g1.at[0, source, :], got.at[1], back)):
            loads_z.append(
                pltpu.make_async_copy(src, load_z.at[n, source, :], lz_s.at[i, n])
            )
    hops = [
        remote(g2.at[1, up, :], near_a, s_s.at[0], r_s.at[0], by_x),
        remote(g2.at[2, down, :], near_b, s_s.at[1], r_s.at[1], by_y),
        remote(mid.at[0], far_back_a, s_s.at[2], r_s.at[2], by_y),
        remote(mid.at[1], far_back_b, s_s.at[3], r_s.at[3], by_x),
    ]
    cols = [(dp, row, lax.rem(col + k, n_col)) for k in range(n_col)]
    line = LineSum(out_z, z_l, z_r, zs_s, zr_s, cols)
    keep = pltpu.make_async_copy(out_own, own, o_s)

    def begin():
        meet([by_x, by_y] + cols[1:])
        for copy in loads + loads_z + hops[:2]:
            copy.start()

    def middle():
        for i in range(2):
            for n in ((0, 2, 3), (1, 4, 5))[i]:
                loads[n].wait()
            mid[i] = (load[2 * i].astype(f32) + load[2 * i + 1].astype(f32)).astype(low)
            hops[2 + i].start()
        for copy in loads_z:
            copy.wait()
        for k in range(n_col):
            at = pl.ds(k * wide, wide)
            value = load_z[0, at, :].astype(f32) + load_z[1, at, :].astype(f32)
            value = (value + load_z[2, at, :].astype(f32)).astype(low)
            if k:
                out_z[k - 1] = value
            else:
                out_own[...] = value
        line.begin()

    def end():
        out_own[...] = line.total(out_own[...].astype(f32)).astype(low)
        keep.start()
        for copy in hops + [keep]:
            copy.wait()
        line.end()

    return begin, middle, end, {2: lambda: line.go(2), 3: lambda: line.go(1)}


ROOT = 0.7978845608028654
CUBE = 0.044715


def cotangent_rider(cot, dz, c_s, c_r, d_s, d_r, *, n_col):
    dp, row, col = here()
    wide = cot.shape[1]
    rows_here = cot.shape[0] // n_col

    def piece(j):
        to_col = 2 * row + j // 2
        k = lax.rem(col + n_col - to_col, n_col)
        src = cot.at[pl.ds(j * rows_here, rows_here), :]
        dst = dz.at[j % 2, :, pl.ds(pl.multiple_of(k * wide, wide), wide)]
        local = (row == j % 2) & (col == to_col)
        return src, dst, k, local, (dp, j % 2, to_col)

    def to_twin(k):
        ref = dz.at[row, :, pl.ds(k * wide, wide)]
        return remote(ref, ref, d_s.at[k], d_r.at[k], (dp, 1 - row, col))

    def begin():
        group = [
            (dp, r, lax.rem(col + k, n_col)) for r in (row, 1 - row) for k in range(n_col)
        ]
        meet(group[1:])
        for j in range(n_col):
            src, dst, k, local, to = piece(j)

            @pl.when(local)
            def _():
                pltpu.make_async_copy(src, dst, c_r.at[k]).start()

            @pl.when(jnp.logical_not(local))
            def _():
                remote(src, dst, c_s.at[j], c_r.at[k], to).start()

    def turn():
        for k in range(n_col):
            pltpu.make_async_copy(
                cot.at[pl.ds(0, rows_here), :], dz.at[row, :, pl.ds(k * wide, wide)], c_r.at[k]
            ).wait()
            to_twin(k).start()

    def end():
        for j in range(n_col):
            src, dst, k, local, to = piece(j)

            @pl.when(jnp.logical_not(local))
            def _():
                remote(src, dst, c_s.at[j], c_r.at[k], to).wait_send()

        for k in range(n_col):
            to_twin(k).wait()

    return begin, turn, end


ORDER = (3, 1, 2, 0)


def part_numbers():
    part = lax.rem(lax.axis_index("dp"), PARTS)
    return part, part + 1 - 2 * lax.rem(part, 2), part + 2 - 4 * (part // 2), PARTS - 1 - part


def weight_copies(own, rest, j, n, to, sem):
    wide, block = own.shape[0], to.shape[1]
    inner = rest.shape[1]
    begin = pl.multiple_of(part_numbers()[j] * inner + n * block, block)
    return [
        pltpu.make_async_copy(own.at[:, pl.ds(begin, block)], to.at[pl.ds(0, wide), :], sem),
        pltpu.make_async_copy(
            rest.at[:, pl.ds(pl.multiple_of(n * block, block), block)],
            to.at[pl.ds(wide, rest.shape[0]), :],
            sem,
        ),
    ]


def hidden_kernel(*refs, numbers, opening, closing, riding, n_col):
    count = len(numbers)
    refs = list(refs)

    def take(n):
        got, refs[:n] = refs[:n], []
        return got

    f_ref, b1_ref, own1, own2 = take(4)
    rest1, rest2 = take(count), take(count)
    if not opening:
        (sum_in,) = take(1)
    if closing:
        x_ref, bias = take(2)
    if riding:
        (cot,) = take(1)
    act_ref, slope_ref = take(2)
    if riding:
        (dz,) = take(1)
    (out_ref,) = take(1)
    total, w1, w2, w_sem = take(4)
    step, steps = pl.program_id(0), pl.num_programs(0)
    dp, row, col = here()
    twin = (dp, 1 - row, col)
    block = w1.shape[2]
    blocks = rest1[0].shape[1] // block
    slot = lax.rem(step, 2)

    def fetch(s):
        for i in range(count):

            @pl.when(s // blocks == i)
            def _():
                n = lax.rem(s, blocks)
                at = lax.rem(s, 2)
                for copy in weight_copies(
                    own1, rest1[i], numbers[i], n, w1.at[at], w_sem.at[0, at]
                ) + weight_copies(own2, rest2[i], numbers[i], n, w2.at[at], w_sem.at[1, at]):
                    copy.start()

    if closing:
        away, came, s_s, s_r = take(4)
    if riding:
        begin, turn, end = cotangent_rider(cot, dz, *take(4), n_col=n_col)

    @pl.when(step == 0)
    def _():
        fetch(step)
        if opening:
            total[...] = jnp.zeros_like(total)
        else:
            total[...] = sum_in[...]
        if closing:
            meet([twin])
        if riding:
            begin()

    @pl.when(step + 1 < steps)
    def _():
        fetch(step + 1)

    for i, w in enumerate((w1, w2)):
        pltpu.make_async_copy(w.at[slot], w.at[slot], w_sem.at[i, slot]).wait()

    if riding:

        @pl.when(step == steps - 1)
        def _():
            turn()

    def one_part(t, carry):
        rows = pl.ds(pl.multiple_of(t * 256, 256), 256)
        h = mm(f_ref[rows, :], w1[slot]) + b1_ref[0]
        square = h * h
        bend = jnp.tanh(h * (ROOT + (ROOT * CUBE) * square))
        half = 0.5 + 0.5 * bend
        act = (h * half).astype(low)
        act_ref[0, rows, :] = act
        slope = half + (0.5 * h) * (1.0 - bend * bend) * (ROOT + (3.0 * ROOT * CUBE) * square)
        slope_ref[0, rows, :] = slope.astype(low)
        total[rows, :] += mm_nt(act, w2[slot])
        return carry

    lax.fori_loop(0, f_ref.shape[0] // 256, one_part, 0)

    @pl.when(step == steps - 1)
    def _():
        if riding:
            end()
        if not closing:
            out_ref[...] = total[...]
        else:
            rows = came.shape[0]
            sent = []
            for t in range(rows // CUT):
                at = pl.ds(t * CUT, CUT)
                begin = pl.multiple_of((1 - row) * rows + t * CUT, CUT)
                away[at, :] = total[pl.ds(begin, CUT), :].astype(low)
                copy = remote(away.at[at, :], came.at[at, :], s_s.at[t], s_r.at[t], twin)
                copy.start()
                sent.append(copy)
            for t in range(rows // CUT):
                at = pl.ds(t * CUT, CUT)
                begin = pl.multiple_of(row * rows + t * CUT, CUT)
                sent[t].wait()
                branch = total[pl.ds(begin, CUT), :] + came[at, :].astype(f32)
                out_ref[at, :] = (x_ref[at, :] + (branch + bias[...])).astype(low)

def hidden_forward(f, b1, own1, own2, rest1, rest2, numbers, number, sum_in=None, x=None, bias=None,
                   cotangent=None, n_col=0):
    tokens, width = f.shape
    inner = rest1[0].shape[1]
    count = len(numbers)
    block = min(512, inner)
    blocks = inner // block
    rows = tokens // 2
    opening, closing = sum_in is None, x is not None
    dma = pltpu.SemaphoreType.DMA

    def still(shape):
        return pl.BlockSpec(shape, lambda s: (0,) * len(shape))

    active = pl.BlockSpec((1, tokens, block), lambda s: (s // blocks, 0, lax.rem(s, blocks)))
    args = [f, b1, own1, own2, *rest1, *rest2]
    in_specs = [
        still((tokens, width)),
        pl.BlockSpec((1, 1, block), lambda s: (s // blocks, 0, lax.rem(s, blocks))),
    ] + [ANYWHERE] * (2 + 2 * count)
    out_specs = [active, active]
    out_shape = [jax.ShapeDtypeStruct((count, tokens, inner), low)] * 2
    scratch = [
        pltpu.VMEM((tokens, width), f32),
        pltpu.VMEM((2, width, block), low),
        pltpu.VMEM((2, width, block), low),
        dma((2, 2)),
    ]
    if not opening:
        args.append(sum_in)
        in_specs.append(still((tokens, width)))
    if closing:
        args += [x, bias[None]]
        in_specs += [still((rows, width)), still((1, width))]
        out_shape.append(jax.ShapeDtypeStruct((rows, width), low))
        scratch += [pltpu.VMEM((rows, width), low), pltpu.VMEM((rows, width), low)]
        scratch += [dma((rows // CUT,)), dma((rows // CUT,))]
    else:
        out_shape.append(jax.ShapeDtypeStruct((tokens, width), f32))
    out_specs.append(still(out_shape[-1].shape))
    if cotangent is not None:
        args.append(cotangent)
        in_specs.append(still(cotangent.shape))
        out_shape.insert(2, jax.ShapeDtypeStruct((2, rows, width), low))
        out_specs.insert(2, ANYWHERE)
        scratch += [dma((n_col,))] * 4
    params = dict(vmem_limit_bytes=VMEM)
    if closing or cotangent is not None:
        params.update(collective_id=number, has_side_effects=True)
    return pl.pallas_call(
        functools.partial(
            hidden_kernel, numbers=numbers, opening=opening, closing=closing,
            riding=cotangent is not None, n_col=n_col,
        ),
        grid=(count * blocks,),
        in_specs=in_specs,
        out_specs=out_specs,
        out_shape=out_shape,
        scratch_shapes=scratch,
        compiler_params=pltpu.CompilerParams(**params),
        name="hidden_forward",
    )(*args)


def hidden_back_kernel(
    dz_ref, dzt_ref, ft_ref, rows_out, own1, own2, *refs, n_col, places,
):
    rest1, rest2 = refs[:PARTS], refs[PARTS : 2 * PARTS]
    calls = 1 + max(p[0] for p in places)
    acts, slopes = refs[2 * PARTS : 2 * PARTS + calls], refs[2 * PARTS + calls : 2 * (PARTS + calls)]
    (
        g1_ref, g2_ref, gb_ref, df_ref, got_a, got_b, home, far_a, far_b, dh_low, total, away_a, away_b,
        s_s, r_s, h_s, h_r, away_f, f_s, f_r, w1, w2, act_ref, slope_ref, w_sem,
    ) = refs[2 * (PARTS + calls) :]
    block = g1_ref.shape[2]
    inners = rest1[0].shape[1] // block
    step = pl.program_id(0)
    last = pl.num_programs(0) - 1
    order, inner = step // inners, lax.rem(step, inners)
    slot = lax.rem(step, 2)

    def fetch(s):
        for i, j in enumerate(ORDER):

            @pl.when(s // inners == i)
            def _():
                n, at = lax.rem(s, inners), lax.rem(s, 2)
                lanes = pl.ds(pl.multiple_of(n * block, block), block)
                call, index = places[j]
                copies = weight_copies(own1, rest1[j], j, n, w1.at[at], w_sem.at[0, at])
                copies += weight_copies(own2, rest2[j], j, n, w2.at[at], w_sem.at[1, at])
                for src, to, k in ((acts, act_ref, 2), (slopes, slope_ref, 3)):
                    copies.append(
                        pltpu.make_async_copy(
                            src[call].at[index, :, lanes], to.at[at], w_sem.at[k, at]
                        )
                    )
                for copy in copies:
                    copy.start()

    by_x, by_y = plane()
    half = got_a.shape[1]
    dp, row, col = here()

    @pl.when(step == 0)
    def _():
        group = [
            (dp, r, lax.rem(col + k, n_col)) for r in (row, 1 - row) for k in range(n_col)
        ]
        meet(group[1:] + [by_x, by_y])
        total[...] = jnp.zeros_like(total)
        send_home(rows_out, home, h_s, h_r, n_col)
        fetch(step)

    @pl.when(step < last)
    def _():
        fetch(step + 1)

    gb_ref[...] = jnp.zeros_like(gb_ref)
    for i, w in enumerate((w1, w2, act_ref, slope_ref)):
        pltpu.make_async_copy(w.at[slot], w.at[slot], w_sem.at[i, slot]).wait()

    def one_part(t, carry):
        rows = pl.ds(pl.multiple_of(t * 256, 256), 256)
        dh = (mm(dz_ref[rows, :], w2[slot]) * slope_ref[slot, rows, :].astype(f32)).astype(low)
        dh_low[rows, :] = dh
        gb_ref[0] += jnp.sum(dh.astype(f32), axis=0, keepdims=True)
        total[rows, :] += mm_nt(dh, w1[slot])
        return carry

    lax.fori_loop(0, dz_ref.shape[0] // 256, one_part, 0)

    def one_grad(t, carry):
        rows = pl.ds(pl.multiple_of(t * 256, 256), 256)
        g2_ref[0, rows, :] = mm(dzt_ref[rows, :], act_ref[slot]).astype(low)
        g1_ref[0, rows, :] = mm(ft_ref[rows, :], dh_low[...]).astype(low)
        return carry

    lax.fori_loop(0, ft_ref.shape[0] // 256, one_grad, 0)

    lanes = pl.ds(pl.multiple_of(inner * block, block), block)

    def hop(which, slot, n):
        away, got, to = [(away_a, got_a, by_x), (away_b, got_b, by_y)][which]
        at = pl.ds(n * block, block)
        return remote(
            away.at[slot, :, at], got.at[slot, :, at], s_s.at[which, slot, n],
            r_s.at[which, slot, n], to,
        )

    def far_hop(which):
        got, to = [(far_a, by_x), (far_b, by_y)][which]
        return remote(away_f.at[which], got, f_s.at[which], f_r.at[which], to)

    for at, which, slot in ((0, 0, 0), (0, 1, 0), (1, 0, 1), (2, 1, 1)):

        @pl.when(order == at)
        def _():
            away = (away_a, away_b)[which]
            away[slot, :, lanes] = g1_ref[0, which * half : (which + 1) * half, :]

        for n in range(got_a.shape[2] // block):

            @pl.when((order == at) & (inner == n))
            def _():
                hop(which, slot, n).start()

    @pl.when((order == 0) & (inner == 0))
    def _():
        for which in range(2):
            away_f[which] = g2_ref[0, which * half : (which + 1) * half, :]
            far_hop(which).start()

    @pl.when(step == last)
    def _():
        for which in range(2):
            far_hop(which).wait()
        df_ref[...] = total[...].astype(low)
        for which in range(2):
            for slot in range(2):
                for n in range(got_a.shape[2] // block):
                    hop(which, slot, n).wait()
        wait_home(rows_out, home, h_s, h_r, n_col)


def hidden_backward(dz, f, own1, own2, rest1, rest2, acts, slopes, places, rows_out, n_col, number):
    tokens, width = f.shape
    inner = rest1[0].shape[1]
    block = min(512, inner)
    blocks = inner // block

    def number_of(s):
        j = s // blocks
        return jnp.where(j == 0, PARTS - 1, jnp.where(j == PARTS - 1, 0, j))

    def still(shape):
        return pl.BlockSpec(shape, lambda s: (0,) * len(shape))

    weight = pl.BlockSpec((1, width, block), lambda s: (number_of(s), 0, lax.rem(s, blocks)))
    landing = jax.ShapeDtypeStruct((2, width // 2, inner), low)
    grad = jax.ShapeDtypeStruct((PARTS, width, inner), low)
    vm, dma = pltpu.VMEM, pltpu.SemaphoreType.DMA
    return pl.pallas_call(
        functools.partial(hidden_back_kernel, n_col=n_col, places=places),
        grid=(PARTS * blocks,),
        in_specs=[still((tokens, width)), still((width, tokens)), still((width, tokens))]
        + [still(rows_out.shape)]
        + [ANYWHERE] * (2 + 2 * PARTS + 2 * len(acts)),
        out_specs=[
            weight,
            weight,
            pl.BlockSpec((1, 1, block), lambda s: (number_of(s), 0, lax.rem(s, blocks))),
            still((tokens, width)),
            ANYWHERE, ANYWHERE, ANYWHERE, ANYWHERE, ANYWHERE,
        ],
        out_shape=[
            grad,
            grad,
            jax.ShapeDtypeStruct((PARTS, 1, inner), f32),
            jax.ShapeDtypeStruct((tokens, width), low),
            landing,
            landing,
            jax.ShapeDtypeStruct((n_col * rows_out.shape[0], width // n_col), low),
            jax.ShapeDtypeStruct((width // 2, block), low),
            jax.ShapeDtypeStruct((width // 2, block), low),
        ],
        scratch_shapes=[
            vm((tokens, block), low),
            vm((tokens, width), f32),
            vm(landing.shape, low),
            vm(landing.shape, low),
            dma((2, 2, blocks)),
            dma((2, 2, blocks)),
            dma((n_col,)),
            dma((n_col,)),
            vm((2, width // 2, block), low),
            dma((2,)),
            dma((2,)),
            vm((2, width, block), low),
            vm((2, width, block), low),
            vm((2, tokens, block), low),
            vm((2, tokens, block), low),
            dma((4, 2)),
        ],
        compiler_params=pltpu.CompilerParams(
            vmem_limit_bytes=VMEM, collective_id=number, has_side_effects=True
        ),
        name="hidden_backward",
    )(dz, dz.T, f.T, rows_out, own1, own2, *rest1, *rest2, *acts, *slopes)


def start_kernel(
    tokens, encoder, vec_f, vec_c, *refs, n_col,
):
    weights, (x_ext, enc, all_f, all_c), full = refs[:8], refs[8:12], refs[12:20]
    (zeros, w_send, w_recv, w_own, t_send, t_recv, v_send, v_recv, z_sem, z_send, z_recv, e_send,
     e_recv, o_sem) = refs[20:]
    dp, row, col = here()
    part = lax.rem(dp, PARTS)
    twin = (dp, 1 - row, col)
    flip = [
        dp + 1 - 2 * lax.rem(dp, 2),
        dp + 2 - 4 * lax.rem(dp // 2, 2),
    ]
    by_x, by_y = (flip[0], row, col), (flip[1], row, col)
    part_x, part_y = lax.rem(flip[0], PARTS), lax.rem(flip[1], PARTS)
    shift = [lax.rem(col + k, n_col) for k in range(n_col)]
    group = [(dp, r, c) for r in (row, 1 - row) for c in shift][1:]
    meet(group + [by_x, by_y])

    wide = tokens.shape[1]
    deep = n_col * wide
    rest = deep - wide

    def chunk(index, size):
        return pl.ds(pl.multiple_of(index * size, size), size)

    to_right, to_left = (dp, row, lax.rem(col + 1, n_col)), (dp, row, lax.rem(col + n_col - 1, n_col))

    def weight_chunk(i, k):
        w = weights[i]
        if i % 4 < 3:
            return full[i].at[pl.ds(k * wide, wide), chunk(part, w.shape[1] // PARTS)]
        return full[i].at[chunk(part, w.shape[0] // PARTS), pl.ds(k * wide, wide)]

    def weight_slice(i):
        w = weights[i]
        if i % 4 < 3:
            return w.at[:, chunk(part, w.shape[1] // PARTS)]
        return w.at[chunk(part, w.shape[0] // PARTS), :]

    def enc_chunk(k):
        return enc.at[chunk(row, encoder.shape[0]), pl.ds(k * wide, wide)]

    def piece(i, k):
        if i == 8:
            return enc_chunk(k)
        return weight_chunk(i, k)

    def own_piece(i):
        return encoder if i == 8 else weight_slice(i)

    def enc_twin(k):
        return remote(own_piece(8) if k == 0 else enc_chunk(k), enc_chunk(k), e_send.at[k],
                      e_recv.at[k], twin)

    def rightward(i, h):
        src = own_piece(i) if h == 1 else piece(i, n_col + 1 - h)
        k = n_col - h
        return remote(src, piece(i, k), z_send.at[i, 0, h - 1], z_recv.at[i, k - 1], to_right)

    def leftward(i, h):
        src = own_piece(i) if h == 1 else piece(i, h - 1)
        return remote(src, piece(i, h), z_send.at[i, 1, h - 1], z_recv.at[i, h - 1], to_left)

    def right_valid(h):
        return (col >= h - 1) & (col < n_col - 1)

    def left_valid(h):
        return (col <= n_col - h) & (col > 0)

    def send_along(i, h):
        @pl.when(right_valid(h))
        def _():
            rightward(i, h).start()

        @pl.when(left_valid(h))
        def _():
            leftward(i, h).start()

    def take(i, h):
        @pl.when(col >= h)
        def _():
            rightward(i, h).wait_recv()

        @pl.when(col < n_col - h)
        def _():
            leftward(i, h).wait_recv()

    def weight_own(i):
        w = weights[i]
        place = full[i].at[pl.ds(0, wide), :] if i % 4 < 3 else full[i].at[:, pl.ds(0, wide)]
        return pltpu.make_async_copy(w, place, w_own.at[i])

    def weight_part(i, which, begin, size):
        if i % 4 < 3:
            return full[i].at[pl.ds(begin, size), chunk(which, weights[i].shape[1] // PARTS)]
        return full[i].at[chunk(which, weights[i].shape[0] // PARTS), pl.ds(begin, size)]

    def weight_plane(i, stage):
        half = rest // 2
        which, begin, size, to = [
            (part, wide, rest, by_x),
            (part, wide, rest, by_y),
            (part_x, wide, half, by_y),
            (part_y, wide + half, half, by_x),
        ][stage]
        ref = weight_part(i, which, begin, size)
        return remote(ref, ref, w_send.at[i, stage], w_recv.at[i, stage], to)

    def token_piece(j, slot):
        rows = tokens.shape[0] // n_col
        to_col = 2 * row + j // 2 + (1 - slot)
        k = lax.rem(col + n_col - lax.rem(to_col, n_col), n_col)
        src = tokens.at[pl.ds(j * rows, rows), :]
        dst = x_ext.at[slot, :, chunk(k, wide)]
        local = (row == j % 2) & (col == to_col)
        valid = to_col < n_col
        return src, dst, k, local, valid, (dp, j % 2, to_col)

    def send_tokens(slot):
        for j in range(n_col):
            src, dst, k, local, valid, to = token_piece(j, slot)

            @pl.when(valid & local)
            def _():
                pltpu.make_async_copy(src, dst, t_recv.at[slot, k]).start()

            @pl.when(valid & jnp.logical_not(local))
            def _():
                remote(src, dst, t_send.at[slot, j], t_recv.at[slot, k], to).start()

    def vectors(k):
        to = (dp, row, lax.rem(col + n_col - k, n_col))
        return [
            remote(vec_f, all_f.at[:, pl.ds(k * wide, wide)], v_send.at[0, k], v_recv.at[0, k], to),
            remote(vec_c, all_c.at[col], v_send.at[1, k], v_recv.at[1, k], to),
        ]

    own_vectors = [
        pltpu.make_async_copy(encoder, enc_chunk(0), o_sem),
        pltpu.make_async_copy(vec_f, all_f.at[:, pl.ds(0, wide)], v_recv.at[0, 0]),
        pltpu.make_async_copy(vec_c, all_c.at[col], v_recv.at[1, 0]),
    ]
    ks = range(1, n_col)
    for i in range(8):
        send_along(i, 1)
    for k in ks:
        for copy in vectors(k):
            copy.start()
    for i in range(8):
        weight_own(i).start()
    for copy in own_vectors:
        copy.start()
    enc_twin(0).start()
    for h in (1, 2):
        for i in range(8):
            take(i, h)
            send_along(i, h + 1)
    send_along(8, 1)
    send_tokens(1)
    for i in range(8):
        take(i, 3)
        weight_plane(i, 0).start()
        weight_plane(i, 1).start()
    take(8, 1)
    send_along(8, 2)
    send_tokens(0)

    @pl.when(col == 0)
    def _():
        zeros[...] = jnp.zeros_like(zeros)
        clear = pltpu.make_async_copy(zeros, x_ext.at[0], z_sem)
        clear.start()
        clear.wait()

    for i in range(8):
        weight_plane(i, 0).wait_recv()
        weight_plane(i, 2).start()
        weight_plane(i, 1).wait_recv()
        weight_plane(i, 3).start()
        if i == 3:
            take(8, 2)
            send_along(8, 3)
    take(8, 3)
    for k in ks:
        enc_twin(k).start()
    for i in range(8):
        weight_plane(i, 2).wait_recv()
        weight_plane(i, 3).wait_recv()
        weight_own(i).wait()
        for stage in range(4):
            weight_plane(i, stage).wait_send()
    for k in range(n_col):
        enc_twin(k).wait()
    for i in range(9):
        for h in ks:

            @pl.when(right_valid(h))
            def _():
                rightward(i, h).wait_send()

            @pl.when(left_valid(h))
            def _():
                leftward(i, h).wait_send()

    for copy in own_vectors:
        copy.wait()
    for k in ks:
        for copy in vectors(k):
            copy.wait()
    for slot in (1, 0):
        for j in range(n_col):
            src, dst, k, local, valid, to = token_piece(j, slot)

            @pl.when(valid & jnp.logical_not(local))
            def _():
                remote(src, dst, t_send.at[slot, j], t_recv.at[slot, k], to).wait_send()

        for k in range(n_col):
            rows = tokens.shape[0] // n_col
            came = pltpu.make_async_copy(
                tokens.at[pl.ds(0, rows), :],
                x_ext.at[slot, :, pl.ds(k * wide, wide)],
                t_recv.at[slot, k],
            )
            if slot == 1:
                came.wait()
            else:

                @pl.when(col > 0)
                def _():
                    came.wait()


def start(tokens, encoder, vec_f, vec_c, weights, n_col):
    wide = tokens.shape[1]
    deep = n_col * wide
    rows = tokens.shape[0] // n_col
    shapes = [
        jax.ShapeDtypeStruct((2, rows, deep), low),
        jax.ShapeDtypeStruct((2 * encoder.shape[0], deep), low),
        jax.ShapeDtypeStruct((vec_f.shape[0], deep), f32),
        jax.ShapeDtypeStruct((n_col,) + vec_c.shape, f32),
    ]
    for i, w in enumerate(weights):
        shapes.append(
            jax.ShapeDtypeStruct((deep, w.shape[1]) if i % 4 < 3 else (w.shape[0], deep), low)
        )
    dma = pltpu.SemaphoreType.DMA
    return pl.pallas_call(
        functools.partial(start_kernel, n_col=n_col),
        in_specs=[IN_VMEM] * 12,
        out_specs=[ANYWHERE] * 12,
        out_shape=shapes,
        scratch_shapes=[
            pltpu.VMEM((rows, deep), low),
            dma((8, 4)), dma((8, 4)), dma((8,)),
            dma((2, n_col)), dma((2, n_col)),
            dma((2, n_col)), dma((2, n_col)),
            dma, dma((9, 2, n_col - 1)), dma((9, n_col - 1)), dma((n_col,)), dma((n_col,)), dma,
        ],
        compiler_params=pltpu.CompilerParams(
            collective_id=1, has_side_effects=True, vmem_limit_bytes=VMEM
        ),
        name="start",
    )(tokens, encoder, vec_f, vec_c, *weights)


def norm_rows(x):
    center = jnp.mean(x, axis=1, keepdims=True)
    spread = jnp.mean(x * x, axis=1, keepdims=True) - center * center
    scaling = lax.rsqrt(spread + norm_epsilon)
    return (x - center) * scaling, scaling


CUT = 256


def enter_kernel(x_ref, gain, shift, a_ref, sends, recvs):
    dp, row, col = here()
    twin = (dp, 1 - row, col)
    meet([twin])
    slots, rows = x_ref.shape[:2]

    def place(slot):
        return a_ref.at[slot, pl.ds(pl.multiple_of(row * rows, rows), rows), :]

    copies = []
    for slot in reversed(range(slots)):
        for t in range(rows // CUT):
            normed, _ = norm_rows(x_ref[slot, pl.ds(t * CUT, CUT), :].astype(f32))
            begin = pl.multiple_of(row * rows + t * CUT, CUT)
            a_ref[slot, pl.ds(begin, CUT), :] = (normed * gain[...] + shift[...]).astype(low)
        copy = remote(place(slot), place(slot), sends.at[slot], recvs.at[slot], twin)
        copy.start()
        copies.append(copy)
    for copy in copies:
        copy.wait()


def enter(x_ext, gain, shift, number):
    slots, rows, deep = x_ext.shape
    return pl.pallas_call(
        enter_kernel,
        in_specs=[IN_VMEM] * 3,
        out_specs=IN_VMEM,
        out_shape=jax.ShapeDtypeStruct((slots, 2 * rows, deep), low),
        scratch_shapes=[pltpu.SemaphoreType.DMA((slots,)), pltpu.SemaphoreType.DMA((slots,))],
        compiler_params=pltpu.CompilerParams(
            collective_id=number, has_side_effects=True, vmem_limit_bytes=VMEM
        ),
        name="enter",
    )(x_ext, gain[None], shift[None])


def junction_kernel(*refs, kinds, mode):
    dp, row, col = here()
    twin = (dp, 1 - row, col)
    meet([twin])
    refs = list(refs)
    sources = []
    for kind in kinds:
        sources.append((kind, refs.pop(0), refs.pop(0) if kind != "sum" else None))
    if mode == "forward":
        x_ref, bias, gain, shift, x_out, full, away, came, s1, r1, s2, r2 = refs
    elif mode == "backward":
        res_ref, x_ref, gain, dx_out, full, stats, away, came, s1, r1, s2, r2 = refs
    else:
        out, away, came, s1, r1 = refs
    rows = came.shape[0]
    cuts = rows // CUT

    def partial(begin):
        total = None
        for kind, g, w in sources:
            part = g[pl.ds(begin, CUT), :]
            if kind == "sum":
                part = part.astype(f32)
            elif kind == "nt":
                part = mm_nt(part, w[...])
            else:
                part = mm(part, w[...])
            total = part if total is None else total + part
        return total

    sent = []
    for t in range(cuts):
        at = pl.ds(t * CUT, CUT)
        away[at, :] = partial(pl.multiple_of((1 - row) * rows + t * CUT, CUT)).astype(low)
        copy = remote(away.at[at, :], came.at[at, :], s1.at[t], r1.at[t], twin)
        copy.start()
        sent.append(copy)
    gathered = []
    sums = [0.0] * 4
    for t in range(cuts):
        at = pl.ds(t * CUT, CUT)
        begin = pl.multiple_of(row * rows + t * CUT, CUT)
        own = partial(begin)
        sent[t].wait_recv()
        total = own + came[at, :].astype(f32)
        if mode == "sum":
            out[at, :] = total.astype(low)
            continue
        if mode == "forward":
            x = x_ref[at, :].astype(f32) + (total + bias[...])
            x_out[at, :] = x
            normed, _ = norm_rows(x)
            result = (normed * gain[...] + shift[...]).astype(low)
        else:
            normed, scaling = norm_rows(x_ref[at, :].astype(f32))
            upstream = total * gain[...]
            mean_up = jnp.mean(upstream, axis=1, keepdims=True)
            mean_both = jnp.mean(upstream * normed, axis=1, keepdims=True)
            res = res_ref[at if res_ref.shape[0] == rows else pl.ds(begin, CUT), :].astype(f32)
            dx = res + scaling * (upstream - mean_up - normed * mean_both)
            dx_out[at, :] = dx.astype(dx_out.dtype)
            result = dx.astype(low)
            for i, value in enumerate((total * normed, total, result.astype(f32), res)):
                sums[i] = sums[i] + jnp.sum(value, axis=0, keepdims=True)
        full[pl.ds(begin, CUT), :] = result
        place = full.at[pl.ds(begin, CUT), :]
        copy = remote(place, place, s2.at[t], r2.at[t], twin)
        copy.start()
        gathered.append(copy)
    if mode == "backward":
        for i in range(4):
            stats[i : i + 1, :] = sums[i]
    for copy in sent:
        copy.wait_send()
    for copy in gathered:
        copy.wait()


def junction(mode, sources, others, number):
    kinds = [x[0] for x in sources]
    first = sources[0]
    tokens = first[1].shape[0]
    deep = first[1].shape[1]
    if first[0] != "sum":
        deep = first[2].shape[0 if first[0] == "nt" else 1]
    rows = tokens // 2
    flat = [x for source in sources for x in source[1:]]
    dma = pltpu.SemaphoreType.DMA((rows // CUT,))
    wide_rows = jax.ShapeDtypeStruct((rows, deep), f32)
    every = jax.ShapeDtypeStruct((tokens, deep), low)
    shapes = {
        "forward": [wide_rows, every],
        "backward": [wide_rows, every, jax.ShapeDtypeStruct((8, deep), f32)],
        "sum": [jax.ShapeDtypeStruct((rows, deep), low)],
    }[mode]
    scratch = [pltpu.VMEM((rows, deep), low), pltpu.VMEM((rows, deep), low), dma, dma]
    if mode in ("forward", "backward"):
        scratch += [dma, dma]
    args = flat + [x[None] if x.ndim == 1 else x for x in others]
    out = pl.pallas_call(
        functools.partial(junction_kernel, kinds=kinds, mode=mode),
        in_specs=[IN_VMEM] * len(args),
        out_specs=[IN_VMEM] * len(shapes),
        out_shape=shapes,
        scratch_shapes=scratch,
        compiler_params=pltpu.CompilerParams(
            collective_id=number, has_side_effects=True, vmem_limit_bytes=VMEM
        ),
        name="junction_" + mode,
    )(*args)
    return out if len(out) > 1 else out[0]


def plane_copies(full, part, parts, by_x, by_y, sends, recvs):
    size = full.shape[1]
    half = size // 2

    def copy(stage):
        which, begin, count, to = [
            (part, 0, size, by_x), (part, 0, size, by_y),
            (parts[1], 0, half, by_y), (parts[2], half, half, by_x),
        ][stage]
        ref = full.at[which, pl.ds(begin, count), :]
        return remote(ref, ref, sends.at[stage], recvs.at[stage], to)

    return copy


def with_other_bits(value, store, which, sends, recvs, partners):
    for i, partner in enumerate(partners):
        store[i, 0] = value.astype(low)
        copy = remote(
            store.at[i, 0], store.at[i, 1 + which], sends.at[which, i], recvs.at[which, i], partner
        )
        copy.start()
        copy.wait()
        value = value + store[i, 1 + which].astype(f32)
    return value


def bit_partners(n_dp):
    dp, row, col = here()
    bits = [1 << b for b in range(n_dp.bit_length() - 1)]
    return [(dp + b - 2 * b * lax.rem(dp // b, 2), row, col) for b in bits]


class PlaneSum:
    def __init__(self, src, first, mid, second, sems, n_col):
        self.src, self.first, self.mid, self.second = src, first, mid, second
        self.f_s, self.f_r, self.m_s, self.m_r = sems
        self.n_col, self.size = n_col, mid.shape[0] // n_col
        self.parts, self.ways = part_numbers(), plane()
        self.turns = [q for pair in zip(range(n_col // 2), range(n_col // 2, n_col)) for q in pair]

    def rows(self, q):
        return pl.ds(q * self.size, self.size)

    def upper(self, q):
        return 2 * q < self.n_col

    def hop(self, which, q):
        to, side = (self.ways[1], 2) if self.upper(q) else (self.ways[0], 1)
        src = self.src.at[self.parts[3] if which else self.parts[side], self.rows(q), :]
        dst = self.first.at[which, self.rows(q), :]
        return remote(src, dst, self.f_s.at[which, q], self.f_r.at[which, q], to)

    def hop2(self, q):
        to = self.ways[0] if self.upper(q) else self.ways[1]
        at = self.rows(q)
        return remote(self.mid.at[at, :], self.second.at[at, :], self.m_s.at[q], self.m_r.at[q], to)

    def start(self):
        for q in self.turns:
            self.hop(1, q).start()

    def turn(self):
        for q in self.turns:
            at = self.rows(q)
            self.hop(1, q).wait_recv()
            keep = self.parts[1] if self.upper(q) else self.parts[2]
            value = self.src[keep, at, :].astype(f32) + self.first[1, at, :].astype(f32)
            self.mid[at, :] = value.astype(low)
            self.hop2(q).start()
            self.hop(0, q).start()

    def finish(self, out):
        for q in self.turns:
            at = self.rows(q)
            self.hop(0, q).wait_recv()
            self.hop2(q).wait_recv()
            value = self.src[self.parts[0], at, :].astype(f32) + self.first[0, at, :].astype(f32)
            out[at, :] = (value + self.second[at, :].astype(f32)).astype(low)

    def end(self):
        for q in self.turns:
            self.hop(0, q).wait_send()
            self.hop(1, q).wait_send()
            self.hop2(q).wait_send()


def fold_kernel(
    dq, dk, dv, a_ext, wk, wv, res, gain, ga, enc_in,
    dy_in, o_in, wq_in, x0_in, g2, near_a, near_b, far_back_a, far_back_b, own1,
    sums, tg, stats, a_sum, b_sum, hidden0, q_own, enc_out,
    load, load_own, own_q, h_out, h_l, h_r, gb, fa, ma, sa, fb, mb, sb, away_b, came_b, away_l,
    came_l, da_got, enc_got, extra,
    l_s, lo_s, r_s, hz_s, hz_r, fa_s, fa_r, ma_s, ma_r, fb_s, fb_r, mb_s, mb_r, b_s, b_r, c_s, c_r,
    d_s, d_r, e_s, e_r, g_s, g_r, x_s, x_r,
    *, n_col, n_dp,
):
    dp, row, col = here()
    parts = part_numbers()
    part = parts[0]
    by_bit = bit_partners(n_dp)
    by_x, by_y = by_bit[:2]
    twin = (dp, 1 - row, col)
    cols = [(dp, row, lax.rem(col + k, n_col)) for k in range(n_col)]
    left = cols[n_col - 1]
    meet([twin] + by_bit + cols[1:])
    ks = range(1, n_col)
    deep = tg.shape[1]
    wide = deep // n_col
    half = near_a.shape[0]
    rows = tg.shape[0]
    cuts = rows // CUT
    window = dk.shape[0] - dq.shape[0]
    sum_a = PlaneSum(ga, fa, ma, sa, (fa_s, fa_r, ma_s, ma_r), n_col)
    sum_b = PlaneSum(gb, fb, mb, sb, (fb_s, fb_r, mb_s, mb_r), n_col)
    line = LineSum(h_out, h_l, h_r, hz_s, hz_r, cols)

    loads = []
    for i, sources in enumerate(((near_a, far_back_a), (near_b, far_back_b))):
        spot = pl.ds(i * half, half)
        for n, src in enumerate((g2.at[0, spot, :],) + sources):
            loads.append(pltpu.make_async_copy(src, load.at[n, spot, :], l_s.at[i, n]))
    load_p = pltpu.make_async_copy(own1, load_own, lo_s)
    count = dq.shape[1]
    dy, x0 = load.at[0], load.at[1, pl.ds(0, rows), :]
    o, wq = load.at[2, :, pl.ds(0, count)], load.at[2, :, pl.ds(count, count)]
    reloads = [
        pltpu.make_async_copy(src, dst, r_s.at[n])
        for n, (src, dst) in enumerate(((dy_in, dy), (x0_in, x0), (o_in, o), (wq_in, wq)))
    ]

    def enc_hop(k):
        src = enc_in.at[:, pl.ds(k * wide, wide)]
        return remote(src, enc_got.at[k - 1], e_s.at[k - 1], e_r.at[k - 1], cols[k])

    for copy in loads + [load_p]:
        copy.start()
    sum_a.start()
    for copy in loads:
        copy.wait()
    for k in range(n_col):
        at = pl.ds(k * wide, wide)
        value = load[0, at, :].astype(f32) + load[1, at, :].astype(f32)
        value = (value + load[2, at, :].astype(f32)).astype(low)
        if k:
            h_out[k - 1] = value
        else:
            own_q[...] = value
    line.begin()
    for copy in reloads:
        copy.start()

    def before(begin):
        spot = pl.ds(begin, CUT)
        return mm_nt(dk[spot, :], wk[...]) + mm_nt(dv[spot, :], wv[...])

    def exchange(away, came, sends, recvs, t):
        spot = pl.ds(t * CUT, CUT)
        return remote(away.at[spot, :], came.at[spot, :], sends.at[t], recvs.at[t], twin)

    for t in range(cuts):
        spot = pl.ds(t * CUT, CUT)
        away_b[spot, :] = before(pl.multiple_of((1 - row) * rows + t * CUT, CUT)).astype(low)
        exchange(away_b, came_b, b_s, b_r, t).start()
    for t in range(cuts):
        spot = pl.ds(t * CUT, CUT)
        own = before(pl.multiple_of(row * rows + t * CUT, CUT))
        exchange(away_b, came_b, b_s, b_r, t).wait_recv()
        came_b[spot, :] = (own + came_b[spot, :].astype(f32)).astype(low)
    da_hop = remote(came_b, da_got, d_s, d_r, left)

    @pl.when(col > 0)
    def _():
        da_hop.start()

    @pl.when(col == n_col - 1)
    def _():
        da_got[...] = jnp.zeros_like(da_got)

    sum_a.turn()
    load_p.wait()
    value = with_other_bits(load_own[...].astype(f32), extra, 0, x_s, x_r, by_bit[2:])
    hidden0[part] = value.astype(low)
    spread = plane_copies(hidden0, part, parts, by_x, by_y, g_s, g_r)
    spread(0).start()
    spread(1).start()
    line.go(2)
    for copy in reloads:
        copy.wait()

    def last(begin):
        spot = pl.ds(begin, CUT)
        later = pl.ds(window + begin, CUT)
        value = mm_nt(dq[spot, :], wq[...]) + mm_nt(dk[later, :], wk[...])
        return value + mm_nt(dv[later, :], wv[...])

    for t in range(cuts):
        spot = pl.ds(t * CUT, CUT)
        away_l[spot, :] = last(pl.multiple_of((1 - row) * rows + t * CUT, CUT)).astype(low)
        exchange(away_l, came_l, c_s, c_r, t).start()

    size = gb.shape[2] // 4
    pairs = ((window, dq), (0, dk), (0, dv), (None, o))

    def one_block(i, carry):
        lanes = pl.ds(pl.multiple_of(i * wide, wide), wide)
        for n, (begin, other) in enumerate(pairs):
            source = dy[:, lanes] if begin is None else a_ext[pl.ds(begin, other.shape[0]), lanes]
            value = mm_tn(source, other[...]).astype(low)
            for p in range(PARTS):
                gb[p, lanes, n * size : (n + 1) * size] = value[:, p * size : (p + 1) * size]
        return carry

    lax.fori_loop(0, n_col, one_block, 0)
    sum_b.start()
    line.go(1)
    for k in ks:
        enc_hop(k).start()
    for n, (_, other) in enumerate(pairs):
        sums[n : n + 1, :] = jnp.sum(other[...].astype(f32), axis=0, keepdims=True)
    sum_a.finish(a_sum)
    sum_b.turn()

    @pl.when(col < n_col - 1)
    def _():
        da_hop.wait_recv()

    totals = [0.0, 0.0]
    for t in range(cuts):
        spot = pl.ds(t * CUT, CUT)
        own = last(pl.multiple_of(row * rows + t * CUT, CUT))
        exchange(away_l, came_l, c_s, c_r, t).wait_recv()
        total = own + came_l[spot, :].astype(f32)
        after = [da_got[spot, pl.ds(deep - wide, wide)], da_got[spot, pl.ds(0, deep - wide)]]
        total = total + jnp.concatenate(after, axis=1).astype(f32)
        normed, scaling = norm_rows(x0[spot, :].astype(f32))
        upstream = total * gain[...]
        mean_up = jnp.mean(upstream, axis=1, keepdims=True)
        mean_both = jnp.mean(upstream * normed, axis=1, keepdims=True)
        dx = res[spot, :] + scaling * (upstream - mean_up - normed * mean_both)
        tg[spot, :] = dx.astype(low)
        for i, value in enumerate((total * normed, total)):
            totals[i] = totals[i] + jnp.sum(value, axis=0, keepdims=True)
    for i in range(2):
        stats[i : i + 1, :] = totals[i]
    for stage in range(2):
        spread(stage).wait_recv()
        spread(2 + stage).start()
    value = line.total(own_q[...].astype(f32))
    value = with_other_bits(value, extra, 1, x_s, x_r, by_bit[2:])
    q_own[...] = value.astype(low)
    sum_b.finish(b_sum)
    spread(2).wait_recv()
    spread(3).wait_recv()
    value = enc_in[:, pl.ds(0, wide)].astype(f32)
    for k in ks:
        enc_hop(k).wait()
        value = value + enc_got[k - 1].astype(f32)
    enc_out[...] = value
    for stage in range(4):
        spread(stage).wait_send()
    line.end()
    sum_a.end()
    sum_b.end()
    for t in range(cuts):
        exchange(away_b, came_b, b_s, b_r, t).wait_send()
        exchange(away_l, came_l, c_s, c_r, t).wait_send()

    @pl.when(col > 0)
    def _():
        da_hop.wait_send()


def fold(dq, dk, dv, a_ext, dy, o, weights, res, x0, gain, ga, enc_in, riding, n_col, n_dp):
    sd, vm, dma = jax.ShapeDtypeStruct, pltpu.VMEM, pltpu.SemaphoreType.DMA
    rows, deep = x0.shape
    wide = deep // n_col
    columns, hidden = ga.shape[2], riding[0].shape[2]
    others, cuts = n_col - 1, rows // CUT
    more = max(n_dp.bit_length() - 3, 1)
    by_rows = vm((rows, deep), low)
    plane_memory = [vm((2, deep, columns), low), vm((deep, columns), low), vm((deep, columns), low)]
    plane_sems = [dma((2, n_col)), dma((2, n_col)), dma((n_col,)), dma((n_col,))]
    wq, wk, wv = weights
    return pl.pallas_call(
        functools.partial(fold_kernel, n_col=n_col, n_dp=n_dp),
        in_specs=[IN_VMEM] * 10 + [ANYWHERE] * 10,
        out_specs=[IN_VMEM] * 8,
        out_shape=[
            sd((8, dq.shape[1]), f32),
            sd((rows, deep), low),
            sd((8, deep), f32),
            sd((deep, columns), low),
            sd((deep, columns), low),
            sd((PARTS, wide, hidden), low),
            sd((wide, hidden), low),
            sd((enc_in.shape[0], wide), f32),
        ],
        scratch_shapes=[
            vm((3, deep, hidden), low),
            vm((wide, hidden), low),
            vm((wide, hidden), low),
            vm((others, wide, hidden), low),
            vm((others, wide, hidden), low),
            vm((others, wide, hidden), low),
            vm(ga.shape, low),
            *plane_memory, *plane_memory,
            by_rows, by_rows, by_rows, by_rows, by_rows,
            vm((others, enc_in.shape[0], wide), low),
            vm((more, 3, wide, hidden) if n_dp > PARTS else (1, 3, 16, 128), low),
            dma((2, 3)), dma, dma((4,)),
            dma((2, others)), dma((2, others)),
            *plane_sems, *plane_sems,
            dma((cuts,)), dma((cuts,)), dma((cuts,)), dma((cuts,)),
            dma, dma,
            dma((others,)), dma((others,)),
            dma((4,)), dma((4,)),
            dma((2, more)), dma((2, more)),
        ],
        compiler_params=pltpu.CompilerParams(
            collective_id=21, has_side_effects=True, vmem_limit_bytes=62 * 1024 * 1024
        ),
        name="fold",
    )(dq, dk, dv, a_ext, wk, wv, res, gain[None], ga, enc_in, dy, o, wq, x0, *riding)


def finish_kernel(
    a_sum, b_sum, q_own, small, tg,
    full_a, full_b, hidden1, small_out, tg_out,
    za, za_l, za_r, zb, zb_l, zb_r, s_cur, s_got, s_z, extra,
    za_s, za_t, zb_s, zb_t, g_s, g_r, s_s, s_r, sz_s, sz_r, t_s, t_r, x_s, x_r,
    *, n_col, n_dp,
):
    dp, row, col = here()
    parts = part_numbers()
    part = parts[0]
    by_bit = bit_partners(n_dp)
    by_x, by_y = by_bit[:2]
    twin = (dp, 1 - row, col)
    cols = [(dp, row, lax.rem(col + k, n_col)) for k in range(n_col)]
    meet([twin] + [(dp, 1 - row, c[2]) for c in cols[1:]] + cols[1:] + by_bit)
    wide = a_sum.shape[0] // n_col
    ks = range(1, n_col)
    line_a = LineSum(za, za_l, za_r, za_s, za_t, cols)
    line_b = LineSum(zb, zb_l, zb_r, zb_s, zb_t, cols)

    partners = [twin] + by_bit

    def small_hop(i):
        return remote(s_cur.at[i], s_got.at[i], s_s.at[i], s_r.at[i], partners[i])

    def small_z(k):
        return remote(
            s_cur.at[len(partners), k], s_z.at[k - 1], sz_s.at[k - 1], sz_r.at[k - 1], cols[k]
        )

    def small_step(i):
        if i == 0:
            s_cur[0] = small[...]
        elif i <= len(partners):
            small_hop(i - 1).wait_recv()
            got = s_got[i - 1]
            if i == 1:
                lane = lax.broadcasted_iota(jnp.int32, got.shape, 2)
                got = jnp.where(lane < wide, got, 0.0)
            s_cur[i] = s_cur[i - 1] + got
        if i < len(partners):
            small_hop(i).start()
        elif i == len(partners):
            for k in ks:
                small_z(k).start()
        else:
            value = s_cur[len(partners), 0]
            for k in ks:
                small_z(k).wait_recv()
                value = value + s_z[k - 1]
            small_out[...] = value

    spread_q = plane_copies(hidden1, part, parts, by_x, by_y, g_s.at[0], g_r.at[0])
    spread_a = plane_copies(full_a, part, parts, by_x, by_y, g_s.at[1], g_r.at[1])
    spread_b = plane_copies(full_b, part, parts, by_x, by_y, g_s.at[2], g_r.at[2])
    spreads = (spread_q, spread_a, spread_b)

    small_step(0)
    for line, buf, whole in ((line_a, za, a_sum), (line_b, zb, b_sum)):
        for k in ks:
            buf[k - 1] = whole[pl.ds(k * wide, wide), :]
        line.begin()
    for i in range(1, len(partners)):
        small_step(i)
    hidden1[part] = q_own[...]
    spread_q(0).start()
    spread_q(1).start()
    for d in range(n_col - 2, 0, -1):
        line_a.go(d)
        line_b.go(d)
    small_step(len(partners))
    send_home(tg, tg_out, t_s, t_r, n_col)
    for i, (line, whole, full, spread) in enumerate((
        (line_a, a_sum, full_a, spread_a), (line_b, b_sum, full_b, spread_b),
    )):
        value = line.total(whole[pl.ds(0, wide), :].astype(f32))
        value = with_other_bits(value, extra, i, x_s, x_r, by_bit[2:])
        full[part] = value.astype(low)
        spread(0).start()
        spread(1).start()
    for spread in spreads:
        for stage in range(2):
            spread(stage).wait_recv()
            spread(2 + stage).start()
    small_step(len(partners) + 1)
    for spread in spreads:
        spread(2).wait_recv()
        spread(3).wait_recv()
        for stage in range(4):
            spread(stage).wait_send()
    line_a.end()
    line_b.end()
    for k in ks:
        small_z(k).wait_send()
    for i in range(len(partners)):
        small_hop(i).wait_send()
    wait_home(tg, tg_out, t_s, t_r, n_col)


def finish(a_sum, b_sum, q_own, small, tg, n_col, n_dp):
    columns = a_sum.shape[1]
    wide, hidden = q_own.shape
    steps = n_dp.bit_length()
    sd, vm, dma = jax.ShapeDtypeStruct, pltpu.VMEM, pltpu.SemaphoreType.DMA
    more = max(n_dp.bit_length() - 3, 1)
    others = n_col - 1
    return pl.pallas_call(
        functools.partial(finish_kernel, n_col=n_col, n_dp=n_dp),
        in_specs=[IN_VMEM] * 5,
        out_specs=[IN_VMEM] * 4 + [ANYWHERE],
        out_shape=[
            sd((PARTS, wide, columns), low),
            sd((PARTS, wide, columns), low),
            sd((PARTS, wide, hidden), low),
            sd(small.shape[1:], f32),
            sd((n_col * tg.shape[0], wide), low),
        ],
        scratch_shapes=[
            *[vm((others, wide, columns), low)] * 6,
            vm((steps + 1,) + small.shape, f32),
            vm((steps,) + small.shape, f32),
            vm((others,) + small.shape[1:], f32),
            vm((more, 3, wide, columns), low),
            *[dma((2, others))] * 4,
            dma((3, 4)), dma((3, 4)),
            dma((steps,)), dma((steps,)),
            dma((others,)), dma((others,)),
            dma((n_col,)), dma((n_col,)),
            dma((2, more)), dma((2, more)),
        ],
        compiler_params=pltpu.CompilerParams(
            collective_id=20, has_side_effects=True, vmem_limit_bytes=VMEM
        ),
        name="finish",
    )(a_sum, b_sum, q_own, small, tg)


def column_grads_kernel(*refs, pairs, firsts):
    count = len(pairs)
    firsts_refs, others = refs[:firsts], refs[firsts : firsts + count]
    out, sums = refs[firsts + count :]
    size = out.shape[2] // count
    for i, (which, begin) in enumerate(pairs):
        a, b = firsts_refs[which], others[i]
        value = mm_tn(a[pl.ds(begin, b.shape[0]), :], b[...]).astype(low)
        for p in range(out.shape[0]):
            out[p, :, i * size : (i + 1) * size] = value[:, p * size : (p + 1) * size]

    @pl.when(pl.program_id(0) == 0)
    def _():
        for i in range(count):
            sums[i : i + 1, :] = jnp.sum(others[i][...].astype(f32), axis=0, keepdims=True)


def column_grads_of(firsts, pairs, others):
    deep, width = firsts[0].shape[1], others[0].shape[1]
    block = 256
    return pl.pallas_call(
        functools.partial(column_grads_kernel, pairs=pairs, firsts=len(firsts)),
        grid=(deep // block,),
        in_specs=[pl.BlockSpec((x.shape[0], block), lambda i: (0, i)) for x in firsts]
        + [pl.BlockSpec(x.shape, lambda i: (0, 0)) for x in others],
        out_specs=[
            pl.BlockSpec((PARTS, block, width), lambda i: (0, i, 0)),
            pl.BlockSpec((8, width), lambda i: (0, 0)),
        ],
        out_shape=[
            jax.ShapeDtypeStruct((PARTS, deep, width), low),
            jax.ShapeDtypeStruct((8, width), f32),
        ],
        compiler_params=pltpu.CompilerParams(vmem_limit_bytes=VMEM),
        name="column_grads",
    )(*firsts, *others)


def unpack_kernel(full_a, full_b, hidden0, hidden1, *outs):
    size = full_a.shape[2] // 4
    for g, full in enumerate((full_a, full_b)):
        for i in range(4):
            value = full[0, :, i * size : (i + 1) * size].astype(f32)
            outs[4 * g + i][...] = value if i < 3 else jnp.transpose(value)
    outs[8][...] = hidden0[0].astype(f32)
    outs[9][...] = jnp.transpose(hidden1[0].astype(f32))


def unpack(full_a, full_b, hidden0, hidden1):
    parts, wide, columns = full_a.shape
    inner = hidden0.shape[2]
    size = columns // 4
    into = (pl.BlockSpec((wide, size), lambda p: (0, p)), (wide, parts * size))
    out_of = (pl.BlockSpec((size, wide), lambda p: (p, 0)), (parts * size, wide))
    layouts = [into, into, into, out_of] * 2 + [
        (pl.BlockSpec((wide, inner), lambda p: (0, p)), (wide, parts * inner)),
        (pl.BlockSpec((inner, wide), lambda p: (p, 0)), (parts * inner, wide)),
    ]
    return pl.pallas_call(
        unpack_kernel,
        grid=(parts,),
        in_specs=[
            pl.BlockSpec((1, wide, x.shape[2]), lambda p: (p, 0, 0))
            for x in (full_a, full_b, hidden0, hidden1)
        ],
        out_specs=[x[0] for x in layouts],
        out_shape=[jax.ShapeDtypeStruct(x[1], f32) for x in layouts],
        compiler_params=pltpu.CompilerParams(vmem_limit_bytes=VMEM),
        name="unpack",
    )(full_a, full_b, hidden0, hidden1)


def build_local(mesh):
    n_dp, n_col = mesh.shape["dp"], mesh.shape["col"]

    def from_col(x, k):
        return lax.ppermute(x, "col", [(i, (i - k) % n_col) for i in range(n_col)])

    def across(x, bit):
        return lax.ppermute(x, "dp", [(i, i ^ bit) for i in range(n_dp)])

    def local(
        tokens, encoder, cotangent, dec_lengths, src_lengths,
        self_norm_gain, self_norm_bias, self_query, self_key, self_value,
        self_query_bias, self_value_bias, self_out, self_out_bias,
        cross_norm_gain, cross_norm_bias, cross_query, cross_key, cross_value,
        cross_query_bias, cross_value_bias, cross_out, cross_out_bias,
        hidden_norm_gain, hidden_norm_bias, hidden_in, hidden_in_bias,
        hidden_out, hidden_out_bias,
    ):
        row, col = lax.axis_index("row"), lax.axis_index("col")
        place = lax.axis_index("dp") % PARTS
        wide = tokens.shape[1]
        chunk = tokens.shape[0] // n_col
        span = 2 * chunk

        def in_order(parts):
            stacked = jnp.stack(parts)
            return [
                lax.dynamic_index_in_dim(stacked, i ^ place, 0, keepdims=False)
                for i in range(PARTS)
            ]

        def own_columns(w, j):
            size = w.shape[1] // PARTS
            return lax.dynamic_slice_in_dim(w, (place ^ j) * size, size, 1)

        def along_col(w):
            return [from_col(own_columns(w, 0), k) for k in range(1, n_col)]

        vec_f = jnp.stack([
            self_norm_gain, self_norm_bias, self_out_bias, cross_norm_gain, cross_norm_bias,
            cross_out_bias, hidden_norm_gain, hidden_norm_bias, hidden_out_bias,
        ])
        vec_f = jnp.pad(vec_f, ((0, 7), (0, 0)))
        vec_c = jnp.concatenate(
            [self_query_bias, self_value_bias, cross_query_bias, cross_value_bias, hidden_in_bias]
        ).reshape(-1, 128)
        vec_c = jnp.pad(vec_c, ((0, -vec_c.shape[0] % 8), (0, 0)))
        weights = [
            self_query, self_key, self_value, self_out,
            cross_query, cross_key, cross_value, cross_out,
        ]
        x_ext, enc, vectors, columns, *full = start(tokens, encoder, vec_f, vec_c, weights, n_col)
        wq1, wk1, wv1, wo1, wq2, wk2, wv2, wo2 = full
        (gain1, shift1, out_bias1, gain2, shift2, out_bias2, gain3, shift3, out_bias3) = vectors[:9]
        size = self_query_bias.shape[0]

        def column_vector(start, size):
            return columns.reshape(n_col, -1)[:, start : start + size].reshape(-1)

        q_bias1 = column_vector(0, size)
        v_bias1 = column_vector(size, size)
        q_bias2 = column_vector(2 * size, size)
        v_bias2 = column_vector(3 * size, size)
        hidden_bias = column_vector(4 * size, hidden_in_bias.shape[0]).reshape(PARTS, -1)
        hidden_bias = jnp.stack(
            [lax.dynamic_index_in_dim(hidden_bias, place ^ j, 0) for j in range(PARTS)]
        )

        hidden_in, x_ext = lax.optimization_barrier((hidden_in, x_ext))
        hidden_out_t = hidden_out.T
        pieces1 = along_col(hidden_in)

        dec_ids = doc_numbers(dec_lengths, SEQ_LEN)[0]
        src_ids = doc_numbers(src_lengths, ENC)[0]
        padded = jnp.pad(dec_ids, (WIN, 0), constant_values=-1)
        key_ids = lax.dynamic_slice_in_dim(padded, col * span, WIN + span, 0)
        query_ids = key_ids[WIN:]

        scale = low(HEAD_DIM**-0.5)
        x0 = x_ext[1]
        a_ext = enter(x_ext, gain1, shift1, 2).reshape(WIN + span, -1)
        a = a_ext[WIN:]
        hidden_out_t, a_ext = lax.optimization_barrier((hidden_out_t, a_ext))
        pieces2 = along_col(hidden_out_t)
        q1 = (mm(a, wq1) + q_bias1).astype(low) * scale
        k1 = mm(a_ext, wk1).astype(low)
        v1 = (mm(a_ext, wv1) + v_bias1).astype(low)
        dma = pltpu.SemaphoreType.DMA
        dma = pltpu.SemaphoreType.DMA
        o1, lse1 = attend(q1, k1, v1, query_ids, key_ids, True)
        pieces1, o1 = lax.optimization_barrier((pieces1, o1))
        rest1 = jnp.concatenate(pieces1, axis=0)
        near1 = [across(rest1, 1), across(rest1, 2)]
        x1, c = junction("forward", [("nn", o1, wo1)], [x0, out_bias1, gain2, shift2], 3)

        pieces2, c = lax.optimization_barrier((pieces2, c))
        rest2 = jnp.concatenate(pieces2, axis=0)
        near2 = [across(rest2, 1), across(rest2, 2)]
        q2 = (mm(c, wq2) + q_bias2).astype(low) * scale
        k2 = mm(enc, wk2).astype(low)
        v2 = (mm(enc, wv2) + v_bias2).astype(low)
        o2, lse2 = attend(q2, k2, v2, query_ids, src_ids, False)
        near1, o2 = lax.optimization_barrier((near1, o2))
        far1 = across(near1[0], 2)
        x2, f = junction("forward", [("nn", o2, wo2)], [x1, out_bias2, gain3, shift3], 4)
        rests1, rests2 = [rest1, *near1], [rest2, *near2]
        act0, slope0, part_sum = hidden_forward(
            f, hidden_bias[:1], hidden_in, hidden_out_t, rests1[:1], rests2[:1], (0,), 0
        )
        near2, part_sum = lax.optimization_barrier((near2, part_sum))
        far2 = across(near2[1], 1)
        rests1, rests2 = [rest1, *near1, far1], [rest2, *near2, far2]
        act1, slope1, dz, part_sum = hidden_forward(
            f, hidden_bias[1:3], hidden_in, hidden_out_t, rests1[1:3], rests2[1:3], (1, 2), 14,
            sum_in=part_sum, cotangent=cotangent, n_col=n_col,
        )
        act2, slope2, rows_out = hidden_forward(
            f, hidden_bias[3:], hidden_in, hidden_out_t, rests1[3:], rests2[3:], (3,), 5,
            sum_in=part_sum, x=x2, bias=out_bias3,
        )
        dz = dz.reshape(span, -1)

        g1, g2, hidden_bias_grad, df, got_a, got_b, layer_out, far_a, far_b = hidden_backward(
            dz, f, hidden_in, hidden_out_t, rests1, rests2, [act0, act1, act2],
            [slope0, slope1, slope2], ((0, 0), (1, 0), (1, 1), (2, 0)), rows_out, n_col, 11,
        )
        inner = g1.shape[2]
        half = g1.shape[1] // 2
        one = ((half, inner), low)
        dx2, dyc, stats3 = junction("backward", [("sum", df)], [dz, x2, gain3], 6)

        doc = mm_nt(dyc, wo2).astype(low)
        later = ((half, inner - far_a.shape[1]), low)
        dq2, dk2, dv2, back_a, back_b, far_c, far_d = attend_back(
            q2, k2, v2, doc, o2, lse2, query_ids, src_ids, False,
            first_rider, [g1, g2, got_a, got_b], [one] * 2 + [later] * 2,
            [
                pltpu.VMEM((4, half, inner), low), pltpu.VMEM((2, half, inner), low),
                dma((4,)), dma((4,)), dma((4,)),
            ],
            12,
        )
        cross_grads, cross_columns = column_grads_of(
            [c, enc, dyc], [(0, 0), (1, 0), (1, 0), (2, 0)], [dq2, dk2, dv2, o2]
        )
        enc_back = junction("sum", [("nt", dk2, wk2), ("nt", dv2, wv2)], [], 7)
        dx1, dy, stats2 = junction("backward", [("nt", dq2, wq2)], [dx2, x1, gain2], 8)

        cross_grads, enc_back, dy = lax.optimization_barrier((cross_grads, enc_back, dy))
        do = mm_nt(dy, wo1).astype(low)
        (
            dq1, dk1, dv1, near_a, near_b, far_back_a, far_back_b, own1
        ) = attend_back(
            q1, k1, v1, do, o1, lse1, query_ids, key_ids, True,
            functools.partial(second_rider, n_col=n_col),
            [g1, g2, got_a, got_b, back_a, back_b, far_a, far_b, far_c, far_d],
            [one] * 4 + [((wide, inner), low)],
            [
                pltpu.VMEM((4, half, inner), low), pltpu.VMEM((2, half, inner), low),
                pltpu.VMEM((3, 2 * half, inner), low), pltpu.VMEM((n_col - 1, wide, inner), low),
                pltpu.VMEM((wide, inner), low), pltpu.VMEM((n_col - 1, wide, inner), low),
                pltpu.VMEM((n_col - 1, wide, inner), low),
                dma((6,)), dma((2, 3)), dma((4,)), dma((4,)),
                dma((2, n_col - 1)), dma((2, n_col - 1)), dma,
            ],
            13,
        )
        self_columns, x0_grad, stats1, a_sum, b_sum, hidden0, q_own, encoder_grad = fold(
            dq1, dk1, dv1, a_ext, dy, o1, [wq1, wk1, wv1], dx1, x0, gain1, cross_grads, enc_back,
            [g2, near_a, near_b, far_back_a, far_back_b, own1], n_col, n_dp,
        )

        feature_grads = jnp.concatenate([
            stats1[:2], stats2[2:3], stats2[:2], stats3[2:3], stats3[:2], stats3[3:4],
        ])
        feature_grads = jnp.moveaxis(feature_grads.reshape(-1, n_col, wide), 1, 0)
        column_grads = []
        for vector in (self_columns[0], self_columns[2], cross_columns[0], cross_columns[2]):
            column_grads.append(vector.reshape(n_col, -1))
        column_grads.append(
            jnp.stack(in_order([hidden_bias_grad[j] for j in range(PARTS)])).reshape(n_col, -1)
        )
        column_grads = jnp.concatenate(column_grads, axis=1).reshape(n_col, -1, 128)
        column_grads = lax.dynamic_slice_in_dim(
            jnp.concatenate([column_grads, column_grads]), col, n_col, 0
        )
        lines = -(-max(feature_grads.shape[1], column_grads.shape[1]) // 8) * 8
        small = jnp.concatenate(
            [
                jnp.pad(x, ((0, 0), (0, lines - x.shape[1]), (0, 0)))
                for x in (feature_grads, column_grads)
            ],
            axis=2,
        )
        full_a, full_b, hidden1, small, tokens_grad = finish(
            a_sum, b_sum, q_own, small, x0_grad, n_col, n_dp
        )
        grads = unpack(full_a, full_b, hidden0, hidden1)
        tokens_grad = tokens_grad.astype(f32)
        feature_grads = small[:, :wide]
        column_grads = small[:, wide:].reshape(-1)

        return (
            layer_out,
            tokens_grad,
            encoder_grad,
            feature_grads[0],
            feature_grads[1],
            grads[4],
            grads[5],
            grads[6],
            column_grads[:size],
            column_grads[size : 2 * size],
            grads[7],
            feature_grads[2],
            feature_grads[3],
            feature_grads[4],
            grads[0],
            grads[1],
            grads[2],
            column_grads[2 * size : 3 * size],
            column_grads[3 * size : 4 * size],
            grads[3],
            feature_grads[5],
            feature_grads[6],
            feature_grads[7],
            grads[8],
            column_grads[4 * size : 4 * size + hidden_in_bias.shape[0]],
            grads[9],
            feature_grads[8],
        )

    return local


def solution(mesh):
    rows = P(("dp", "row"), "col")
    features = P("col")
    columns = P(("row", "col"))
    into, out_of = P("col", "row"), P("row", "col")
    attention = (into, into, into, columns, columns, out_of, features)
    norm = (features, features)
    weights = (
        norm
        + attention
        + norm
        + attention
        + norm
        + (into, columns, out_of, features)
    )
    return jax.shard_map(
        build_local(mesh),
        mesh=mesh,
        in_specs=(rows, rows, rows, P("dp", None), P("dp", None)) + weights,
        out_specs=(rows, rows, rows) + weights,
        check_vma=False,
    )
```

```python
import functools

import jax
import jax.numpy as jnp
from jax import lax
from jax.experimental import pallas as pl
from jax.experimental.pallas import tpu as pltpu
from jax.sharding import PartitionSpec as P

D = 1024
HEAD_DIM = 64
SEQ_LEN = 4096
ENC = 1024
WIN = 1024

norm_epsilon = 1e-05
masked_fill = -1e30
low = jnp.bfloat16
f32 = jnp.float32
PARTS = 4
PAIR = 2 * HEAD_DIM
QUERY_ROWS = 256
VMEM = 56 * 1024 * 1024


def doc_numbers(lengths, positions):
    bounds = jnp.cumsum(lengths, axis=1, dtype=jnp.int32)
    places = jnp.arange(positions, dtype=jnp.int32)
    return jnp.sum(
        (places[None, :, None] >= bounds[:, None, :]).astype(jnp.int32), axis=2, dtype=jnp.int32
    )


def mm(a, b):
    return lax.dot_general(a, b, (((1,), (0,)), ((), ())), preferred_element_type=f32)


def mm_nt(a, b):
    return lax.dot_general(a, b, (((1,), (1,)), ((), ())), preferred_element_type=f32)


def mm_tn(a, b):
    return lax.dot_general(a, b, (((0,), (0,)), ((), ())), preferred_element_type=f32)


MESH = pl.DeviceIdType.MESH
ANYWHERE = pl.BlockSpec(memory_space=pl.ANY)
IN_VMEM = pl.BlockSpec(memory_space=pltpu.VMEM)


def here():
    return lax.axis_index("dp"), lax.axis_index("row"), lax.axis_index("col")


def meet(partners):
    barrier = pltpu.get_barrier_semaphore()
    for partner in partners:
        pl.semaphore_signal(barrier, inc=1, device_id=partner, device_id_type=MESH)
    pl.semaphore_wait(barrier, len(partners))


def remote(src, dst, sends, recvs, device):
    return pltpu.make_async_remote_copy(
        src_ref=src, dst_ref=dst, send_sem=sends, recv_sem=recvs, device_id=device,
        device_id_type=MESH,
    )


def home_hop(rows, home, sends, recvs, n_col, k):
    dp, row, col = here()
    wide, count = home.shape[1], rows.shape[0]
    to_row, at = col // 2, 2 * lax.rem(col, 2) + row
    src = rows.at[:, pl.ds(k * wide, wide)]
    dst = home.at[pl.ds(pl.multiple_of(at * count, count), count), :]
    copy = remote(src, dst, sends.at[k], recvs.at[at], (dp, to_row, lax.rem(col + k, n_col)))
    return copy, pltpu.make_async_copy(src, dst, recvs.at[at]), to_row == row


def send_home(rows, home, sends, recvs, n_col):
    for k in range(n_col):
        away, here_copy, same = home_hop(rows, home, sends, recvs, n_col, k)
        if k:
            away.start()
            continue

        @pl.when(same)
        def _():
            here_copy.start()

        @pl.when(jnp.logical_not(same))
        def _():
            away.start()


def wait_home(rows, home, sends, recvs, n_col):
    wide, count = home.shape[1], rows.shape[0]
    for k in range(n_col):
        away, _, same = home_hop(rows, home, sends, recvs, n_col, k)
        if k:
            away.wait_send()
        else:

            @pl.when(jnp.logical_not(same))
            def _():
                away.wait_send()

        src = rows.at[:, pl.ds(k * wide, wide)]
        pltpu.make_async_copy(src, home.at[pl.ds(k * count, count), :], recvs.at[k]).wait()


class LineSum:
    def __init__(self, buf, in_l, in_r, sends, recvs, cols):
        self.buf, self.in_l, self.in_r, self.sends, self.recvs = buf, in_l, in_r, sends, recvs
        self.cols, self.n, self.col = cols, len(cols), lax.axis_index("col")

    def right(self, d):
        return remote(
            self.buf.at[d - 1], self.in_l.at[d - 1], self.sends.at[0, d - 1],
            self.recvs.at[0, d - 1], self.cols[1],
        )

    def left(self, d):
        return remote(
            self.buf.at[self.n - d - 1], self.in_r.at[d - 1], self.sends.at[1, d - 1],
            self.recvs.at[1, d - 1], self.cols[self.n - 1],
        )

    def add(self, k, got):
        self.buf[k - 1] = (self.buf[k - 1].astype(f32) + got.astype(f32)).astype(low)

    def begin(self):
        @pl.when(self.col == 0)
        def _():
            self.in_l[0] = jnp.zeros(self.in_l.shape[1:], low)
            for d in range(self.n - 1, 0, -1):
                self.right(d).start()

        @pl.when(self.col == self.n - 1)
        def _():
            self.in_r[0] = jnp.zeros(self.in_r.shape[1:], low)
            for d in range(self.n - 1, 0, -1):
                self.left(d).start()

    def go(self, d):
        @pl.when((self.col > 0) & (self.col <= self.n - 1 - d))
        def _():
            self.right(d + 1).wait_recv()
            self.add(d, self.in_l[d])
            self.right(d).start()

        @pl.when((self.col < self.n - 1) & (self.col >= d))
        def _():
            self.left(d + 1).wait_recv()
            self.add(self.n - d, self.in_r[d])
            self.left(d).start()

    def total(self, value):
        @pl.when(self.col > 0)
        def _():
            self.right(1).wait_recv()

        @pl.when(self.col < self.n - 1)
        def _():
            self.left(1).wait_recv()

        return value + self.in_l[0].astype(f32) + self.in_r[0].astype(f32)

    def end(self):
        for d in range(1, self.n):

            @pl.when(self.col <= self.n - 1 - d)
            def _():
                self.right(d).wait_send()

            @pl.when(self.col >= d)
            def _():
                self.left(d).wait_send()


def plane():
    dp, row, col = here()
    flips = [dp + b - 2 * b * lax.rem(dp // b, 2) for b in (1, 2)]
    return (flips[0], row, col), (flips[1], row, col)


def head_masks():
    lane = lax.broadcasted_iota(jnp.int32, (1, PAIR), 1)
    first = jnp.where(lane < HEAD_DIM, 1.0, 0.0)
    return first.astype(low), (1.0 - first).astype(low), lane < HEAD_DIM


def attend_kernel(q_ref, k_ref, v_ref, qid_ref, kid_ref, o_ref, lse_ref, bias, *, span, windowed):
    rows = q_ref.shape[0]
    pairs = q_ref.shape[1] // PAIR
    step = pl.program_id(0)
    start = step * rows if windowed else 0
    if windowed:
        start = pl.multiple_of(start, rows)
    allowed = qid_ref[...] == kid_ref[0:1, pl.ds(start, span)]
    if windowed:
        at_row = lax.broadcasted_iota(jnp.int32, (rows, span), 0)
        at_key = lax.broadcasted_iota(jnp.int32, (rows, span), 1)
        allowed = allowed & (at_key > at_row) & (at_key <= at_row + WIN)
    bias[...] = jnp.where(allowed, 0.0, masked_fill)
    first, second, is_first = head_masks()

    def one_pair(p, carry):
        lanes = pl.ds(pl.multiple_of(p * PAIR, PAIR), PAIR)
        q2 = q_ref[:, lanes]
        k2 = k_ref[pl.ds(start, span), lanes]
        v2 = v_ref[pl.ds(start, span), lanes]
        outs, logs = [], []
        for mask in (first, second):
            s = mm_nt(q2 * mask, k2) + bias[...]
            top = jnp.max(s, axis=1, keepdims=True)
            e = jnp.exp(s - top)
            total = jnp.sum(e, axis=1, keepdims=True)
            outs.append(mm(e.astype(low), v2) / total)
            logs.append(top + jnp.log(total))
        o_ref[:, lanes] = jnp.where(is_first, outs[0], outs[1]).astype(low)
        stats = jnp.where(is_first, logs[0], logs[1])
        turned = jnp.transpose(stats)
        lse_ref[p, 0:1, :] = turned[0:1]
        lse_ref[p, 1:2, :] = turned[HEAD_DIM : HEAD_DIM + 1]
        return carry

    lax.fori_loop(0, pairs, one_pair, 0)


def attend(q, k, v, qid, kid, windowed):
    tokens, width = q.shape
    keys = k.shape[0]
    pairs = width // PAIR
    rows = QUERY_ROWS
    span = WIN + rows if windowed else keys
    return pl.pallas_call(
        functools.partial(attend_kernel, span=span, windowed=windowed),
        grid=(tokens // rows,),
        in_specs=[
            pl.BlockSpec((rows, width), lambda i: (i, 0)),
            pl.BlockSpec((keys, width), lambda i: (0, 0)),
            pl.BlockSpec((keys, width), lambda i: (0, 0)),
            pl.BlockSpec((rows, 1), lambda i: (i, 0)),
            pl.BlockSpec((1, keys), lambda i: (0, 0)),
        ],
        out_specs=[
            pl.BlockSpec((rows, width), lambda i: (i, 0)),
            pl.BlockSpec((pairs, 8, rows), lambda i: (0, 0, i)),
        ],
        out_shape=[
            jax.ShapeDtypeStruct((tokens, width), low),
            jax.ShapeDtypeStruct((pairs, 8, tokens), f32),
        ],
        scratch_shapes=[pltpu.VMEM((rows, span), f32)],
        compiler_params=pltpu.CompilerParams(vmem_limit_bytes=VMEM),
        name="attend",
    )(q, k, v, qid[:, None], kid[None, :])


def attend_back_kernel(*refs, span, windowed, rider, n_ins, n_outs):
    refs = list(refs)
    q_ref, k_ref, v_ref, do_ref, o_ref, lse_ref, qid_ref, kid_ref = refs[:8]
    rider_refs = refs[8 : 8 + n_ins]
    refs = refs[8 + n_ins :]
    dq_ref, dk_ref, dv_ref = refs[:3]
    rider_refs += refs[3 : 3 + n_outs]
    bias, dk_sum, dv_sum = refs[3 + n_outs : 6 + n_outs]
    rider_refs += refs[6 + n_outs :]
    rows = q_ref.shape[0]
    pairs = q_ref.shape[1] // PAIR
    step = pl.program_id(0)
    start = pl.multiple_of(step * rows, rows) if windowed else 0
    keys = pl.ds(start, span)
    begin, middle, end, later = rider(*rider_refs)

    @pl.when(step == 0)
    def _():
        begin()
        dk_sum[...] = jnp.zeros_like(dk_sum)
        dv_sum[...] = jnp.zeros_like(dv_sum)

    for at, hook in later.items():

        @pl.when(step == at)
        def _():
            hook()

    allowed = kid_ref[keys, :] == qid_ref[...]
    if windowed:
        at_key = lax.broadcasted_iota(jnp.int32, (span, rows), 0)
        at_row = lax.broadcasted_iota(jnp.int32, (span, rows), 1)
        allowed = allowed & (at_key > at_row) & (at_key <= at_row + WIN)
    bias[...] = jnp.where(allowed, 0.0, masked_fill)
    first, second, is_first = head_masks()

    def one_pair(p, carry):
        lanes = pl.ds(pl.multiple_of(p * PAIR, PAIR), PAIR)
        q2 = q_ref[:, lanes]
        k2 = k_ref[keys, lanes]
        v2 = v_ref[keys, lanes]
        do2 = do_ref[:, lanes]
        turned = jnp.transpose(do2.astype(f32) * o_ref[:, lanes].astype(f32))
        dk, dv, dqs = 0.0, 0.0, []
        for h, mask in enumerate((first, second)):
            qm, dom = q2 * mask, do2 * mask
            inner = jnp.sum(turned[h * HEAD_DIM : (h + 1) * HEAD_DIM], axis=0, keepdims=True)
            s = mm_nt(k2, qm) + bias[...]
            share = jnp.exp(s - lse_ref[p, h : h + 1, :])
            ds = (share * (mm_nt(v2, dom) - inner)).astype(low)
            dv = dv + mm(share.astype(low), dom)
            dk = dk + mm(ds, qm)
            dqs.append(mm_tn(ds, k2))
        dk_sum[keys, lanes] += dk
        dv_sum[keys, lanes] += dv
        dq_ref[:, lanes] = (jnp.where(is_first, dqs[0], dqs[1]) * HEAD_DIM**-0.5).astype(low)

        @pl.when((step == 0) & (p == 0))
        def _():
            middle()

        return carry

    lax.fori_loop(0, pairs, one_pair, 0)

    @pl.when(step == pl.num_programs(0) - 1)
    def _():
        dk_ref[...] = dk_sum[...].astype(low)
        dv_ref[...] = dv_sum[...].astype(low)
        end()


def attend_back(q, k, v, do, o, lse, qid, kid, windowed, rider, riding, shapes, scratch, number):
    tokens, width = q.shape
    keys = k.shape[0]
    pairs = width // PAIR
    rows = QUERY_ROWS
    span = WIN + rows if windowed else keys
    by_row = pl.BlockSpec((rows, width), lambda i: (i, 0))
    whole = pl.BlockSpec((keys, width), lambda i: (0, 0))
    return pl.pallas_call(
        functools.partial(
            attend_back_kernel, span=span, windowed=windowed, rider=rider, n_ins=len(riding),
            n_outs=len(shapes),
        ),
        grid=(tokens // rows,),
        in_specs=[
            by_row,
            whole,
            whole,
            by_row,
            by_row,
            pl.BlockSpec((pairs, 8, rows), lambda i: (0, 0, i)),
            pl.BlockSpec((1, rows), lambda i: (0, i)),
            pl.BlockSpec((keys, 1), lambda i: (0, 0)),
        ]
        + [ANYWHERE] * len(riding),
        out_specs=[by_row, whole, whole] + [ANYWHERE] * len(shapes),
        out_shape=[
            jax.ShapeDtypeStruct((tokens, width), low),
            jax.ShapeDtypeStruct((keys, width), low),
            jax.ShapeDtypeStruct((keys, width), low),
        ]
        + [jax.ShapeDtypeStruct(*x) for x in shapes],
        scratch_shapes=[
            pltpu.VMEM((span, rows), f32),
            pltpu.VMEM((keys, width), f32),
            pltpu.VMEM((keys, width), f32),
        ]
        + scratch,
        compiler_params=pltpu.CompilerParams(
            vmem_limit_bytes=VMEM, collective_id=number, has_side_effects=True
        ),
        name="attend_back",
    )(q, k, v, do, o, lse, qid[None, :], kid[:, None], *riding)


def first_rider(g1, g2, got_a, got_b, back_a, back_b, far_a, far_b, load, mid, l_s, s_s, r_s):
    by_x, by_y = plane()
    half = back_a.shape[0]
    up, down = pl.ds(0, half), pl.ds(half, half)
    loads = [
        pltpu.make_async_copy(src, load.at[i], l_s.at[i])
        for i, src in enumerate((g1.at[2, up, :], got_a.at[0], g1.at[1, down, :], got_b.at[0]))
    ]
    hops = [
        remote(mid.at[0], back_a, s_s.at[0], r_s.at[0], by_y),
        remote(mid.at[1], back_b, s_s.at[1], r_s.at[1], by_x),
    ]
    count = far_a.shape[1]
    lanes = pl.ds(g2.shape[2] - count, count)
    far = [
        remote(g2.at[3, up, lanes], far_a, s_s.at[2], r_s.at[2], by_x),
        remote(g2.at[3, down, lanes], far_b, s_s.at[3], r_s.at[3], by_y),
    ]

    def begin():
        meet([by_x, by_y])
        for copy in loads + far:
            copy.start()

    def middle():
        for i in range(2):
            loads[2 * i].wait()
            loads[2 * i + 1].wait()
            mid[i] = (load[2 * i].astype(f32) + load[2 * i + 1].astype(f32)).astype(low)
            hops[i].start()

    def end():
        for copy in hops + far:
            copy.wait()

    return begin, middle, end, {}


def second_rider(
    g1, g2, got_a, got_b, back_a, back_b, far_a, far_b, far_c, far_d,
    near_a, near_b, far_back_a, far_back_b, own,
    load, mid, load_z, out_z, out_own, z_l, z_r, l_s, lz_s, s_s, r_s, zs_s, zr_s, o_s,
    *, n_col,
):
    dp, row, col = here()
    by_x, by_y = plane()
    half = back_a.shape[0]
    wide = own.shape[0]
    up, down = pl.ds(0, half), pl.ds(half, half)
    loads = [
        pltpu.make_async_copy(src, load.at[i], l_s.at[i])
        for i, src in ((0, g2.at[2, up, :]), (2, g2.at[1, down, :]))
    ]
    cut = far_a.shape[1]
    for i, (one, two) in ((1, (far_a, far_c)), (3, (far_b, far_d))):
        loads += [
            pltpu.make_async_copy(one, load.at[i, :, pl.ds(0, cut)], l_s.at[i]),
            pltpu.make_async_copy(
                two, load.at[i, :, pl.ds(cut, two.shape[1])], l_s.at[4 + i // 2]
            ),
        ]
    loads_z = []
    for i, (source, got, back) in enumerate(((up, got_a, back_a), (down, got_b, back_b))):
        for n, src in enumerate((g1.at[0, source, :], got.at[1], back)):
            loads_z.append(
                pltpu.make_async_copy(src, load_z.at[n, source, :], lz_s.at[i, n])
            )
    hops = [
        remote(g2.at[1, up, :], near_a, s_s.at[0], r_s.at[0], by_x),
        remote(g2.at[2, down, :], near_b, s_s.at[1], r_s.at[1], by_y),
        remote(mid.at[0], far_back_a, s_s.at[2], r_s.at[2], by_y),
        remote(mid.at[1], far_back_b, s_s.at[3], r_s.at[3], by_x),
    ]
    cols = [(dp, row, lax.rem(col + k, n_col)) for k in range(n_col)]
    line = LineSum(out_z, z_l, z_r, zs_s, zr_s, cols)
    keep = pltpu.make_async_copy(out_own, own, o_s)

    def begin():
        meet([by_x, by_y] + cols[1:])
        for copy in loads + loads_z + hops[:2]:
            copy.start()

    def middle():
        for i in range(2):
            for n in ((0, 2, 3), (1, 4, 5))[i]:
                loads[n].wait()
            mid[i] = (load[2 * i].astype(f32) + load[2 * i + 1].astype(f32)).astype(low)
            hops[2 + i].start()
        for copy in loads_z:
            copy.wait()
        for k in range(n_col):
            at = pl.ds(k * wide, wide)
            value = load_z[0, at, :].astype(f32) + load_z[1, at, :].astype(f32)
            value = (value + load_z[2, at, :].astype(f32)).astype(low)
            if k:
                out_z[k - 1] = value
            else:
                out_own[...] = value
        line.begin()

    def end():
        out_own[...] = line.total(out_own[...].astype(f32)).astype(low)
        keep.start()
        for copy in hops + [keep]:
            copy.wait()
        line.end()

    return begin, middle, end, {2: lambda: line.go(2), 3: lambda: line.go(1)}


ROOT = 0.7978845608028654
CUBE = 0.044715


def cotangent_rider(cot, dz, c_s, c_r, d_s, d_r, *, n_col):
    dp, row, col = here()
    wide = cot.shape[1]
    rows_here = cot.shape[0] // n_col

    def piece(j):
        to_col = 2 * row + j // 2
        k = lax.rem(col + n_col - to_col, n_col)
        src = cot.at[pl.ds(j * rows_here, rows_here), :]
        dst = dz.at[j % 2, :, pl.ds(pl.multiple_of(k * wide, wide), wide)]
        local = (row == j % 2) & (col == to_col)
        return src, dst, k, local, (dp, j % 2, to_col)

    def to_twin(k):
        ref = dz.at[row, :, pl.ds(k * wide, wide)]
        return remote(ref, ref, d_s.at[k], d_r.at[k], (dp, 1 - row, col))

    def begin():
        group = [
            (dp, r, lax.rem(col + k, n_col)) for r in (row, 1 - row) for k in range(n_col)
        ]
        meet(group[1:])
        for j in range(n_col):
            src, dst, k, local, to = piece(j)

            @pl.when(local)
            def _():
                pltpu.make_async_copy(src, dst, c_r.at[k]).start()

            @pl.when(jnp.logical_not(local))
            def _():
                remote(src, dst, c_s.at[j], c_r.at[k], to).start()

    def turn():
        for k in range(n_col):
            pltpu.make_async_copy(
                cot.at[pl.ds(0, rows_here), :], dz.at[row, :, pl.ds(k * wide, wide)], c_r.at[k]
            ).wait()
            to_twin(k).start()

    def end():
        for j in range(n_col):
            src, dst, k, local, to = piece(j)

            @pl.when(jnp.logical_not(local))
            def _():
                remote(src, dst, c_s.at[j], c_r.at[k], to).wait_send()

        for k in range(n_col):
            to_twin(k).wait()

    return begin, turn, end


ORDER = (3, 1, 2, 0)


def part_numbers():
    part = lax.rem(lax.axis_index("dp"), PARTS)
    return part, part + 1 - 2 * lax.rem(part, 2), part + 2 - 4 * (part // 2), PARTS - 1 - part


def weight_copies(own, rest, j, n, to, sem):
    wide, block = own.shape[0], to.shape[1]
    inner = rest.shape[1]
    begin = pl.multiple_of(part_numbers()[j] * inner + n * block, block)
    return [
        pltpu.make_async_copy(own.at[:, pl.ds(begin, block)], to.at[pl.ds(0, wide), :], sem),
        pltpu.make_async_copy(
            rest.at[:, pl.ds(pl.multiple_of(n * block, block), block)],
            to.at[pl.ds(wide, rest.shape[0]), :],
            sem,
        ),
    ]


def hidden_kernel(*refs, numbers, opening, closing, riding, n_col):
    count = len(numbers)
    refs = list(refs)

    def take(n):
        got, refs[:n] = refs[:n], []
        return got

    f_ref, b1_ref, own1, own2 = take(4)
    rest1, rest2 = take(count), take(count)
    if not opening:
        (sum_in,) = take(1)
    if closing:
        x_ref, bias = take(2)
    if riding:
        (cot,) = take(1)
    act_ref, slope_ref = take(2)
    if riding:
        (dz,) = take(1)
    (out_ref,) = take(1)
    total, w1, w2, w_sem = take(4)
    step, steps = pl.program_id(0), pl.num_programs(0)
    dp, row, col = here()
    twin = (dp, 1 - row, col)
    block = w1.shape[2]
    blocks = rest1[0].shape[1] // block
    slot = lax.rem(step, 2)

    def fetch(s):
        for i in range(count):

            @pl.when(s // blocks == i)
            def _():
                n = lax.rem(s, blocks)
                at = lax.rem(s, 2)
                for copy in weight_copies(
                    own1, rest1[i], numbers[i], n, w1.at[at], w_sem.at[0, at]
                ) + weight_copies(own2, rest2[i], numbers[i], n, w2.at[at], w_sem.at[1, at]):
                    copy.start()

    if closing:
        away, came, s_s, s_r = take(4)
    if riding:
        begin, turn, end = cotangent_rider(cot, dz, *take(4), n_col=n_col)

    @pl.when(step == 0)
    def _():
        fetch(step)
        if opening:
            total[...] = jnp.zeros_like(total)
        else:
            total[...] = sum_in[...]
        if closing:
            meet([twin])
        if riding:
            begin()

    @pl.when(step + 1 < steps)
    def _():
        fetch(step + 1)

    for i, w in enumerate((w1, w2)):
        pltpu.make_async_copy(w.at[slot], w.at[slot], w_sem.at[i, slot]).wait()

    if riding:

        @pl.when(step == steps - 1)
        def _():
            turn()

    def one_part(t, carry):
        rows = pl.ds(pl.multiple_of(t * 256, 256), 256)
        h = mm(f_ref[rows, :], w1[slot]) + b1_ref[0]
        square = h * h
        bend = jnp.tanh(h * (ROOT + (ROOT * CUBE) * square))
        half = 0.5 + 0.5 * bend
        act = (h * half).astype(low)
        act_ref[0, rows, :] = act
        slope = half + (0.5 * h) * (1.0 - bend * bend) * (ROOT + (3.0 * ROOT * CUBE) * square)
        slope_ref[0, rows, :] = slope.astype(low)
        total[rows, :] += mm_nt(act, w2[slot])
        return carry

    lax.fori_loop(0, f_ref.shape[0] // 256, one_part, 0)

    @pl.when(step == steps - 1)
    def _():
        if riding:
            end()
        if not closing:
            out_ref[...] = total[...]
        else:
            rows = came.shape[0]
            sent = []
            for t in range(rows // CUT):
                at = pl.ds(t * CUT, CUT)
                begin = pl.multiple_of((1 - row) * rows + t * CUT, CUT)
                away[at, :] = total[pl.ds(begin, CUT), :].astype(low)
                copy = remote(away.at[at, :], came.at[at, :], s_s.at[t], s_r.at[t], twin)
                copy.start()
                sent.append(copy)
            for t in range(rows // CUT):
                at = pl.ds(t * CUT, CUT)
                begin = pl.multiple_of(row * rows + t * CUT, CUT)
                sent[t].wait()
                branch = total[pl.ds(begin, CUT), :] + came[at, :].astype(f32)
                out_ref[at, :] = (x_ref[at, :] + (branch + bias[...])).astype(low)

def hidden_forward(f, b1, own1, own2, rest1, rest2, numbers, number, sum_in=None, x=None, bias=None,
                   cotangent=None, n_col=0):
    tokens, width = f.shape
    inner = rest1[0].shape[1]
    count = len(numbers)
    block = min(512, inner)
    blocks = inner // block
    rows = tokens // 2
    opening, closing = sum_in is None, x is not None
    dma = pltpu.SemaphoreType.DMA

    def still(shape):
        return pl.BlockSpec(shape, lambda s: (0,) * len(shape))

    active = pl.BlockSpec((1, tokens, block), lambda s: (s // blocks, 0, lax.rem(s, blocks)))
    args = [f, b1, own1, own2, *rest1, *rest2]
    in_specs = [
        still((tokens, width)),
        pl.BlockSpec((1, 1, block), lambda s: (s // blocks, 0, lax.rem(s, blocks))),
    ] + [ANYWHERE] * (2 + 2 * count)
    out_specs = [active, active]
    out_shape = [jax.ShapeDtypeStruct((count, tokens, inner), low)] * 2
    scratch = [
        pltpu.VMEM((tokens, width), f32),
        pltpu.VMEM((2, width, block), low),
        pltpu.VMEM((2, width, block), low),
        dma((2, 2)),
    ]
    if not opening:
        args.append(sum_in)
        in_specs.append(still((tokens, width)))
    if closing:
        args += [x, bias[None]]
        in_specs += [still((rows, width)), still((1, width))]
        out_shape.append(jax.ShapeDtypeStruct((rows, width), low))
        scratch += [pltpu.VMEM((rows, width), low), pltpu.VMEM((rows, width), low)]
        scratch += [dma((rows // CUT,)), dma((rows // CUT,))]
    else:
        out_shape.append(jax.ShapeDtypeStruct((tokens, width), f32))
    out_specs.append(still(out_shape[-1].shape))
    if cotangent is not None:
        args.append(cotangent)
        in_specs.append(still(cotangent.shape))
        out_shape.insert(2, jax.ShapeDtypeStruct((2, rows, width), low))
        out_specs.insert(2, ANYWHERE)
        scratch += [dma((n_col,))] * 4
    params = dict(vmem_limit_bytes=VMEM)
    if closing or cotangent is not None:
        params.update(collective_id=number, has_side_effects=True)
    return pl.pallas_call(
        functools.partial(
            hidden_kernel, numbers=numbers, opening=opening, closing=closing,
            riding=cotangent is not None, n_col=n_col,
        ),
        grid=(count * blocks,),
        in_specs=in_specs,
        out_specs=out_specs,
        out_shape=out_shape,
        scratch_shapes=scratch,
        compiler_params=pltpu.CompilerParams(**params),
        name="hidden_forward",
    )(*args)


def hidden_back_kernel(
    dz_ref, dzt_ref, ft_ref, rows_out, own1, own2, *refs, n_col, places,
):
    rest1, rest2 = refs[:PARTS], refs[PARTS : 2 * PARTS]
    calls = 1 + max(p[0] for p in places)
    acts, slopes = refs[2 * PARTS : 2 * PARTS + calls], refs[2 * PARTS + calls : 2 * (PARTS + calls)]
    (
        g1_ref, g2_ref, gb_ref, df_ref, got_a, got_b, home, far_a, far_b, dh_low, total, away_a, away_b,
        s_s, r_s, h_s, h_r, away_f, f_s, f_r, w1, w2, act_ref, slope_ref, w_sem,
    ) = refs[2 * (PARTS + calls) :]
    block = g1_ref.shape[2]
    inners = rest1[0].shape[1] // block
    step = pl.program_id(0)
    last = pl.num_programs(0) - 1
    order, inner = step // inners, lax.rem(step, inners)
    slot = lax.rem(step, 2)

    def fetch(s):
        for i, j in enumerate(ORDER):

            @pl.when(s // inners == i)
            def _():
                n, at = lax.rem(s, inners), lax.rem(s, 2)
                lanes = pl.ds(pl.multiple_of(n * block, block), block)
                call, index = places[j]
                copies = weight_copies(own1, rest1[j], j, n, w1.at[at], w_sem.at[0, at])
                copies += weight_copies(own2, rest2[j], j, n, w2.at[at], w_sem.at[1, at])
                for src, to, k in ((acts, act_ref, 2), (slopes, slope_ref, 3)):
                    copies.append(
                        pltpu.make_async_copy(
                            src[call].at[index, :, lanes], to.at[at], w_sem.at[k, at]
                        )
                    )
                for copy in copies:
                    copy.start()

    by_x, by_y = plane()
    half = got_a.shape[1]
    dp, row, col = here()

    @pl.when(step == 0)
    def _():
        group = [
            (dp, r, lax.rem(col + k, n_col)) for r in (row, 1 - row) for k in range(n_col)
        ]
        meet(group[1:] + [by_x, by_y])
        total[...] = jnp.zeros_like(total)
        send_home(rows_out, home, h_s, h_r, n_col)
        fetch(step)

    @pl.when(step < last)
    def _():
        fetch(step + 1)

    gb_ref[...] = jnp.zeros_like(gb_ref)
    for i, w in enumerate((w1, w2, act_ref, slope_ref)):
        pltpu.make_async_copy(w.at[slot], w.at[slot], w_sem.at[i, slot]).wait()

    def one_part(t, carry):
        rows = pl.ds(pl.multiple_of(t * 256, 256), 256)
        dh = (mm(dz_ref[rows, :], w2[slot]) * slope_ref[slot, rows, :].astype(f32)).astype(low)
        dh_low[rows, :] = dh
        gb_ref[0] += jnp.sum(dh.astype(f32), axis=0, keepdims=True)
        total[rows, :] += mm_nt(dh, w1[slot])
        return carry

    lax.fori_loop(0, dz_ref.shape[0] // 256, one_part, 0)

    def one_grad(t, carry):
        rows = pl.ds(pl.multiple_of(t * 256, 256), 256)
        g2_ref[0, rows, :] = mm(dzt_ref[rows, :], act_ref[slot]).astype(low)
        g1_ref[0, rows, :] = mm(ft_ref[rows, :], dh_low[...]).astype(low)
        return carry

    lax.fori_loop(0, ft_ref.shape[0] // 256, one_grad, 0)

    lanes = pl.ds(pl.multiple_of(inner * block, block), block)

    def hop(which, slot, n):
        away, got, to = [(away_a, got_a, by_x), (away_b, got_b, by_y)][which]
        at = pl.ds(n * block, block)
        return remote(
            away.at[slot, :, at], got.at[slot, :, at], s_s.at[which, slot, n],
            r_s.at[which, slot, n], to,
        )

    def far_hop(which):
        got, to = [(far_a, by_x), (far_b, by_y)][which]
        return remote(away_f.at[which], got, f_s.at[which], f_r.at[which], to)

    for at, which, slot in ((0, 0, 0), (0, 1, 0), (1, 0, 1), (2, 1, 1)):

        @pl.when(order == at)
        def _():
            away = (away_a, away_b)[which]
            away[slot, :, lanes] = g1_ref[0, which * half : (which + 1) * half, :]

        for n in range(got_a.shape[2] // block):

            @pl.when((order == at) & (inner == n))
            def _():
                hop(which, slot, n).start()

    @pl.when((order == 0) & (inner == 0))
    def _():
        for which in range(2):
            away_f[which] = g2_ref[0, which * half : (which + 1) * half, :]
            far_hop(which).start()

    @pl.when(step == last)
    def _():
        for which in range(2):
            far_hop(which).wait()
        df_ref[...] = total[...].astype(low)
        for which in range(2):
            for slot in range(2):
                for n in range(got_a.shape[2] // block):
                    hop(which, slot, n).wait()
        wait_home(rows_out, home, h_s, h_r, n_col)


def hidden_backward(dz, f, own1, own2, rest1, rest2, acts, slopes, places, rows_out, n_col, number):
    tokens, width = f.shape
    inner = rest1[0].shape[1]
    block = min(512, inner)
    blocks = inner // block

    def number_of(s):
        j = s // blocks
        return jnp.where(j == 0, PARTS - 1, jnp.where(j == PARTS - 1, 0, j))

    def still(shape):
        return pl.BlockSpec(shape, lambda s: (0,) * len(shape))

    weight = pl.BlockSpec((1, width, block), lambda s: (number_of(s), 0, lax.rem(s, blocks)))
    landing = jax.ShapeDtypeStruct((2, width // 2, inner), low)
    grad = jax.ShapeDtypeStruct((PARTS, width, inner), low)
    vm, dma = pltpu.VMEM, pltpu.SemaphoreType.DMA
    return pl.pallas_call(
        functools.partial(hidden_back_kernel, n_col=n_col, places=places),
        grid=(PARTS * blocks,),
        in_specs=[still((tokens, width)), still((width, tokens)), still((width, tokens))]
        + [still(rows_out.shape)]
        + [ANYWHERE] * (2 + 2 * PARTS + 2 * len(acts)),
        out_specs=[
            weight,
            weight,
            pl.BlockSpec((1, 1, block), lambda s: (number_of(s), 0, lax.rem(s, blocks))),
            still((tokens, width)),
            ANYWHERE, ANYWHERE, ANYWHERE, ANYWHERE, ANYWHERE,
        ],
        out_shape=[
            grad,
            grad,
            jax.ShapeDtypeStruct((PARTS, 1, inner), f32),
            jax.ShapeDtypeStruct((tokens, width), low),
            landing,
            landing,
            jax.ShapeDtypeStruct((n_col * rows_out.shape[0], width // n_col), low),
            jax.ShapeDtypeStruct((width // 2, block), low),
            jax.ShapeDtypeStruct((width // 2, block), low),
        ],
        scratch_shapes=[
            vm((tokens, block), low),
            vm((tokens, width), f32),
            vm(landing.shape, low),
            vm(landing.shape, low),
            dma((2, 2, blocks)),
            dma((2, 2, blocks)),
            dma((n_col,)),
            dma((n_col,)),
            vm((2, width // 2, block), low),
            dma((2,)),
            dma((2,)),
            vm((2, width, block), low),
            vm((2, width, block), low),
            vm((2, tokens, block), low),
            vm((2, tokens, block), low),
            dma((4, 2)),
        ],
        compiler_params=pltpu.CompilerParams(
            vmem_limit_bytes=VMEM, collective_id=number, has_side_effects=True
        ),
        name="hidden_backward",
    )(dz, dz.T, f.T, rows_out, own1, own2, *rest1, *rest2, *acts, *slopes)


def start_kernel(
    tokens, encoder, vec_f, vec_c, *refs, n_col,
):
    weights, (x_ext, enc, all_f, all_c), full = refs[:8], refs[8:12], refs[12:20]
    (zeros, w_send, w_recv, w_own, t_send, t_recv, v_send, v_recv, z_sem, z_send, z_recv, e_send,
     e_recv, o_sem) = refs[20:]
    dp, row, col = here()
    part = lax.rem(dp, PARTS)
    twin = (dp, 1 - row, col)
    flip = [
        dp + 1 - 2 * lax.rem(dp, 2),
        dp + 2 - 4 * lax.rem(dp // 2, 2),
    ]
    by_x, by_y = (flip[0], row, col), (flip[1], row, col)
    part_x, part_y = lax.rem(flip[0], PARTS), lax.rem(flip[1], PARTS)
    shift = [lax.rem(col + k, n_col) for k in range(n_col)]
    group = [(dp, r, c) for r in (row, 1 - row) for c in shift][1:]
    meet(group + [by_x, by_y])

    wide = tokens.shape[1]
    deep = n_col * wide
    rest = deep - wide

    def chunk(index, size):
        return pl.ds(pl.multiple_of(index * size, size), size)

    to_right, to_left = (dp, row, lax.rem(col + 1, n_col)), (dp, row, lax.rem(col + n_col - 1, n_col))

    def weight_chunk(i, k):
        w = weights[i]
        if i % 4 < 3:
            return full[i].at[pl.ds(k * wide, wide), chunk(part, w.shape[1] // PARTS)]
        return full[i].at[chunk(part, w.shape[0] // PARTS), pl.ds(k * wide, wide)]

    def weight_slice(i):
        w = weights[i]
        if i % 4 < 3:
            return w.at[:, chunk(part, w.shape[1] // PARTS)]
        return w.at[chunk(part, w.shape[0] // PARTS), :]

    def enc_chunk(k):
        return enc.at[chunk(row, encoder.shape[0]), pl.ds(k * wide, wide)]

    def piece(i, k):
        if i == 8:
            return enc_chunk(k)
        return weight_chunk(i, k)

    def own_piece(i):
        return encoder if i == 8 else weight_slice(i)

    def enc_twin(k):
        return remote(own_piece(8) if k == 0 else enc_chunk(k), enc_chunk(k), e_send.at[k],
                      e_recv.at[k], twin)

    def rightward(i, h):
        src = own_piece(i) if h == 1 else piece(i, n_col + 1 - h)
        k = n_col - h
        return remote(src, piece(i, k), z_send.at[i, 0, h - 1], z_recv.at[i, k - 1], to_right)

    def leftward(i, h):
        src = own_piece(i) if h == 1 else piece(i, h - 1)
        return remote(src, piece(i, h), z_send.at[i, 1, h - 1], z_recv.at[i, h - 1], to_left)

    def right_valid(h):
        return (col >= h - 1) & (col < n_col - 1)

    def left_valid(h):
        return (col <= n_col - h) & (col > 0)

    def send_along(i, h):
        @pl.when(right_valid(h))
        def _():
            rightward(i, h).start()

        @pl.when(left_valid(h))
        def _():
            leftward(i, h).start()

    def take(i, h):
        @pl.when(col >= h)
        def _():
            rightward(i, h).wait_recv()

        @pl.when(col < n_col - h)
        def _():
            leftward(i, h).wait_recv()

    def weight_own(i):
        w = weights[i]
        place = full[i].at[pl.ds(0, wide), :] if i % 4 < 3 else full[i].at[:, pl.ds(0, wide)]
        return pltpu.make_async_copy(w, place, w_own.at[i])

    def weight_part(i, which, begin, size):
        if i % 4 < 3:
            return full[i].at[pl.ds(begin, size), chunk(which, weights[i].shape[1] // PARTS)]
        return full[i].at[chunk(which, weights[i].shape[0] // PARTS), pl.ds(begin, size)]

    def weight_plane(i, stage):
        half = rest // 2
        which, begin, size, to = [
            (part, wide, rest, by_x),
            (part, wide, rest, by_y),
            (part_x, wide, half, by_y),
            (part_y, wide + half, half, by_x),
        ][stage]
        ref = weight_part(i, which, begin, size)
        return remote(ref, ref, w_send.at[i, stage], w_recv.at[i, stage], to)

    def token_piece(j, slot):
        rows = tokens.shape[0] // n_col
        to_col = 2 * row + j // 2 + (1 - slot)
        k = lax.rem(col + n_col - lax.rem(to_col, n_col), n_col)
        src = tokens.at[pl.ds(j * rows, rows), :]
        dst = x_ext.at[slot, :, chunk(k, wide)]
        local = (row == j % 2) & (col == to_col)
        valid = to_col < n_col
        return src, dst, k, local, valid, (dp, j % 2, to_col)

    def send_tokens(slot):
        for j in range(n_col):
            src, dst, k, local, valid, to = token_piece(j, slot)

            @pl.when(valid & local)
            def _():
                pltpu.make_async_copy(src, dst, t_recv.at[slot, k]).start()

            @pl.when(valid & jnp.logical_not(local))
            def _():
                remote(src, dst, t_send.at[slot, j], t_recv.at[slot, k], to).start()

    def vectors(k):
        to = (dp, row, lax.rem(col + n_col - k, n_col))
        return [
            remote(vec_f, all_f.at[:, pl.ds(k * wide, wide)], v_send.at[0, k], v_recv.at[0, k], to),
            remote(vec_c, all_c.at[col], v_send.at[1, k], v_recv.at[1, k], to),
        ]

    own_vectors = [
        pltpu.make_async_copy(encoder, enc_chunk(0), o_sem),
        pltpu.make_async_copy(vec_f, all_f.at[:, pl.ds(0, wide)], v_recv.at[0, 0]),
        pltpu.make_async_copy(vec_c, all_c.at[col], v_recv.at[1, 0]),
    ]
    ks = range(1, n_col)
    for i in range(8):
        send_along(i, 1)
    for k in ks:
        for copy in vectors(k):
            copy.start()
    for i in range(8):
        weight_own(i).start()
    for copy in own_vectors:
        copy.start()
    enc_twin(0).start()
    for h in (1, 2):
        for i in range(8):
            take(i, h)
            send_along(i, h + 1)
    send_along(8, 1)
    send_tokens(1)
    for i in range(8):
        take(i, 3)
        weight_plane(i, 0).start()
        weight_plane(i, 1).start()
    take(8, 1)
    send_along(8, 2)
    send_tokens(0)

    @pl.when(col == 0)
    def _():
        zeros[...] = jnp.zeros_like(zeros)
        clear = pltpu.make_async_copy(zeros, x_ext.at[0], z_sem)
        clear.start()
        clear.wait()

    for i in range(8):
        weight_plane(i, 0).wait_recv()
        weight_plane(i, 2).start()
        weight_plane(i, 1).wait_recv()
        weight_plane(i, 3).start()
        if i == 3:
            take(8, 2)
            send_along(8, 3)
    take(8, 3)
    for k in ks:
        enc_twin(k).start()
    for i in range(8):
        weight_plane(i, 2).wait_recv()
        weight_plane(i, 3).wait_recv()
        weight_own(i).wait()
        for stage in range(4):
            weight_plane(i, stage).wait_send()
    for k in range(n_col):
        enc_twin(k).wait()
    for i in range(9):
        for h in ks:

            @pl.when(right_valid(h))
            def _():
                rightward(i, h).wait_send()

            @pl.when(left_valid(h))
            def _():
                leftward(i, h).wait_send()

    for copy in own_vectors:
        copy.wait()
    for k in ks:
        for copy in vectors(k):
            copy.wait()
    for slot in (1, 0):
        for j in range(n_col):
            src, dst, k, local, valid, to = token_piece(j, slot)

            @pl.when(valid & jnp.logical_not(local))
            def _():
                remote(src, dst, t_send.at[slot, j], t_recv.at[slot, k], to).wait_send()

        for k in range(n_col):
            rows = tokens.shape[0] // n_col
            came = pltpu.make_async_copy(
                tokens.at[pl.ds(0, rows), :],
                x_ext.at[slot, :, pl.ds(k * wide, wide)],
                t_recv.at[slot, k],
            )
            if slot == 1:
                came.wait()
            else:

                @pl.when(col > 0)
                def _():
                    came.wait()


def start(tokens, encoder, vec_f, vec_c, weights, n_col):
    wide = tokens.shape[1]
    deep = n_col * wide
    rows = tokens.shape[0] // n_col
    shapes = [
        jax.ShapeDtypeStruct((2, rows, deep), low),
        jax.ShapeDtypeStruct((2 * encoder.shape[0], deep), low),
        jax.ShapeDtypeStruct((vec_f.shape[0], deep), f32),
        jax.ShapeDtypeStruct((n_col,) + vec_c.shape, f32),
    ]
    for i, w in enumerate(weights):
        shapes.append(
            jax.ShapeDtypeStruct((deep, w.shape[1]) if i % 4 < 3 else (w.shape[0], deep), low)
        )
    dma = pltpu.SemaphoreType.DMA
    return pl.pallas_call(
        functools.partial(start_kernel, n_col=n_col),
        in_specs=[IN_VMEM] * 12,
        out_specs=[ANYWHERE] * 12,
        out_shape=shapes,
        scratch_shapes=[
            pltpu.VMEM((rows, deep), low),
            dma((8, 4)), dma((8, 4)), dma((8,)),
            dma((2, n_col)), dma((2, n_col)),
            dma((2, n_col)), dma((2, n_col)),
            dma, dma((9, 2, n_col - 1)), dma((9, n_col - 1)), dma((n_col,)), dma((n_col,)), dma,
        ],
        compiler_params=pltpu.CompilerParams(
            collective_id=1, has_side_effects=True, vmem_limit_bytes=VMEM
        ),
        name="start",
    )(tokens, encoder, vec_f, vec_c, *weights)


def norm_rows(x):
    center = jnp.mean(x, axis=1, keepdims=True)
    spread = jnp.mean(x * x, axis=1, keepdims=True) - center * center
    scaling = lax.rsqrt(spread + norm_epsilon)
    return (x - center) * scaling, scaling


CUT = 256


def enter_kernel(x_ref, gain, shift, a_ref, sends, recvs):
    dp, row, col = here()
    twin = (dp, 1 - row, col)
    meet([twin])
    slots, rows = x_ref.shape[:2]

    def place(slot):
        return a_ref.at[slot, pl.ds(pl.multiple_of(row * rows, rows), rows), :]

    copies = []
    for slot in reversed(range(slots)):
        for t in range(rows // CUT):
            normed, _ = norm_rows(x_ref[slot, pl.ds(t * CUT, CUT), :].astype(f32))
            begin = pl.multiple_of(row * rows + t * CUT, CUT)
            a_ref[slot, pl.ds(begin, CUT), :] = (normed * gain[...] + shift[...]).astype(low)
        copy = remote(place(slot), place(slot), sends.at[slot], recvs.at[slot], twin)
        copy.start()
        copies.append(copy)
    for copy in copies:
        copy.wait()


def enter(x_ext, gain, shift, number):
    slots, rows, deep = x_ext.shape
    return pl.pallas_call(
        enter_kernel,
        in_specs=[IN_VMEM] * 3,
        out_specs=IN_VMEM,
        out_shape=jax.ShapeDtypeStruct((slots, 2 * rows, deep), low),
        scratch_shapes=[pltpu.SemaphoreType.DMA((slots,)), pltpu.SemaphoreType.DMA((slots,))],
        compiler_params=pltpu.CompilerParams(
            collective_id=number, has_side_effects=True, vmem_limit_bytes=VMEM
        ),
        name="enter",
    )(x_ext, gain[None], shift[None])


def junction_kernel(*refs, kinds, mode, then):
    dp, row, col = here()
    twin = (dp, 1 - row, col)
    meet([twin])
    refs = list(refs)
    sources = []
    for kind in kinds:
        sources.append((kind, refs.pop(0), refs.pop(0) if kind != "sum" else None))
    if then:
        then_w, then_b = refs.pop(0), refs.pop(0)
    if mode == "forward":
        x_ref, bias, gain, shift, x_out, full, *refs = refs
    elif mode == "backward":
        res_ref, x_ref, gain, dx_out, full, stats, *refs = refs
    if mode != "sum":
        if then:
            then_out = refs.pop(0)
        away, came, s1, r1, s2, r2 = refs
    else:
        out, away, came, s1, r1 = refs
    rows = came.shape[0]
    cuts = rows // CUT

    def follow(begin):
        at = pl.ds(begin, CUT)
        if then == "queries":
            value = (mm(full[at, :], then_w[...]) + then_b[...]).astype(low)
            then_out[at, :] = value * low(HEAD_DIM**-0.5)
        elif then:
            then_out[at, :] = mm_nt(full[at, :], then_w[...]).astype(low)

    def partial(begin):
        total = None
        for kind, g, w in sources:
            part = g[pl.ds(begin, CUT), :]
            if kind == "sum":
                part = part.astype(f32)
            elif kind == "nt":
                part = mm_nt(part, w[...])
            else:
                part = mm(part, w[...])
            total = part if total is None else total + part
        return total

    sent = []
    for t in range(cuts):
        at = pl.ds(t * CUT, CUT)
        away[at, :] = partial(pl.multiple_of((1 - row) * rows + t * CUT, CUT)).astype(low)
        copy = remote(away.at[at, :], came.at[at, :], s1.at[t], r1.at[t], twin)
        copy.start()
        sent.append(copy)
    gathered = []
    sums = [0.0] * 4
    for t in range(cuts):
        at = pl.ds(t * CUT, CUT)
        begin = pl.multiple_of(row * rows + t * CUT, CUT)
        own = partial(begin)
        sent[t].wait_recv()
        total = own + came[at, :].astype(f32)
        if mode == "sum":
            out[at, :] = total.astype(low)
            continue
        if mode == "forward":
            x = x_ref[at, :].astype(f32) + (total + bias[...])
            x_out[at, :] = x
            normed, _ = norm_rows(x)
            result = (normed * gain[...] + shift[...]).astype(low)
        else:
            normed, scaling = norm_rows(x_ref[at, :].astype(f32))
            upstream = total * gain[...]
            mean_up = jnp.mean(upstream, axis=1, keepdims=True)
            mean_both = jnp.mean(upstream * normed, axis=1, keepdims=True)
            res = res_ref[at if res_ref.shape[0] == rows else pl.ds(begin, CUT), :].astype(f32)
            dx = res + scaling * (upstream - mean_up - normed * mean_both)
            dx_out[at, :] = dx.astype(dx_out.dtype)
            result = dx.astype(low)
            for i, value in enumerate((total * normed, total, result.astype(f32), res)):
                sums[i] = sums[i] + jnp.sum(value, axis=0, keepdims=True)
        full[pl.ds(begin, CUT), :] = result
        place = full.at[pl.ds(begin, CUT), :]
        copy = remote(place, place, s2.at[t], r2.at[t], twin)
        copy.start()
        gathered.append(copy)
        follow(begin)
    if mode == "backward":
        for i in range(4):
            stats[i : i + 1, :] = sums[i]
    for copy in sent:
        copy.wait_send()
    for t, copy in enumerate(gathered):
        copy.wait()
        follow(pl.multiple_of((1 - row) * rows + t * CUT, CUT))


def junction(mode, sources, others, number, then=None):
    kinds = [x[0] for x in sources]
    first = sources[0]
    tokens = first[1].shape[0]
    deep = first[1].shape[1]
    if first[0] != "sum":
        deep = first[2].shape[0 if first[0] == "nt" else 1]
    rows = tokens // 2
    flat = [x for source in sources for x in source[1:]]
    dma = pltpu.SemaphoreType.DMA((rows // CUT,))
    wide_rows = jax.ShapeDtypeStruct((rows, deep), f32)
    every = jax.ShapeDtypeStruct((tokens, deep), low)
    shapes = {
        "forward": [wide_rows, every],
        "backward": [wide_rows, every, jax.ShapeDtypeStruct((8, deep), f32)],
        "sum": [jax.ShapeDtypeStruct((rows, deep), low)],
    }[mode]
    scratch = [pltpu.VMEM((rows, deep), low), pltpu.VMEM((rows, deep), low), dma, dma]
    if mode in ("forward", "backward"):
        scratch += [dma, dma]
    if then:
        columns = then[1].shape[1 if then[0] == "queries" else 0]
        shapes.append(jax.ShapeDtypeStruct((tokens, columns), low))
        others = [*then[1:], *others]
    args = flat + [x[None] if x.ndim == 1 else x for x in others]
    out = pl.pallas_call(
        functools.partial(
            junction_kernel, kinds=kinds, mode=mode, then=then[0] if then else None
        ),
        in_specs=[IN_VMEM] * len(args),
        out_specs=[IN_VMEM] * len(shapes),
        out_shape=shapes,
        scratch_shapes=scratch,
        compiler_params=pltpu.CompilerParams(
            collective_id=number, has_side_effects=True, vmem_limit_bytes=VMEM
        ),
        name="junction_" + mode,
    )(*args)
    return out if len(out) > 1 else out[0]


def plane_copies(full, part, parts, by_x, by_y, sends, recvs):
    size = full.shape[1]
    half = size // 2

    def copy(stage):
        which, begin, count, to = [
            (part, 0, size, by_x), (part, 0, size, by_y),
            (parts[1], 0, half, by_y), (parts[2], half, half, by_x),
        ][stage]
        ref = full.at[which, pl.ds(begin, count), :]
        return remote(ref, ref, sends.at[stage], recvs.at[stage], to)

    return copy


def with_other_bits(value, store, which, sends, recvs, partners):
    for i, partner in enumerate(partners):
        store[i, 0] = value.astype(low)
        copy = remote(
            store.at[i, 0], store.at[i, 1 + which], sends.at[which, i], recvs.at[which, i], partner
        )
        copy.start()
        copy.wait()
        value = value + store[i, 1 + which].astype(f32)
    return value


def bit_partners(n_dp):
    dp, row, col = here()
    bits = [1 << b for b in range(n_dp.bit_length() - 1)]
    return [(dp + b - 2 * b * lax.rem(dp // b, 2), row, col) for b in bits]


class PlaneSum:
    def __init__(self, src, first, mid, second, sems, n_col):
        self.src, self.first, self.mid, self.second = src, first, mid, second
        self.f_s, self.f_r, self.m_s, self.m_r = sems
        self.n_col, self.size = n_col, mid.shape[0] // n_col
        self.parts, self.ways = part_numbers(), plane()
        self.turns = [q for pair in zip(range(n_col // 2), range(n_col // 2, n_col)) for q in pair]

    def rows(self, q):
        return pl.ds(q * self.size, self.size)

    def upper(self, q):
        return 2 * q < self.n_col

    def hop(self, which, q):
        to, side = (self.ways[1], 2) if self.upper(q) else (self.ways[0], 1)
        src = self.src.at[self.parts[3] if which else self.parts[side], self.rows(q), :]
        dst = self.first.at[which, self.rows(q), :]
        return remote(src, dst, self.f_s.at[which, q], self.f_r.at[which, q], to)

    def hop2(self, q):
        to = self.ways[0] if self.upper(q) else self.ways[1]
        at = self.rows(q)
        return remote(self.mid.at[at, :], self.second.at[at, :], self.m_s.at[q], self.m_r.at[q], to)

    def start(self):
        for q in self.turns:
            self.hop(1, q).start()

    def turn(self):
        for q in self.turns:
            at = self.rows(q)
            self.hop(1, q).wait_recv()
            keep = self.parts[1] if self.upper(q) else self.parts[2]
            value = self.src[keep, at, :].astype(f32) + self.first[1, at, :].astype(f32)
            self.mid[at, :] = value.astype(low)
            self.hop2(q).start()
            self.hop(0, q).start()

    def finish(self, out):
        for q in self.turns:
            at = self.rows(q)
            self.hop(0, q).wait_recv()
            self.hop2(q).wait_recv()
            value = self.src[self.parts[0], at, :].astype(f32) + self.first[0, at, :].astype(f32)
            out[at, :] = (value + self.second[at, :].astype(f32)).astype(low)

    def end(self):
        for q in self.turns:
            self.hop(0, q).wait_send()
            self.hop(1, q).wait_send()
            self.hop2(q).wait_send()


def fold_kernel(
    dq, dk, dv, a_ext, wk, wv, res, gain, ga, enc_in,
    dy_in, o_in, wq_in, x0_in, g2, near_a, near_b, far_back_a, far_back_b, own1,
    sums, tg, stats, a_sum, b_sum, hidden0, q_own, enc_out,
    load, load_own, own_q, h_out, h_l, h_r, gb, fa, ma, sa, fb, mb, sb, away_b, came_b, away_l,
    came_l, da_got, enc_got, extra,
    l_s, lo_s, r_s, hz_s, hz_r, fa_s, fa_r, ma_s, ma_r, fb_s, fb_r, mb_s, mb_r, b_s, b_r, c_s, c_r,
    d_s, d_r, e_s, e_r, g_s, g_r, x_s, x_r,
    *, n_col, n_dp,
):
    dp, row, col = here()
    parts = part_numbers()
    part = parts[0]
    by_bit = bit_partners(n_dp)
    by_x, by_y = by_bit[:2]
    twin = (dp, 1 - row, col)
    cols = [(dp, row, lax.rem(col + k, n_col)) for k in range(n_col)]
    left = cols[n_col - 1]
    meet([twin] + by_bit + cols[1:])
    ks = range(1, n_col)
    deep = tg.shape[1]
    wide = deep // n_col
    half = near_a.shape[0]
    rows = tg.shape[0]
    cuts = rows // CUT
    window = dk.shape[0] - dq.shape[0]
    sum_a = PlaneSum(ga, fa, ma, sa, (fa_s, fa_r, ma_s, ma_r), n_col)
    sum_b = PlaneSum(gb, fb, mb, sb, (fb_s, fb_r, mb_s, mb_r), n_col)
    line = LineSum(h_out, h_l, h_r, hz_s, hz_r, cols)

    loads = []
    for i, sources in enumerate(((near_a, far_back_a), (near_b, far_back_b))):
        spot = pl.ds(i * half, half)
        for n, src in enumerate((g2.at[0, spot, :],) + sources):
            loads.append(pltpu.make_async_copy(src, load.at[n, spot, :], l_s.at[i, n]))
    load_p = pltpu.make_async_copy(own1, load_own, lo_s)
    count = dq.shape[1]
    dy, x0 = load.at[0], load.at[1, pl.ds(0, rows), :]
    o, wq = load.at[2, :, pl.ds(0, count)], load.at[2, :, pl.ds(count, count)]
    reloads = [
        pltpu.make_async_copy(src, dst, r_s.at[n])
        for n, (src, dst) in enumerate(((dy_in, dy), (x0_in, x0), (o_in, o), (wq_in, wq)))
    ]

    def enc_hop(k):
        src = enc_in.at[:, pl.ds(k * wide, wide)]
        return remote(src, enc_got.at[k - 1], e_s.at[k - 1], e_r.at[k - 1], cols[k])

    for copy in loads + [load_p]:
        copy.start()
    sum_a.start()
    for copy in loads:
        copy.wait()
    for k in range(n_col):
        at = pl.ds(k * wide, wide)
        value = load[0, at, :].astype(f32) + load[1, at, :].astype(f32)
        value = (value + load[2, at, :].astype(f32)).astype(low)
        if k:
            h_out[k - 1] = value
        else:
            own_q[...] = value
    line.begin()
    for copy in reloads:
        copy.start()

    def before(begin):
        spot = pl.ds(begin, CUT)
        return mm_nt(dk[spot, :], wk[...]) + mm_nt(dv[spot, :], wv[...])

    def exchange(away, came, sends, recvs, t):
        spot = pl.ds(t * CUT, CUT)
        return remote(away.at[spot, :], came.at[spot, :], sends.at[t], recvs.at[t], twin)

    for t in range(cuts):
        spot = pl.ds(t * CUT, CUT)
        away_b[spot, :] = before(pl.multiple_of((1 - row) * rows + t * CUT, CUT)).astype(low)
        exchange(away_b, came_b, b_s, b_r, t).start()
    for t in range(cuts):
        spot = pl.ds(t * CUT, CUT)
        own = before(pl.multiple_of(row * rows + t * CUT, CUT))
        exchange(away_b, came_b, b_s, b_r, t).wait_recv()
        came_b[spot, :] = (own + came_b[spot, :].astype(f32)).astype(low)
    da_hop = remote(came_b, da_got, d_s, d_r, left)

    @pl.when(col > 0)
    def _():
        da_hop.start()

    @pl.when(col == n_col - 1)
    def _():
        da_got[...] = jnp.zeros_like(da_got)

    sum_a.turn()
    load_p.wait()
    value = with_other_bits(load_own[...].astype(f32), extra, 0, x_s, x_r, by_bit[2:])
    hidden0[part] = value.astype(low)
    spread = plane_copies(hidden0, part, parts, by_x, by_y, g_s, g_r)
    spread(0).start()
    spread(1).start()
    line.go(2)
    for copy in reloads:
        copy.wait()

    def last(begin):
        spot = pl.ds(begin, CUT)
        later = pl.ds(window + begin, CUT)
        value = mm_nt(dq[spot, :], wq[...]) + mm_nt(dk[later, :], wk[...])
        return value + mm_nt(dv[later, :], wv[...])

    for t in range(cuts):
        spot = pl.ds(t * CUT, CUT)
        away_l[spot, :] = last(pl.multiple_of((1 - row) * rows + t * CUT, CUT)).astype(low)
        exchange(away_l, came_l, c_s, c_r, t).start()

    size = gb.shape[2] // 4
    pairs = ((window, dq), (0, dk), (0, dv), (None, o))

    def one_block(i, carry):
        lanes = pl.ds(pl.multiple_of(i * wide, wide), wide)
        for n, (begin, other) in enumerate(pairs):
            source = dy[:, lanes] if begin is None else a_ext[pl.ds(begin, other.shape[0]), lanes]
            value = mm_tn(source, other[...]).astype(low)
            for p in range(PARTS):
                gb[p, lanes, n * size : (n + 1) * size] = value[:, p * size : (p + 1) * size]
        return carry

    lax.fori_loop(0, n_col, one_block, 0)
    sum_b.start()
    line.go(1)
    for k in ks:
        enc_hop(k).start()
    for n, (_, other) in enumerate(pairs):
        sums[n : n + 1, :] = jnp.sum(other[...].astype(f32), axis=0, keepdims=True)
    sum_a.finish(a_sum)
    sum_b.turn()

    @pl.when(col < n_col - 1)
    def _():
        da_hop.wait_recv()

    totals = [0.0, 0.0]
    for t in range(cuts):
        spot = pl.ds(t * CUT, CUT)
        own = last(pl.multiple_of(row * rows + t * CUT, CUT))
        exchange(away_l, came_l, c_s, c_r, t).wait_recv()
        total = own + came_l[spot, :].astype(f32)
        after = [da_got[spot, pl.ds(deep - wide, wide)], da_got[spot, pl.ds(0, deep - wide)]]
        total = total + jnp.concatenate(after, axis=1).astype(f32)
        normed, scaling = norm_rows(x0[spot, :].astype(f32))
        upstream = total * gain[...]
        mean_up = jnp.mean(upstream, axis=1, keepdims=True)
        mean_both = jnp.mean(upstream * normed, axis=1, keepdims=True)
        dx = res[spot, :] + scaling * (upstream - mean_up - normed * mean_both)
        tg[spot, :] = dx.astype(low)
        for i, value in enumerate((total * normed, total)):
            totals[i] = totals[i] + jnp.sum(value, axis=0, keepdims=True)
    for i in range(2):
        stats[i : i + 1, :] = totals[i]
    for stage in range(2):
        spread(stage).wait_recv()
        spread(2 + stage).start()
    value = line.total(own_q[...].astype(f32))
    value = with_other_bits(value, extra, 1, x_s, x_r, by_bit[2:])
    q_own[...] = value.astype(low)
    sum_b.finish(b_sum)
    spread(2).wait_recv()
    spread(3).wait_recv()
    value = enc_in[:, pl.ds(0, wide)].astype(f32)
    for k in ks:
        enc_hop(k).wait()
        value = value + enc_got[k - 1].astype(f32)
    enc_out[...] = value
    for stage in range(4):
        spread(stage).wait_send()
    line.end()
    sum_a.end()
    sum_b.end()
    for t in range(cuts):
        exchange(away_b, came_b, b_s, b_r, t).wait_send()
        exchange(away_l, came_l, c_s, c_r, t).wait_send()

    @pl.when(col > 0)
    def _():
        da_hop.wait_send()


def fold(dq, dk, dv, a_ext, dy, o, weights, res, x0, gain, ga, enc_in, riding, n_col, n_dp):
    sd, vm, dma = jax.ShapeDtypeStruct, pltpu.VMEM, pltpu.SemaphoreType.DMA
    rows, deep = x0.shape
    wide = deep // n_col
    columns, hidden = ga.shape[2], riding[0].shape[2]
    others, cuts = n_col - 1, rows // CUT
    more = max(n_dp.bit_length() - 3, 1)
    by_rows = vm((rows, deep), low)
    plane_memory = [vm((2, deep, columns), low), vm((deep, columns), low), vm((deep, columns), low)]
    plane_sems = [dma((2, n_col)), dma((2, n_col)), dma((n_col,)), dma((n_col,))]
    wq, wk, wv = weights
    return pl.pallas_call(
        functools.partial(fold_kernel, n_col=n_col, n_dp=n_dp),
        in_specs=[IN_VMEM] * 10 + [ANYWHERE] * 10,
        out_specs=[IN_VMEM] * 8,
        out_shape=[
            sd((8, dq.shape[1]), f32),
            sd((rows, deep), low),
            sd((8, deep), f32),
            sd((deep, columns), low),
            sd((deep, columns), low),
            sd((PARTS, wide, hidden), low),
            sd((wide, hidden), low),
            sd((enc_in.shape[0], wide), f32),
        ],
        scratch_shapes=[
            vm((3, deep, hidden), low),
            vm((wide, hidden), low),
            vm((wide, hidden), low),
            vm((others, wide, hidden), low),
            vm((others, wide, hidden), low),
            vm((others, wide, hidden), low),
            vm(ga.shape, low),
            *plane_memory, *plane_memory,
            by_rows, by_rows, by_rows, by_rows, by_rows,
            vm((others, enc_in.shape[0], wide), low),
            vm((more, 3, wide, hidden) if n_dp > PARTS else (1, 3, 16, 128), low),
            dma((2, 3)), dma, dma((4,)),
            dma((2, others)), dma((2, others)),
            *plane_sems, *plane_sems,
            dma((cuts,)), dma((cuts,)), dma((cuts,)), dma((cuts,)),
            dma, dma,
            dma((others,)), dma((others,)),
            dma((4,)), dma((4,)),
            dma((2, more)), dma((2, more)),
        ],
        compiler_params=pltpu.CompilerParams(
            collective_id=21, has_side_effects=True, vmem_limit_bytes=62 * 1024 * 1024
        ),
        name="fold",
    )(dq, dk, dv, a_ext, wk, wv, res, gain[None], ga, enc_in, dy, o, wq, x0, *riding)


def finish_kernel(
    a_sum, b_sum, q_own, small, tg,
    full_a, full_b, hidden1, small_out, tg_out,
    za, za_l, za_r, zb, zb_l, zb_r, s_cur, s_got, s_z, extra,
    za_s, za_t, zb_s, zb_t, g_s, g_r, s_s, s_r, sz_s, sz_r, t_s, t_r, x_s, x_r,
    *, n_col, n_dp,
):
    dp, row, col = here()
    parts = part_numbers()
    part = parts[0]
    by_bit = bit_partners(n_dp)
    by_x, by_y = by_bit[:2]
    twin = (dp, 1 - row, col)
    cols = [(dp, row, lax.rem(col + k, n_col)) for k in range(n_col)]
    meet([twin] + [(dp, 1 - row, c[2]) for c in cols[1:]] + cols[1:] + by_bit)
    wide = a_sum.shape[0] // n_col
    ks = range(1, n_col)
    line_a = LineSum(za, za_l, za_r, za_s, za_t, cols)
    line_b = LineSum(zb, zb_l, zb_r, zb_s, zb_t, cols)

    partners = [twin] + by_bit

    def small_hop(i):
        return remote(s_cur.at[i], s_got.at[i], s_s.at[i], s_r.at[i], partners[i])

    def small_z(k):
        return remote(
            s_cur.at[len(partners), k], s_z.at[k - 1], sz_s.at[k - 1], sz_r.at[k - 1], cols[k]
        )

    def small_step(i):
        if i == 0:
            s_cur[0] = small[...]
        elif i <= len(partners):
            small_hop(i - 1).wait_recv()
            got = s_got[i - 1]
            if i == 1:
                lane = lax.broadcasted_iota(jnp.int32, got.shape, 2)
                got = jnp.where(lane < wide, got, 0.0)
            s_cur[i] = s_cur[i - 1] + got
        if i < len(partners):
            small_hop(i).start()
        elif i == len(partners):
            for k in ks:
                small_z(k).start()
        else:
            value = s_cur[len(partners), 0]
            for k in ks:
                small_z(k).wait_recv()
                value = value + s_z[k - 1]
            small_out[...] = value

    spread_q = plane_copies(hidden1, part, parts, by_x, by_y, g_s.at[0], g_r.at[0])
    spread_a = plane_copies(full_a, part, parts, by_x, by_y, g_s.at[1], g_r.at[1])
    spread_b = plane_copies(full_b, part, parts, by_x, by_y, g_s.at[2], g_r.at[2])
    spreads = (spread_q, spread_a, spread_b)

    small_step(0)
    for line, buf, whole in ((line_a, za, a_sum), (line_b, zb, b_sum)):
        for k in ks:
            buf[k - 1] = whole[pl.ds(k * wide, wide), :]
        line.begin()
    for i in range(1, len(partners)):
        small_step(i)
    hidden1[part] = q_own[...]
    spread_q(0).start()
    spread_q(1).start()
    for d in range(n_col - 2, 0, -1):
        line_a.go(d)
        line_b.go(d)
    small_step(len(partners))
    send_home(tg, tg_out, t_s, t_r, n_col)
    for i, (line, whole, full, spread) in enumerate((
        (line_a, a_sum, full_a, spread_a), (line_b, b_sum, full_b, spread_b),
    )):
        value = line.total(whole[pl.ds(0, wide), :].astype(f32))
        value = with_other_bits(value, extra, i, x_s, x_r, by_bit[2:])
        full[part] = value.astype(low)
        spread(0).start()
        spread(1).start()
    for spread in spreads:
        for stage in range(2):
            spread(stage).wait_recv()
            spread(2 + stage).start()
    small_step(len(partners) + 1)
    for spread in spreads:
        spread(2).wait_recv()
        spread(3).wait_recv()
        for stage in range(4):
            spread(stage).wait_send()
    line_a.end()
    line_b.end()
    for k in ks:
        small_z(k).wait_send()
    for i in range(len(partners)):
        small_hop(i).wait_send()
    wait_home(tg, tg_out, t_s, t_r, n_col)


def finish(a_sum, b_sum, q_own, small, tg, n_col, n_dp):
    columns = a_sum.shape[1]
    wide, hidden = q_own.shape
    steps = n_dp.bit_length()
    sd, vm, dma = jax.ShapeDtypeStruct, pltpu.VMEM, pltpu.SemaphoreType.DMA
    more = max(n_dp.bit_length() - 3, 1)
    others = n_col - 1
    return pl.pallas_call(
        functools.partial(finish_kernel, n_col=n_col, n_dp=n_dp),
        in_specs=[IN_VMEM] * 5,
        out_specs=[IN_VMEM] * 4 + [ANYWHERE],
        out_shape=[
            sd((PARTS, wide, columns), low),
            sd((PARTS, wide, columns), low),
            sd((PARTS, wide, hidden), low),
            sd(small.shape[1:], f32),
            sd((n_col * tg.shape[0], wide), low),
        ],
        scratch_shapes=[
            *[vm((others, wide, columns), low)] * 6,
            vm((steps + 1,) + small.shape, f32),
            vm((steps,) + small.shape, f32),
            vm((others,) + small.shape[1:], f32),
            vm((more, 3, wide, columns), low),
            *[dma((2, others))] * 4,
            dma((3, 4)), dma((3, 4)),
            dma((steps,)), dma((steps,)),
            dma((others,)), dma((others,)),
            dma((n_col,)), dma((n_col,)),
            dma((2, more)), dma((2, more)),
        ],
        compiler_params=pltpu.CompilerParams(
            collective_id=20, has_side_effects=True, vmem_limit_bytes=VMEM
        ),
        name="finish",
    )(a_sum, b_sum, q_own, small, tg)


def column_grads_kernel(*refs, pairs, firsts):
    count = len(pairs)
    firsts_refs, others = refs[:firsts], refs[firsts : firsts + count]
    out, sums = refs[firsts + count :]
    size = out.shape[2] // count
    for i, (which, begin) in enumerate(pairs):
        a, b = firsts_refs[which], others[i]
        value = mm_tn(a[pl.ds(begin, b.shape[0]), :], b[...]).astype(low)
        for p in range(out.shape[0]):
            out[p, :, i * size : (i + 1) * size] = value[:, p * size : (p + 1) * size]

    @pl.when(pl.program_id(0) == 0)
    def _():
        for i in range(count):
            sums[i : i + 1, :] = jnp.sum(others[i][...].astype(f32), axis=0, keepdims=True)


def column_grads_of(firsts, pairs, others):
    deep, width = firsts[0].shape[1], others[0].shape[1]
    block = 256
    return pl.pallas_call(
        functools.partial(column_grads_kernel, pairs=pairs, firsts=len(firsts)),
        grid=(deep // block,),
        in_specs=[pl.BlockSpec((x.shape[0], block), lambda i: (0, i)) for x in firsts]
        + [pl.BlockSpec(x.shape, lambda i: (0, 0)) for x in others],
        out_specs=[
            pl.BlockSpec((PARTS, block, width), lambda i: (0, i, 0)),
            pl.BlockSpec((8, width), lambda i: (0, 0)),
        ],
        out_shape=[
            jax.ShapeDtypeStruct((PARTS, deep, width), low),
            jax.ShapeDtypeStruct((8, width), f32),
        ],
        compiler_params=pltpu.CompilerParams(vmem_limit_bytes=VMEM),
        name="column_grads",
    )(*firsts, *others)


def unpack_kernel(full_a, full_b, hidden0, hidden1, rows, *outs):
    size = full_a.shape[2] // 4
    for g, full in enumerate((full_a, full_b)):
        for i in range(4):
            value = full[0, :, i * size : (i + 1) * size].astype(f32)
            outs[4 * g + i][...] = value if i < 3 else jnp.transpose(value)
    outs[8][...] = hidden0[0].astype(f32)
    outs[9][...] = jnp.transpose(hidden1[0].astype(f32))
    outs[10][...] = rows[...].astype(f32)


def unpack(full_a, full_b, hidden0, hidden1, rows):
    parts, wide, columns = full_a.shape
    inner = hidden0.shape[2]
    size = columns // 4
    into = (pl.BlockSpec((wide, size), lambda p: (0, p)), (wide, parts * size))
    out_of = (pl.BlockSpec((size, wide), lambda p: (p, 0)), (parts * size, wide))
    layouts = [into, into, into, out_of] * 2 + [
        (pl.BlockSpec((wide, inner), lambda p: (0, p)), (wide, parts * inner)),
        (pl.BlockSpec((inner, wide), lambda p: (p, 0)), (parts * inner, wide)),
    ]
    by_rows = pl.BlockSpec((rows.shape[0] // parts, wide), lambda p: (p, 0))
    layouts.append((by_rows, rows.shape))
    return pl.pallas_call(
        unpack_kernel,
        grid=(parts,),
        in_specs=[
            pl.BlockSpec((1, wide, x.shape[2]), lambda p: (p, 0, 0))
            for x in (full_a, full_b, hidden0, hidden1)
        ]
        + [by_rows],
        out_specs=[x[0] for x in layouts],
        out_shape=[jax.ShapeDtypeStruct(x[1], f32) for x in layouts],
        compiler_params=pltpu.CompilerParams(vmem_limit_bytes=VMEM),
        name="unpack",
    )(full_a, full_b, hidden0, hidden1, rows)


def build_local(mesh):
    n_dp, n_col = mesh.shape["dp"], mesh.shape["col"]

    def from_col(x, k):
        return lax.ppermute(x, "col", [(i, (i - k) % n_col) for i in range(n_col)])

    def across(x, bit):
        return lax.ppermute(x, "dp", [(i, i ^ bit) for i in range(n_dp)])

    def local(
        tokens, encoder, cotangent, dec_lengths, src_lengths,
        self_norm_gain, self_norm_bias, self_query, self_key, self_value,
        self_query_bias, self_value_bias, self_out, self_out_bias,
        cross_norm_gain, cross_norm_bias, cross_query, cross_key, cross_value,
        cross_query_bias, cross_value_bias, cross_out, cross_out_bias,
        hidden_norm_gain, hidden_norm_bias, hidden_in, hidden_in_bias,
        hidden_out, hidden_out_bias,
    ):
        row, col = lax.axis_index("row"), lax.axis_index("col")
        place = lax.axis_index("dp") % PARTS
        wide = tokens.shape[1]
        chunk = tokens.shape[0] // n_col
        span = 2 * chunk

        def in_order(parts):
            stacked = jnp.stack(parts)
            return [
                lax.dynamic_index_in_dim(stacked, i ^ place, 0, keepdims=False)
                for i in range(PARTS)
            ]

        def own_columns(w, j):
            size = w.shape[1] // PARTS
            return lax.dynamic_slice_in_dim(w, (place ^ j) * size, size, 1)

        def along_col(w):
            return [from_col(own_columns(w, 0), k) for k in range(1, n_col)]

        vec_f = jnp.stack([
            self_norm_gain, self_norm_bias, self_out_bias, cross_norm_gain, cross_norm_bias,
            cross_out_bias, hidden_norm_gain, hidden_norm_bias, hidden_out_bias,
        ])
        vec_f = jnp.pad(vec_f, ((0, 7), (0, 0)))
        vec_c = jnp.concatenate(
            [self_query_bias, self_value_bias, cross_query_bias, cross_value_bias, hidden_in_bias]
        ).reshape(-1, 128)
        vec_c = jnp.pad(vec_c, ((0, -vec_c.shape[0] % 8), (0, 0)))
        weights = [
            self_query, self_key, self_value, self_out,
            cross_query, cross_key, cross_value, cross_out,
        ]
        x_ext, enc, vectors, columns, *full = start(tokens, encoder, vec_f, vec_c, weights, n_col)
        wq1, wk1, wv1, wo1, wq2, wk2, wv2, wo2 = full
        (gain1, shift1, out_bias1, gain2, shift2, out_bias2, gain3, shift3, out_bias3) = vectors[:9]
        size = self_query_bias.shape[0]

        def column_vector(start, size):
            return columns.reshape(n_col, -1)[:, start : start + size].reshape(-1)

        q_bias1 = column_vector(0, size)
        v_bias1 = column_vector(size, size)
        q_bias2 = column_vector(2 * size, size)
        v_bias2 = column_vector(3 * size, size)
        hidden_bias = column_vector(4 * size, hidden_in_bias.shape[0]).reshape(PARTS, -1)
        hidden_bias = jnp.stack(
            [lax.dynamic_index_in_dim(hidden_bias, place ^ j, 0) for j in range(PARTS)]
        )

        hidden_in, x_ext = lax.optimization_barrier((hidden_in, x_ext))
        hidden_out_t = hidden_out.T
        pieces1 = along_col(hidden_in)

        dec_ids = doc_numbers(dec_lengths, SEQ_LEN)[0]
        src_ids = doc_numbers(src_lengths, ENC)[0]
        padded = jnp.pad(dec_ids, (WIN, 0), constant_values=-1)
        key_ids = lax.dynamic_slice_in_dim(padded, col * span, WIN + span, 0)
        query_ids = key_ids[WIN:]

        scale = low(HEAD_DIM**-0.5)
        x0 = x_ext[1]
        a_ext = enter(x_ext, gain1, shift1, 2).reshape(WIN + span, -1)
        a = a_ext[WIN:]
        hidden_out_t, a_ext = lax.optimization_barrier((hidden_out_t, a_ext))
        pieces2 = along_col(hidden_out_t)
        q1 = (mm(a, wq1) + q_bias1).astype(low) * scale
        k1 = mm(a_ext, wk1).astype(low)
        v1 = (mm(a_ext, wv1) + v_bias1).astype(low)
        dma = pltpu.SemaphoreType.DMA
        dma = pltpu.SemaphoreType.DMA
        o1, lse1 = attend(q1, k1, v1, query_ids, key_ids, True)
        pieces1, o1 = lax.optimization_barrier((pieces1, o1))
        rest1 = jnp.concatenate(pieces1, axis=0)
        near1 = [across(rest1, 1), across(rest1, 2)]
        x1, c, q2 = junction(
            "forward", [("nn", o1, wo1)], [x0, out_bias1, gain2, shift2], 3,
            ("queries", wq2, q_bias2),
        )

        pieces2, q2 = lax.optimization_barrier((pieces2, q2))
        rest2 = jnp.concatenate(pieces2, axis=0)
        near2 = [across(rest2, 1), across(rest2, 2)]
        k2 = mm(enc, wk2).astype(low)
        v2 = (mm(enc, wv2) + v_bias2).astype(low)
        o2, lse2 = attend(q2, k2, v2, query_ids, src_ids, False)
        near1, o2 = lax.optimization_barrier((near1, o2))
        far1 = across(near1[0], 2)
        x2, f = junction("forward", [("nn", o2, wo2)], [x1, out_bias2, gain3, shift3], 4)
        rests1, rests2 = [rest1, *near1], [rest2, *near2]
        act0, slope0, part_sum = hidden_forward(
            f, hidden_bias[:1], hidden_in, hidden_out_t, rests1[:1], rests2[:1], (0,), 0
        )
        near2, part_sum = lax.optimization_barrier((near2, part_sum))
        far2 = across(near2[1], 1)
        rests1, rests2 = [rest1, *near1, far1], [rest2, *near2, far2]
        act1, slope1, dz, part_sum = hidden_forward(
            f, hidden_bias[1:3], hidden_in, hidden_out_t, rests1[1:3], rests2[1:3], (1, 2), 14,
            sum_in=part_sum, cotangent=cotangent, n_col=n_col,
        )
        act2, slope2, rows_out = hidden_forward(
            f, hidden_bias[3:], hidden_in, hidden_out_t, rests1[3:], rests2[3:], (3,), 5,
            sum_in=part_sum, x=x2, bias=out_bias3,
        )
        dz = dz.reshape(span, -1)

        g1, g2, hidden_bias_grad, df, got_a, got_b, layer_out, far_a, far_b = hidden_backward(
            dz, f, hidden_in, hidden_out_t, rests1, rests2, [act0, act1, act2],
            [slope0, slope1, slope2], ((0, 0), (1, 0), (1, 1), (2, 0)), rows_out, n_col, 11,
        )
        inner = g1.shape[2]
        half = g1.shape[1] // 2
        one = ((half, inner), low)
        dx2, dyc, stats3, doc = junction(
            "backward", [("sum", df)], [dz, x2, gain3], 6, ("turned", wo2, gain3)
        )

        later = ((half, inner - far_a.shape[1]), low)
        dq2, dk2, dv2, back_a, back_b, far_c, far_d = attend_back(
            q2, k2, v2, doc, o2, lse2, query_ids, src_ids, False,
            first_rider, [g1, g2, got_a, got_b], [one] * 2 + [later] * 2,
            [
                pltpu.VMEM((4, half, inner), low), pltpu.VMEM((2, half, inner), low),
                dma((4,)), dma((4,)), dma((4,)),
            ],
            12,
        )
        cross_grads, cross_columns = column_grads_of(
            [c, enc, dyc], [(0, 0), (1, 0), (1, 0), (2, 0)], [dq2, dk2, dv2, o2]
        )
        enc_back = junction("sum", [("nt", dk2, wk2), ("nt", dv2, wv2)], [], 7)
        dx1, dy, stats2, do = junction(
            "backward", [("nt", dq2, wq2)], [dx2, x1, gain2], 8, ("turned", wo1, gain2)
        )

        cross_grads, enc_back, do = lax.optimization_barrier((cross_grads, enc_back, do))
        (
            dq1, dk1, dv1, near_a, near_b, far_back_a, far_back_b, own1
        ) = attend_back(
            q1, k1, v1, do, o1, lse1, query_ids, key_ids, True,
            functools.partial(second_rider, n_col=n_col),
            [g1, g2, got_a, got_b, back_a, back_b, far_a, far_b, far_c, far_d],
            [one] * 4 + [((wide, inner), low)],
            [
                pltpu.VMEM((4, half, inner), low), pltpu.VMEM((2, half, inner), low),
                pltpu.VMEM((3, 2 * half, inner), low), pltpu.VMEM((n_col - 1, wide, inner), low),
                pltpu.VMEM((wide, inner), low), pltpu.VMEM((n_col - 1, wide, inner), low),
                pltpu.VMEM((n_col - 1, wide, inner), low),
                dma((6,)), dma((2, 3)), dma((4,)), dma((4,)),
                dma((2, n_col - 1)), dma((2, n_col - 1)), dma,
            ],
            13,
        )
        self_columns, x0_grad, stats1, a_sum, b_sum, hidden0, q_own, encoder_grad = fold(
            dq1, dk1, dv1, a_ext, dy, o1, [wq1, wk1, wv1], dx1, x0, gain1, cross_grads, enc_back,
            [g2, near_a, near_b, far_back_a, far_back_b, own1], n_col, n_dp,
        )

        feature_grads = jnp.concatenate([
            stats1[:2], stats2[2:3], stats2[:2], stats3[2:3], stats3[:2], stats3[3:4],
        ])
        feature_grads = jnp.moveaxis(feature_grads.reshape(-1, n_col, wide), 1, 0)
        column_grads = []
        for vector in (self_columns[0], self_columns[2], cross_columns[0], cross_columns[2]):
            column_grads.append(vector.reshape(n_col, -1))
        column_grads.append(
            jnp.stack(in_order([hidden_bias_grad[j] for j in range(PARTS)])).reshape(n_col, -1)
        )
        column_grads = jnp.concatenate(column_grads, axis=1).reshape(n_col, -1, 128)
        column_grads = lax.dynamic_slice_in_dim(
            jnp.concatenate([column_grads, column_grads]), col, n_col, 0
        )
        lines = -(-max(feature_grads.shape[1], column_grads.shape[1]) // 8) * 8
        small = jnp.concatenate(
            [
                jnp.pad(x, ((0, 0), (0, lines - x.shape[1]), (0, 0)))
                for x in (feature_grads, column_grads)
            ],
            axis=2,
        )
        full_a, full_b, hidden1, small, tokens_grad = finish(
            a_sum, b_sum, q_own, small, x0_grad, n_col, n_dp
        )
        grads = unpack(full_a, full_b, hidden0, hidden1, tokens_grad)
        tokens_grad = grads[10]
        feature_grads = small[:, :wide]
        column_grads = small[:, wide:].reshape(-1)

        return (
            layer_out,
            tokens_grad,
            encoder_grad,
            feature_grads[0],
            feature_grads[1],
            grads[4],
            grads[5],
            grads[6],
            column_grads[:size],
            column_grads[size : 2 * size],
            grads[7],
            feature_grads[2],
            feature_grads[3],
            feature_grads[4],
            grads[0],
            grads[1],
            grads[2],
            column_grads[2 * size : 3 * size],
            column_grads[3 * size : 4 * size],
            grads[3],
            feature_grads[5],
            feature_grads[6],
            feature_grads[7],
            grads[8],
            column_grads[4 * size : 4 * size + hidden_in_bias.shape[0]],
            grads[9],
            feature_grads[8],
        )

    return local


def solution(mesh):
    rows = P(("dp", "row"), "col")
    features = P("col")
    columns = P(("row", "col"))
    into, out_of = P("col", "row"), P("row", "col")
    attention = (into, into, into, columns, columns, out_of, features)
    norm = (features, features)
    weights = (
        norm
        + attention
        + norm
        + attention
        + norm
        + (into, columns, out_of, features)
    )
    return jax.shard_map(
        build_local(mesh),
        mesh=mesh,
        in_specs=(rows, rows, rows, P("dp", None), P("dp", None)) + weights,
        out_specs=(rows, rows, rows) + weights,
        check_vma=False,
    )
```

```python
import functools

import jax
import jax.numpy as jnp
from jax import lax
from jax.experimental import pallas as pl
from jax.experimental.pallas import tpu as pltpu
from jax.sharding import PartitionSpec as P

D = 1024
HEAD_DIM = 64
SEQ_LEN = 4096
ENC = 1024
WIN = 1024

norm_epsilon = 1e-05
masked_fill = -1e30
low = jnp.bfloat16
f32 = jnp.float32
PARTS = 4
PAIR = 2 * HEAD_DIM
QUERY_ROWS = 256
VMEM = 56 * 1024 * 1024


def doc_numbers(lengths, positions):
    bounds = jnp.cumsum(lengths, axis=1, dtype=jnp.int32)
    places = jnp.arange(positions, dtype=jnp.int32)
    return jnp.sum(
        (places[None, :, None] >= bounds[:, None, :]).astype(jnp.int32), axis=2, dtype=jnp.int32
    )


def mm(a, b):
    return lax.dot_general(a, b, (((1,), (0,)), ((), ())), preferred_element_type=f32)


def mm_nt(a, b):
    return lax.dot_general(a, b, (((1,), (1,)), ((), ())), preferred_element_type=f32)


def mm_tn(a, b):
    return lax.dot_general(a, b, (((0,), (0,)), ((), ())), preferred_element_type=f32)


MESH = pl.DeviceIdType.MESH
ANYWHERE = pl.BlockSpec(memory_space=pl.ANY)
IN_VMEM = pl.BlockSpec(memory_space=pltpu.VMEM)


def here():
    return lax.axis_index("dp"), lax.axis_index("row"), lax.axis_index("col")


def meet(partners):
    barrier = pltpu.get_barrier_semaphore()
    for partner in partners:
        pl.semaphore_signal(barrier, inc=1, device_id=partner, device_id_type=MESH)
    pl.semaphore_wait(barrier, len(partners))


def remote(src, dst, sends, recvs, device):
    return pltpu.make_async_remote_copy(
        src_ref=src, dst_ref=dst, send_sem=sends, recv_sem=recvs, device_id=device,
        device_id_type=MESH,
    )


def home_hop(rows, home, sends, recvs, n_col, k):
    dp, row, col = here()
    wide, count = home.shape[1], rows.shape[0]
    to_row, at = col // 2, 2 * lax.rem(col, 2) + row
    src = rows.at[:, pl.ds(k * wide, wide)]
    dst = home.at[pl.ds(pl.multiple_of(at * count, count), count), :]
    copy = remote(src, dst, sends.at[k], recvs.at[at], (dp, to_row, lax.rem(col + k, n_col)))
    return copy, pltpu.make_async_copy(src, dst, recvs.at[at]), to_row == row


def send_home(rows, home, sends, recvs, n_col):
    for k in range(n_col):
        away, here_copy, same = home_hop(rows, home, sends, recvs, n_col, k)
        if k:
            away.start()
            continue

        @pl.when(same)
        def _():
            here_copy.start()

        @pl.when(jnp.logical_not(same))
        def _():
            away.start()


def wait_home(rows, home, sends, recvs, n_col):
    wide, count = home.shape[1], rows.shape[0]
    for k in range(n_col):
        away, _, same = home_hop(rows, home, sends, recvs, n_col, k)
        if k:
            away.wait_send()
        else:

            @pl.when(jnp.logical_not(same))
            def _():
                away.wait_send()

        src = rows.at[:, pl.ds(k * wide, wide)]
        pltpu.make_async_copy(src, home.at[pl.ds(k * count, count), :], recvs.at[k]).wait()


class LineSum:
    def __init__(self, buf, in_l, in_r, sends, recvs, cols):
        self.buf, self.in_l, self.in_r, self.sends, self.recvs = buf, in_l, in_r, sends, recvs
        self.cols, self.n, self.col = cols, len(cols), lax.axis_index("col")

    def right(self, d):
        return remote(
            self.buf.at[d - 1], self.in_l.at[d - 1], self.sends.at[0, d - 1],
            self.recvs.at[0, d - 1], self.cols[1],
        )

    def left(self, d):
        return remote(
            self.buf.at[self.n - d - 1], self.in_r.at[d - 1], self.sends.at[1, d - 1],
            self.recvs.at[1, d - 1], self.cols[self.n - 1],
        )

    def add(self, k, got):
        self.buf[k - 1] = (self.buf[k - 1].astype(f32) + got.astype(f32)).astype(low)

    def begin(self):
        @pl.when(self.col == 0)
        def _():
            self.in_l[0] = jnp.zeros(self.in_l.shape[1:], low)
            for d in range(self.n - 1, 0, -1):
                self.right(d).start()

        @pl.when(self.col == self.n - 1)
        def _():
            self.in_r[0] = jnp.zeros(self.in_r.shape[1:], low)
            for d in range(self.n - 1, 0, -1):
                self.left(d).start()

    def go(self, d):
        @pl.when((self.col > 0) & (self.col <= self.n - 1 - d))
        def _():
            self.right(d + 1).wait_recv()
            self.add(d, self.in_l[d])
            self.right(d).start()

        @pl.when((self.col < self.n - 1) & (self.col >= d))
        def _():
            self.left(d + 1).wait_recv()
            self.add(self.n - d, self.in_r[d])
            self.left(d).start()

    def total(self, value):
        @pl.when(self.col > 0)
        def _():
            self.right(1).wait_recv()

        @pl.when(self.col < self.n - 1)
        def _():
            self.left(1).wait_recv()

        return value + self.in_l[0].astype(f32) + self.in_r[0].astype(f32)

    def end(self):
        for d in range(1, self.n):

            @pl.when(self.col <= self.n - 1 - d)
            def _():
                self.right(d).wait_send()

            @pl.when(self.col >= d)
            def _():
                self.left(d).wait_send()


def plane():
    dp, row, col = here()
    flips = [dp + b - 2 * b * lax.rem(dp // b, 2) for b in (1, 2)]
    return (flips[0], row, col), (flips[1], row, col)


def head_masks():
    lane = lax.broadcasted_iota(jnp.int32, (1, PAIR), 1)
    first = jnp.where(lane < HEAD_DIM, 1.0, 0.0)
    return first.astype(low), (1.0 - first).astype(low), lane < HEAD_DIM


def attend_kernel(q_ref, k_ref, v_ref, qid_ref, kid_ref, o_ref, lse_ref, bias, *, span, windowed):
    rows = q_ref.shape[0]
    pairs = q_ref.shape[1] // PAIR
    step = pl.program_id(0)
    start = step * rows if windowed else 0
    if windowed:
        start = pl.multiple_of(start, rows)
    allowed = qid_ref[...] == kid_ref[0:1, pl.ds(start, span)]
    if windowed:
        at_row = lax.broadcasted_iota(jnp.int32, (rows, span), 0)
        at_key = lax.broadcasted_iota(jnp.int32, (rows, span), 1)
        allowed = allowed & (at_key > at_row) & (at_key <= at_row + WIN)
    bias[...] = jnp.where(allowed, 0.0, masked_fill)
    first, second, is_first = head_masks()

    def one_pair(p, carry):
        lanes = pl.ds(pl.multiple_of(p * PAIR, PAIR), PAIR)
        q2 = q_ref[:, lanes]
        k2 = k_ref[pl.ds(start, span), lanes]
        v2 = v_ref[pl.ds(start, span), lanes]
        outs, logs = [], []
        for mask in (first, second):
            s = mm_nt(q2 * mask, k2) + bias[...]
            top = jnp.max(s, axis=1, keepdims=True)
            e = jnp.exp(s - top)
            total = jnp.sum(e, axis=1, keepdims=True)
            outs.append(mm(e.astype(low), v2) / total)
            logs.append(top + jnp.log(total))
        o_ref[:, lanes] = jnp.where(is_first, outs[0], outs[1]).astype(low)
        stats = jnp.where(is_first, logs[0], logs[1])
        turned = jnp.transpose(stats)
        lse_ref[p, 0:1, :] = turned[0:1]
        lse_ref[p, 1:2, :] = turned[HEAD_DIM : HEAD_DIM + 1]
        return carry

    lax.fori_loop(0, pairs, one_pair, 0)


def attend(q, k, v, qid, kid, windowed):
    tokens, width = q.shape
    keys = k.shape[0]
    pairs = width // PAIR
    rows = QUERY_ROWS
    span = WIN + rows if windowed else keys
    return pl.pallas_call(
        functools.partial(attend_kernel, span=span, windowed=windowed),
        grid=(tokens // rows,),
        in_specs=[
            pl.BlockSpec((rows, width), lambda i: (i, 0)),
            pl.BlockSpec((keys, width), lambda i: (0, 0)),
            pl.BlockSpec((keys, width), lambda i: (0, 0)),
            pl.BlockSpec((rows, 1), lambda i: (i, 0)),
            pl.BlockSpec((1, keys), lambda i: (0, 0)),
        ],
        out_specs=[
            pl.BlockSpec((rows, width), lambda i: (i, 0)),
            pl.BlockSpec((pairs, 8, rows), lambda i: (0, 0, i)),
        ],
        out_shape=[
            jax.ShapeDtypeStruct((tokens, width), low),
            jax.ShapeDtypeStruct((pairs, 8, tokens), f32),
        ],
        scratch_shapes=[pltpu.VMEM((rows, span), f32)],
        compiler_params=pltpu.CompilerParams(vmem_limit_bytes=VMEM),
        name="attend",
    )(q, k, v, qid[:, None], kid[None, :])


def attend_back_kernel(*refs, span, windowed, rider, n_ins, n_outs):
    refs = list(refs)
    q_ref, k_ref, v_ref, do_ref, o_ref, lse_ref, qid_ref, kid_ref = refs[:8]
    rider_refs = refs[8 : 8 + n_ins]
    refs = refs[8 + n_ins :]
    dq_ref, dk_ref, dv_ref = refs[:3]
    rider_refs += refs[3 : 3 + n_outs]
    bias, dk_sum, dv_sum = refs[3 + n_outs : 6 + n_outs]
    rider_refs += refs[6 + n_outs :]
    rows = q_ref.shape[0]
    pairs = q_ref.shape[1] // PAIR
    step = pl.program_id(0)
    start = pl.multiple_of(step * rows, rows) if windowed else 0
    keys = pl.ds(start, span)
    begin, middle, end, later = rider(*rider_refs)

    @pl.when(step == 0)
    def _():
        begin()
        dk_sum[...] = jnp.zeros_like(dk_sum)
        dv_sum[...] = jnp.zeros_like(dv_sum)

    for at, hook in later.items():

        @pl.when(step == at)
        def _():
            hook()

    allowed = kid_ref[keys, :] == qid_ref[...]
    if windowed:
        at_key = lax.broadcasted_iota(jnp.int32, (span, rows), 0)
        at_row = lax.broadcasted_iota(jnp.int32, (span, rows), 1)
        allowed = allowed & (at_key > at_row) & (at_key <= at_row + WIN)
    bias[...] = jnp.where(allowed, 0.0, masked_fill)
    first, second, is_first = head_masks()

    def one_pair(p, carry):
        lanes = pl.ds(pl.multiple_of(p * PAIR, PAIR), PAIR)
        q2 = q_ref[:, lanes]
        k2 = k_ref[keys, lanes]
        v2 = v_ref[keys, lanes]
        do2 = do_ref[:, lanes]
        turned = jnp.transpose(do2.astype(f32) * o_ref[:, lanes].astype(f32))
        dk, dv, dqs = 0.0, 0.0, []
        for h, mask in enumerate((first, second)):
            qm, dom = q2 * mask, do2 * mask
            inner = jnp.sum(turned[h * HEAD_DIM : (h + 1) * HEAD_DIM], axis=0, keepdims=True)
            s = mm_nt(k2, qm) + bias[...]
            share = jnp.exp(s - lse_ref[p, h : h + 1, :])
            ds = (share * (mm_nt(v2, dom) - inner)).astype(low)
            dv = dv + mm(share.astype(low), dom)
            dk = dk + mm(ds, qm)
            dqs.append(mm_tn(ds, k2))
        dk_sum[keys, lanes] += dk
        dv_sum[keys, lanes] += dv
        dq_ref[:, lanes] = (jnp.where(is_first, dqs[0], dqs[1]) * HEAD_DIM**-0.5).astype(low)

        @pl.when((step == 0) & (p == 0))
        def _():
            middle()

        return carry

    lax.fori_loop(0, pairs, one_pair, 0)

    @pl.when(step == pl.num_programs(0) - 1)
    def _():
        dk_ref[...] = dk_sum[...].astype(low)
        dv_ref[...] = dv_sum[...].astype(low)
        end()


def attend_back(q, k, v, do, o, lse, qid, kid, windowed, rider, riding, shapes, scratch, number):
    tokens, width = q.shape
    keys = k.shape[0]
    pairs = width // PAIR
    rows = QUERY_ROWS
    span = WIN + rows if windowed else keys
    by_row = pl.BlockSpec((rows, width), lambda i: (i, 0))
    whole = pl.BlockSpec((keys, width), lambda i: (0, 0))
    return pl.pallas_call(
        functools.partial(
            attend_back_kernel, span=span, windowed=windowed, rider=rider, n_ins=len(riding),
            n_outs=len(shapes),
        ),
        grid=(tokens // rows,),
        in_specs=[
            by_row,
            whole,
            whole,
            by_row,
            by_row,
            pl.BlockSpec((pairs, 8, rows), lambda i: (0, 0, i)),
            pl.BlockSpec((1, rows), lambda i: (0, i)),
            pl.BlockSpec((keys, 1), lambda i: (0, 0)),
        ]
        + [ANYWHERE] * len(riding),
        out_specs=[by_row, whole, whole] + [ANYWHERE] * len(shapes),
        out_shape=[
            jax.ShapeDtypeStruct((tokens, width), low),
            jax.ShapeDtypeStruct((keys, width), low),
            jax.ShapeDtypeStruct((keys, width), low),
        ]
        + [jax.ShapeDtypeStruct(*x) for x in shapes],
        scratch_shapes=[
            pltpu.VMEM((span, rows), f32),
            pltpu.VMEM((keys, width), f32),
            pltpu.VMEM((keys, width), f32),
        ]
        + scratch,
        compiler_params=pltpu.CompilerParams(
            vmem_limit_bytes=VMEM, collective_id=number, has_side_effects=True
        ),
        name="attend_back",
    )(q, k, v, do, o, lse, qid[None, :], kid[:, None], *riding)


def first_rider(g1, g2, got_a, got_b, back_a, back_b, far_a, far_b, load, mid, l_s, s_s, r_s):
    by_x, by_y = plane()
    half = back_a.shape[0]
    up, down = pl.ds(0, half), pl.ds(half, half)
    loads = [
        pltpu.make_async_copy(src, load.at[i], l_s.at[i])
        for i, src in enumerate((g1.at[2, up, :], got_a.at[0], g1.at[1, down, :], got_b.at[0]))
    ]
    hops = [
        remote(mid.at[0], back_a, s_s.at[0], r_s.at[0], by_y),
        remote(mid.at[1], back_b, s_s.at[1], r_s.at[1], by_x),
    ]
    count = far_a.shape[1]
    lanes = pl.ds(g2.shape[2] - count, count)
    far = [
        remote(g2.at[3, up, lanes], far_a, s_s.at[2], r_s.at[2], by_x),
        remote(g2.at[3, down, lanes], far_b, s_s.at[3], r_s.at[3], by_y),
    ]

    def begin():
        meet([by_x, by_y])
        for copy in loads + far:
            copy.start()

    def middle():
        for i in range(2):
            loads[2 * i].wait()
            loads[2 * i + 1].wait()
            mid[i] = (load[2 * i].astype(f32) + load[2 * i + 1].astype(f32)).astype(low)
            hops[i].start()

    def end():
        for copy in hops + far:
            copy.wait()

    return begin, middle, end, {}


def second_rider(
    g1, g2, got_a, got_b, back_a, back_b, far_a, far_b, far_c, far_d,
    near_a, near_b, far_back_a, far_back_b, own,
    load, mid, load_z, out_z, out_own, z_l, z_r, l_s, lz_s, s_s, r_s, zs_s, zr_s, o_s,
    *, n_col,
):
    dp, row, col = here()
    by_x, by_y = plane()
    half = back_a.shape[0]
    wide = own.shape[0]
    up, down = pl.ds(0, half), pl.ds(half, half)
    loads = [
        pltpu.make_async_copy(src, load.at[i], l_s.at[i])
        for i, src in ((0, g2.at[2, up, :]), (2, g2.at[1, down, :]))
    ]
    cut = far_a.shape[1]
    for i, (one, two) in ((1, (far_a, far_c)), (3, (far_b, far_d))):
        loads += [
            pltpu.make_async_copy(one, load.at[i, :, pl.ds(0, cut)], l_s.at[i]),
            pltpu.make_async_copy(
                two, load.at[i, :, pl.ds(cut, two.shape[1])], l_s.at[4 + i // 2]
            ),
        ]
    loads_z = []
    for i, (source, got, back) in enumerate(((up, got_a, back_a), (down, got_b, back_b))):
        for n, src in enumerate((g1.at[0, source, :], got.at[1], back)):
            loads_z.append(
                pltpu.make_async_copy(src, load_z.at[n, source, :], lz_s.at[i, n])
            )
    hops = [
        remote(g2.at[1, up, :], near_a, s_s.at[0], r_s.at[0], by_x),
        remote(g2.at[2, down, :], near_b, s_s.at[1], r_s.at[1], by_y),
        remote(mid.at[0], far_back_a, s_s.at[2], r_s.at[2], by_y),
        remote(mid.at[1], far_back_b, s_s.at[3], r_s.at[3], by_x),
    ]
    cols = [(dp, row, lax.rem(col + k, n_col)) for k in range(n_col)]
    line = LineSum(out_z, z_l, z_r, zs_s, zr_s, cols)
    keep = pltpu.make_async_copy(out_own, own, o_s)

    def begin():
        meet([by_x, by_y] + cols[1:])
        for copy in loads + loads_z + hops[:2]:
            copy.start()

    def middle():
        for i in range(2):
            for n in ((0, 2, 3), (1, 4, 5))[i]:
                loads[n].wait()
            mid[i] = (load[2 * i].astype(f32) + load[2 * i + 1].astype(f32)).astype(low)
            hops[2 + i].start()
        for copy in loads_z:
            copy.wait()
        for k in range(n_col):
            at = pl.ds(k * wide, wide)
            value = load_z[0, at, :].astype(f32) + load_z[1, at, :].astype(f32)
            value = (value + load_z[2, at, :].astype(f32)).astype(low)
            if k:
                out_z[k - 1] = value
            else:
                out_own[...] = value
        line.begin()

    def end():
        out_own[...] = line.total(out_own[...].astype(f32)).astype(low)
        keep.start()
        for copy in hops + [keep]:
            copy.wait()
        line.end()

    return begin, middle, end, {2: lambda: line.go(2), 3: lambda: line.go(1)}


ROOT = 0.7978845608028654
CUBE = 0.044715


def cotangent_rider(cot, dz, c_s, c_r, d_s, d_r, *, n_col):
    dp, row, col = here()
    wide = cot.shape[1]
    rows_here = cot.shape[0] // n_col

    def piece(j):
        to_col = 2 * row + j // 2
        k = lax.rem(col + n_col - to_col, n_col)
        src = cot.at[pl.ds(j * rows_here, rows_here), :]
        dst = dz.at[j % 2, :, pl.ds(pl.multiple_of(k * wide, wide), wide)]
        local = (row == j % 2) & (col == to_col)
        return src, dst, k, local, (dp, j % 2, to_col)

    def to_twin(k):
        ref = dz.at[row, :, pl.ds(k * wide, wide)]
        return remote(ref, ref, d_s.at[k], d_r.at[k], (dp, 1 - row, col))

    def begin():
        group = [
            (dp, r, lax.rem(col + k, n_col)) for r in (row, 1 - row) for k in range(n_col)
        ]
        meet(group[1:])
        for j in range(n_col):
            src, dst, k, local, to = piece(j)

            @pl.when(local)
            def _():
                pltpu.make_async_copy(src, dst, c_r.at[k]).start()

            @pl.when(jnp.logical_not(local))
            def _():
                remote(src, dst, c_s.at[j], c_r.at[k], to).start()

    def turn():
        for k in range(n_col):
            pltpu.make_async_copy(
                cot.at[pl.ds(0, rows_here), :], dz.at[row, :, pl.ds(k * wide, wide)], c_r.at[k]
            ).wait()
            to_twin(k).start()

    def end():
        for j in range(n_col):
            src, dst, k, local, to = piece(j)

            @pl.when(jnp.logical_not(local))
            def _():
                remote(src, dst, c_s.at[j], c_r.at[k], to).wait_send()

        for k in range(n_col):
            to_twin(k).wait()

    return begin, turn, end


ORDER = (3, 1, 2, 0)


def part_numbers():
    part = lax.rem(lax.axis_index("dp"), PARTS)
    return part, part + 1 - 2 * lax.rem(part, 2), part + 2 - 4 * (part // 2), PARTS - 1 - part


def weight_copies(own, rest, j, n, to, sem):
    wide, block = own.shape[0], to.shape[1]
    inner = rest.shape[1]
    begin = pl.multiple_of(part_numbers()[j] * inner + n * block, block)
    return [
        pltpu.make_async_copy(own.at[:, pl.ds(begin, block)], to.at[pl.ds(0, wide), :], sem),
        pltpu.make_async_copy(
            rest.at[:, pl.ds(pl.multiple_of(n * block, block), block)],
            to.at[pl.ds(wide, rest.shape[0]), :],
            sem,
        ),
    ]


def hidden_kernel(*refs, numbers, opening, closing, riding, n_col):
    count = len(numbers)
    refs = list(refs)

    def take(n):
        got, refs[:n] = refs[:n], []
        return got

    f_ref, b1_ref, own1, own2 = take(4)
    rest1, rest2 = take(count), take(count)
    if not opening:
        (sum_in,) = take(1)
    if closing:
        x_ref, bias = take(2)
    if riding:
        (cot,) = take(1)
    act_ref, slope_ref = take(2)
    if riding:
        (dz,) = take(1)
    (out_ref,) = take(1)
    total, w1, w2, w_sem = take(4)
    step, steps = pl.program_id(0), pl.num_programs(0)
    dp, row, col = here()
    twin = (dp, 1 - row, col)
    block = w1.shape[2]
    blocks = rest1[0].shape[1] // block
    slot = lax.rem(step, 2)

    def fetch(s):
        for i in range(count):

            @pl.when(s // blocks == i)
            def _():
                n = lax.rem(s, blocks)
                at = lax.rem(s, 2)
                for copy in weight_copies(
                    own1, rest1[i], numbers[i], n, w1.at[at], w_sem.at[0, at]
                ) + weight_copies(own2, rest2[i], numbers[i], n, w2.at[at], w_sem.at[1, at]):
                    copy.start()

    if closing:
        away, came, s_s, s_r = take(4)
    if riding:
        begin, turn, end = cotangent_rider(cot, dz, *take(4), n_col=n_col)

    @pl.when(step == 0)
    def _():
        fetch(step)
        if opening:
            total[...] = jnp.zeros_like(total)
        else:
            total[...] = sum_in[...]
        if closing:
            meet([twin])
        if riding:
            begin()

    @pl.when(step + 1 < steps)
    def _():
        fetch(step + 1)

    for i, w in enumerate((w1, w2)):
        pltpu.make_async_copy(w.at[slot], w.at[slot], w_sem.at[i, slot]).wait()

    def one_part(t, carry):
        rows = pl.ds(pl.multiple_of(t * 256, 256), 256)
        h = mm(f_ref[rows, :], w1[slot]) + b1_ref[0]
        square = h * h
        bend = jnp.tanh(h * (ROOT + (ROOT * CUBE) * square))
        half = 0.5 + 0.5 * bend
        act = (h * half).astype(low)
        act_ref[0, rows, :] = act
        slope = half + (0.5 * h) * (1.0 - bend * bend) * (ROOT + (3.0 * ROOT * CUBE) * square)
        slope_ref[0, rows, :] = slope.astype(low)
        total[rows, :] += mm_nt(act, w2[slot])
        return carry

    lax.fori_loop(0, f_ref.shape[0] // 256, one_part, 0)

    @pl.when(step == steps - 1)
    def _():
        if riding:
            turn()
        if not closing:
            out_ref[...] = total[...]
        else:
            rows = came.shape[0]
            sent = []
            for t in range(rows // CUT):
                at = pl.ds(t * CUT, CUT)
                begin = pl.multiple_of((1 - row) * rows + t * CUT, CUT)
                away[at, :] = total[pl.ds(begin, CUT), :].astype(low)
                copy = remote(away.at[at, :], came.at[at, :], s_s.at[t], s_r.at[t], twin)
                copy.start()
                sent.append(copy)
            for t in range(rows // CUT):
                at = pl.ds(t * CUT, CUT)
                begin = pl.multiple_of(row * rows + t * CUT, CUT)
                sent[t].wait()
                branch = total[pl.ds(begin, CUT), :] + came[at, :].astype(f32)
                out_ref[at, :] = (x_ref[at, :] + (branch + bias[...])).astype(low)
        if riding:
            end()


def hidden_forward(f, b1, own1, own2, rest1, rest2, numbers, number, sum_in=None, x=None, bias=None,
                   cotangent=None, n_col=0):
    tokens, width = f.shape
    inner = rest1[0].shape[1]
    count = len(numbers)
    block = min(512, inner)
    blocks = inner // block
    rows = tokens // 2
    opening, closing = sum_in is None, x is not None
    dma = pltpu.SemaphoreType.DMA

    def still(shape):
        return pl.BlockSpec(shape, lambda s: (0,) * len(shape))

    active = pl.BlockSpec((1, tokens, block), lambda s: (s // blocks, 0, lax.rem(s, blocks)))
    args = [f, b1, own1, own2, *rest1, *rest2]
    in_specs = [
        still((tokens, width)),
        pl.BlockSpec((1, 1, block), lambda s: (s // blocks, 0, lax.rem(s, blocks))),
    ] + [ANYWHERE] * (2 + 2 * count)
    out_specs = [active, active]
    out_shape = [jax.ShapeDtypeStruct((count, tokens, inner), low)] * 2
    scratch = [
        pltpu.VMEM((tokens, width), f32),
        pltpu.VMEM((2, width, block), low),
        pltpu.VMEM((2, width, block), low),
        dma((2, 2)),
    ]
    if not opening:
        args.append(sum_in)
        in_specs.append(still((tokens, width)))
    if closing:
        args += [x, bias[None]]
        in_specs += [still((rows, width)), still((1, width))]
        out_shape.append(jax.ShapeDtypeStruct((rows, width), low))
        scratch += [pltpu.VMEM((rows, width), low), pltpu.VMEM((rows, width), low)]
        scratch += [dma((rows // CUT,)), dma((rows // CUT,))]
    else:
        out_shape.append(jax.ShapeDtypeStruct((tokens, width), f32))
    out_specs.append(still(out_shape[-1].shape))
    if cotangent is not None:
        args.append(cotangent)
        in_specs.append(still(cotangent.shape))
        out_shape.insert(2, jax.ShapeDtypeStruct((2, rows, width), low))
        out_specs.insert(2, ANYWHERE)
        scratch += [dma((n_col,))] * 4
    params = dict(vmem_limit_bytes=VMEM)
    if closing or cotangent is not None:
        params.update(collective_id=number, has_side_effects=True)
    return pl.pallas_call(
        functools.partial(
            hidden_kernel, numbers=numbers, opening=opening, closing=closing,
            riding=cotangent is not None, n_col=n_col,
        ),
        grid=(count * blocks,),
        in_specs=in_specs,
        out_specs=out_specs,
        out_shape=out_shape,
        scratch_shapes=scratch,
        compiler_params=pltpu.CompilerParams(**params),
        name="hidden_forward",
    )(*args)


def hidden_back_kernel(
    dz_ref, dzt_ref, ft_ref, rows_out, own1, own2, *refs, n_col, places,
):
    rest1, rest2 = refs[:PARTS], refs[PARTS : 2 * PARTS]
    calls = 1 + max(p[0] for p in places)
    acts, slopes = refs[2 * PARTS : 2 * PARTS + calls], refs[2 * PARTS + calls : 2 * (PARTS + calls)]
    (
        g1_ref, g2_ref, gb_ref, df_ref, got_a, got_b, home, far_a, far_b, dh_low, total, away_a, away_b,
        s_s, r_s, h_s, h_r, away_f, f_s, f_r, w1, w2, act_ref, slope_ref, w_sem,
    ) = refs[2 * (PARTS + calls) :]
    block = g1_ref.shape[2]
    inners = rest1[0].shape[1] // block
    step = pl.program_id(0)
    last = pl.num_programs(0) - 1
    order, inner = step // inners, lax.rem(step, inners)
    slot = lax.rem(step, 2)

    def fetch(s):
        for i, j in enumerate(ORDER):

            @pl.when(s // inners == i)
            def _():
                n, at = lax.rem(s, inners), lax.rem(s, 2)
                lanes = pl.ds(pl.multiple_of(n * block, block), block)
                call, index = places[j]
                copies = weight_copies(own1, rest1[j], j, n, w1.at[at], w_sem.at[0, at])
                copies += weight_copies(own2, rest2[j], j, n, w2.at[at], w_sem.at[1, at])
                for src, to, k in ((acts, act_ref, 2), (slopes, slope_ref, 3)):
                    copies.append(
                        pltpu.make_async_copy(
                            src[call].at[index, :, lanes], to.at[at], w_sem.at[k, at]
                        )
                    )
                for copy in copies:
                    copy.start()

    by_x, by_y = plane()
    half = got_a.shape[1]
    dp, row, col = here()

    @pl.when(step == 0)
    def _():
        group = [
            (dp, r, lax.rem(col + k, n_col)) for r in (row, 1 - row) for k in range(n_col)
        ]
        meet(group[1:] + [by_x, by_y])
        total[...] = jnp.zeros_like(total)
        send_home(rows_out, home, h_s, h_r, n_col)
        fetch(step)

    @pl.when(step < last)
    def _():
        fetch(step + 1)

    gb_ref[...] = jnp.zeros_like(gb_ref)
    for i, w in enumerate((w1, w2, act_ref, slope_ref)):
        pltpu.make_async_copy(w.at[slot], w.at[slot], w_sem.at[i, slot]).wait()

    def one_part(t, carry):
        rows = pl.ds(pl.multiple_of(t * 256, 256), 256)
        dh = (mm(dz_ref[rows, :], w2[slot]) * slope_ref[slot, rows, :].astype(f32)).astype(low)
        dh_low[rows, :] = dh
        gb_ref[0] += jnp.sum(dh.astype(f32), axis=0, keepdims=True)
        total[rows, :] += mm_nt(dh, w1[slot])
        return carry

    lax.fori_loop(0, dz_ref.shape[0] // 256, one_part, 0)

    def one_grad(t, carry):
        rows = pl.ds(pl.multiple_of(t * 256, 256), 256)
        g2_ref[0, rows, :] = mm(dzt_ref[rows, :], act_ref[slot]).astype(low)
        g1_ref[0, rows, :] = mm(ft_ref[rows, :], dh_low[...]).astype(low)
        return carry

    lax.fori_loop(0, ft_ref.shape[0] // 256, one_grad, 0)

    lanes = pl.ds(pl.multiple_of(inner * block, block), block)

    def hop(which, slot, n):
        away, got, to = [(away_a, got_a, by_x), (away_b, got_b, by_y)][which]
        at = pl.ds(n * block, block)
        return remote(
            away.at[slot, :, at], got.at[slot, :, at], s_s.at[which, slot, n],
            r_s.at[which, slot, n], to,
        )

    def far_hop(which):
        got, to = [(far_a, by_x), (far_b, by_y)][which]
        return remote(away_f.at[which], got, f_s.at[which], f_r.at[which], to)

    for at, which, slot in ((0, 0, 0), (0, 1, 0), (1, 0, 1), (2, 1, 1)):

        @pl.when(order == at)
        def _():
            away = (away_a, away_b)[which]
            away[slot, :, lanes] = g1_ref[0, which * half : (which + 1) * half, :]

        for n in range(got_a.shape[2] // block):

            @pl.when((order == at) & (inner == n))
            def _():
                hop(which, slot, n).start()

    @pl.when((order == 0) & (inner == 0))
    def _():
        for which in range(2):
            away_f[which] = g2_ref[0, which * half : (which + 1) * half, :]
            far_hop(which).start()

    @pl.when(step == last)
    def _():
        for which in range(2):
            far_hop(which).wait()
        df_ref[...] = total[...].astype(low)
        for which in range(2):
            for slot in range(2):
                for n in range(got_a.shape[2] // block):
                    hop(which, slot, n).wait()
        wait_home(rows_out, home, h_s, h_r, n_col)


def hidden_backward(dz, f, own1, own2, rest1, rest2, acts, slopes, places, rows_out, n_col, number):
    tokens, width = f.shape
    inner = rest1[0].shape[1]
    block = min(512, inner)
    blocks = inner // block

    def number_of(s):
        j = s // blocks
        return jnp.where(j == 0, PARTS - 1, jnp.where(j == PARTS - 1, 0, j))

    def still(shape):
        return pl.BlockSpec(shape, lambda s: (0,) * len(shape))

    weight = pl.BlockSpec((1, width, block), lambda s: (number_of(s), 0, lax.rem(s, blocks)))
    landing = jax.ShapeDtypeStruct((2, width // 2, inner), low)
    grad = jax.ShapeDtypeStruct((PARTS, width, inner), low)
    vm, dma = pltpu.VMEM, pltpu.SemaphoreType.DMA
    return pl.pallas_call(
        functools.partial(hidden_back_kernel, n_col=n_col, places=places),
        grid=(PARTS * blocks,),
        in_specs=[still((tokens, width)), still((width, tokens)), still((width, tokens))]
        + [still(rows_out.shape)]
        + [ANYWHERE] * (2 + 2 * PARTS + 2 * len(acts)),
        out_specs=[
            weight,
            weight,
            pl.BlockSpec((1, 1, block), lambda s: (number_of(s), 0, lax.rem(s, blocks))),
            still((tokens, width)),
            ANYWHERE, ANYWHERE, ANYWHERE, ANYWHERE, ANYWHERE,
        ],
        out_shape=[
            grad,
            grad,
            jax.ShapeDtypeStruct((PARTS, 1, inner), f32),
            jax.ShapeDtypeStruct((tokens, width), low),
            landing,
            landing,
            jax.ShapeDtypeStruct((n_col * rows_out.shape[0], width // n_col), low),
            jax.ShapeDtypeStruct((width // 2, block), low),
            jax.ShapeDtypeStruct((width // 2, block), low),
        ],
        scratch_shapes=[
            vm((tokens, block), low),
            vm((tokens, width), f32),
            vm(landing.shape, low),
            vm(landing.shape, low),
            dma((2, 2, blocks)),
            dma((2, 2, blocks)),
            dma((n_col,)),
            dma((n_col,)),
            vm((2, width // 2, block), low),
            dma((2,)),
            dma((2,)),
            vm((2, width, block), low),
            vm((2, width, block), low),
            vm((2, tokens, block), low),
            vm((2, tokens, block), low),
            dma((4, 2)),
        ],
        compiler_params=pltpu.CompilerParams(
            vmem_limit_bytes=VMEM, collective_id=number, has_side_effects=True
        ),
        name="hidden_backward",
    )(dz, dz.T, f.T, rows_out, own1, own2, *rest1, *rest2, *acts, *slopes)


def start_kernel(
    tokens, encoder, vec_f, vec_c, *refs, n_col,
):
    weights, (x_ext, enc, all_f, all_c), full = refs[:8], refs[8:12], refs[12:20]
    (zeros, w_send, w_recv, w_own, t_send, t_recv, v_send, v_recv, z_sem, z_send, z_recv, e_send,
     e_recv, o_sem) = refs[20:]
    dp, row, col = here()
    part = lax.rem(dp, PARTS)
    twin = (dp, 1 - row, col)
    flip = [
        dp + 1 - 2 * lax.rem(dp, 2),
        dp + 2 - 4 * lax.rem(dp // 2, 2),
    ]
    by_x, by_y = (flip[0], row, col), (flip[1], row, col)
    part_x, part_y = lax.rem(flip[0], PARTS), lax.rem(flip[1], PARTS)
    shift = [lax.rem(col + k, n_col) for k in range(n_col)]
    group = [(dp, r, c) for r in (row, 1 - row) for c in shift][1:]
    meet(group + [by_x, by_y])

    wide = tokens.shape[1]
    deep = n_col * wide
    rest = deep - wide

    def chunk(index, size):
        return pl.ds(pl.multiple_of(index * size, size), size)

    to_right, to_left = (dp, row, lax.rem(col + 1, n_col)), (dp, row, lax.rem(col + n_col - 1, n_col))

    def weight_chunk(i, k):
        w = weights[i]
        if i % 4 < 3:
            return full[i].at[pl.ds(k * wide, wide), chunk(part, w.shape[1] // PARTS)]
        return full[i].at[chunk(part, w.shape[0] // PARTS), pl.ds(k * wide, wide)]

    def weight_slice(i):
        w = weights[i]
        if i % 4 < 3:
            return w.at[:, chunk(part, w.shape[1] // PARTS)]
        return w.at[chunk(part, w.shape[0] // PARTS), :]

    def enc_chunk(k):
        return enc.at[chunk(row, encoder.shape[0]), pl.ds(k * wide, wide)]

    def piece(i, k):
        if i == 8:
            return enc_chunk(k)
        return weight_chunk(i, k)

    def own_piece(i):
        return encoder if i == 8 else weight_slice(i)

    def enc_twin(k):
        return remote(own_piece(8) if k == 0 else enc_chunk(k), enc_chunk(k), e_send.at[k],
                      e_recv.at[k], twin)

    def rightward(i, h):
        src = own_piece(i) if h == 1 else piece(i, n_col + 1 - h)
        k = n_col - h
        return remote(src, piece(i, k), z_send.at[i, 0, h - 1], z_recv.at[i, k - 1], to_right)

    def leftward(i, h):
        src = own_piece(i) if h == 1 else piece(i, h - 1)
        return remote(src, piece(i, h), z_send.at[i, 1, h - 1], z_recv.at[i, h - 1], to_left)

    def right_valid(h):
        return (col >= h - 1) & (col < n_col - 1)

    def left_valid(h):
        return (col <= n_col - h) & (col > 0)

    def send_along(i, h):
        @pl.when(right_valid(h))
        def _():
            rightward(i, h).start()

        @pl.when(left_valid(h))
        def _():
            leftward(i, h).start()

    def take(i, h):
        @pl.when(col >= h)
        def _():
            rightward(i, h).wait_recv()

        @pl.when(col < n_col - h)
        def _():
            leftward(i, h).wait_recv()

    def weight_own(i):
        w = weights[i]
        place = full[i].at[pl.ds(0, wide), :] if i % 4 < 3 else full[i].at[:, pl.ds(0, wide)]
        return pltpu.make_async_copy(w, place, w_own.at[i])

    def weight_part(i, which, begin, size):
        if i % 4 < 3:
            return full[i].at[pl.ds(begin, size), chunk(which, weights[i].shape[1] // PARTS)]
        return full[i].at[chunk(which, weights[i].shape[0] // PARTS), pl.ds(begin, size)]

    def weight_plane(i, stage):
        half = rest // 2
        which, begin, size, to = [
            (part, wide, rest, by_x),
            (part, wide, rest, by_y),
            (part_x, wide, half, by_y),
            (part_y, wide + half, half, by_x),
        ][stage]
        ref = weight_part(i, which, begin, size)
        return remote(ref, ref, w_send.at[i, stage], w_recv.at[i, stage], to)

    def token_piece(j, slot):
        rows = tokens.shape[0] // n_col
        to_col = 2 * row + j // 2 + (1 - slot)
        k = lax.rem(col + n_col - lax.rem(to_col, n_col), n_col)
        src = tokens.at[pl.ds(j * rows, rows), :]
        dst = x_ext.at[slot, :, chunk(k, wide)]
        local = (row == j % 2) & (col == to_col)
        valid = to_col < n_col
        return src, dst, k, local, valid, (dp, j % 2, to_col)

    def send_tokens(slot):
        for j in range(n_col):
            src, dst, k, local, valid, to = token_piece(j, slot)

            @pl.when(valid & local)
            def _():
                pltpu.make_async_copy(src, dst, t_recv.at[slot, k]).start()

            @pl.when(valid & jnp.logical_not(local))
            def _():
                remote(src, dst, t_send.at[slot, j], t_recv.at[slot, k], to).start()

    def vectors(k):
        to = (dp, row, lax.rem(col + n_col - k, n_col))
        return [
            remote(vec_f, all_f.at[:, pl.ds(k * wide, wide)], v_send.at[0, k], v_recv.at[0, k], to),
            remote(vec_c, all_c.at[col], v_send.at[1, k], v_recv.at[1, k], to),
        ]

    own_vectors = [
        pltpu.make_async_copy(encoder, enc_chunk(0), o_sem),
        pltpu.make_async_copy(vec_f, all_f.at[:, pl.ds(0, wide)], v_recv.at[0, 0]),
        pltpu.make_async_copy(vec_c, all_c.at[col], v_recv.at[1, 0]),
    ]
    ks = range(1, n_col)
    for i in range(8):
        send_along(i, 1)
    for k in ks:
        for copy in vectors(k):
            copy.start()
    for i in range(8):
        weight_own(i).start()
    for copy in own_vectors:
        copy.start()
    enc_twin(0).start()
    for h in (1, 2):
        for i in range(8):
            take(i, h)
            send_along(i, h + 1)
    send_along(8, 1)
    send_tokens(1)
    for i in range(8):
        take(i, 3)
        weight_plane(i, 0).start()
        weight_plane(i, 1).start()
    take(8, 1)
    send_along(8, 2)
    send_tokens(0)

    @pl.when(col == 0)
    def _():
        zeros[...] = jnp.zeros_like(zeros)
        clear = pltpu.make_async_copy(zeros, x_ext.at[0], z_sem)
        clear.start()
        clear.wait()

    for i in range(8):
        weight_plane(i, 0).wait_recv()
        weight_plane(i, 2).start()
        weight_plane(i, 1).wait_recv()
        weight_plane(i, 3).start()
        if i == 3:
            take(8, 2)
            send_along(8, 3)
    take(8, 3)
    for k in ks:
        enc_twin(k).start()
    for i in range(8):
        weight_plane(i, 2).wait_recv()
        weight_plane(i, 3).wait_recv()
        weight_own(i).wait()
        for stage in range(4):
            weight_plane(i, stage).wait_send()
    for k in range(n_col):
        enc_twin(k).wait()
    for i in range(9):
        for h in ks:

            @pl.when(right_valid(h))
            def _():
                rightward(i, h).wait_send()

            @pl.when(left_valid(h))
            def _():
                leftward(i, h).wait_send()

    for copy in own_vectors:
        copy.wait()
    for k in ks:
        for copy in vectors(k):
            copy.wait()
    for slot in (1, 0):
        for j in range(n_col):
            src, dst, k, local, valid, to = token_piece(j, slot)

            @pl.when(valid & jnp.logical_not(local))
            def _():
                remote(src, dst, t_send.at[slot, j], t_recv.at[slot, k], to).wait_send()

        for k in range(n_col):
            rows = tokens.shape[0] // n_col
            came = pltpu.make_async_copy(
                tokens.at[pl.ds(0, rows), :],
                x_ext.at[slot, :, pl.ds(k * wide, wide)],
                t_recv.at[slot, k],
            )
            if slot == 1:
                came.wait()
            else:

                @pl.when(col > 0)
                def _():
                    came.wait()


def start(tokens, encoder, vec_f, vec_c, weights, n_col):
    wide = tokens.shape[1]
    deep = n_col * wide
    rows = tokens.shape[0] // n_col
    shapes = [
        jax.ShapeDtypeStruct((2, rows, deep), low),
        jax.ShapeDtypeStruct((2 * encoder.shape[0], deep), low),
        jax.ShapeDtypeStruct((vec_f.shape[0], deep), f32),
        jax.ShapeDtypeStruct((n_col,) + vec_c.shape, f32),
    ]
    for i, w in enumerate(weights):
        shapes.append(
            jax.ShapeDtypeStruct((deep, w.shape[1]) if i % 4 < 3 else (w.shape[0], deep), low)
        )
    dma = pltpu.SemaphoreType.DMA
    return pl.pallas_call(
        functools.partial(start_kernel, n_col=n_col),
        in_specs=[IN_VMEM] * 12,
        out_specs=[ANYWHERE] * 12,
        out_shape=shapes,
        scratch_shapes=[
            pltpu.VMEM((rows, deep), low),
            dma((8, 4)), dma((8, 4)), dma((8,)),
            dma((2, n_col)), dma((2, n_col)),
            dma((2, n_col)), dma((2, n_col)),
            dma, dma((9, 2, n_col - 1)), dma((9, n_col - 1)), dma((n_col,)), dma((n_col,)), dma,
        ],
        compiler_params=pltpu.CompilerParams(
            collective_id=1, has_side_effects=True, vmem_limit_bytes=VMEM
        ),
        name="start",
    )(tokens, encoder, vec_f, vec_c, *weights)


def norm_rows(x):
    center = jnp.mean(x, axis=1, keepdims=True)
    spread = jnp.mean(x * x, axis=1, keepdims=True) - center * center
    scaling = lax.rsqrt(spread + norm_epsilon)
    return (x - center) * scaling, scaling


CUT = 256


def enter_kernel(x_ref, gain, shift, a_ref, sends, recvs):
    dp, row, col = here()
    twin = (dp, 1 - row, col)
    meet([twin])
    slots, rows = x_ref.shape[:2]

    def place(slot):
        return a_ref.at[slot, pl.ds(pl.multiple_of(row * rows, rows), rows), :]

    copies = []
    for slot in reversed(range(slots)):
        for t in range(rows // CUT):
            normed, _ = norm_rows(x_ref[slot, pl.ds(t * CUT, CUT), :].astype(f32))
            begin = pl.multiple_of(row * rows + t * CUT, CUT)
            a_ref[slot, pl.ds(begin, CUT), :] = (normed * gain[...] + shift[...]).astype(low)
        copy = remote(place(slot), place(slot), sends.at[slot], recvs.at[slot], twin)
        copy.start()
        copies.append(copy)
    for copy in copies:
        copy.wait()


def enter(x_ext, gain, shift, number):
    slots, rows, deep = x_ext.shape
    return pl.pallas_call(
        enter_kernel,
        in_specs=[IN_VMEM] * 3,
        out_specs=IN_VMEM,
        out_shape=jax.ShapeDtypeStruct((slots, 2 * rows, deep), low),
        scratch_shapes=[pltpu.SemaphoreType.DMA((slots,)), pltpu.SemaphoreType.DMA((slots,))],
        compiler_params=pltpu.CompilerParams(
            collective_id=number, has_side_effects=True, vmem_limit_bytes=VMEM
        ),
        name="enter",
    )(x_ext, gain[None], shift[None])


def junction_kernel(*refs, kinds, mode, then):
    dp, row, col = here()
    twin = (dp, 1 - row, col)
    meet([twin])
    refs = list(refs)
    sources = []
    for kind in kinds:
        sources.append((kind, refs.pop(0), refs.pop(0) if kind != "sum" else None))
    if then:
        then_w, then_b = refs.pop(0), refs.pop(0)
    if mode == "forward":
        x_ref, bias, gain, shift, x_out, full, *refs = refs
    elif mode == "backward":
        res_ref, x_ref, gain, dx_out, full, stats, *refs = refs
    if mode != "sum":
        if then:
            then_out = refs.pop(0)
        away, came, s1, r1, s2, r2 = refs
    else:
        out, away, came, s1, r1 = refs
    rows = came.shape[0]
    cuts = rows // CUT

    def follow(begin):
        at = pl.ds(begin, CUT)
        if then == "queries":
            value = (mm(full[at, :], then_w[...]) + then_b[...]).astype(low)
            then_out[at, :] = value * low(HEAD_DIM**-0.5)
        elif then:
            then_out[at, :] = mm_nt(full[at, :], then_w[...]).astype(low)

    def partial(begin):
        total = None
        for kind, g, w in sources:
            part = g[pl.ds(begin, CUT), :]
            if kind == "sum":
                part = part.astype(f32)
            elif kind == "nt":
                part = mm_nt(part, w[...])
            else:
                part = mm(part, w[...])
            total = part if total is None else total + part
        return total

    sent = []
    for t in range(cuts):
        at = pl.ds(t * CUT, CUT)
        away[at, :] = partial(pl.multiple_of((1 - row) * rows + t * CUT, CUT)).astype(low)
        copy = remote(away.at[at, :], came.at[at, :], s1.at[t], r1.at[t], twin)
        copy.start()
        sent.append(copy)
    gathered = []
    sums = [0.0] * 4
    for t in range(cuts):
        at = pl.ds(t * CUT, CUT)
        begin = pl.multiple_of(row * rows + t * CUT, CUT)
        own = partial(begin)
        sent[t].wait_recv()
        total = own + came[at, :].astype(f32)
        if mode == "sum":
            out[at, :] = total.astype(low)
            continue
        if mode == "forward":
            x = x_ref[at, :].astype(f32) + (total + bias[...])
            x_out[at, :] = x
            normed, _ = norm_rows(x)
            result = (normed * gain[...] + shift[...]).astype(low)
        else:
            normed, scaling = norm_rows(x_ref[at, :].astype(f32))
            upstream = total * gain[...]
            mean_up = jnp.mean(upstream, axis=1, keepdims=True)
            mean_both = jnp.mean(upstream * normed, axis=1, keepdims=True)
            res = res_ref[at if res_ref.shape[0] == rows else pl.ds(begin, CUT), :].astype(f32)
            dx = res + scaling * (upstream - mean_up - normed * mean_both)
            dx_out[at, :] = dx.astype(dx_out.dtype)
            result = dx.astype(low)
            for i, value in enumerate((total * normed, total, result.astype(f32), res)):
                sums[i] = sums[i] + jnp.sum(value, axis=0, keepdims=True)
        full[pl.ds(begin, CUT), :] = result
        place = full.at[pl.ds(begin, CUT), :]
        copy = remote(place, place, s2.at[t], r2.at[t], twin)
        copy.start()
        gathered.append(copy)
        follow(begin)
    if mode == "backward":
        for i in range(4):
            stats[i : i + 1, :] = sums[i]
    for copy in sent:
        copy.wait_send()
    for t, copy in enumerate(gathered):
        copy.wait()
        follow(pl.multiple_of((1 - row) * rows + t * CUT, CUT))


def junction(mode, sources, others, number, then=None):
    kinds = [x[0] for x in sources]
    first = sources[0]
    tokens = first[1].shape[0]
    deep = first[1].shape[1]
    if first[0] != "sum":
        deep = first[2].shape[0 if first[0] == "nt" else 1]
    rows = tokens // 2
    flat = [x for source in sources for x in source[1:]]
    dma = pltpu.SemaphoreType.DMA((rows // CUT,))
    wide_rows = jax.ShapeDtypeStruct((rows, deep), f32)
    every = jax.ShapeDtypeStruct((tokens, deep), low)
    shapes = {
        "forward": [wide_rows, every],
        "backward": [wide_rows, every, jax.ShapeDtypeStruct((8, deep), f32)],
        "sum": [jax.ShapeDtypeStruct((rows, deep), low)],
    }[mode]
    scratch = [pltpu.VMEM((rows, deep), low), pltpu.VMEM((rows, deep), low), dma, dma]
    if mode in ("forward", "backward"):
        scratch += [dma, dma]
    if then:
        columns = then[1].shape[1 if then[0] == "queries" else 0]
        shapes.append(jax.ShapeDtypeStruct((tokens, columns), low))
        others = [*then[1:], *others]
    args = flat + [x[None] if x.ndim == 1 else x for x in others]
    out = pl.pallas_call(
        functools.partial(
            junction_kernel, kinds=kinds, mode=mode, then=then[0] if then else None
        ),
        in_specs=[IN_VMEM] * len(args),
        out_specs=[IN_VMEM] * len(shapes),
        out_shape=shapes,
        scratch_shapes=scratch,
        compiler_params=pltpu.CompilerParams(
            collective_id=number, has_side_effects=True, vmem_limit_bytes=VMEM
        ),
        name="junction_" + mode,
    )(*args)
    return out if len(out) > 1 else out[0]


def plane_copies(full, part, parts, by_x, by_y, sends, recvs):
    size = full.shape[1]
    half = size // 2

    def copy(stage):
        which, begin, count, to = [
            (part, 0, size, by_x), (part, 0, size, by_y),
            (parts[1], 0, half, by_y), (parts[2], half, half, by_x),
        ][stage]
        ref = full.at[which, pl.ds(begin, count), :]
        return remote(ref, ref, sends.at[stage], recvs.at[stage], to)

    return copy


def with_other_bits(value, store, which, sends, recvs, partners):
    for i, partner in enumerate(partners):
        store[i, 0] = value.astype(low)
        copy = remote(
            store.at[i, 0], store.at[i, 1 + which], sends.at[which, i], recvs.at[which, i], partner
        )
        copy.start()
        copy.wait()
        value = value + store[i, 1 + which].astype(f32)
    return value


def bit_partners(n_dp):
    dp, row, col = here()
    bits = [1 << b for b in range(n_dp.bit_length() - 1)]
    return [(dp + b - 2 * b * lax.rem(dp // b, 2), row, col) for b in bits]


class PlaneSum:
    def __init__(self, src, first, mid, second, sems, n_col):
        self.src, self.first, self.mid, self.second = src, first, mid, second
        self.f_s, self.f_r, self.m_s, self.m_r = sems
        self.n_col, self.size = n_col, mid.shape[0] // n_col
        self.parts, self.ways = part_numbers(), plane()
        self.turns = [q for pair in zip(range(n_col // 2), range(n_col // 2, n_col)) for q in pair]

    def rows(self, q):
        return pl.ds(q * self.size, self.size)

    def upper(self, q):
        return 2 * q < self.n_col

    def hop(self, which, q):
        to, side = (self.ways[1], 2) if self.upper(q) else (self.ways[0], 1)
        src = self.src.at[self.parts[3] if which else self.parts[side], self.rows(q), :]
        dst = self.first.at[which, self.rows(q), :]
        return remote(src, dst, self.f_s.at[which, q], self.f_r.at[which, q], to)

    def hop2(self, q):
        to = self.ways[0] if self.upper(q) else self.ways[1]
        at = self.rows(q)
        return remote(self.mid.at[at, :], self.second.at[at, :], self.m_s.at[q], self.m_r.at[q], to)

    def start(self):
        for q in self.turns:
            self.hop(1, q).start()

    def turn(self):
        for q in self.turns:
            at = self.rows(q)
            self.hop(1, q).wait_recv()
            keep = self.parts[1] if self.upper(q) else self.parts[2]
            value = self.src[keep, at, :].astype(f32) + self.first[1, at, :].astype(f32)
            self.mid[at, :] = value.astype(low)
            self.hop2(q).start()
            self.hop(0, q).start()

    def finish(self, out):
        for q in self.turns:
            at = self.rows(q)
            self.hop(0, q).wait_recv()
            self.hop2(q).wait_recv()
            value = self.src[self.parts[0], at, :].astype(f32) + self.first[0, at, :].astype(f32)
            out[at, :] = (value + self.second[at, :].astype(f32)).astype(low)

    def end(self):
        for q in self.turns:
            self.hop(0, q).wait_send()
            self.hop(1, q).wait_send()
            self.hop2(q).wait_send()


def fold_kernel(
    dq, dk, dv, a_ext, wk, wv, res, gain, ga, enc_in,
    dy_in, o_in, wq_in, x0_in, g2, near_a, near_b, far_back_a, far_back_b, own1,
    sums, tg, stats, a_sum, b_sum, hidden0, q_own, enc_out,
    load, load_own, own_q, h_out, h_l, h_r, gb, fa, ma, sa, fb, mb, sb, away_b, came_b, away_l,
    came_l, da_got, enc_got, extra,
    l_s, lo_s, r_s, hz_s, hz_r, fa_s, fa_r, ma_s, ma_r, fb_s, fb_r, mb_s, mb_r, b_s, b_r, c_s, c_r,
    d_s, d_r, e_s, e_r, g_s, g_r, x_s, x_r,
    *, n_col, n_dp,
):
    dp, row, col = here()
    parts = part_numbers()
    part = parts[0]
    by_bit = bit_partners(n_dp)
    by_x, by_y = by_bit[:2]
    twin = (dp, 1 - row, col)
    cols = [(dp, row, lax.rem(col + k, n_col)) for k in range(n_col)]
    left = cols[n_col - 1]
    meet([twin] + by_bit + cols[1:])
    ks = range(1, n_col)
    deep = tg.shape[1]
    wide = deep // n_col
    half = near_a.shape[0]
    rows = tg.shape[0]
    cuts = rows // CUT
    window = dk.shape[0] - dq.shape[0]
    sum_a = PlaneSum(ga, fa, ma, sa, (fa_s, fa_r, ma_s, ma_r), n_col)
    sum_b = PlaneSum(gb, fb, mb, sb, (fb_s, fb_r, mb_s, mb_r), n_col)
    line = LineSum(h_out, h_l, h_r, hz_s, hz_r, cols)

    loads = []
    for i, sources in enumerate(((near_a, far_back_a), (near_b, far_back_b))):
        spot = pl.ds(i * half, half)
        for n, src in enumerate((g2.at[0, spot, :],) + sources):
            loads.append(pltpu.make_async_copy(src, load.at[n, spot, :], l_s.at[i, n]))
    load_p = pltpu.make_async_copy(own1, load_own, lo_s)
    count = dq.shape[1]
    dy, x0 = load.at[0], load.at[1, pl.ds(0, rows), :]
    o, wq = load.at[2, :, pl.ds(0, count)], load.at[2, :, pl.ds(count, count)]
    reloads = [
        pltpu.make_async_copy(src, dst, r_s.at[n])
        for n, (src, dst) in enumerate(((dy_in, dy), (x0_in, x0), (o_in, o), (wq_in, wq)))
    ]

    def enc_hop(k):
        src = enc_in.at[:, pl.ds(k * wide, wide)]
        return remote(src, enc_got.at[k - 1], e_s.at[k - 1], e_r.at[k - 1], cols[k])

    for copy in loads + [load_p]:
        copy.start()
    sum_a.start()
    for copy in loads:
        copy.wait()
    for k in range(n_col):
        at = pl.ds(k * wide, wide)
        value = load[0, at, :].astype(f32) + load[1, at, :].astype(f32)
        value = (value + load[2, at, :].astype(f32)).astype(low)
        if k:
            h_out[k - 1] = value
        else:
            own_q[...] = value
    line.begin()
    for copy in reloads:
        copy.start()

    def before(begin):
        spot = pl.ds(begin, CUT)
        return mm_nt(dk[spot, :], wk[...]) + mm_nt(dv[spot, :], wv[...])

    def exchange(away, came, sends, recvs, t):
        spot = pl.ds(t * CUT, CUT)
        return remote(away.at[spot, :], came.at[spot, :], sends.at[t], recvs.at[t], twin)

    for t in range(cuts):
        spot = pl.ds(t * CUT, CUT)
        away_b[spot, :] = before(pl.multiple_of((1 - row) * rows + t * CUT, CUT)).astype(low)
        exchange(away_b, came_b, b_s, b_r, t).start()
    for t in range(cuts):
        spot = pl.ds(t * CUT, CUT)
        own = before(pl.multiple_of(row * rows + t * CUT, CUT))
        exchange(away_b, came_b, b_s, b_r, t).wait_recv()
        came_b[spot, :] = (own + came_b[spot, :].astype(f32)).astype(low)
    da_hop = remote(came_b, da_got, d_s, d_r, left)

    @pl.when(col > 0)
    def _():
        da_hop.start()

    @pl.when(col == n_col - 1)
    def _():
        da_got[...] = jnp.zeros_like(da_got)

    sum_a.turn()
    load_p.wait()
    value = with_other_bits(load_own[...].astype(f32), extra, 0, x_s, x_r, by_bit[2:])
    hidden0[part] = value.astype(low)
    spread = plane_copies(hidden0, part, parts, by_x, by_y, g_s, g_r)
    spread(0).start()
    spread(1).start()
    line.go(2)
    for copy in reloads:
        copy.wait()

    def last(begin):
        spot = pl.ds(begin, CUT)
        later = pl.ds(window + begin, CUT)
        value = mm_nt(dq[spot, :], wq[...]) + mm_nt(dk[later, :], wk[...])
        return value + mm_nt(dv[later, :], wv[...])

    for t in range(cuts):
        spot = pl.ds(t * CUT, CUT)
        away_l[spot, :] = last(pl.multiple_of((1 - row) * rows + t * CUT, CUT)).astype(low)
        exchange(away_l, came_l, c_s, c_r, t).start()

    size = gb.shape[2] // 4
    pairs = ((window, dq), (0, dk), (0, dv), (None, o))

    def one_block(i, carry):
        lanes = pl.ds(pl.multiple_of(i * wide, wide), wide)
        for n, (begin, other) in enumerate(pairs):
            source = dy[:, lanes] if begin is None else a_ext[pl.ds(begin, other.shape[0]), lanes]
            value = mm_tn(source, other[...]).astype(low)
            for p in range(PARTS):
                gb[p, lanes, n * size : (n + 1) * size] = value[:, p * size : (p + 1) * size]
        return carry

    lax.fori_loop(0, n_col, one_block, 0)
    sum_b.start()
    line.go(1)
    for k in ks:
        enc_hop(k).start()
    for n, (_, other) in enumerate(pairs):
        sums[n : n + 1, :] = jnp.sum(other[...].astype(f32), axis=0, keepdims=True)
    sum_a.finish(a_sum)
    sum_b.turn()

    @pl.when(col < n_col - 1)
    def _():
        da_hop.wait_recv()

    totals = [0.0, 0.0]
    for t in range(cuts):
        spot = pl.ds(t * CUT, CUT)
        own = last(pl.multiple_of(row * rows + t * CUT, CUT))
        exchange(away_l, came_l, c_s, c_r, t).wait_recv()
        total = own + came_l[spot, :].astype(f32)
        after = [da_got[spot, pl.ds(deep - wide, wide)], da_got[spot, pl.ds(0, deep - wide)]]
        total = total + jnp.concatenate(after, axis=1).astype(f32)
        normed, scaling = norm_rows(x0[spot, :].astype(f32))
        upstream = total * gain[...]
        mean_up = jnp.mean(upstream, axis=1, keepdims=True)
        mean_both = jnp.mean(upstream * normed, axis=1, keepdims=True)
        dx = res[spot, :] + scaling * (upstream - mean_up - normed * mean_both)
        tg[spot, :] = dx.astype(low)
        for i, value in enumerate((total * normed, total)):
            totals[i] = totals[i] + jnp.sum(value, axis=0, keepdims=True)
    for i in range(2):
        stats[i : i + 1, :] = totals[i]
    for stage in range(2):
        spread(stage).wait_recv()
        spread(2 + stage).start()
    value = line.total(own_q[...].astype(f32))
    value = with_other_bits(value, extra, 1, x_s, x_r, by_bit[2:])
    q_own[...] = value.astype(low)
    sum_b.finish(b_sum)
    spread(2).wait_recv()
    spread(3).wait_recv()
    value = enc_in[:, pl.ds(0, wide)].astype(f32)
    for k in ks:
        enc_hop(k).wait()
        value = value + enc_got[k - 1].astype(f32)
    enc_out[...] = value
    for stage in range(4):
        spread(stage).wait_send()
    line.end()
    sum_a.end()
    sum_b.end()
    for t in range(cuts):
        exchange(away_b, came_b, b_s, b_r, t).wait_send()
        exchange(away_l, came_l, c_s, c_r, t).wait_send()

    @pl.when(col > 0)
    def _():
        da_hop.wait_send()


def fold(dq, dk, dv, a_ext, dy, o, weights, res, x0, gain, ga, enc_in, riding, n_col, n_dp):
    sd, vm, dma = jax.ShapeDtypeStruct, pltpu.VMEM, pltpu.SemaphoreType.DMA
    rows, deep = x0.shape
    wide = deep // n_col
    columns, hidden = ga.shape[2], riding[0].shape[2]
    others, cuts = n_col - 1, rows // CUT
    more = max(n_dp.bit_length() - 3, 1)
    by_rows = vm((rows, deep), low)
    plane_memory = [vm((2, deep, columns), low), vm((deep, columns), low), vm((deep, columns), low)]
    plane_sems = [dma((2, n_col)), dma((2, n_col)), dma((n_col,)), dma((n_col,))]
    wq, wk, wv = weights
    return pl.pallas_call(
        functools.partial(fold_kernel, n_col=n_col, n_dp=n_dp),
        in_specs=[IN_VMEM] * 10 + [ANYWHERE] * 10,
        out_specs=[IN_VMEM] * 8,
        out_shape=[
            sd((8, dq.shape[1]), f32),
            sd((rows, deep), low),
            sd((8, deep), f32),
            sd((deep, columns), low),
            sd((deep, columns), low),
            sd((PARTS, wide, hidden), low),
            sd((wide, hidden), low),
            sd((enc_in.shape[0], wide), f32),
        ],
        scratch_shapes=[
            vm((3, deep, hidden), low),
            vm((wide, hidden), low),
            vm((wide, hidden), low),
            vm((others, wide, hidden), low),
            vm((others, wide, hidden), low),
            vm((others, wide, hidden), low),
            vm(ga.shape, low),
            *plane_memory, *plane_memory,
            by_rows, by_rows, by_rows, by_rows, by_rows,
            vm((others, enc_in.shape[0], wide), low),
            vm((more, 3, wide, hidden) if n_dp > PARTS else (1, 3, 16, 128), low),
            dma((2, 3)), dma, dma((4,)),
            dma((2, others)), dma((2, others)),
            *plane_sems, *plane_sems,
            dma((cuts,)), dma((cuts,)), dma((cuts,)), dma((cuts,)),
            dma, dma,
            dma((others,)), dma((others,)),
            dma((4,)), dma((4,)),
            dma((2, more)), dma((2, more)),
        ],
        compiler_params=pltpu.CompilerParams(
            collective_id=21, has_side_effects=True, vmem_limit_bytes=62 * 1024 * 1024
        ),
        name="fold",
    )(dq, dk, dv, a_ext, wk, wv, res, gain[None], ga, enc_in, dy, o, wq, x0, *riding)


def finish_kernel(
    a_sum, b_sum, q_own, small, tg,
    full_a, full_b, hidden1, small_out, tg_out,
    za, za_l, za_r, zb, zb_l, zb_r, s_cur, s_got, s_z, extra,
    za_s, za_t, zb_s, zb_t, g_s, g_r, s_s, s_r, sz_s, sz_r, t_s, t_r, x_s, x_r,
    *, n_col, n_dp,
):
    dp, row, col = here()
    parts = part_numbers()
    part = parts[0]
    by_bit = bit_partners(n_dp)
    by_x, by_y = by_bit[:2]
    twin = (dp, 1 - row, col)
    cols = [(dp, row, lax.rem(col + k, n_col)) for k in range(n_col)]
    meet([twin] + [(dp, 1 - row, c[2]) for c in cols[1:]] + cols[1:] + by_bit)
    wide = a_sum.shape[0] // n_col
    ks = range(1, n_col)
    line_a = LineSum(za, za_l, za_r, za_s, za_t, cols)
    line_b = LineSum(zb, zb_l, zb_r, zb_s, zb_t, cols)

    partners = [twin] + by_bit

    def small_hop(i):
        return remote(s_cur.at[i], s_got.at[i], s_s.at[i], s_r.at[i], partners[i])

    def small_z(k):
        return remote(
            s_cur.at[len(partners), k], s_z.at[k - 1], sz_s.at[k - 1], sz_r.at[k - 1], cols[k]
        )

    def small_step(i):
        if i == 0:
            s_cur[0] = small[...]
        elif i <= len(partners):
            small_hop(i - 1).wait_recv()
            got = s_got[i - 1]
            if i == 1:
                lane = lax.broadcasted_iota(jnp.int32, got.shape, 2)
                got = jnp.where(lane < wide, got, 0.0)
            s_cur[i] = s_cur[i - 1] + got
        if i < len(partners):
            small_hop(i).start()
        elif i == len(partners):
            for k in ks:
                small_z(k).start()
        else:
            value = s_cur[len(partners), 0]
            for k in ks:
                small_z(k).wait_recv()
                value = value + s_z[k - 1]
            small_out[...] = value

    spread_q = plane_copies(hidden1, part, parts, by_x, by_y, g_s.at[0], g_r.at[0])
    spread_a = plane_copies(full_a, part, parts, by_x, by_y, g_s.at[1], g_r.at[1])
    spread_b = plane_copies(full_b, part, parts, by_x, by_y, g_s.at[2], g_r.at[2])
    spreads = (spread_q, spread_a, spread_b)

    small_step(0)
    for line, buf, whole in ((line_a, za, a_sum), (line_b, zb, b_sum)):
        for k in ks:
            buf[k - 1] = whole[pl.ds(k * wide, wide), :]
        line.begin()
    send_home(tg, tg_out, t_s, t_r, n_col)
    for i in range(1, len(partners)):
        small_step(i)
    hidden1[part] = q_own[...]
    spread_q(0).start()
    spread_q(1).start()
    for d in range(n_col - 2, 0, -1):
        line_a.go(d)
        line_b.go(d)
    small_step(len(partners))
    for i, (line, whole, full, spread) in enumerate((
        (line_a, a_sum, full_a, spread_a), (line_b, b_sum, full_b, spread_b),
    )):
        value = line.total(whole[pl.ds(0, wide), :].astype(f32))
        value = with_other_bits(value, extra, i, x_s, x_r, by_bit[2:])
        full[part] = value.astype(low)
        spread(0).start()
        spread(1).start()
    for spread in spreads:
        for stage in range(2):
            spread(stage).wait_recv()
            spread(2 + stage).start()
    small_step(len(partners) + 1)
    for spread in spreads:
        spread(2).wait_recv()
        spread(3).wait_recv()
        for stage in range(4):
            spread(stage).wait_send()
    line_a.end()
    line_b.end()
    for k in ks:
        small_z(k).wait_send()
    for i in range(len(partners)):
        small_hop(i).wait_send()
    wait_home(tg, tg_out, t_s, t_r, n_col)


def finish(a_sum, b_sum, q_own, small, tg, n_col, n_dp):
    columns = a_sum.shape[1]
    wide, hidden = q_own.shape
    steps = n_dp.bit_length()
    sd, vm, dma = jax.ShapeDtypeStruct, pltpu.VMEM, pltpu.SemaphoreType.DMA
    more = max(n_dp.bit_length() - 3, 1)
    others = n_col - 1
    return pl.pallas_call(
        functools.partial(finish_kernel, n_col=n_col, n_dp=n_dp),
        in_specs=[IN_VMEM] * 5,
        out_specs=[IN_VMEM] * 4 + [ANYWHERE],
        out_shape=[
            sd((PARTS, wide, columns), low),
            sd((PARTS, wide, columns), low),
            sd((PARTS, wide, hidden), low),
            sd(small.shape[1:], f32),
            sd((n_col * tg.shape[0], wide), low),
        ],
        scratch_shapes=[
            *[vm((others, wide, columns), low)] * 6,
            vm((steps + 1,) + small.shape, f32),
            vm((steps,) + small.shape, f32),
            vm((others,) + small.shape[1:], f32),
            vm((more, 3, wide, columns), low),
            *[dma((2, others))] * 4,
            dma((3, 4)), dma((3, 4)),
            dma((steps,)), dma((steps,)),
            dma((others,)), dma((others,)),
            dma((n_col,)), dma((n_col,)),
            dma((2, more)), dma((2, more)),
        ],
        compiler_params=pltpu.CompilerParams(
            collective_id=20, has_side_effects=True, vmem_limit_bytes=VMEM
        ),
        name="finish",
    )(a_sum, b_sum, q_own, small, tg)


def column_grads_kernel(*refs, pairs, firsts):
    count = len(pairs)
    firsts_refs, others = refs[:firsts], refs[firsts : firsts + count]
    out, sums = refs[firsts + count :]
    size = out.shape[2] // count
    for i, (which, begin) in enumerate(pairs):
        a, b = firsts_refs[which], others[i]
        value = mm_tn(a[pl.ds(begin, b.shape[0]), :], b[...]).astype(low)
        for p in range(out.shape[0]):
            out[p, :, i * size : (i + 1) * size] = value[:, p * size : (p + 1) * size]

    @pl.when(pl.program_id(0) == 0)
    def _():
        for i in range(count):
            sums[i : i + 1, :] = jnp.sum(others[i][...].astype(f32), axis=0, keepdims=True)


def column_grads_of(firsts, pairs, others):
    deep, width = firsts[0].shape[1], others[0].shape[1]
    block = 256
    return pl.pallas_call(
        functools.partial(column_grads_kernel, pairs=pairs, firsts=len(firsts)),
        grid=(deep // block,),
        in_specs=[pl.BlockSpec((x.shape[0], block), lambda i: (0, i)) for x in firsts]
        + [pl.BlockSpec(x.shape, lambda i: (0, 0)) for x in others],
        out_specs=[
            pl.BlockSpec((PARTS, block, width), lambda i: (0, i, 0)),
            pl.BlockSpec((8, width), lambda i: (0, 0)),
        ],
        out_shape=[
            jax.ShapeDtypeStruct((PARTS, deep, width), low),
            jax.ShapeDtypeStruct((8, width), f32),
        ],
        compiler_params=pltpu.CompilerParams(vmem_limit_bytes=VMEM),
        name="column_grads",
    )(*firsts, *others)


def unpack_kernel(full_a, full_b, hidden0, hidden1, rows, *outs):
    size = full_a.shape[2] // 4
    for g, full in enumerate((full_a, full_b)):
        for i in range(4):
            value = full[0, :, i * size : (i + 1) * size].astype(f32)
            outs[4 * g + i][...] = value if i < 3 else jnp.transpose(value)
    outs[8][...] = hidden0[0].astype(f32)
    outs[9][...] = jnp.transpose(hidden1[0].astype(f32))
    outs[10][...] = rows[...].astype(f32)


def unpack(full_a, full_b, hidden0, hidden1, rows):
    parts, wide, columns = full_a.shape
    inner = hidden0.shape[2]
    size = columns // 4
    into = (pl.BlockSpec((wide, size), lambda p: (0, p)), (wide, parts * size))
    out_of = (pl.BlockSpec((size, wide), lambda p: (p, 0)), (parts * size, wide))
    layouts = [into, into, into, out_of] * 2 + [
        (pl.BlockSpec((wide, inner), lambda p: (0, p)), (wide, parts * inner)),
        (pl.BlockSpec((inner, wide), lambda p: (p, 0)), (parts * inner, wide)),
    ]
    by_rows = pl.BlockSpec((rows.shape[0] // parts, wide), lambda p: (p, 0))
    layouts.append((by_rows, rows.shape))
    return pl.pallas_call(
        unpack_kernel,
        grid=(parts,),
        in_specs=[
            pl.BlockSpec((1, wide, x.shape[2]), lambda p: (p, 0, 0))
            for x in (full_a, full_b, hidden0, hidden1)
        ]
        + [by_rows],
        out_specs=[x[0] for x in layouts],
        out_shape=[jax.ShapeDtypeStruct(x[1], f32) for x in layouts],
        compiler_params=pltpu.CompilerParams(vmem_limit_bytes=VMEM),
        name="unpack",
    )(full_a, full_b, hidden0, hidden1, rows)


def build_local(mesh):
    n_dp, n_col = mesh.shape["dp"], mesh.shape["col"]

    def from_col(x, k):
        return lax.ppermute(x, "col", [(i, (i - k) % n_col) for i in range(n_col)])

    def across(x, bit):
        return lax.ppermute(x, "dp", [(i, i ^ bit) for i in range(n_dp)])

    def local(
        tokens, encoder, cotangent, dec_lengths, src_lengths,
        self_norm_gain, self_norm_bias, self_query, self_key, self_value,
        self_query_bias, self_value_bias, self_out, self_out_bias,
        cross_norm_gain, cross_norm_bias, cross_query, cross_key, cross_value,
        cross_query_bias, cross_value_bias, cross_out, cross_out_bias,
        hidden_norm_gain, hidden_norm_bias, hidden_in, hidden_in_bias,
        hidden_out, hidden_out_bias,
    ):
        row, col = lax.axis_index("row"), lax.axis_index("col")
        place = lax.axis_index("dp") % PARTS
        wide = tokens.shape[1]
        chunk = tokens.shape[0] // n_col
        span = 2 * chunk

        def in_order(parts):
            stacked = jnp.stack(parts)
            return [
                lax.dynamic_index_in_dim(stacked, i ^ place, 0, keepdims=False)
                for i in range(PARTS)
            ]

        def own_columns(w, j):
            size = w.shape[1] // PARTS
            return lax.dynamic_slice_in_dim(w, (place ^ j) * size, size, 1)

        def along_col(w):
            return [from_col(own_columns(w, 0), k) for k in range(1, n_col)]

        vec_f = jnp.stack([
            self_norm_gain, self_norm_bias, self_out_bias, cross_norm_gain, cross_norm_bias,
            cross_out_bias, hidden_norm_gain, hidden_norm_bias, hidden_out_bias,
        ])
        vec_f = jnp.pad(vec_f, ((0, 7), (0, 0)))
        vec_c = jnp.concatenate(
            [self_query_bias, self_value_bias, cross_query_bias, cross_value_bias, hidden_in_bias]
        ).reshape(-1, 128)
        vec_c = jnp.pad(vec_c, ((0, -vec_c.shape[0] % 8), (0, 0)))
        weights = [
            self_query, self_key, self_value, self_out,
            cross_query, cross_key, cross_value, cross_out,
        ]
        x_ext, enc, vectors, columns, *full = start(tokens, encoder, vec_f, vec_c, weights, n_col)
        wq1, wk1, wv1, wo1, wq2, wk2, wv2, wo2 = full
        (gain1, shift1, out_bias1, gain2, shift2, out_bias2, gain3, shift3, out_bias3) = vectors[:9]
        size = self_query_bias.shape[0]

        def column_vector(start, size):
            return columns.reshape(n_col, -1)[:, start : start + size].reshape(-1)

        q_bias1 = column_vector(0, size)
        v_bias1 = column_vector(size, size)
        q_bias2 = column_vector(2 * size, size)
        v_bias2 = column_vector(3 * size, size)
        hidden_bias = column_vector(4 * size, hidden_in_bias.shape[0]).reshape(PARTS, -1)
        hidden_bias = jnp.stack(
            [lax.dynamic_index_in_dim(hidden_bias, place ^ j, 0) for j in range(PARTS)]
        )

        hidden_in, x_ext = lax.optimization_barrier((hidden_in, x_ext))
        hidden_out_t = hidden_out.T
        pieces1 = along_col(hidden_in)

        dec_ids = doc_numbers(dec_lengths, SEQ_LEN)[0]
        src_ids = doc_numbers(src_lengths, ENC)[0]
        padded = jnp.pad(dec_ids, (WIN, 0), constant_values=-1)
        key_ids = lax.dynamic_slice_in_dim(padded, col * span, WIN + span, 0)
        query_ids = key_ids[WIN:]

        scale = low(HEAD_DIM**-0.5)
        x0 = x_ext[1]
        a_ext = enter(x_ext, gain1, shift1, 2).reshape(WIN + span, -1)
        a = a_ext[WIN:]
        hidden_out_t, a_ext = lax.optimization_barrier((hidden_out_t, a_ext))
        pieces2 = along_col(hidden_out_t)
        q1 = (mm(a, wq1) + q_bias1).astype(low) * scale
        k1 = mm(a_ext, wk1).astype(low)
        v1 = (mm(a_ext, wv1) + v_bias1).astype(low)
        dma = pltpu.SemaphoreType.DMA
        dma = pltpu.SemaphoreType.DMA
        o1, lse1 = attend(q1, k1, v1, query_ids, key_ids, True)
        pieces1, o1 = lax.optimization_barrier((pieces1, o1))
        rest1 = jnp.concatenate(pieces1, axis=0)
        near1 = [across(rest1, 1), across(rest1, 2)]
        x1, c, q2 = junction(
            "forward", [("nn", o1, wo1)], [x0, out_bias1, gain2, shift2], 3,
            ("queries", wq2, q_bias2),
        )

        pieces2, q2 = lax.optimization_barrier((pieces2, q2))
        rest2 = jnp.concatenate(pieces2, axis=0)
        near2 = [across(rest2, 1), across(rest2, 2)]
        k2 = mm(enc, wk2).astype(low)
        v2 = (mm(enc, wv2) + v_bias2).astype(low)
        o2, lse2 = attend(q2, k2, v2, query_ids, src_ids, False)
        near1, o2 = lax.optimization_barrier((near1, o2))
        far1 = across(near1[0], 2)
        x2, f = junction("forward", [("nn", o2, wo2)], [x1, out_bias2, gain3, shift3], 4)
        rests1, rests2 = [rest1, *near1], [rest2, *near2]
        act0, slope0, part_sum = hidden_forward(
            f, hidden_bias[:1], hidden_in, hidden_out_t, rests1[:1], rests2[:1], (0,), 0
        )
        near2, part_sum = lax.optimization_barrier((near2, part_sum))
        far2 = across(near2[1], 1)
        rests1, rests2 = [rest1, *near1, far1], [rest2, *near2, far2]
        act1, slope1, dz, part_sum = hidden_forward(
            f, hidden_bias[1:3], hidden_in, hidden_out_t, rests1[1:3], rests2[1:3], (1, 2), 14,
            sum_in=part_sum, cotangent=cotangent, n_col=n_col,
        )
        act2, slope2, rows_out = hidden_forward(
            f, hidden_bias[3:], hidden_in, hidden_out_t, rests1[3:], rests2[3:], (3,), 5,
            sum_in=part_sum, x=x2, bias=out_bias3,
        )
        dz = dz.reshape(span, -1)

        g1, g2, hidden_bias_grad, df, got_a, got_b, layer_out, far_a, far_b = hidden_backward(
            dz, f, hidden_in, hidden_out_t, rests1, rests2, [act0, act1, act2],
            [slope0, slope1, slope2], ((0, 0), (1, 0), (1, 1), (2, 0)), rows_out, n_col, 11,
        )
        inner = g1.shape[2]
        half = g1.shape[1] // 2
        one = ((half, inner), low)
        dx2, dyc, stats3, doc = junction(
            "backward", [("sum", df)], [dz, x2, gain3], 6, ("turned", wo2, gain3)
        )

        later = ((half, inner - far_a.shape[1]), low)
        dq2, dk2, dv2, back_a, back_b, far_c, far_d = attend_back(
            q2, k2, v2, doc, o2, lse2, query_ids, src_ids, False,
            first_rider, [g1, g2, got_a, got_b], [one] * 2 + [later] * 2,
            [
                pltpu.VMEM((4, half, inner), low), pltpu.VMEM((2, half, inner), low),
                dma((4,)), dma((4,)), dma((4,)),
            ],
            12,
        )
        cross_grads, cross_columns = column_grads_of(
            [c, enc, dyc], [(0, 0), (1, 0), (1, 0), (2, 0)], [dq2, dk2, dv2, o2]
        )
        enc_back = junction("sum", [("nt", dk2, wk2), ("nt", dv2, wv2)], [], 7)
        dx1, dy, stats2, do = junction(
            "backward", [("nt", dq2, wq2)], [dx2, x1, gain2], 8, ("turned", wo1, gain2)
        )

        cross_grads, enc_back, do = lax.optimization_barrier((cross_grads, enc_back, do))
        (
            dq1, dk1, dv1, near_a, near_b, far_back_a, far_back_b, own1
        ) = attend_back(
            q1, k1, v1, do, o1, lse1, query_ids, key_ids, True,
            functools.partial(second_rider, n_col=n_col),
            [g1, g2, got_a, got_b, back_a, back_b, far_a, far_b, far_c, far_d],
            [one] * 4 + [((wide, inner), low)],
            [
                pltpu.VMEM((4, half, inner), low), pltpu.VMEM((2, half, inner), low),
                pltpu.VMEM((3, 2 * half, inner), low), pltpu.VMEM((n_col - 1, wide, inner), low),
                pltpu.VMEM((wide, inner), low), pltpu.VMEM((n_col - 1, wide, inner), low),
                pltpu.VMEM((n_col - 1, wide, inner), low),
                dma((6,)), dma((2, 3)), dma((4,)), dma((4,)),
                dma((2, n_col - 1)), dma((2, n_col - 1)), dma,
            ],
            13,
        )
        self_columns, x0_grad, stats1, a_sum, b_sum, hidden0, q_own, encoder_grad = fold(
            dq1, dk1, dv1, a_ext, dy, o1, [wq1, wk1, wv1], dx1, x0, gain1, cross_grads, enc_back,
            [g2, near_a, near_b, far_back_a, far_back_b, own1], n_col, n_dp,
        )

        feature_grads = jnp.concatenate([
            stats1[:2], stats2[2:3], stats2[:2], stats3[2:3], stats3[:2], stats3[3:4],
        ])
        feature_grads = jnp.moveaxis(feature_grads.reshape(-1, n_col, wide), 1, 0)
        column_grads = []
        for vector in (self_columns[0], self_columns[2], cross_columns[0], cross_columns[2]):
            column_grads.append(vector.reshape(n_col, -1))
        column_grads.append(
            jnp.stack(in_order([hidden_bias_grad[j] for j in range(PARTS)])).reshape(n_col, -1)
        )
        column_grads = jnp.concatenate(column_grads, axis=1).reshape(n_col, -1, 128)
        column_grads = lax.dynamic_slice_in_dim(
            jnp.concatenate([column_grads, column_grads]), col, n_col, 0
        )
        lines = -(-max(feature_grads.shape[1], column_grads.shape[1]) // 8) * 8
        small = jnp.concatenate(
            [
                jnp.pad(x, ((0, 0), (0, lines - x.shape[1]), (0, 0)))
                for x in (feature_grads, column_grads)
            ],
            axis=2,
        )
        full_a, full_b, hidden1, small, tokens_grad = finish(
            a_sum, b_sum, q_own, small, x0_grad, n_col, n_dp
        )
        grads = unpack(full_a, full_b, hidden0, hidden1, tokens_grad)
        tokens_grad = grads[10]
        feature_grads = small[:, :wide]
        column_grads = small[:, wide:].reshape(-1)

        return (
            layer_out,
            tokens_grad,
            encoder_grad,
            feature_grads[0],
            feature_grads[1],
            grads[4],
            grads[5],
            grads[6],
            column_grads[:size],
            column_grads[size : 2 * size],
            grads[7],
            feature_grads[2],
            feature_grads[3],
            feature_grads[4],
            grads[0],
            grads[1],
            grads[2],
            column_grads[2 * size : 3 * size],
            column_grads[3 * size : 4 * size],
            grads[3],
            feature_grads[5],
            feature_grads[6],
            feature_grads[7],
            grads[8],
            column_grads[4 * size : 4 * size + hidden_in_bias.shape[0]],
            grads[9],
            feature_grads[8],
        )

    return local


def solution(mesh):
    rows = P(("dp", "row"), "col")
    features = P("col")
    columns = P(("row", "col"))
    into, out_of = P("col", "row"), P("row", "col")
    attention = (into, into, into, columns, columns, out_of, features)
    norm = (features, features)
    weights = (
        norm
        + attention
        + norm
        + attention
        + norm
        + (into, columns, out_of, features)
    )
    return jax.shard_map(
        build_local(mesh),
        mesh=mesh,
        in_specs=(rows, rows, rows, P("dp", None), P("dp", None)) + weights,
        out_specs=(rows, rows, rows) + weights,
        check_vma=False,
    )
```
